32 devices in a mesh: expert: 8 (over z, x), tensor: 4 (over y, core).
Axes of the slice: x: 2, y: 2, z: 4, core: 2. Of those that a mesh axis runs over, the one named last changes fastest.
Arguments:
- tokens: bfloat16 [4096, 2048], P('expert'), may hold values from -6 to 6
- documents: int32 [4096], P('expert'), may hold values from 0 to 4095, as said below
- routes: int32 [4096, 8], P('expert'), may hold values from 0 to 15, all different within a row; in each aligned block of 512 rows (0 to 511, 512 to 1023, ...) at most 512 rows name the same one
- norm1_gain: float32 [2048], replicated, may hold values from 0.1 to 1.9
- q_gain: float32 [16, 128], P('tensor'), may hold values from 0.1 to 1.9
- k_gain: float32 [16, 128], P('tensor'), may hold values from 0.1 to 1.9
- w_query: bfloat16 [2048, 2048], P(None, 'tensor'), may hold values from -0.125 to 0.125
- w_key: bfloat16 [2048, 2048], P(None, 'tensor'), may hold values from -0.125 to 0.125
- w_value: bfloat16 [2048, 2048], P(None, 'tensor'), may hold values from -0.125 to 0.125
- w_out: bfloat16 [2048, 2048], P('tensor'), may hold values from -2 to 2
- norm2_gain: float32 [2048], replicated, may hold values from 0.1 to 1.9
- router_w: bfloat16 [2048, 16], replicated, may hold values from -0.0625 to 0.0625
- w_gate: bfloat16 [16, 2048, 1024], P('expert', None, 'tensor'), may hold values from -0.125 to 0.125
- w_up: bfloat16 [16, 2048, 1024], P('expert', None, 'tensor'), may hold values from -0.125 to 0.125
- w_down: bfloat16 [16, 1024, 2048], P('expert', 'tensor'), may hold values from -1.5 to 1.5
- out_grad: bfloat16 [4096, 2048], P('expert'), may hold values from -6 to 6
Outputs:
- output: bfloat16 [4096, 2048], P('expert')
- input_grad: float32 [4096, 2048], P('expert')
- norm1_gain_grad: float32 [2048], P('expert')
- q_gain_grad: float32 [16, 128], P('tensor', 'expert')
- k_gain_grad: float32 [16, 128], P('tensor', 'expert')
- w_query_grad: float32 [2048, 2048], P('expert', 'tensor')
- w_key_grad: float32 [2048, 2048], P('expert', 'tensor')
- w_value_grad: float32 [2048, 2048], P('expert', 'tensor')
- w_out_grad: float32 [2048, 2048], P('tensor', 'expert')
- norm2_gain_grad: float32 [2048], P('expert')
- router_grad: float32 [2048, 16], P('expert')
- w_gate_grad: float32 [16, 2048, 1024], P('expert', None, 'tensor')
- w_up_grad: float32 [16, 2048, 1024], P('expert', None, 'tensor')
- w_down_grad: float32 [16, 1024, 2048], P('expert', 'tensor')
The draws below stay inside these ranges and needn't reach their ends.
Inputs may be any that keep to these rules, and one draw needn't show every extreme that they name: `documents`: document numbers never fall; those of the tokens s * 2048 to s * 2048 + 2047 lie in s * 2048 to s * 2048 + 2047, so that no document crosses the end of a sequence; in one sequence a single document fills it. `routes`: A token's 8 experts differ. Among the picks of the 512 tokens of one index of the expert axis (aligned blocks of 512 tokens) no expert is named more than 512 times, and in every draw some expert is named exactly 512 times.
All inputs are finite; a program needn't handle non-finite values.
Results may differ from the reference program's by a relative error of at most 0.023.
Values may be sent and summed in bfloat16 or wider, within the bound.
A program may use at most 448 MiB of HBM per device.

```python
import math
import jax
import jax.numpy as jnp
import numpy as np
from jax import lax

D = 2048
HEADS = 16
HD = 128
FF = 1024
TOP = 8
WINDOW = 1024
EXPERTS = 16
TOK_DEV = 512
LENGTH = 2048
TOKENS = 4096
CAP = 512
N_TENSOR = 4


def draw_documents(key, part):
    key = jax.random.fold_in(key, 7)
    cut_key, whole_key = jax.random.split(key)
    sequences = TOKENS // LENGTH
    cut_flags = (jax.random.randint(cut_key, (sequences, LENGTH), 0, max(LENGTH // 3, 2)) == 0).astype(jnp.int32)
    inside = (jnp.arange(LENGTH) > 0).astype(jnp.int32)
    whole_sequence = jax.random.randint(whole_key, (), 0, sequences)
    keep_flags = (jnp.arange(sequences) != whole_sequence).astype(jnp.int32)
    cut_flags = cut_flags * inside[None, :] * keep_flags[:, None]
    counted = jnp.cumsum(cut_flags, axis=1)
    starts = jnp.arange(sequences, dtype=jnp.int32)[:, None] * LENGTH
    upward = starts + counted
    downward = starts + (LENGTH - 1) - (counted[:, -1:] - counted)
    last_row = (jnp.arange(sequences) == sequences - 1)[:, None]
    numbers = jnp.where(last_row, downward, upward)
    return numbers.reshape(-1).astype(jnp.int32)


def steps_of(rng, dims, cuts, smallest, largest):
    def one(position, parts):
        steps = jax.random.uniform(jax.random.fold_in(jax.random.fold_in(rng, 6), position), (parts,), jnp.float32, smallest / len(cuts), largest / len(cuts))
        return jnp.repeat(jnp.exp(steps), dims[position] // parts).reshape((-1,) + (1,) * (len(dims) - position - 1))

    level = one(*cuts[0])
    for cut in cuts[1:]:
        level = level * one(*cut)
    return level


def assign_block(own_key, own, number, rows, amount, top, most, slope):
    ranking = jax.random.permutation(own_key, amount)
    heavy_load, common = shares(amount, rows * top, most, slope, True), shares(amount, rows * top, most, slope, False)
    places = jnp.arange(amount)

    def named(lengths, rotation):
        used = int((lengths > 0).sum())
        fixed = max(1, used // 4)
        shifted = fixed + (places - fixed + rotation * (used - fixed)) % max(1, amount - fixed)
        return jnp.zeros((amount,), jnp.int32).at[ranking[jnp.where(places < fixed, places, shifted)]].set(jnp.asarray(lengths, jnp.int32))

    lengths = jnp.where(number % 4 == 0, named(heavy_load, number // 4), named(common, number - number // 4 - 1))
    mixed = jax.random.permutation(jax.random.fold_in(own, 3), amount)
    giver, receiver = mixed[0:amount // 2 * 2:2], mixed[1:amount // 2 * 2:2]
    slack = jnp.minimum(lengths[giver] - 1, most - lengths[receiver]) // 2
    slack = jnp.where((giver == ranking[0]) | (receiver == ranking[0]) | (lengths[receiver] == 0), 0, jnp.maximum(slack, 0))
    shifted = jax.random.randint(jax.random.fold_in(own, 4), (amount // 2,), 0, 1 << 20) % (slack + 1)
    lengths = lengths.at[giver].add(-shifted).at[receiver].add(shifted)
    members = jnp.searchsorted(jnp.cumsum(lengths), jnp.arange(rows * top), side="right").astype(jnp.int32)
    grid = members.reshape(top, rows).T
    grid = grid[jax.random.permutation(jax.random.fold_in(own, 1), rows)]
    rotation = jax.random.randint(jax.random.fold_in(own, 2), (rows, 1), 0, top)
    return jnp.take_along_axis(grid, (jnp.arange(top)[None, :] + rotation) % top, axis=1)


def shares(amount, total, limit, lean, full):
    loads = [(1 << 20) // math.isqrt(rank ** lean) + 1 for rank in range(1, amount + 1)]
    largest = limit if full else min(limit, max(-(-total // amount), total * loads[0] // sum(loads)))
    least = 1 if total - largest >= amount - 1 else 0
    given, rest = [largest] + [least] * (amount - 1), total - largest - least * (amount - 1)
    while rest > 0:
        movable = [i for i in range(1, amount) if given[i] < largest] or [i for i in range(1, amount) if given[i] < limit]
        mass, left = sum([loads[i] for i in movable]), rest
        for i in movable:
            addition = min(limit - given[i], max(1, left * loads[i] // mass), rest)
            given[i] = given[i] + addition
            rest = rest - addition
    return np.array(given)


def centred(key, shape, scale, limit, cuts=(), kind=jnp.bfloat16):
    values = jax.random.normal(key, shape, jnp.float32) * scale
    if len(cuts) > 0:
        values = steps_of(key, shape, cuts, -0.22, 0.18) * values
    return jnp.clip(values, min=-limit, max=limit).astype(kind)


def setup_inputs(seed: int = 0) -> dict:
    arg_keys = jax.random.split(jax.random.key(seed), 17)
    tokens = centred(arg_keys[0], (TOKENS, D), 1.0, 6.0, ((0, 8),))
    documents = draw_documents(jax.random.fold_in(arg_keys[16], 71), 0)
    routes_keys = jax.random.split(jax.random.fold_in(arg_keys[2], 1), TOKENS // TOK_DEV)
    routes_turns = jax.random.permutation(jax.random.fold_in(arg_keys[2], 3), TOKENS // TOK_DEV)
    routes = jax.vmap(lambda own, number: assign_block(jax.random.fold_in(arg_keys[2], 2), own, number, TOK_DEV, EXPERTS, TOP, CAP, 1))(routes_keys, routes_turns).reshape((TOKENS, TOP))
    norm1_gain = jnp.clip(1.0 + 0.18 * jax.random.normal(arg_keys[3], (D,), jnp.float32), 0.1, 1.9)
    q_gain = jnp.clip(1.0 + 0.18 * jax.random.normal(arg_keys[4], (HEADS, HD), jnp.float32), 0.1, 1.9)
    k_gain = jnp.clip(1.0 + 0.18 * jax.random.normal(arg_keys[5], (HEADS, HD), jnp.float32), 0.1, 1.9)
    w_query = centred(arg_keys[6], (D, D), D ** -0.5, 0.125, ((1, 4),))
    w_key = centred(arg_keys[7], (D, D), D ** -0.5, 0.125, ((1, 4),))
    w_value = centred(arg_keys[8], (D, D), D ** -0.5, 0.125, ((1, 4),))
    w_out = centred(arg_keys[9], (D, D), (max(1, D // 256)) ** -0.5, 2.0, ((0, 4),))
    norm2_gain = jnp.clip(1.0 + 0.18 * jax.random.normal(arg_keys[10], (D,), jnp.float32), 0.1, 1.9)
    router_w = centred(arg_keys[11], (D, EXPERTS), (4 * D) ** -0.5, 0.0625)
    w_gate = centred(arg_keys[12], (EXPERTS, D, FF), D ** -0.5, 0.125, ((0, 8), (2, 4)))
    w_up = centred(arg_keys[13], (EXPERTS, D, FF), D ** -0.5, 0.125, ((0, 8), (2, 4)))
    w_down = centred(arg_keys[14], (EXPERTS, FF, D), (max(1, FF * 4 // (EXPERTS * EXPERTS))) ** -0.5, 1.5, ((0, 8), (1, 4)))
    out_grad = centred(arg_keys[15], (TOKENS, D), 1.0, 6.0, ((0, 8),))
    return dict(tokens=tokens, documents=documents, routes=routes, norm1_gain=norm1_gain, q_gain=q_gain, k_gain=k_gain, w_query=w_query, w_key=w_key, w_value=w_value, w_out=w_out, norm2_gain=norm2_gain, router_w=router_w, w_gate=w_gate, w_up=w_up, w_down=w_down, out_grad=out_grad)


NORM_EPSILON = 1e-05
HIGHEST_PRECISION = lax.Precision.HIGHEST

@jax.custom_vjp
def low(v):
    return lax.optimization_barrier(v.astype(jnp.bfloat16)).astype(jnp.float32)

@jax.custom_vjp
def low_back(v):
    return v

def low_keep(v):
    return (low(v), None)

def low_pass(kept, grad):
    return (grad,)

def back_keep(v):
    return (v, None)

def back_low(kept, grad):
    return (low(grad),)
low.defvjp(low_keep, low_pass)
low_back.defvjp(back_keep, back_low)

def product(left, right):
    return jnp.dot(left, right, precision=HIGHEST_PRECISION, preferred_element_type=jnp.float32)

def rms_norm(values, gain):
    factor = lax.rsqrt(lax.optimization_barrier(jnp.mean(values * values, axis=-1, keepdims=True)) + NORM_EPSILON)
    return values * factor * gain

def rope_tables(positions):
    half_width = HD // 2
    frequency = 10000.0 ** (-jnp.arange(half_width, dtype=jnp.float32) * 2.0 / HD)
    angles = positions.astype(jnp.float32)[:, None] * frequency[None, :]
    angles = jnp.concatenate([angles, angles], axis=-1)
    return (jnp.cos(angles)[:, None, :], jnp.sin(angles)[:, None, :])

def rotate(values, cosine, sine):
    half_width = values.shape[-1] // 2
    turned = jnp.concatenate([-values[..., half_width:], values[..., :half_width]], axis=-1)
    return values * cosine + turned * sine

def slot_tables(routes):
    blocks = TOKENS // TOK_DEV
    flat_routes = routes.reshape(blocks, TOK_DEV * TOP)
    onehot = (flat_routes[:, :, None] == jnp.arange(EXPERTS, dtype=jnp.int32)[None, None, :]).astype(jnp.int32)
    slot_index = lax.optimization_barrier(jnp.sum(jnp.cumsum(onehot, axis=1) * onehot, axis=2)) - 1
    target = flat_routes * (blocks * CAP) + jnp.arange(blocks, dtype=jnp.int32)[:, None] * CAP + slot_index
    picks = jnp.arange(TOKENS * TOP, dtype=jnp.int32)
    source = jnp.full((EXPERTS * blocks * CAP,), -1, jnp.int32).at[target.reshape(-1).astype(jnp.int32)].set(picks)
    return source.reshape(EXPERTS, blocks * CAP)

def sequence_attention(operand):
    queries, key_heads, value_heads, documents = operand
    block_rows = min(512, LENGTH)
    key_pos = jnp.arange(LENGTH, dtype=jnp.int32)
    score_scale = HD ** (-0.5)

    def query_block(start):
        block_query = lax.dynamic_slice_in_dim(queries, start, block_rows, 0)
        block_docs = lax.dynamic_slice_in_dim(documents, start, block_rows, 0)
        row_pos = start + jnp.arange(block_rows, dtype=jnp.int32)
        allowed = (block_docs[:, None] == documents[None, :]) & (key_pos[None, :] <= row_pos[:, None]) & (row_pos[:, None] - key_pos[None, :] < WINDOW)
        scores = low_back(jnp.einsum('qhd,khd->hqk', block_query, key_heads, precision=HIGHEST_PRECISION) * score_scale)
        masked = jnp.where(allowed[None], scores, -1e+30)
        highest = lax.optimization_barrier(jnp.max(masked, axis=-1, keepdims=True))
        weights = jnp.where(allowed[None], jnp.exp(masked - highest), 0.0)
        attn_probs = weights / lax.optimization_barrier(jnp.sum(weights, axis=-1, keepdims=True))
        attended = jnp.einsum('hqk,khd->qhd', low(attn_probs), value_heads, precision=HIGHEST_PRECISION)
        return low(low_back(attended))
    starts = (jnp.arange(LENGTH // block_rows, dtype=jnp.int32) * block_rows).astype(jnp.int32)
    blocks_out = lax.map(jax.checkpoint(query_block), starts)
    return blocks_out.reshape(LENGTH, HEADS, HD)

def layer_forward(inputs, gain_one, gain_query, gain_key, w_query, w_key, w_value, w_out, gain_two, w_router, w_gate, w_up, w_down, documents, routes, source):
    sequences = TOKENS // LENGTH
    normed_one = low(rms_norm(inputs, gain_one))
    query_raw = low_back(product(normed_one, w_query))
    key_raw = low_back(product(normed_one, w_key))
    values = low(low_back(product(normed_one, w_value)))
    query_norm = rms_norm(query_raw, gain_query.reshape(-1))
    key_norm = rms_norm(key_raw, gain_key.reshape(-1))
    cosine, sine = rope_tables(jnp.arange(TOKENS, dtype=jnp.int32) % LENGTH)
    queries = low(rotate(query_norm.reshape(TOKENS, HEADS, HD), cosine, sine))
    key_heads = low(rotate(key_norm.reshape(TOKENS, HEADS, HD), cosine, sine))
    shaped = (queries.reshape(sequences, LENGTH, HEADS, HD), key_heads.reshape(sequences, LENGTH, HEADS, HD), values.reshape(sequences, LENGTH, HEADS, HD), documents.reshape(sequences, LENGTH))
    attended = lax.map(jax.checkpoint(sequence_attention), shaped).reshape(TOKENS, D)
    state = inputs + low_back(product(attended, w_out))
    normed_two = low(rms_norm(state, gain_two))
    router_probs = jax.nn.softmax(product(normed_two, w_router), axis=-1)
    gates = jnp.take_along_axis(router_probs, routes, axis=1).reshape(-1)
    part_width = FF // N_TENSOR

    def expert_step(mixture, operand):
        slots, gate_weight, up_weight, down_weight = operand
        live_slot = (slots >= 0).astype(jnp.float32)
        picks = jnp.maximum(slots, 0)
        token_index = picks // TOP
        rows_in = normed_two[token_index] * live_slot[:, None]
        slot_gates = gates[picks] * live_slot
        produced = jnp.zeros((slots.shape[0], D), jnp.float32)
        for part_index in range(N_TENSOR):
            lower = part_index * part_width
            part_in = low_back(rows_in)
            gate_pre = low_back(product(part_in, gate_weight[:, lower:lower + part_width]))
            up_pre = low_back(product(part_in, up_weight[:, lower:lower + part_width]))
            inner_act = low(jax.nn.silu(gate_pre) * up_pre)
            produced = produced + low(low_back(product(inner_act, down_weight[lower:lower + part_width, :])))
        return (mixture.at[token_index].add(produced * slot_gates[:, None]), None)
    mixture, unused = lax.scan(jax.checkpoint(expert_step), jnp.zeros((TOKENS, D), jnp.float32), (source, w_gate, w_up, w_down))
    return state + mixture

def reference(tokens, documents, routes, norm1_gain, q_gain, k_gain, w_query, w_key, w_value, w_out, norm2_gain, router_w, w_gate, w_up, w_down, out_grad):
    source = slot_tables(routes)

    def forward(inputs, gain_one, gain_query, gain_key, query_w, key_w, value_w, out_w, gain_two, routing_w, gate_w, up_w, down_w):
        return layer_forward(inputs, gain_one, gain_query, gain_key, query_w, key_w, value_w, out_w, gain_two, routing_w, gate_w, up_w, down_w, documents, routes, source)
    result, pullback = jax.vjp(forward, tokens.astype(jnp.float32), norm1_gain.astype(jnp.float32), q_gain.astype(jnp.float32), k_gain.astype(jnp.float32), w_query.astype(jnp.float32), w_key.astype(jnp.float32), w_value.astype(jnp.float32), w_out.astype(jnp.float32), norm2_gain.astype(jnp.float32), router_w.astype(jnp.float32), w_gate.astype(jnp.float32), w_up.astype(jnp.float32), w_down.astype(jnp.float32))
    gradients = pullback(out_grad.astype(jnp.float32))
    return (result.astype(jnp.bfloat16), gradients[0], gradients[1], gradients[2], gradients[3], gradients[4], gradients[5], gradients[6], gradients[7], gradients[8], gradients[9], gradients[10], gradients[11], gradients[12])
```

```python
import functools

import jax
import jax.numpy as jnp
from jax import lax
from jax.experimental import pallas as pl
from jax.experimental.pallas import tpu as pltpu
from jax.sharding import PartitionSpec as P

HD = 128
TOP = 8
WINDOW = 1024
LENGTH = 2048


NORM_EPSILON = 1e-05
HIGHEST_PRECISION = lax.Precision.HIGHEST


def for_sending(value):
    return jax.tree.map(lambda a: a.astype(jnp.bfloat16) if a.dtype == jnp.float32 else a, value)


def shifted(value, axis, steps):
    count = lax.axis_size(axis)
    initial, last = (max(0, -steps), min(count, count - steps))
    return lax.ppermute(value, axis, [(source, source + steps) for source in range(initial, last)])


def rope_tables(positions):
    half_width = HD // 2
    frequency = 10000.0 ** (-jnp.arange(half_width, dtype=jnp.float32) * 2.0 / HD)
    angles = positions.astype(jnp.float32)[:, None] * frequency[None, :]
    angles = jnp.concatenate([angles, angles], axis=-1)
    return (jnp.cos(angles)[:, None, :], jnp.sin(angles)[:, None, :])


def rotate(values, cosine, sine):
    half_width = values.shape[-1] // 2
    turned = jnp.concatenate([-values[..., half_width:], values[..., :half_width]], axis=-1)
    return values * cosine + turned * sine


def rotate_back(grads, cosine, sine):
    half_width = grads.shape[-1] // 2
    scaled = grads * sine
    turned = jnp.concatenate([scaled[..., half_width:], -scaled[..., :half_width]], axis=-1)
    return grads * cosine + turned


def previous_block(pieces):
    return jax.tree.map(
        lambda part, own: part.astype(own.dtype), shifted(for_sending(pieces), "expert", 1), pieces
    )


def following_block(pieces):
    return shifted((for_sending(pieces[0]), for_sending(pieces[1])), "expert", -1)


def body_routed(
    tokens,
    documents,
    routes,
    norm1_gain,
    q_gain,
    k_gain,
    w_query,
    w_key,
    w_value,
    w_out,
    norm2_gain,
    router_w,
    w_gate,
    w_up,
    w_down,
    out_grad,
):
    row_count, model_width = tokens.shape
    groups = lax.axis_size("expert")
    local_experts = w_gate.shape[0]
    experts = local_experts * groups
    capacity = 2 * row_count * TOP // experts
    slots_group = local_experts * capacity
    heads = w_query.shape[1] // HD
    score_scale = HD ** (-0.5)
    first_row = lax.axis_index("expert") * row_count
    positions = first_row + jnp.arange(row_count, dtype=jnp.int32)
    cosine, sine = rope_tables(positions % LENGTH)
    inputs = tokens.astype(jnp.float32)
    scale_one = lax.rsqrt(jnp.mean(inputs * inputs, axis=-1, keepdims=True) + NORM_EPSILON)
    normed_one = (inputs * scale_one * norm1_gain).astype(jnp.bfloat16)
    query_raw = jnp.dot(normed_one, w_query, preferred_element_type=jnp.float32)
    key_raw = jnp.dot(normed_one, w_key, preferred_element_type=jnp.float32)
    values = jnp.dot(normed_one, w_value, preferred_element_type=jnp.float32).astype(jnp.bfloat16)
    query_square, key_square = lax.psum(
        (jnp.sum(query_raw * query_raw, axis=-1), jnp.sum(key_raw * key_raw, axis=-1)), "tensor"
    )
    query_scale = lax.rsqrt(query_square / model_width + NORM_EPSILON)[:, None]
    key_scale = lax.rsqrt(key_square / model_width + NORM_EPSILON)[:, None]
    query_gain = q_gain.reshape(-1)
    key_gain = k_gain.reshape(-1)
    queries = rotate(
        (query_raw * query_scale * query_gain).reshape(row_count, heads, HD), cosine, sine
    ).astype(jnp.bfloat16)
    key_heads = rotate(
        (key_raw * key_scale * key_gain).reshape(row_count, heads, HD), cosine, sine
    ).astype(jnp.bfloat16)
    value_heads = values.reshape(row_count, heads, HD)
    labels = jnp.stack([documents // 256, documents % 256]).astype(jnp.bfloat16)
    previous_one = previous_block((key_heads, value_heads, labels))
    previous_two = previous_block(previous_one)
    all_keys = jnp.concatenate([previous_two[0], previous_one[0], key_heads], axis=0)
    all_values = jnp.concatenate([previous_two[1], previous_one[1], value_heads], axis=0)
    all_labels = jnp.concatenate([previous_two[2], previous_one[2], labels], axis=1)
    key_pos = first_row - 2 * row_count + jnp.arange(3 * row_count, dtype=jnp.int32)
    same_doc = (all_labels[0][None, :] == labels[0][:, None]) & (
        all_labels[1][None, :] == labels[1][:, None]
    )
    allowed = (
        same_doc
        & (key_pos[None, :] <= positions[:, None])
        & (positions[:, None] - key_pos[None, :] < WINDOW)
        & (key_pos[None, :] >= 0)
    )

    def masked_scores():
        raw_scores = (
            jnp.einsum("qhd,khd->hqk", queries, all_keys, preferred_element_type=jnp.float32)
            * score_scale
        )
        return jnp.where(allowed[None], raw_scores, -1e30)

    scores = masked_scores()
    highest = jnp.max(scores, axis=-1, keepdims=True)
    weights = jnp.where(allowed[None], jnp.exp(scores - highest), 0.0)
    denominator = jnp.sum(weights, axis=-1, keepdims=True)
    log_total = highest + jnp.log(denominator)
    attn_probs = weights / denominator
    attended = jnp.einsum(
        "hqk,khd->qhd",
        attn_probs.astype(jnp.bfloat16),
        all_values,
        preferred_element_type=jnp.float32,
    )
    attended = attended.reshape(row_count, -1).astype(jnp.bfloat16)
    attention = lax.psum(jnp.dot(attended, w_out, preferred_element_type=jnp.float32), "tensor")
    state = inputs + attention
    scale_two = lax.rsqrt(jnp.mean(state * state, axis=-1, keepdims=True) + NORM_EPSILON)
    normed_two = (state * scale_two * norm2_gain).astype(jnp.bfloat16)
    router_probs = jax.nn.softmax(
        jnp.dot(normed_two, router_w, preferred_element_type=jnp.float32), axis=-1
    )
    chosen = (routes[:, :, None] == jnp.arange(experts, dtype=jnp.int32)[None, None, :]).astype(
        jnp.float32
    )
    gates = jnp.sum(chosen * router_probs[:, None, :], axis=-1)
    flat_routes = routes.reshape(-1)
    onehot = (flat_routes[:, None] == jnp.arange(experts, dtype=jnp.int32)[None, :]).astype(
        jnp.int32
    )
    slot_index = jnp.sum(jnp.cumsum(onehot, axis=0) * onehot, axis=1) - 1
    target = flat_routes * capacity + slot_index
    source = (
        jnp.full((experts * capacity,), -1, jnp.int32)
        .at[target]
        .set(jnp.arange(row_count * TOP, dtype=jnp.int32))
    )
    live_slot = source >= 0
    pick_index = jnp.maximum(source, 0)
    send_rows = jnp.where(
        live_slot[:, None], normed_two[pick_index // TOP], jnp.zeros((), jnp.bfloat16)
    ).reshape(groups, slots_group, model_width)
    grad_float = out_grad.astype(jnp.float32)
    pick_grads = (
        (gates[:, :, None] * grad_float[:, None, :])
        .astype(jnp.bfloat16)
        .reshape(row_count * TOP, model_width)
    )
    send_grads = jnp.where(
        live_slot[:, None], pick_grads[pick_index], jnp.zeros((), jnp.bfloat16)
    ).reshape(groups, slots_group, model_width)
    arrived = lax.all_to_all(send_rows, "expert", split_axis=0, concat_axis=0, tiled=True)
    stacked = arrived.reshape(groups, local_experts, capacity, model_width)
    gate_pre = jnp.einsum("secd,edf->secf", stacked, w_gate, preferred_element_type=jnp.float32)
    up_pre = jnp.einsum("secd,edf->secf", stacked, w_up, preferred_element_type=jnp.float32)
    activated = jax.nn.silu(gate_pre)
    inner_act = (activated * up_pre).astype(jnp.bfloat16)
    produced = jnp.einsum(
        "secf,efd->secd", inner_act, w_down, preferred_element_type=jnp.float32
    ).astype(jnp.bfloat16)
    returned = lax.all_to_all(
        produced.reshape(groups, slots_group, model_width),
        "expert",
        split_axis=0,
        concat_axis=0,
        tiled=True,
    )
    back_rows = (
        returned.reshape(experts * capacity, model_width)[target]
        .reshape(row_count, TOP, model_width)
        .astype(jnp.float32)
    )
    expert_part = jnp.sum(gates[:, :, None] * back_rows, axis=1)
    expert_mix = lax.psum(expert_part.astype(jnp.bfloat16), "tensor").astype(jnp.float32)
    output = (state + expert_mix).astype(jnp.bfloat16)
    gate_part = jnp.sum(grad_float[:, None, :] * back_rows, axis=-1)
    arrived_grad = lax.all_to_all(send_grads, "expert", split_axis=0, concat_axis=0, tiled=True)
    slot_grad = arrived_grad.reshape(groups, local_experts, capacity, model_width)
    w_down_grad = jnp.einsum(
        "secf,secd->efd", inner_act, slot_grad, preferred_element_type=jnp.float32
    )
    inner_grad = jnp.einsum("secd,efd->secf", slot_grad, w_down, preferred_element_type=jnp.float32)
    logistic = jax.nn.sigmoid(gate_pre)
    gate_pre_grad = (inner_grad * up_pre * logistic * (1.0 + gate_pre * (1.0 - logistic))).astype(
        jnp.bfloat16
    )
    up_pre_grad = (inner_grad * activated).astype(jnp.bfloat16)
    w_gate_grad = jnp.einsum(
        "secd,secf->edf", stacked, gate_pre_grad, preferred_element_type=jnp.float32
    )
    w_up_grad = jnp.einsum(
        "secd,secf->edf", stacked, up_pre_grad, preferred_element_type=jnp.float32
    )
    row_grad = jnp.einsum(
        "secf,edf->secd", gate_pre_grad, w_gate, preferred_element_type=jnp.float32
    )
    row_grad = (
        row_grad
        + jnp.einsum("secf,edf->secd", up_pre_grad, w_up, preferred_element_type=jnp.float32)
    ).astype(jnp.bfloat16)
    grad_back = lax.all_to_all(
        row_grad.reshape(groups, slots_group, model_width),
        "expert",
        split_axis=0,
        concat_axis=0,
        tiled=True,
    )
    grad_picks = (
        grad_back.reshape(experts * capacity, model_width)[target]
        .reshape(row_count, TOP, model_width)
        .astype(jnp.float32)
    )
    normed_part = jnp.sum(grad_picks, axis=1)
    normed_two_grad, gate_cot = lax.psum((normed_part, gate_part), "tensor")
    prob_cot = jnp.sum(gate_cot[:, :, None] * chosen, axis=1)
    logit_cot = router_probs * (prob_cot - jnp.sum(router_probs * prob_cot, axis=-1, keepdims=True))
    router_float = router_w.astype(jnp.float32)
    normed_two_grad = normed_two_grad + jnp.einsum(
        "te,de->td", logit_cot, router_float, precision=HIGHEST_PRECISION
    )
    router_grad = jnp.einsum(
        "td,te->de", normed_two.astype(jnp.float32), logit_cot, precision=HIGHEST_PRECISION
    )
    norm2_grad = jnp.sum(normed_two_grad * state * scale_two, axis=0)
    inner_two = jnp.sum(normed_two_grad * norm2_gain * state, axis=-1, keepdims=True)
    state_cot = (
        grad_float
        + scale_two * norm2_gain * normed_two_grad
        - state * scale_two**3 * inner_two / model_width
    )
    state_low = state_cot.astype(jnp.bfloat16)
    w_out_grad = jnp.einsum("tf,td->fd", attended, state_low, preferred_element_type=jnp.float32)
    attended_cot = (
        jnp.einsum("td,fd->tf", state_low, w_out, preferred_element_type=jnp.float32)
        .astype(jnp.bfloat16)
        .reshape(row_count, heads, HD)
    )
    scores = masked_scores()
    attn_probs = jnp.where(allowed[None], jnp.exp(scores - log_total), 0.0)
    value_cot_all = jnp.einsum(
        "hqk,qhd->khd",
        attn_probs.astype(jnp.bfloat16),
        attended_cot,
        preferred_element_type=jnp.float32,
    )
    prob_grad = jnp.einsum(
        "qhd,khd->hqk", attended_cot, all_values, preferred_element_type=jnp.float32
    )
    delta = jnp.sum(attn_probs * prob_grad, axis=-1, keepdims=True)
    score_cot = (attn_probs * (prob_grad - delta)).astype(jnp.bfloat16)
    query_cot = (
        jnp.einsum("hqk,khd->qhd", score_cot, all_keys, preferred_element_type=jnp.float32)
        * score_scale
    )
    key_cot_all = (
        jnp.einsum("hqk,qhd->khd", score_cot, queries, preferred_element_type=jnp.float32)
        * score_scale
    )
    carried = following_block((key_cot_all[:row_count], value_cot_all[:row_count]))
    carried = following_block(
        (
            key_cot_all[row_count : 2 * row_count] + carried[0],
            value_cot_all[row_count : 2 * row_count] + carried[1],
        )
    )
    key_cot = key_cot_all[2 * row_count :] + carried[0]
    value_cot = value_cot_all[2 * row_count :] + carried[1]
    query_norm_cot = rotate_back(query_cot, cosine, sine).reshape(row_count, -1)
    key_norm_cot = rotate_back(key_cot, cosine, sine).reshape(row_count, -1)
    q_gain_local = jnp.sum(query_norm_cot * query_raw * query_scale, axis=0).reshape(heads, HD)
    k_gain_local = jnp.sum(key_norm_cot * key_raw * key_scale, axis=0).reshape(heads, HD)
    query_inner, key_inner = lax.psum(
        (
            jnp.sum(query_norm_cot * query_gain * query_raw, axis=-1),
            jnp.sum(key_norm_cot * key_gain * key_raw, axis=-1),
        ),
        "tensor",
    )
    query_raw_cot = (
        query_scale * query_gain * query_norm_cot
        - query_raw * query_scale**3 * query_inner[:, None] / model_width
    ).astype(jnp.bfloat16)
    key_raw_cot = (
        key_scale * key_gain * key_norm_cot
        - key_raw * key_scale**3 * key_inner[:, None] / model_width
    ).astype(jnp.bfloat16)
    value_low = value_cot.reshape(row_count, -1).astype(jnp.bfloat16)
    w_query_local = jnp.einsum(
        "td,tf->df", normed_one, query_raw_cot, preferred_element_type=jnp.float32
    )
    w_key_local = jnp.einsum(
        "td,tf->df", normed_one, key_raw_cot, preferred_element_type=jnp.float32
    )
    w_value_local = jnp.einsum(
        "td,tf->df", normed_one, value_low, preferred_element_type=jnp.float32
    )
    normed_part_one = jnp.einsum(
        "tf,df->td", query_raw_cot, w_query, preferred_element_type=jnp.float32
    )
    normed_part_one = normed_part_one + jnp.einsum(
        "tf,df->td", key_raw_cot, w_key, preferred_element_type=jnp.float32
    )
    normed_part_one = normed_part_one + jnp.einsum(
        "tf,df->td", value_low, w_value, preferred_element_type=jnp.float32
    )
    normed_one_grad = lax.psum(normed_part_one.astype(jnp.bfloat16), "tensor").astype(jnp.float32)
    norm1_grad = jnp.sum(normed_one_grad * inputs * scale_one, axis=0)
    inner_one = jnp.sum(normed_one_grad * norm1_gain * inputs, axis=-1, keepdims=True)
    input_grad = (
        state_cot
        + scale_one * norm1_gain * normed_one_grad
        - inputs * scale_one**3 * inner_one / model_width
    )
    summed = (
        lax.psum_scatter(
            w_query_local.astype(jnp.bfloat16), "expert", scatter_dimension=0, tiled=True
        ).astype(jnp.float32),
        lax.psum_scatter(
            w_key_local.astype(jnp.bfloat16), "expert", scatter_dimension=0, tiled=True
        ).astype(jnp.float32),
        lax.psum_scatter(
            w_value_local.astype(jnp.bfloat16), "expert", scatter_dimension=0, tiled=True
        ).astype(jnp.float32),
        lax.psum_scatter(
            w_out_grad.astype(jnp.bfloat16), "expert", scatter_dimension=1, tiled=True
        ).astype(jnp.float32),
        lax.psum_scatter(
            router_grad.astype(jnp.bfloat16), "expert", scatter_dimension=0, tiled=True
        ).astype(jnp.float32),
        lax.psum_scatter(
            norm1_grad.astype(jnp.bfloat16), "expert", scatter_dimension=0, tiled=True
        ).astype(jnp.float32),
        lax.psum_scatter(
            norm2_grad.astype(jnp.bfloat16), "expert", scatter_dimension=0, tiled=True
        ).astype(jnp.float32),
        lax.psum_scatter(
            q_gain_local.astype(jnp.bfloat16), "expert", scatter_dimension=1, tiled=True
        ).astype(jnp.float32),
        lax.psum_scatter(
            k_gain_local.astype(jnp.bfloat16), "expert", scatter_dimension=1, tiled=True
        ).astype(jnp.float32),
    )
    return (
        output,
        input_grad,
        summed[5],
        summed[7],
        summed[8],
        summed[0],
        summed[1],
        summed[2],
        summed[3],
        summed[6],
        summed[4],
        w_gate_grad,
        w_up_grad,
        w_down_grad,
    )


MESH = pl.DeviceIdType.MESH
ANY = pl.BlockSpec(memory_space=pl.ANY)
VMEM = pl.BlockSpec(memory_space=pltpu.VMEM)
VMEM_BYTES = 60 * 1024 * 1024
LOW = jnp.bfloat16
FULL = jnp.float32


def place():
    group, part = lax.axis_index("expert"), lax.axis_index("tensor")
    return group // 2, group % 2, part // 2, part % 2


def device(z, x, y, core):
    return (2 * z + x, 2 * y + core)


def swapped(index, step):
    result, bit = index, 1
    while bit <= step:
        if step & bit:
            result = result + bit - 2 * bit * ((index // bit) % 2)
        bit *= 2
    return result


def greet(partners):
    barrier = pltpu.get_barrier_semaphore()
    for partner in partners:
        pl.semaphore_signal(barrier, inc=1, device_id=partner, device_id_type=MESH)
    pl.semaphore_wait(barrier, len(partners))


def remote(source, target, send, arrive, to):
    return pltpu.make_async_remote_copy(
        src_ref=source, dst_ref=target, send_sem=send, recv_sem=arrive, device_id=to, device_id_type=MESH
    )


def dma(*shape):
    return pltpu.SemaphoreType.DMA(shape)


def comm_params(number):
    return pltpu.CompilerParams(collective_id=number, has_side_effects=True, vmem_limit_bytes=VMEM_BYTES)


def add_rows(target, sources, rows, step=16):
    @pl.loop(0, rows // step)
    def _(index):
        part = pl.ds(index * step, step)
        total = sources[0][part].astype(FULL)
        for source in sources[1:]:
            total = total + source[part].astype(FULL)
        target[part] = total.astype(target.dtype)


def gather_rows_kernel(depth, rows, x_ref, small_ref, o_ref, smalls_ref, z_send, z_recv, p_send, p_recv, s_send, s_recv, local):
    z, x, y, core = place()
    here = 2 * x + y
    over_x, over_y = (z, 1 - x, y, core), (z, x, 1 - y, core)
    half = rows // 2
    upper, lower = pl.ds(0, half), pl.ds(half, half)
    others = []
    for step in range(depth):
        for turn in range(4):
            if step or turn:
                other = (swapped(z, step), swapped(x, turn // 2), swapped(y, turn % 2), core)
                others.append((step * 4 + turn, other))
    greet([device(*other) for _, other in others])
    own = pltpu.make_async_copy(x_ref, o_ref.at[z, here], local.at[0])
    own.start()
    own_small = pltpu.make_async_copy(small_ref, smalls_ref.at[z, here], local.at[1])
    own_small.start()
    pending = []

    def start(copy):
        copy.start()
        pending.append(copy)
        return copy

    along_z = []
    for step in range(1, depth):
        along_z.append(
            start(remote(x_ref, o_ref.at[z, here], z_send.at[step], z_recv.at[step], device(swapped(z, step), x, y, core)))
        )
    for number, other in others:
        start(remote(small_ref, smalls_ref.at[z, here], s_send.at[number], s_recv.at[number], device(*other)))
    own.wait()
    own_small.wait()
    forwards = []
    for step in range(depth):
        if step:
            along_z[step - 1].wait_recv()
        at = swapped(z, step)
        mine = o_ref.at[at, here]
        x_up = start(remote(mine.at[upper], mine.at[upper], p_send.at[step, 0], p_recv.at[step, 0], device(*over_x)))
        y_low = start(remote(mine.at[lower], mine.at[lower], p_send.at[step, 1], p_recv.at[step, 1], device(*over_y)))
        start(remote(mine.at[lower], mine.at[lower], p_send.at[step, 2], p_recv.at[step, 2], device(*over_x)))
        start(remote(mine.at[upper], mine.at[upper], p_send.at[step, 3], p_recv.at[step, 3], device(*over_y)))
        forwards.append((step, at, x_up, y_low))
    for step, at, x_up, y_low in forwards:
        x_up.wait_recv()
        from_x = o_ref.at[at, 2 * (1 - x) + y, upper]
        start(remote(from_x, from_x, p_send.at[step, 4], p_recv.at[step, 4], device(*over_y)))
        y_low.wait_recv()
        from_y = o_ref.at[at, 2 * x + 1 - y, lower]
        start(remote(from_y, from_y, p_send.at[step, 5], p_recv.at[step, 5], device(*over_x)))
    received = set(id(c) for c in along_z) | set(id(c) for f in forwards for c in f[2:])
    for copy in pending:
        copy.wait_send()
        if id(copy) not in received:
            copy.wait_recv()


def gather_rows(block, small, depth, number):
    rows = block.shape[0]
    return pl.pallas_call(
        functools.partial(gather_rows_kernel, depth, rows),
        out_shape=(
            jax.ShapeDtypeStruct((depth, 4) + block.shape, block.dtype),
            jax.ShapeDtypeStruct((depth, 4) + small.shape, small.dtype),
        ),
        in_specs=[ANY, ANY],
        out_specs=(ANY, ANY),
        scratch_shapes=[dma(depth), dma(depth), dma(depth, 6), dma(depth, 6), dma(4 * depth), dma(4 * depth), dma(2)],
        compiler_params=comm_params(number),
    )(block, small)


def scatter_rows_kernel(
    depth, rows, p_ref, small_ref, o_ref, smalls_ref,
    work, diagonal, from_x, from_y, passing, from_z,
    load, d_send, d_recv, x_send, x_recv, y_send, y_recv, z_send, z_recv, s_send, s_recv, local,
):
    z, x, y, core = place()
    here, x_place, y_place, far = 2 * x + y, 2 * (1 - x) + y, 2 * x + 1 - y, 2 * (1 - x) + 1 - y
    over_x, over_y = device(z, 1 - x, y, core), device(z, x, 1 - y, core)
    half = rows // 2
    upper, lower = pl.ds(0, half), pl.ds(half, half)
    others = []
    for step in range(depth):
        for turn in range(4):
            if step or turn:
                other = (swapped(z, step), swapped(x, turn // 2), swapped(y, turn % 2), core)
                others.append((step * 4 + turn, other))
    greet([device(*other) for _, other in others])
    pending = []

    def start(copy):
        copy.start()
        pending.append(copy)
        return copy

    for number, (oz, ox, oy, oc) in others:
        start(
            remote(
                small_ref.at[oz, 2 * ox + oy], smalls_ref.at[z, here], s_send.at[number], s_recv.at[number], device(oz, ox, oy, oc)
            )
        )
    own_small = pltpu.make_async_copy(small_ref.at[z, here], smalls_ref.at[z, here], local.at[0])
    own_small.start()
    loads = []
    order = [step for step in range(1, depth)] + [0]
    for step in order:
        at = swapped(z, step)
        copy = pltpu.make_async_copy(p_ref.at[at], work.at[step], load.at[step])
        copy.start()
        loads.append(copy)
    diagonals, sides = {}, {}
    for step, copy in zip(order, loads):
        copy.wait()
        diagonals[step] = (
            start(remote(work.at[step, far, upper], diagonal.at[step, 0], d_send.at[step, 0], d_recv.at[step, 0], over_y)),
            start(remote(work.at[step, far, lower], diagonal.at[step, 1], d_send.at[step, 1], d_recv.at[step, 1], over_x)),
        )
    for step in order:
        via_y, via_x = diagonals[step]
        via_y.wait_recv()
        add_rows(work.at[step, x_place, upper], [work.at[step, x_place, upper], diagonal.at[step, 0]], half)
        to_x = start(remote(work.at[step, x_place], from_x.at[step], x_send.at[step], x_recv.at[step], over_x))
        via_x.wait_recv()
        add_rows(work.at[step, y_place, lower], [work.at[step, y_place, lower], diagonal.at[step, 1]], half)
        to_y = start(remote(work.at[step, y_place], from_y.at[step], y_send.at[step], y_recv.at[step], over_y))
        sides[step] = (to_x, to_y)
    along_z = []
    for step in order:
        for side in sides[step]:
            side.wait_recv()
        terms = [work.at[step, here], from_x.at[step], from_y.at[step]]
        if step:
            add_rows(passing.at[step], terms, rows)
            along_z.append(
                start(
                    remote(
                        passing.at[step], from_z.at[step], z_send.at[step], z_recv.at[step], device(swapped(z, step), x, y, core)
                    )
                )
            )
    for copy in along_z:
        copy.wait_recv()
    add_rows(o_ref, [work.at[0, here], from_x.at[0], from_y.at[0]] + [from_z.at[step] for step in range(1, depth)], rows)
    own_small.wait()
    received = set(id(c) for c in along_z) | set(id(c) for v in list(diagonals.values()) + list(sides.values()) for c in v)
    for copy in pending:
        copy.wait_send()
        if id(copy) not in received:
            copy.wait_recv()


def scatter_rows(parts, small, number):
    depth, _, rows, width = parts.shape
    return pl.pallas_call(
        functools.partial(scatter_rows_kernel, depth, rows),
        out_shape=(jax.ShapeDtypeStruct((rows, width), FULL), jax.ShapeDtypeStruct(small.shape, small.dtype)),
        in_specs=[ANY, ANY],
        out_specs=(VMEM, ANY),
        scratch_shapes=[
            pltpu.VMEM(parts.shape, parts.dtype),
            pltpu.VMEM((depth, 2, rows // 2, width), parts.dtype),
            pltpu.VMEM((depth, rows, width), parts.dtype),
            pltpu.VMEM((depth, rows, width), parts.dtype),
            pltpu.VMEM((depth, rows, width), parts.dtype),
            pltpu.VMEM((depth, rows, width), parts.dtype),
            dma(depth), dma(depth, 2), dma(depth, 2), dma(depth), dma(depth), dma(depth), dma(depth), dma(depth), dma(depth),
            dma(4 * depth), dma(4 * depth), dma(1),
        ],
        compiler_params=comm_params(number),
    )(parts, small)


def pair_weights_kernel(count, *refs):
    ins, outs, (send, recv, local) = refs[:count], refs[count : 2 * count], refs[2 * count :]
    z, x, y, core = place()
    sibling = device(z, x, y, 1 - core)
    greet([sibling])
    waits = []
    for index in range(count):
        copy = remote(ins[index], outs[index].at[core], send.at[index], recv.at[index], sibling)
        copy.start()
        mine = pltpu.make_async_copy(ins[index], outs[index].at[core], local.at[index])
        mine.start()
        waits += [copy, mine]
    for copy in waits:
        copy.wait()


def pair_weights(arrays, number):
    count = len(arrays)
    return pl.pallas_call(
        functools.partial(pair_weights_kernel, count),
        out_shape=tuple(jax.ShapeDtypeStruct((2,) + a.shape, a.dtype) for a in arrays),
        in_specs=[ANY] * count,
        out_specs=(ANY,) * count,
        scratch_shapes=[dma(count), dma(count), dma(count)],
        compiler_params=comm_params(number),
    )(*arrays)


def pair_swap_kernel(count, *refs):
    ins, outs, (send, recv) = refs[:count], refs[count : 2 * count], refs[2 * count :]
    z, x, y, core = place()
    sibling = device(z, x, y, 1 - core)
    greet([sibling])
    waits = []
    for index in range(count):
        copy = remote(ins[index].at[1 - core], outs[index], send.at[index], recv.at[index], sibling)
        copy.start()
        waits.append(copy)
    for copy in waits:
        copy.wait()


def pair_swap(arrays, number):
    count = len(arrays)
    return pl.pallas_call(
        functools.partial(pair_swap_kernel, count),
        out_shape=tuple(jax.ShapeDtypeStruct(a.shape[1:], a.dtype) for a in arrays),
        in_specs=[ANY] * count,
        out_specs=(ANY,) * count,
        scratch_shapes=[dma(count), dma(count)],
        compiler_params=comm_params(number),
    )(*arrays)


def tensor_scatter_kernel(rows, p_ref, o_ref, work, from_pair, from_y, load, send, recv):
    z, x, y, core = place()
    sibling, over_y = device(z, x, y, 1 - core), device(z, x, 1 - y, core)
    greet([sibling, over_y])
    fetch = pltpu.make_async_copy(p_ref, work, load.at[0])
    fetch.start()
    pairs = []
    for turn in (1, 0):
        row = swapped(y, turn)
        copy = remote(p_ref.at[row, 1 - core], from_pair.at[turn], send.at[turn], recv.at[turn], sibling)
        copy.start()
        pairs.append(copy)
    fetch.wait()
    pairs[0].wait_recv()
    add_rows(work.at[1 - y, core], [work.at[1 - y, core], from_pair.at[1]], rows)
    across = remote(work.at[1 - y, core], from_y, send.at[2], recv.at[2], over_y)
    across.start()
    pairs[1].wait_recv()
    across.wait_recv()
    add_rows(o_ref, [work.at[y, core], from_pair.at[0], from_y], rows)
    for copy in pairs + [across]:
        copy.wait_send()


def tensor_scatter(parts, number):
    rows, width = parts.shape[0] // 4, parts.shape[1]
    shaped = parts.reshape(2, 2, rows, width)
    return pl.pallas_call(
        functools.partial(tensor_scatter_kernel, rows),
        out_shape=jax.ShapeDtypeStruct((rows, width), FULL),
        in_specs=[ANY],
        out_specs=VMEM,
        scratch_shapes=[
            pltpu.VMEM(shaped.shape, parts.dtype),
            pltpu.VMEM((2, rows, width), parts.dtype),
            pltpu.VMEM((rows, width), parts.dtype),
            dma(1), dma(3), dma(3),
        ],
        compiler_params=comm_params(number),
    )(shaped)


def tensor_gather_kernel(x_ref, o_ref, send, recv, local):
    z, x, y, core = place()
    sibling, over_y = device(z, x, y, 1 - core), device(z, x, 1 - y, core)
    greet([sibling, over_y])
    own = pltpu.make_async_copy(x_ref, o_ref.at[y, core], local.at[0])
    own.start()
    across = remote(x_ref, o_ref.at[y, core], send.at[0], recv.at[0], over_y)
    across.start()
    near = remote(x_ref, o_ref.at[y, core], send.at[1], recv.at[1], sibling)
    near.start()
    across.wait_recv()
    block = o_ref.at[1 - y, core]
    passed = remote(block, block, send.at[2], recv.at[2], sibling)
    passed.start()
    own.wait()
    across.wait_send()
    near.wait()
    passed.wait()


def tensor_gather(block, number):
    rows, width = block.shape
    gathered = pl.pallas_call(
        tensor_gather_kernel,
        out_shape=jax.ShapeDtypeStruct((2, 2, rows, width), block.dtype),
        in_specs=[ANY],
        out_specs=ANY,
        scratch_shapes=[dma(3), dma(3), dma(1)],
        compiler_params=comm_params(number),
    )(block)
    return gathered.reshape(4 * rows, width)


def expert_scatter_kernel(depth, rows, p_ref, o_ref, work, from_x, from_z, load, send, recv):
    z, x, y, core = place()
    over_x = device(z, 1 - x, y, core)
    greet([over_x] + [device(swapped(z, step), x, y, core) for step in range(1, depth)])
    order = [step for step in range(1, depth)] + [0]
    sides, along, loads = {}, [], {}
    for step in order:
        at = swapped(z, step)
        sides[step] = remote(p_ref.at[at, 1 - x], from_x.at[step], send.at[0, step], recv.at[0, step], over_x)
        sides[step].start()
        loads[step] = pltpu.make_async_copy(p_ref.at[at, x], work.at[step], load.at[step])
        loads[step].start()
    for step in order:
        loads[step].wait()
        sides[step].wait_recv()
        if step:
            add_rows(work.at[step], [work.at[step], from_x.at[step]], rows)
            copy = remote(work.at[step], from_z.at[step], send.at[1, step], recv.at[1, step], device(swapped(z, step), x, y, core))
            copy.start()
            along.append(copy)
    for copy in along:
        copy.wait_recv()
    add_rows(o_ref, [work.at[0], from_x.at[0]] + [from_z.at[step] for step in range(1, depth)], rows)
    for copy in list(sides.values()) + along:
        copy.wait_send()


def expert_scatter(parts, depth, number):
    rows, width = parts.shape[0] // (2 * depth), parts.shape[1]
    shaped = parts.reshape(depth, 2, rows, width)
    return pl.pallas_call(
        functools.partial(expert_scatter_kernel, depth, rows),
        out_shape=jax.ShapeDtypeStruct((rows, width), FULL),
        in_specs=[ANY],
        out_specs=VMEM,
        scratch_shapes=[
            pltpu.VMEM((depth, rows, width), parts.dtype),
            pltpu.VMEM((depth, rows, width), parts.dtype),
            pltpu.VMEM((depth, rows, width), parts.dtype),
            dma(depth), dma(2, depth), dma(2, depth),
        ],
        compiler_params=comm_params(number),
    )(shaped)


def halo_kernel(chain, forward, count, *refs):
    ins, outs, (send, recv) = refs[:count], refs[count : 2 * count], refs[2 * count :]
    group, part = lax.axis_index("expert"), lax.axis_index("tensor")
    spot = group % chain
    barrier = pltpu.get_barrier_semaphore()
    distances = (1, 2)

    def each(before, after):
        for distance in distances:
            if after is not None:
                pl.when(spot < chain - distance)(functools.partial(after, distance))
            if before is not None:
                pl.when(spot >= distance)(functools.partial(before, distance))

    def signal(to):
        pl.semaphore_signal(barrier, inc=1, device_id=(to, part), device_id_type=MESH)

    each(lambda d: signal(group - d), lambda d: signal(group + d))
    pl.semaphore_wait(barrier, jnp.minimum(spot, 2) + jnp.minimum(chain - 1 - spot, 2))

    def copies(distance, to):
        return [
            remote(
                ins[i] if forward else ins[i].at[2 - distance],
                outs[i].at[2 - distance],
                send.at[i, distance],
                recv.at[i, distance],
                (to, part),
            )
            for i in range(count)
        ]

    def start(sign, distance):
        for copy in copies(distance, group + sign * distance):
            copy.start()

    def finish(sign, distance):
        for copy in copies(distance, group + sign * distance):
            copy.wait_send()

    def take(sign, distance):
        for copy in copies(distance, group - sign * distance):
            copy.wait_recv()

    if forward:
        each(None, functools.partial(start, 1))
        each(functools.partial(take, 1), None)
        each(None, functools.partial(finish, 1))
    else:
        each(functools.partial(start, -1), None)
        each(None, functools.partial(take, -1))
        each(functools.partial(finish, -1), None)


def halo(arrays, chain, forward, number):
    count = len(arrays)
    return pl.pallas_call(
        functools.partial(halo_kernel, chain, forward, count),
        out_shape=tuple(jax.ShapeDtypeStruct(((2,) + a.shape) if forward else a.shape, a.dtype) for a in arrays),
        in_specs=[ANY] * count,
        out_specs=(ANY,) * count,
        scratch_shapes=[dma(count, 3), dma(count, 3)],
        compiler_params=comm_params(number),
    )(*arrays)


def dot(left, right):
    return jnp.dot(left, right, preferred_element_type=FULL)


def dot_t(left, right):
    return lax.dot_general(left, right, (((1,), (1,)), ((), ())), preferred_element_type=FULL)


def t_dot(left, right):
    return lax.dot_general(left, right, (((0,), (0,)), ((), ())), preferred_element_type=FULL)


def body(
    groups, parts,
    tokens, documents, routes, norm1_gain, q_gain, k_gain, w_query, w_key, w_value, w_out, norm2_gain, router_w,
    w_gate, w_up, w_down, out_grad,
):
    row_count, width = tokens.shape
    local_experts, _, hidden = w_gate.shape
    experts = local_experts * groups
    chain = LENGTH // row_count
    if not (parts == 4 and groups % 2 == 0 and experts <= 2 * TOP and row_count * chain == LENGTH and WINDOW == 2 * row_count):
        return body_routed(
            tokens, documents, routes, norm1_gain, q_gain, k_gain, w_query, w_key, w_value, w_out, norm2_gain, router_w,
            w_gate, w_up, w_down, out_grad,
        )
    depth = groups // 2
    rows = row_count // parts
    seen = groups * row_count // 2
    heads = w_query.shape[1] // HD
    score_scale = HD ** (-0.5)
    group, part = lax.axis_index("expert"), lax.axis_index("tensor")
    core = part % 2

    def quarter(array):
        return lax.dynamic_slice_in_dim(array, part * rows, rows, 0)

    gate_pair, up_pair, down_pair = pair_weights([w_gate, w_up, w_down], 1)
    units = 2 * local_experts * hidden
    gate_all = gate_pair.reshape(2 * local_experts, width, hidden).transpose(1, 0, 2).reshape(width, units)
    up_all = up_pair.reshape(2 * local_experts, width, hidden).transpose(1, 0, 2).reshape(width, units)
    down_all = down_pair.reshape(units, width)

    first_row = group * row_count
    positions = first_row + jnp.arange(row_count, dtype=jnp.int32)
    cosine, sine = rope_tables(positions % LENGTH)
    inputs = tokens.astype(FULL)
    scale_one = lax.rsqrt(jnp.mean(inputs * inputs, axis=-1, keepdims=True) + NORM_EPSILON)
    normed_one = (inputs * scale_one * norm1_gain).astype(LOW)
    query_raw = dot(normed_one, w_query)
    key_raw = dot(normed_one, w_key)
    values = dot(normed_one, w_value).astype(LOW)
    squares = lax.psum(
        jnp.stack([jnp.sum(query_raw * query_raw, axis=-1), jnp.sum(key_raw * key_raw, axis=-1)]), "tensor"
    )
    query_scale = lax.rsqrt(squares[0] / width + NORM_EPSILON)[:, None]
    key_scale = lax.rsqrt(squares[1] / width + NORM_EPSILON)[:, None]
    query_gain, key_gain = q_gain.reshape(-1), k_gain.reshape(-1)
    queries = rotate((query_raw * query_scale * query_gain).reshape(row_count, heads, HD), cosine, sine).astype(LOW)
    key_heads = rotate((key_raw * key_scale * key_gain).reshape(row_count, heads, HD), cosine, sine).astype(LOW)
    own_kv = jnp.concatenate([key_heads.reshape(row_count, -1), values], axis=1)
    own_docs = documents.reshape(row_count // 128, 128)
    before_kv, before_docs = halo([own_kv, own_docs], chain, True, 2)
    spot = group % chain
    exists = jnp.stack([spot >= 2, spot >= 1])
    before_kv = jnp.where(exists[:, None, None], before_kv, jnp.zeros((), LOW))
    before_docs = jnp.where(exists[:, None, None], before_docs, -1)
    all_kv = jnp.concatenate([before_kv[0], before_kv[1], own_kv], axis=0)
    all_keys = all_kv[:, : heads * HD].reshape(3 * row_count, heads, HD)
    all_values = all_kv[:, heads * HD :].reshape(3 * row_count, heads, HD)
    all_docs = jnp.concatenate([before_docs[0], before_docs[1], own_docs], axis=0).reshape(-1)
    key_pos = first_row - 2 * row_count + jnp.arange(3 * row_count, dtype=jnp.int32)
    allowed = (
        (all_docs[None, :] == documents[:, None])
        & (key_pos[None, :] <= positions[:, None])
        & (positions[:, None] - key_pos[None, :] < WINDOW)
    )

    def masked_scores():
        raw_scores = jnp.einsum("qhd,khd->hqk", queries, all_keys, preferred_element_type=FULL) * score_scale
        return jnp.where(allowed[None], raw_scores, -1e30)

    scores = masked_scores()
    highest = jnp.max(scores, axis=-1, keepdims=True)
    weights = jnp.where(allowed[None], jnp.exp(scores - highest), 0.0)
    denominator = jnp.sum(weights, axis=-1, keepdims=True)
    log_total = highest + jnp.log(denominator)
    attn_probs = weights / denominator
    attended = jnp.einsum("hqk,khd->qhd", attn_probs.astype(LOW), all_values, preferred_element_type=FULL)
    attended = attended.reshape(row_count, -1).astype(LOW)
    attention = tensor_scatter(dot(attended, w_out).astype(LOW), 3)

    own_inputs = quarter(tokens).astype(FULL)
    own_grad = quarter(out_grad)
    own_grad_float = own_grad.astype(FULL)
    state = own_inputs + attention
    scale_two = lax.rsqrt(jnp.mean(state * state, axis=-1, keepdims=True) + NORM_EPSILON)
    normed_two = (state * scale_two * norm2_gain).astype(LOW)
    router_probs = jax.nn.softmax(dot(normed_two, router_w), axis=-1)
    picked = jnp.any(
        quarter(routes)[:, :, None] == jnp.arange(experts, dtype=jnp.int32)[None, None, :], axis=1
    ).astype(FULL)

    no_small = jnp.zeros((8, 128), FULL)
    all_grad, _ = gather_rows(own_grad, no_small, depth, 4)
    all_normed, all_gates = gather_rows(normed_two, (router_probs * picked).T, depth, 5)
    all_normed = all_normed.reshape(seen, width)
    all_grad = all_grad.reshape(seen, width)
    own_gates = lax.dynamic_slice_in_dim(all_gates, group * local_experts, local_experts, 2)
    own_gates = own_gates.transpose(0, 1, 3, 2).reshape(seen, 1, local_experts, 1)
    split = (seen, 2, local_experts, hidden)
    gate_pre = dot(all_normed, gate_all)
    up_pre = dot(all_normed, up_all)
    logistic = jax.nn.sigmoid(gate_pre)
    activated = gate_pre * logistic
    inner_act = activated * up_pre
    inner_back = dot_t(all_grad, down_all)
    gate_cot = jnp.sum((inner_act * inner_back).reshape(split), axis=(1, 3))
    gate_wide = jnp.broadcast_to(own_gates, split).reshape(seen, units)
    gated = (gate_wide * inner_act).astype(LOW)
    inner_grad = gate_wide * inner_back
    gate_pre_grad = (inner_grad * up_pre * logistic * (1.0 + gate_pre * (1.0 - logistic))).astype(LOW)
    up_pre_grad = (inner_grad * activated).astype(LOW)
    produced = dot(gated, down_all).astype(LOW).reshape(depth, 4, rows, width)
    row_grad = (dot_t(gate_pre_grad, gate_all) + dot_t(up_pre_grad, up_all)).astype(LOW).reshape(depth, 4, rows, width)
    gate_cot = gate_cot.reshape(depth, 4, rows, local_experts).transpose(0, 1, 3, 2)
    gate_cot = jnp.concatenate([gate_cot, jnp.zeros((depth, 4, 8 - local_experts, rows), FULL)], axis=2)
    normed_two_grad, gate_cots = scatter_rows(row_grad, gate_cot, 6)
    expert_mix, _ = scatter_rows(produced, jnp.zeros((depth, 4, 8, 128), FULL), 7)

    def expert_grads(left, right):
        return t_dot(left, right)

    gate_wgrad = expert_grads(all_normed, gate_pre_grad).reshape(width, 2, local_experts, hidden).transpose(1, 2, 0, 3)
    up_wgrad = expert_grads(all_normed, up_pre_grad).reshape(width, 2, local_experts, hidden).transpose(1, 2, 0, 3)
    down_wgrad = expert_grads(gated, all_grad).reshape(2, local_experts, hidden, width)
    swaps = pair_swap([gate_wgrad, up_wgrad, down_wgrad], 8)
    w_gate_grad, w_up_grad, w_down_grad = (
        lax.dynamic_index_in_dim(mine, core, 0, keepdims=False) + other
        for mine, other in zip((gate_wgrad, up_wgrad, down_wgrad), swaps)
    )

    output = tensor_gather((state + expert_mix).astype(LOW), 9)

    prob_cot = gate_cots[:, :, :local_experts].reshape(depth, 2, 2, local_experts, rows).sum(axis=2)
    prob_cot = prob_cot.reshape(experts, rows).T * picked
    logit_cot = router_probs * (prob_cot - jnp.sum(router_probs * prob_cot, axis=-1, keepdims=True))
    normed_two_grad = normed_two_grad + jnp.einsum(
        "te,de->td", logit_cot, router_w.astype(FULL), precision=HIGHEST_PRECISION
    )
    router_grad = jnp.einsum("td,te->ed", normed_two.astype(FULL), logit_cot, precision=HIGHEST_PRECISION)
    norm2_grad = jnp.sum(normed_two_grad * state * scale_two, axis=0)
    inner_two = jnp.sum(normed_two_grad * norm2_gain * state, axis=-1, keepdims=True)
    state_cot = own_grad_float + scale_two * norm2_gain * normed_two_grad - state * scale_two**3 * inner_two / width
    state_low = tensor_gather(state_cot.astype(LOW), 10)

    w_out_grad = t_dot(state_low, attended)
    attended_cot = dot_t(state_low, w_out).astype(LOW).reshape(row_count, heads, HD)
    scores = masked_scores()
    attn_probs = jnp.where(allowed[None], jnp.exp(scores - log_total), 0.0)
    value_cot_all = jnp.einsum("hqk,qhd->khd", attn_probs.astype(LOW), attended_cot, preferred_element_type=FULL)
    prob_grad = jnp.einsum("qhd,khd->hqk", attended_cot, all_values, preferred_element_type=FULL)
    delta = jnp.sum(attn_probs * prob_grad, axis=-1, keepdims=True)
    score_cot = (attn_probs * (prob_grad - delta)).astype(LOW)
    query_cot = jnp.einsum("hqk,khd->qhd", score_cot, all_keys, preferred_element_type=FULL) * score_scale
    key_cot_all = jnp.einsum("hqk,qhd->khd", score_cot, queries, preferred_element_type=FULL) * score_scale
    kv_cot = jnp.concatenate(
        [key_cot_all.reshape(3, row_count, -1), value_cot_all.reshape(3, row_count, -1)], axis=2
    )
    (after_kv,) = halo([kv_cot[:2].astype(LOW)], chain, False, 11)
    follows = jnp.stack([spot < chain - 2, spot < chain - 1])
    after_kv = jnp.where(follows[:, None, None], after_kv, jnp.zeros((), LOW)).astype(FULL)
    kv_cot = kv_cot[2] + after_kv[0] + after_kv[1]
    key_cot = kv_cot[:, : heads * HD].reshape(row_count, heads, HD)
    value_low = kv_cot[:, heads * HD :].astype(LOW)
    query_norm_cot = rotate_back(query_cot, cosine, sine).reshape(row_count, -1)
    key_norm_cot = rotate_back(key_cot, cosine, sine).reshape(row_count, -1)
    q_gain_local = jnp.sum(query_norm_cot * query_raw * query_scale, axis=0).reshape(heads, HD)
    k_gain_local = jnp.sum(key_norm_cot * key_raw * key_scale, axis=0).reshape(heads, HD)
    inners = lax.psum(
        jnp.stack(
            [
                jnp.sum(query_norm_cot * query_gain * query_raw, axis=-1),
                jnp.sum(key_norm_cot * key_gain * key_raw, axis=-1),
            ]
        ),
        "tensor",
    )
    query_raw_cot = (
        query_scale * query_gain * query_norm_cot - query_raw * query_scale**3 * inners[0][:, None] / width
    ).astype(LOW)
    key_raw_cot = (
        key_scale * key_gain * key_norm_cot - key_raw * key_scale**3 * inners[1][:, None] / width
    ).astype(LOW)
    normed_part = dot_t(query_raw_cot, w_query) + dot_t(key_raw_cot, w_key) + dot_t(value_low, w_value)
    normed_one_grad = tensor_scatter(normed_part.astype(LOW), 12)
    own_scale = quarter(scale_one)
    norm1_grad = jnp.sum(normed_one_grad * own_inputs * own_scale, axis=0)
    inner_one = jnp.sum(normed_one_grad * norm1_gain * own_inputs, axis=-1, keepdims=True)
    input_grad = (
        state_cot + own_scale * norm1_gain * normed_one_grad - own_inputs * own_scale**3 * inner_one / width
    )
    input_grad = tensor_gather(input_grad.astype(LOW), 13).astype(FULL)

    local = jnp.concatenate(
        [
            t_dot(normed_one, query_raw_cot),
            t_dot(normed_one, key_raw_cot),
            t_dot(normed_one, value_low),
            w_out_grad,
        ],
        axis=1,
    ).astype(LOW)
    summed = expert_scatter(local, depth, 14)
    w_query_grad, w_key_grad, w_value_grad, w_out_grad = jnp.split(summed, 4, axis=1)
    vectors = jnp.concatenate([router_grad, norm1_grad[None], norm2_grad[None]], axis=0)
    vectors = lax.psum(lax.psum_scatter(vectors, "expert", scatter_dimension=1, tiled=True), "tensor")
    gains = lax.psum_scatter(
        jnp.concatenate([q_gain_local, k_gain_local], axis=0), "expert", scatter_dimension=1, tiled=True
    )
    return (
        output,
        input_grad,
        vectors[experts],
        gains[:heads],
        gains[heads:],
        w_query_grad,
        w_key_grad,
        w_value_grad,
        w_out_grad.T,
        vectors[experts + 1],
        vectors[:experts].T,
        w_gate_grad,
        w_up_grad,
        w_down_grad,
    )


def solution(mesh):
    placed = (
        P("expert", None),
        P("expert"),
        P("expert", None),
        P(),
        P("tensor", None),
        P("tensor", None),
        P(None, "tensor"),
        P(None, "tensor"),
        P(None, "tensor"),
        P("tensor", None),
        P(),
        P(),
        P("expert", None, "tensor"),
        P("expert", None, "tensor"),
        P("expert", "tensor", None),
        P("expert", None),
    )
    return jax.shard_map(
        functools.partial(body, mesh.shape["expert"], mesh.shape["tensor"]),
        mesh=mesh,
        in_specs=placed,
        out_specs=(
            P("expert", None),
            P("expert", None),
            P("expert"),
            P("tensor", "expert"),
            P("tensor", "expert"),
            P("expert", "tensor"),
            P("expert", "tensor"),
            P("expert", "tensor"),
            P("tensor", "expert"),
            P("expert"),
            P("expert", None),
            P("expert", None, "tensor"),
            P("expert", None, "tensor"),
            P("expert", "tensor", None),
        ),
        check_vma=False,
    )
```

```python
import functools

import jax
import jax.numpy as jnp
from jax import lax
from jax.experimental import pallas as pl
from jax.experimental.pallas import tpu as pltpu
from jax.sharding import PartitionSpec as P

HD = 128
TOP = 8
WINDOW = 1024
LENGTH = 2048


NORM_EPSILON = 1e-05
HIGHEST_PRECISION = lax.Precision.HIGHEST


def for_sending(value):
    return jax.tree.map(lambda a: a.astype(jnp.bfloat16) if a.dtype == jnp.float32 else a, value)


def shifted(value, axis, steps):
    count = lax.axis_size(axis)
    initial, last = (max(0, -steps), min(count, count - steps))
    return lax.ppermute(value, axis, [(source, source + steps) for source in range(initial, last)])


def rope_tables(positions):
    half_width = HD // 2
    frequency = 10000.0 ** (-jnp.arange(half_width, dtype=jnp.float32) * 2.0 / HD)
    angles = positions.astype(jnp.float32)[:, None] * frequency[None, :]
    angles = jnp.concatenate([angles, angles], axis=-1)
    return (jnp.cos(angles)[:, None, :], jnp.sin(angles)[:, None, :])


def rotate(values, cosine, sine):
    half_width = values.shape[-1] // 2
    turned = jnp.concatenate([-values[..., half_width:], values[..., :half_width]], axis=-1)
    return values * cosine + turned * sine


def rotate_back(grads, cosine, sine):
    half_width = grads.shape[-1] // 2
    scaled = grads * sine
    turned = jnp.concatenate([scaled[..., half_width:], -scaled[..., :half_width]], axis=-1)
    return grads * cosine + turned


def previous_block(pieces):
    return jax.tree.map(
        lambda part, own: part.astype(own.dtype), shifted(for_sending(pieces), "expert", 1), pieces
    )


def following_block(pieces):
    return shifted((for_sending(pieces[0]), for_sending(pieces[1])), "expert", -1)


def body_routed(
    tokens,
    documents,
    routes,
    norm1_gain,
    q_gain,
    k_gain,
    w_query,
    w_key,
    w_value,
    w_out,
    norm2_gain,
    router_w,
    w_gate,
    w_up,
    w_down,
    out_grad,
):
    row_count, model_width = tokens.shape
    groups = lax.axis_size("expert")
    local_experts = w_gate.shape[0]
    experts = local_experts * groups
    capacity = 2 * row_count * TOP // experts
    slots_group = local_experts * capacity
    heads = w_query.shape[1] // HD
    score_scale = HD ** (-0.5)
    first_row = lax.axis_index("expert") * row_count
    positions = first_row + jnp.arange(row_count, dtype=jnp.int32)
    cosine, sine = rope_tables(positions % LENGTH)
    inputs = tokens.astype(jnp.float32)
    scale_one = lax.rsqrt(jnp.mean(inputs * inputs, axis=-1, keepdims=True) + NORM_EPSILON)
    normed_one = (inputs * scale_one * norm1_gain).astype(jnp.bfloat16)
    query_raw = jnp.dot(normed_one, w_query, preferred_element_type=jnp.float32)
    key_raw = jnp.dot(normed_one, w_key, preferred_element_type=jnp.float32)
    values = jnp.dot(normed_one, w_value, preferred_element_type=jnp.float32).astype(jnp.bfloat16)
    query_square, key_square = lax.psum(
        (jnp.sum(query_raw * query_raw, axis=-1), jnp.sum(key_raw * key_raw, axis=-1)), "tensor"
    )
    query_scale = lax.rsqrt(query_square / model_width + NORM_EPSILON)[:, None]
    key_scale = lax.rsqrt(key_square / model_width + NORM_EPSILON)[:, None]
    query_gain = q_gain.reshape(-1)
    key_gain = k_gain.reshape(-1)
    queries = rotate(
        (query_raw * query_scale * query_gain).reshape(row_count, heads, HD), cosine, sine
    ).astype(jnp.bfloat16)
    key_heads = rotate(
        (key_raw * key_scale * key_gain).reshape(row_count, heads, HD), cosine, sine
    ).astype(jnp.bfloat16)
    value_heads = values.reshape(row_count, heads, HD)
    labels = jnp.stack([documents // 256, documents % 256]).astype(jnp.bfloat16)
    previous_one = previous_block((key_heads, value_heads, labels))
    previous_two = previous_block(previous_one)
    all_keys = jnp.concatenate([previous_two[0], previous_one[0], key_heads], axis=0)
    all_values = jnp.concatenate([previous_two[1], previous_one[1], value_heads], axis=0)
    all_labels = jnp.concatenate([previous_two[2], previous_one[2], labels], axis=1)
    key_pos = first_row - 2 * row_count + jnp.arange(3 * row_count, dtype=jnp.int32)
    same_doc = (all_labels[0][None, :] == labels[0][:, None]) & (
        all_labels[1][None, :] == labels[1][:, None]
    )
    allowed = (
        same_doc
        & (key_pos[None, :] <= positions[:, None])
        & (positions[:, None] - key_pos[None, :] < WINDOW)
        & (key_pos[None, :] >= 0)
    )

    def masked_scores():
        raw_scores = (
            jnp.einsum("qhd,khd->hqk", queries, all_keys, preferred_element_type=jnp.float32)
            * score_scale
        )
        return jnp.where(allowed[None], raw_scores, -1e30)

    scores = masked_scores()
    highest = jnp.max(scores, axis=-1, keepdims=True)
    weights = jnp.where(allowed[None], jnp.exp(scores - highest), 0.0)
    denominator = jnp.sum(weights, axis=-1, keepdims=True)
    log_total = highest + jnp.log(denominator)
    attn_probs = weights / denominator
    attended = jnp.einsum(
        "hqk,khd->qhd",
        attn_probs.astype(jnp.bfloat16),
        all_values,
        preferred_element_type=jnp.float32,
    )
    attended = attended.reshape(row_count, -1).astype(jnp.bfloat16)
    attention = lax.psum(jnp.dot(attended, w_out, preferred_element_type=jnp.float32), "tensor")
    state = inputs + attention
    scale_two = lax.rsqrt(jnp.mean(state * state, axis=-1, keepdims=True) + NORM_EPSILON)
    normed_two = (state * scale_two * norm2_gain).astype(jnp.bfloat16)
    router_probs = jax.nn.softmax(
        jnp.dot(normed_two, router_w, preferred_element_type=jnp.float32), axis=-1
    )
    chosen = (routes[:, :, None] == jnp.arange(experts, dtype=jnp.int32)[None, None, :]).astype(
        jnp.float32
    )
    gates = jnp.sum(chosen * router_probs[:, None, :], axis=-1)
    flat_routes = routes.reshape(-1)
    onehot = (flat_routes[:, None] == jnp.arange(experts, dtype=jnp.int32)[None, :]).astype(
        jnp.int32
    )
    slot_index = jnp.sum(jnp.cumsum(onehot, axis=0) * onehot, axis=1) - 1
    target = flat_routes * capacity + slot_index
    source = (
        jnp.full((experts * capacity,), -1, jnp.int32)
        .at[target]
        .set(jnp.arange(row_count * TOP, dtype=jnp.int32))
    )
    live_slot = source >= 0
    pick_index = jnp.maximum(source, 0)
    send_rows = jnp.where(
        live_slot[:, None], normed_two[pick_index // TOP], jnp.zeros((), jnp.bfloat16)
    ).reshape(groups, slots_group, model_width)
    grad_float = out_grad.astype(jnp.float32)
    pick_grads = (
        (gates[:, :, None] * grad_float[:, None, :])
        .astype(jnp.bfloat16)
        .reshape(row_count * TOP, model_width)
    )
    send_grads = jnp.where(
        live_slot[:, None], pick_grads[pick_index], jnp.zeros((), jnp.bfloat16)
    ).reshape(groups, slots_group, model_width)
    arrived = lax.all_to_all(send_rows, "expert", split_axis=0, concat_axis=0, tiled=True)
    stacked = arrived.reshape(groups, local_experts, capacity, model_width)
    gate_pre = jnp.einsum("secd,edf->secf", stacked, w_gate, preferred_element_type=jnp.float32)
    up_pre = jnp.einsum("secd,edf->secf", stacked, w_up, preferred_element_type=jnp.float32)
    activated = jax.nn.silu(gate_pre)
    inner_act = (activated * up_pre).astype(jnp.bfloat16)
    produced = jnp.einsum(
        "secf,efd->secd", inner_act, w_down, preferred_element_type=jnp.float32
    ).astype(jnp.bfloat16)
    returned = lax.all_to_all(
        produced.reshape(groups, slots_group, model_width),
        "expert",
        split_axis=0,
        concat_axis=0,
        tiled=True,
    )
    back_rows = (
        returned.reshape(experts * capacity, model_width)[target]
        .reshape(row_count, TOP, model_width)
        .astype(jnp.float32)
    )
    expert_part = jnp.sum(gates[:, :, None] * back_rows, axis=1)
    expert_mix = lax.psum(expert_part.astype(jnp.bfloat16), "tensor").astype(jnp.float32)
    output = (state + expert_mix).astype(jnp.bfloat16)
    gate_part = jnp.sum(grad_float[:, None, :] * back_rows, axis=-1)
    arrived_grad = lax.all_to_all(send_grads, "expert", split_axis=0, concat_axis=0, tiled=True)
    slot_grad = arrived_grad.reshape(groups, local_experts, capacity, model_width)
    w_down_grad = jnp.einsum(
        "secf,secd->efd", inner_act, slot_grad, preferred_element_type=jnp.float32
    )
    inner_grad = jnp.einsum("secd,efd->secf", slot_grad, w_down, preferred_element_type=jnp.float32)
    logistic = jax.nn.sigmoid(gate_pre)
    gate_pre_grad = (inner_grad * up_pre * logistic * (1.0 + gate_pre * (1.0 - logistic))).astype(
        jnp.bfloat16
    )
    up_pre_grad = (inner_grad * activated).astype(jnp.bfloat16)
    w_gate_grad = jnp.einsum(
        "secd,secf->edf", stacked, gate_pre_grad, preferred_element_type=jnp.float32
    )
    w_up_grad = jnp.einsum(
        "secd,secf->edf", stacked, up_pre_grad, preferred_element_type=jnp.float32
    )
    row_grad = jnp.einsum(
        "secf,edf->secd", gate_pre_grad, w_gate, preferred_element_type=jnp.float32
    )
    row_grad = (
        row_grad
        + jnp.einsum("secf,edf->secd", up_pre_grad, w_up, preferred_element_type=jnp.float32)
    ).astype(jnp.bfloat16)
    grad_back = lax.all_to_all(
        row_grad.reshape(groups, slots_group, model_width),
        "expert",
        split_axis=0,
        concat_axis=0,
        tiled=True,
    )
    grad_picks = (
        grad_back.reshape(experts * capacity, model_width)[target]
        .reshape(row_count, TOP, model_width)
        .astype(jnp.float32)
    )
    normed_part = jnp.sum(grad_picks, axis=1)
    normed_two_grad, gate_cot = lax.psum((normed_part, gate_part), "tensor")
    prob_cot = jnp.sum(gate_cot[:, :, None] * chosen, axis=1)
    logit_cot = router_probs * (prob_cot - jnp.sum(router_probs * prob_cot, axis=-1, keepdims=True))
    router_float = router_w.astype(jnp.float32)
    normed_two_grad = normed_two_grad + jnp.einsum(
        "te,de->td", logit_cot, router_float, precision=HIGHEST_PRECISION
    )
    router_grad = jnp.einsum(
        "td,te->de", normed_two.astype(jnp.float32), logit_cot, precision=HIGHEST_PRECISION
    )
    norm2_grad = jnp.sum(normed_two_grad * state * scale_two, axis=0)
    inner_two = jnp.sum(normed_two_grad * norm2_gain * state, axis=-1, keepdims=True)
    state_cot = (
        grad_float
        + scale_two * norm2_gain * normed_two_grad
        - state * scale_two**3 * inner_two / model_width
    )
    state_low = state_cot.astype(jnp.bfloat16)
    w_out_grad = jnp.einsum("tf,td->fd", attended, state_low, preferred_element_type=jnp.float32)
    attended_cot = (
        jnp.einsum("td,fd->tf", state_low, w_out, preferred_element_type=jnp.float32)
        .astype(jnp.bfloat16)
        .reshape(row_count, heads, HD)
    )
    scores = masked_scores()
    attn_probs = jnp.where(allowed[None], jnp.exp(scores - log_total), 0.0)
    value_cot_all = jnp.einsum(
        "hqk,qhd->khd",
        attn_probs.astype(jnp.bfloat16),
        attended_cot,
        preferred_element_type=jnp.float32,
    )
    prob_grad = jnp.einsum(
        "qhd,khd->hqk", attended_cot, all_values, preferred_element_type=jnp.float32
    )
    delta = jnp.sum(attn_probs * prob_grad, axis=-1, keepdims=True)
    score_cot = (attn_probs * (prob_grad - delta)).astype(jnp.bfloat16)
    query_cot = (
        jnp.einsum("hqk,khd->qhd", score_cot, all_keys, preferred_element_type=jnp.float32)
        * score_scale
    )
    key_cot_all = (
        jnp.einsum("hqk,qhd->khd", score_cot, queries, preferred_element_type=jnp.float32)
        * score_scale
    )
    carried = following_block((key_cot_all[:row_count], value_cot_all[:row_count]))
    carried = following_block(
        (
            key_cot_all[row_count : 2 * row_count] + carried[0],
            value_cot_all[row_count : 2 * row_count] + carried[1],
        )
    )
    key_cot = key_cot_all[2 * row_count :] + carried[0]
    value_cot = value_cot_all[2 * row_count :] + carried[1]
    query_norm_cot = rotate_back(query_cot, cosine, sine).reshape(row_count, -1)
    key_norm_cot = rotate_back(key_cot, cosine, sine).reshape(row_count, -1)
    q_gain_local = jnp.sum(query_norm_cot * query_raw * query_scale, axis=0).reshape(heads, HD)
    k_gain_local = jnp.sum(key_norm_cot * key_raw * key_scale, axis=0).reshape(heads, HD)
    query_inner, key_inner = lax.psum(
        (
            jnp.sum(query_norm_cot * query_gain * query_raw, axis=-1),
            jnp.sum(key_norm_cot * key_gain * key_raw, axis=-1),
        ),
        "tensor",
    )
    query_raw_cot = (
        query_scale * query_gain * query_norm_cot
        - query_raw * query_scale**3 * query_inner[:, None] / model_width
    ).astype(jnp.bfloat16)
    key_raw_cot = (
        key_scale * key_gain * key_norm_cot
        - key_raw * key_scale**3 * key_inner[:, None] / model_width
    ).astype(jnp.bfloat16)
    value_low = value_cot.reshape(row_count, -1).astype(jnp.bfloat16)
    w_query_local = jnp.einsum(
        "td,tf->df", normed_one, query_raw_cot, preferred_element_type=jnp.float32
    )
    w_key_local = jnp.einsum(
        "td,tf->df", normed_one, key_raw_cot, preferred_element_type=jnp.float32
    )
    w_value_local = jnp.einsum(
        "td,tf->df", normed_one, value_low, preferred_element_type=jnp.float32
    )
    normed_part_one = jnp.einsum(
        "tf,df->td", query_raw_cot, w_query, preferred_element_type=jnp.float32
    )
    normed_part_one = normed_part_one + jnp.einsum(
        "tf,df->td", key_raw_cot, w_key, preferred_element_type=jnp.float32
    )
    normed_part_one = normed_part_one + jnp.einsum(
        "tf,df->td", value_low, w_value, preferred_element_type=jnp.float32
    )
    normed_one_grad = lax.psum(normed_part_one.astype(jnp.bfloat16), "tensor").astype(jnp.float32)
    norm1_grad = jnp.sum(normed_one_grad * inputs * scale_one, axis=0)
    inner_one = jnp.sum(normed_one_grad * norm1_gain * inputs, axis=-1, keepdims=True)
    input_grad = (
        state_cot
        + scale_one * norm1_gain * normed_one_grad
        - inputs * scale_one**3 * inner_one / model_width
    )
    summed = (
        lax.psum_scatter(
            w_query_local.astype(jnp.bfloat16), "expert", scatter_dimension=0, tiled=True
        ).astype(jnp.float32),
        lax.psum_scatter(
            w_key_local.astype(jnp.bfloat16), "expert", scatter_dimension=0, tiled=True
        ).astype(jnp.float32),
        lax.psum_scatter(
            w_value_local.astype(jnp.bfloat16), "expert", scatter_dimension=0, tiled=True
        ).astype(jnp.float32),
        lax.psum_scatter(
            w_out_grad.astype(jnp.bfloat16), "expert", scatter_dimension=1, tiled=True
        ).astype(jnp.float32),
        lax.psum_scatter(
            router_grad.astype(jnp.bfloat16), "expert", scatter_dimension=0, tiled=True
        ).astype(jnp.float32),
        lax.psum_scatter(
            norm1_grad.astype(jnp.bfloat16), "expert", scatter_dimension=0, tiled=True
        ).astype(jnp.float32),
        lax.psum_scatter(
            norm2_grad.astype(jnp.bfloat16), "expert", scatter_dimension=0, tiled=True
        ).astype(jnp.float32),
        lax.psum_scatter(
            q_gain_local.astype(jnp.bfloat16), "expert", scatter_dimension=1, tiled=True
        ).astype(jnp.float32),
        lax.psum_scatter(
            k_gain_local.astype(jnp.bfloat16), "expert", scatter_dimension=1, tiled=True
        ).astype(jnp.float32),
    )
    return (
        output,
        input_grad,
        summed[5],
        summed[7],
        summed[8],
        summed[0],
        summed[1],
        summed[2],
        summed[3],
        summed[6],
        summed[4],
        w_gate_grad,
        w_up_grad,
        w_down_grad,
    )


MESH = pl.DeviceIdType.MESH
ANY = pl.BlockSpec(memory_space=pl.ANY)
VMEM = pl.BlockSpec(memory_space=pltpu.VMEM)
VMEM_BYTES = 60 * 1024 * 1024
LOW = jnp.bfloat16
FULL = jnp.float32


def place():
    group, part = lax.axis_index("expert"), lax.axis_index("tensor")
    return group // 2, group % 2, part // 2, part % 2


def device(z, x, y, core):
    return (2 * z + x, 2 * y + core)


def swapped(index, step):
    result, bit = index, 1
    while bit <= step:
        if step & bit:
            result = result + bit - 2 * bit * ((index // bit) % 2)
        bit *= 2
    return result


def greet(partners):
    barrier = pltpu.get_barrier_semaphore()
    for partner in partners:
        pl.semaphore_signal(barrier, inc=1, device_id=partner, device_id_type=MESH)
    pl.semaphore_wait(barrier, len(partners))


def remote(source, target, send, arrive, to):
    return pltpu.make_async_remote_copy(
        src_ref=source, dst_ref=target, send_sem=send, recv_sem=arrive, device_id=to, device_id_type=MESH
    )


def dma(*shape):
    return pltpu.SemaphoreType.DMA(shape)


def comm_params(number):
    return pltpu.CompilerParams(collective_id=number, has_side_effects=True, vmem_limit_bytes=VMEM_BYTES)


def add_rows(target, sources, rows, step=16):
    @pl.loop(0, rows // step)
    def _(index):
        part = pl.ds(index * step, step)
        total = sources[0][part].astype(FULL)
        for source in sources[1:]:
            total = total + source[part].astype(FULL)
        target[part] = total.astype(target.dtype)


class Copies:
    def __init__(self):
        self.open = []

    def start(self, copy):
        copy.start()
        self.open.append([copy, True])
        return copy

    def arrived(self, copy):
        copy.wait_recv()
        for entry in self.open:
            if entry[0] is copy:
                entry[1] = False

    def finish(self):
        for copy, receiving in self.open:
            copy.wait_send()
            if receiving:
                copy.wait_recv()


class Gather:
    def __init__(self, copies, block, target, rows, z_send, z_recv, p_send, p_recv):
        self.copies, self.block, self.target, self.rows = copies, block, target, rows
        self.z_send, self.z_recv, self.p_send, self.p_recv = z_send, z_recv, p_send, p_recv
        z, x, y, core = place()
        self.over_x, self.over_y = device(z, 1 - x, y, core), device(z, x, 1 - y, core)
        self.here, self.x_place, self.y_place = 2 * x + y, 2 * (1 - x) + y, 2 * x + 1 - y
        self.column = [device(swapped(z, step), x, y, core) for step in range(target.shape[0])]
        self.along, self.planes, self.diagonals = {}, {}, {}

    def at(self, step, spot, part):
        half = self.rows // 2
        if part is None:
            return self.target.at[step, pl.ds(pl.multiple_of(spot * self.rows, self.rows), self.rows)]
        return self.target.at[step, pl.ds(pl.multiple_of(spot * self.rows + part * half, half), half)]

    def begin(self):
        self.spread(0)
        for step in range(1, len(self.column)):
            self.along[step] = self.copies.start(
                remote(self.block, self.at(step, self.here, None), self.z_send.at[step], self.z_recv.at[step], self.column[step])
            )

    def spread(self, step):
        if step:
            self.copies.arrived(self.along[step])
        half = self.rows // 2
        planes = []
        for number, (to, part) in enumerate([(self.over_x, 0), (self.over_y, 1), (self.over_x, 1), (self.over_y, 0)]):
            here = self.at(step, self.here, part)
            source = here if step else self.block.at[pl.ds(part * half, half)]
            planes.append(self.copies.start(remote(source, here, self.p_send.at[step, number], self.p_recv.at[step, number], to)))
        self.planes[step] = planes

    def turn(self, step):
        self.copies.arrived(self.planes[step][0])
        passed = self.at(step, self.x_place, 0)
        first = self.copies.start(remote(passed, passed, self.p_send.at[step, 4], self.p_recv.at[step, 4], self.over_y))
        self.copies.arrived(self.planes[step][1])
        passed = self.at(step, self.y_place, 1)
        second = self.copies.start(remote(passed, passed, self.p_send.at[step, 5], self.p_recv.at[step, 5], self.over_x))
        self.diagonals[step] = (first, second)

    def complete(self, step):
        for copy in self.planes[step][2:] + list(self.diagonals[step]):
            self.copies.arrived(copy)


class Scatter:
    def __init__(self, copies, work, diagonal, from_x, from_y, from_z, rows, send, recv):
        self.copies, self.work, self.rows, self.send, self.recv = copies, work, rows, send, recv
        self.diagonal, self.from_x, self.from_y, self.from_z = diagonal, from_x, from_y, from_z
        z, x, y, core = place()
        self.over_x, self.over_y = device(z, 1 - x, y, core), device(z, x, 1 - y, core)
        self.here, self.x_place, self.y_place = 2 * x + y, 2 * (1 - x) + y, 2 * x + 1 - y
        self.far = 2 * (1 - x) + 1 - y
        self.column = [device(swapped(z, step), x, y, core) for step in range(work.shape[0])]
        self.corners, self.sides, self.along = {}, {}, {}

    def at(self, step, spot, part=None):
        half = self.rows // 2
        if part is None:
            return self.work.at[step, pl.ds(pl.multiple_of(spot * self.rows, self.rows), self.rows)]
        return self.work.at[step, pl.ds(pl.multiple_of(spot * self.rows + part * half, half), half)]

    def copy(self, step, number, source, target, to):
        return self.copies.start(remote(source, target, self.send.at[step, number], self.recv.at[step, number], to))

    def corner(self, step):
        self.corners[step] = (
            self.copy(step, 0, self.at(step, self.far, 0), self.diagonal.at[step, 0], self.over_y),
            self.copy(step, 1, self.at(step, self.far, 1), self.diagonal.at[step, 1], self.over_x),
        )

    def side(self, step):
        via_y, via_x = self.corners[step]
        self.copies.arrived(via_y)
        add_rows(self.at(step, self.x_place, 0), [self.at(step, self.x_place, 0), self.diagonal.at[step, 0]], self.rows // 2)
        to_x = self.copy(step, 2, self.at(step, self.x_place), self.from_x.at[step], self.over_x)
        self.copies.arrived(via_x)
        add_rows(self.at(step, self.y_place, 1), [self.at(step, self.y_place, 1), self.diagonal.at[step, 1]], self.rows // 2)
        to_y = self.copy(step, 3, self.at(step, self.y_place), self.from_y.at[step], self.over_y)
        self.sides[step] = (to_x, to_y)

    def climb(self, step):
        for copy in self.sides[step]:
            self.copies.arrived(copy)
        if step:
            here = self.at(step, self.here)
            add_rows(here, [here, self.from_x.at[step], self.from_y.at[step]], self.rows)
            self.along[step] = self.copy(step, 4, here, self.from_z.at[step], self.column[step])

    def result(self, target):
        for copy in self.along.values():
            self.copies.arrived(copy)
        terms = [self.at(0, self.here), self.from_x.at[0], self.from_y.at[0]]
        add_rows(target, terms + [self.from_z.at[step] for step in self.along], self.rows)

    @staticmethod
    def scratch(depth, rows, width):
        return [
            pltpu.VMEM((depth, 2, rows // 2, width), LOW),
            pltpu.VMEM((depth, rows, width), LOW),
            pltpu.VMEM((depth, rows, width), LOW),
            pltpu.VMEM((depth, rows, width), LOW),
            dma(depth, 5),
            dma(depth, 5),
        ]


def greet_column_and_plane(depth):
    z, x, y, core = place()
    greet(
        [device(swapped(z, step), x, y, core) for step in range(1, depth)]
        + [device(z, 1 - x, y, core), device(z, x, 1 - y, core)]
    )


def gather_rows_kernel(depth, rows, x_ref, o_ref, z_send, z_recv, p_send, p_recv, local):
    z, x, y, core = place()
    greet_column_and_plane(depth)
    copies = Copies()
    gather = Gather(copies, x_ref, o_ref, rows, z_send, z_recv, p_send, p_recv)
    gather.begin()
    own = pltpu.make_async_copy(x_ref, gather.at(0, gather.here, None), local.at[0])
    own.start()
    for step in range(depth):
        if step:
            gather.spread(step)
        gather.turn(step)
    own.wait()
    copies.finish()


def gather_rows(block, depth, number):
    rows, width = block.shape
    return pl.pallas_call(
        functools.partial(gather_rows_kernel, depth, rows),
        out_shape=jax.ShapeDtypeStruct((depth, 4 * rows, width), block.dtype),
        in_specs=[ANY],
        out_specs=ANY,
        scratch_shapes=[dma(depth), dma(depth), dma(depth, 6), dma(depth, 6), dma(1)],
        compiler_params=comm_params(number),
    )(block)


def experts_kernel(
    depth, rows, local, hidden,
    x_ref, gates_ref, grad_ref, gate_ref, up_ref, down_ref,
    sum_ref, cots_ref, normed_ref, gated_ref, gate_grad_ref, up_grad_ref, produced_ref,
    wg, wu, wd, x_all, grads, work, y_out, gated, gate_grad, up_grad, gates, gate_wide, cots, cot_rows,
    diagonal, from_x, from_y, from_z, r_send, r_recv,
    z_send, z_recv, p_send, p_recv, s_send, s_recv, w_send, w_recv, w_load, g_load, saves, local_sem,
):
    z, x, y, core = place()
    here, sibling = 2 * x + y, device(z, x, y, 1 - core)
    others = [
        (step, turn, (swapped(z, step), swapped(x, turn // 2), swapped(y, turn % 2)))
        for step in range(depth)
        for turn in range(4)
        if step or turn
    ]
    greet([device(*other, core) for _, _, other in others] + [sibling])
    copies = Copies()
    gather = Gather(copies, x_ref, x_all, rows, z_send, z_recv, p_send, p_recv)
    gather.begin()
    plain = []

    def fetch(source, target, sem):
        copy = pltpu.make_async_copy(source, target, sem)
        copy.start()
        return copy

    plain.append(fetch(x_ref, gather.at(0, here, None), local_sem.at[0]))
    weights = []
    for index in range(local):
        first = pl.multiple_of((core * local + index) * hidden, hidden)
        columns = pl.ds(first, hidden)
        for number, (source, target) in enumerate(
            [(gate_ref, wg.at[:, columns]), (up_ref, wu.at[:, columns]), (down_ref, wd.at[columns])]
        ):
            weights.append(copies.start(remote(source.at[index], target, w_send.at[number, index], w_recv.at[number, index], sibling)))
            plain.append(fetch(source.at[index], target, w_load.at[number, index]))
    smalls = []
    for step, turn, other in others:
        oz, ox, oy = other
        smalls.append(
            copies.start(
                remote(
                    gates_ref.at[2 * oz + ox], gates.at[step, here], s_send.at[0, step, turn], s_recv.at[0, step, turn],
                    device(oz, ox, oy, core),
                )
            )
        )
    plain.append(fetch(gates_ref.at[2 * z + x], gates.at[0, here], local_sem.at[1]))
    grad_copies = [fetch(grad_ref.at[0], grads.at[0], g_load.at[0])]
    scatter = Scatter(copies, work, diagonal, from_x, from_y, from_z, rows, r_send, r_recv)
    saving, producing, keeping = [], [], []
    wave_rows = 4 * rows
    lanes = lax.broadcasted_iota(jnp.int32, (wave_rows, 128), 1)

    def first_half(step):
        for copy in saving:
            copy.wait()
        saving.clear()
        for spot in range(4):
            padded = jnp.concatenate([gates[step, spot], jnp.zeros((120, 128), FULL)], axis=0)
            gate_wide[pl.ds(spot * rows, rows), :] = padded.T
        cots[...] = jnp.zeros_like(cots)
        grad_copies[step].wait()
        if step + 1 < depth:
            grad_copies.append(fetch(grad_ref.at[step + 1], grads.at[(step + 1) % 2], g_load.at[(step + 1) % 2]))
        grad = grads.at[step % 2]

        @pl.loop(0, 2 * local)
        def _(unit):
            columns = pl.ds(pl.multiple_of(unit * hidden, hidden), hidden)
            expert = lax.rem(unit, local)
            gate_pre = dot(x_all[step], wg[:, columns])
            up_pre = dot(x_all[step], wu[:, columns])
            back = dot_t(grad[...], wd[columns, :])
            logistic = 1.0 / (1.0 + jnp.exp(-gate_pre))
            activated = gate_pre * logistic
            inner = activated * up_pre
            cot = jnp.sum(inner * back, axis=-1, keepdims=True)
            cots[...] += jnp.where(lanes == expert, cot, 0.0)
            gate = jnp.sum(jnp.where(lanes == expert, gate_wide[...], 0.0), axis=-1, keepdims=True)
            gated[:, columns] = (gate * inner).astype(LOW)
            inner_grad = gate * back
            gate_grad[:, columns] = (inner_grad * up_pre * logistic * (1.0 + gate_pre * (1.0 - logistic))).astype(LOW)
            up_grad[:, columns] = (inner_grad * activated).astype(LOW)

        for spot in range(4):
            cot_rows[step, spot] = cots[pl.ds(spot * rows, rows), :].T[:8]
        for number, (source, target) in enumerate([(gated, gated_ref), (gate_grad, gate_grad_ref), (up_grad, up_grad_ref)]):
            saving.append(fetch(source, target.at[step], saves.at[number]))
        keeping.append(fetch(x_all.at[step], normed_ref.at[step], saves.at[4 + step]))

    def second_half(step):
        for copy in producing:
            copy.wait()
        producing.clear()
        tile = 512

        @pl.loop(0, x_all.shape[2] // tile)
        def _(index):
            columns = pl.ds(pl.multiple_of(index * tile, tile), tile)
            y_out[:, columns] = dot(gated[...], wd[:, columns]).astype(LOW)
            work[step, :, columns] = (dot_t(gate_grad[...], wg[columns, :]) + dot_t(up_grad[...], wu[columns, :])).astype(LOW)

        producing.append(fetch(y_out, produced_ref.at[step], saves.at[3]))

    gather.turn(0)
    if depth > 1:
        gather.spread(1)
    gather.complete(0)
    for copy in plain:
        copy.wait()
    for copy in weights + smalls:
        copies.arrived(copy)
    for step in range(depth):
        if step:
            gather.complete(step)
        first_half(step)
        if step + 1 < depth:
            gather.turn(step + 1)
        if step + 2 < depth:
            gather.spread(step + 2)
        if step >= 1:
            scatter.side(step - 1)
        if step >= 2:
            scatter.climb(step - 2)
        second_half(step)
        scatter.corner(step)
    for step, turn, (oz, ox, oy) in others:
        copies.start(
            remote(
                cot_rows.at[step, 2 * ox + oy], cots_ref.at[step, here], s_send.at[1, step, turn], s_recv.at[1, step, turn],
                device(oz, ox, oy, core),
            )
        )
    own_cots = fetch(cot_rows.at[0, here], cots_ref.at[0, here], local_sem.at[2])
    if depth > 1:
        scatter.climb(depth - 2)
    scatter.side(depth - 1)
    scatter.climb(depth - 1)
    scatter.result(sum_ref)
    own_cots.wait()
    for copy in saving + producing + keeping:
        copy.wait()
    copies.finish()


def run_experts(block, gates, grads, w_gate, w_up, w_down, number):
    depth, wave, width = grads.shape
    rows = wave // 4
    local, _, hidden = w_gate.shape
    units = 2 * local * hidden
    kept = jax.ShapeDtypeStruct((depth, wave, units), LOW)
    wide = jax.ShapeDtypeStruct((depth, wave, width), LOW)
    return pl.pallas_call(
        functools.partial(experts_kernel, depth, rows, local, hidden),
        out_shape=(
            jax.ShapeDtypeStruct((rows, width), FULL),
            jax.ShapeDtypeStruct((depth, 4, 8, 128), FULL),
            wide, kept, kept, kept, wide,
        ),
        in_specs=[ANY] * 6,
        out_specs=(VMEM, VMEM, ANY, ANY, ANY, ANY, ANY),
        scratch_shapes=[
            pltpu.VMEM((width, units), LOW), pltpu.VMEM((width, units), LOW), pltpu.VMEM((units, width), LOW),
            pltpu.VMEM((depth, wave, width), LOW), pltpu.VMEM((2, wave, width), LOW),
            pltpu.VMEM((depth, wave, width), LOW), pltpu.VMEM((wave, width), LOW),
            pltpu.VMEM((wave, units), LOW), pltpu.VMEM((wave, units), LOW), pltpu.VMEM((wave, units), LOW),
            pltpu.VMEM((depth, 4, 8, 128), FULL), pltpu.VMEM((wave, 128), FULL), pltpu.VMEM((wave, 128), FULL),
            pltpu.VMEM((depth, 4, 8, 128), FULL),
        ]
        + Scatter.scratch(depth, rows, width)
        + [
            dma(depth), dma(depth), dma(depth, 6), dma(depth, 6), dma(2, depth, 4), dma(2, depth, 4),
            dma(3, local), dma(3, local), dma(3, local), dma(2), dma(4 + depth), dma(3),
        ],
        compiler_params=comm_params(number),
    )(block, gates, grads, w_gate, w_up, w_down)


def scatter_rows_kernel(depth, rows, p_ref, o_ref, work, diagonal, from_x, from_y, from_z, send, recv, load):
    greet_column_and_plane(depth)
    copies = Copies()
    order = [step for step in range(1, depth)] + [0]
    loads = {}
    for step in order:
        loads[step] = pltpu.make_async_copy(p_ref.at[step], work.at[step], load.at[step])
        loads[step].start()
    scatter = Scatter(copies, work, diagonal, from_x, from_y, from_z, rows, send, recv)
    for step in order:
        loads[step].wait()
        scatter.corner(step)
    for step in order:
        scatter.side(step)
    for step in order:
        scatter.climb(step)
    scatter.result(o_ref)
    copies.finish()


def scatter_rows(parts, number):
    depth, wave, width = parts.shape
    rows = wave // 4
    return pl.pallas_call(
        functools.partial(scatter_rows_kernel, depth, rows),
        out_shape=jax.ShapeDtypeStruct((rows, width), FULL),
        in_specs=[ANY],
        out_specs=VMEM,
        scratch_shapes=[pltpu.VMEM(parts.shape, parts.dtype)] + Scatter.scratch(depth, rows, width) + [dma(depth)],
        compiler_params=comm_params(number),
    )(parts)


def pair_swap_kernel(count, *refs):
    ins, outs, (send, recv) = refs[:count], refs[count : 2 * count], refs[2 * count :]
    z, x, y, core = place()
    sibling = device(z, x, y, 1 - core)
    greet([sibling])
    waits = []
    for index in range(count):
        copy = remote(ins[index].at[1 - core], outs[index], send.at[index], recv.at[index], sibling)
        copy.start()
        waits.append(copy)
    for copy in waits:
        copy.wait()


def pair_swap(arrays, number):
    count = len(arrays)
    return pl.pallas_call(
        functools.partial(pair_swap_kernel, count),
        out_shape=tuple(jax.ShapeDtypeStruct(a.shape[1:], a.dtype) for a in arrays),
        in_specs=[ANY] * count,
        out_specs=(ANY,) * count,
        scratch_shapes=[dma(count), dma(count)],
        compiler_params=comm_params(number),
    )(*arrays)


def tensor_scatter_kernel(rows, p_ref, o_ref, work, from_pair, from_y, load, send, recv):
    z, x, y, core = place()
    sibling, over_y = device(z, x, y, 1 - core), device(z, x, 1 - y, core)
    greet([sibling, over_y])
    fetch = pltpu.make_async_copy(p_ref, work, load.at[0])
    fetch.start()
    pairs = []
    for turn in (1, 0):
        row = swapped(y, turn)
        copy = remote(p_ref.at[row, 1 - core], from_pair.at[turn], send.at[turn], recv.at[turn], sibling)
        copy.start()
        pairs.append(copy)
    fetch.wait()
    pairs[0].wait_recv()
    add_rows(work.at[1 - y, core], [work.at[1 - y, core], from_pair.at[1]], rows)
    across = remote(work.at[1 - y, core], from_y, send.at[2], recv.at[2], over_y)
    across.start()
    pairs[1].wait_recv()
    across.wait_recv()
    add_rows(o_ref, [work.at[y, core], from_pair.at[0], from_y], rows)
    for copy in pairs + [across]:
        copy.wait_send()


def tensor_scatter(parts, number):
    rows, width = parts.shape[0] // 4, parts.shape[1]
    shaped = parts.reshape(2, 2, rows, width)
    return pl.pallas_call(
        functools.partial(tensor_scatter_kernel, rows),
        out_shape=jax.ShapeDtypeStruct((rows, width), FULL),
        in_specs=[ANY],
        out_specs=VMEM,
        scratch_shapes=[
            pltpu.VMEM(shaped.shape, parts.dtype),
            pltpu.VMEM((2, rows, width), parts.dtype),
            pltpu.VMEM((rows, width), parts.dtype),
            dma(1), dma(3), dma(3),
        ],
        compiler_params=comm_params(number),
    )(shaped)


def tensor_gather_kernel(x_ref, o_ref, send, recv, local):
    z, x, y, core = place()
    sibling, over_y = device(z, x, y, 1 - core), device(z, x, 1 - y, core)
    greet([sibling, over_y])
    own = pltpu.make_async_copy(x_ref, o_ref.at[y, core], local.at[0])
    own.start()
    across = remote(x_ref, o_ref.at[y, core], send.at[0], recv.at[0], over_y)
    across.start()
    near = remote(x_ref, o_ref.at[y, core], send.at[1], recv.at[1], sibling)
    near.start()
    across.wait_recv()
    block = o_ref.at[1 - y, core]
    passed = remote(block, block, send.at[2], recv.at[2], sibling)
    passed.start()
    own.wait()
    across.wait_send()
    near.wait()
    passed.wait()


def tensor_gather(block, number):
    rows, width = block.shape
    gathered = pl.pallas_call(
        tensor_gather_kernel,
        out_shape=jax.ShapeDtypeStruct((2, 2, rows, width), block.dtype),
        in_specs=[VMEM],
        out_specs=VMEM,
        scratch_shapes=[dma(3), dma(3), dma(1)],
        compiler_params=comm_params(number),
    )(block)
    return gathered.reshape(4 * rows, width)


def expert_scatter_kernel(depth, rows, p_ref, o_ref, work, from_x, from_z, load, send, recv):
    z, x, y, core = place()
    over_x = device(z, 1 - x, y, core)
    greet([over_x] + [device(swapped(z, step), x, y, core) for step in range(1, depth)])
    order = [step for step in range(1, depth)] + [0]
    sides, along, loads = {}, [], {}
    for step in order:
        at = swapped(z, step)
        sides[step] = remote(p_ref.at[at, 1 - x], from_x.at[step], send.at[0, step], recv.at[0, step], over_x)
        sides[step].start()
        loads[step] = pltpu.make_async_copy(p_ref.at[at, x], work.at[step], load.at[step])
        loads[step].start()
    for step in order:
        loads[step].wait()
        sides[step].wait_recv()
        if step:
            add_rows(work.at[step], [work.at[step], from_x.at[step]], rows)
            copy = remote(work.at[step], from_z.at[step], send.at[1, step], recv.at[1, step], device(swapped(z, step), x, y, core))
            copy.start()
            along.append(copy)
    for copy in along:
        copy.wait_recv()
    add_rows(o_ref, [work.at[0], from_x.at[0]] + [from_z.at[step] for step in range(1, depth)], rows)
    for copy in list(sides.values()) + along:
        copy.wait_send()


def expert_scatter(parts, depth, number):
    rows, width = parts.shape[0] // (2 * depth), parts.shape[1]
    shaped = parts.reshape(depth, 2, rows, width)
    return pl.pallas_call(
        functools.partial(expert_scatter_kernel, depth, rows),
        out_shape=jax.ShapeDtypeStruct((rows, width), FULL),
        in_specs=[ANY],
        out_specs=VMEM,
        scratch_shapes=[
            pltpu.VMEM((depth, rows, width), parts.dtype),
            pltpu.VMEM((depth, rows, width), parts.dtype),
            pltpu.VMEM((depth, rows, width), parts.dtype),
            dma(depth), dma(2, depth), dma(2, depth),
        ],
        compiler_params=comm_params(number),
    )(shaped)


def halo_kernel(chain, forward, count, *refs):
    ins, outs, (send, recv) = refs[:count], refs[count : 2 * count], refs[2 * count :]
    group, part = lax.axis_index("expert"), lax.axis_index("tensor")
    spot = group % chain
    barrier = pltpu.get_barrier_semaphore()
    distances = (1, 2)

    def each(before, after):
        for distance in distances:
            if after is not None:
                pl.when(spot < chain - distance)(functools.partial(after, distance))
            if before is not None:
                pl.when(spot >= distance)(functools.partial(before, distance))

    def signal(to):
        pl.semaphore_signal(barrier, inc=1, device_id=(to, part), device_id_type=MESH)

    each(lambda d: signal(group - d), lambda d: signal(group + d))
    pl.semaphore_wait(barrier, jnp.minimum(spot, 2) + jnp.minimum(chain - 1 - spot, 2))

    def copies(distance, to):
        return [
            remote(
                ins[i] if forward else ins[i].at[2 - distance],
                outs[i].at[2 - distance],
                send.at[i, distance],
                recv.at[i, distance],
                (to, part),
            )
            for i in range(count)
        ]

    def start(sign, distance):
        for copy in copies(distance, group + sign * distance):
            copy.start()

    def finish(sign, distance):
        for copy in copies(distance, group + sign * distance):
            copy.wait_send()

    def take(sign, distance):
        for copy in copies(distance, group - sign * distance):
            copy.wait_recv()

    if forward:
        each(None, functools.partial(start, 1))
        each(functools.partial(take, 1), None)
        each(None, functools.partial(finish, 1))
    else:
        each(functools.partial(start, -1), None)
        each(None, functools.partial(take, -1))
        each(functools.partial(finish, -1), None)


def halo(arrays, chain, forward, number):
    count = len(arrays)
    return pl.pallas_call(
        functools.partial(halo_kernel, chain, forward, count),
        out_shape=tuple(jax.ShapeDtypeStruct(((2,) + a.shape) if forward else a.shape, a.dtype) for a in arrays),
        in_specs=[ANY] * count,
        out_specs=(ANY,) * count,
        scratch_shapes=[dma(count, 3), dma(count, 3)],
        compiler_params=comm_params(number),
    )(*arrays)


def dot(left, right):
    return jnp.dot(left, right, preferred_element_type=FULL)


def dot_t(left, right):
    return lax.dot_general(left, right, (((1,), (1,)), ((), ())), preferred_element_type=FULL)


def t_dot(left, right):
    return lax.dot_general(left, right, (((0,), (0,)), ((), ())), preferred_element_type=FULL)


def body(
    groups, parts,
    tokens, documents, routes, norm1_gain, q_gain, k_gain, w_query, w_key, w_value, w_out, norm2_gain, router_w,
    w_gate, w_up, w_down, out_grad,
):
    row_count, width = tokens.shape
    local_experts, _, hidden = w_gate.shape
    experts = local_experts * groups
    chain = LENGTH // row_count
    if not (parts == 4 and groups % 2 == 0 and experts <= 2 * TOP and row_count * chain == LENGTH and WINDOW == 2 * row_count):
        return body_routed(
            tokens, documents, routes, norm1_gain, q_gain, k_gain, w_query, w_key, w_value, w_out, norm2_gain, router_w,
            w_gate, w_up, w_down, out_grad,
        )
    depth = groups // 2
    rows = row_count // parts
    seen = groups * row_count // 2
    heads = w_query.shape[1] // HD
    score_scale = HD ** (-0.5)
    group, part = lax.axis_index("expert"), lax.axis_index("tensor")
    core = part % 2

    def quarter(array):
        return lax.dynamic_slice_in_dim(array, part * rows, rows, 0)

    first_row = group * row_count
    positions = first_row + jnp.arange(row_count, dtype=jnp.int32)
    cosine, sine = rope_tables(positions % LENGTH)
    inputs = tokens.astype(FULL)
    scale_one = lax.rsqrt(jnp.mean(inputs * inputs, axis=-1, keepdims=True) + NORM_EPSILON)
    normed_one = (inputs * scale_one * norm1_gain).astype(LOW)
    query_raw = dot(normed_one, w_query)
    key_raw = dot(normed_one, w_key)
    values = dot(normed_one, w_value).astype(LOW)
    squares = lax.psum(
        jnp.stack([jnp.sum(query_raw * query_raw, axis=-1), jnp.sum(key_raw * key_raw, axis=-1)]), "tensor"
    )
    query_scale = lax.rsqrt(squares[0] / width + NORM_EPSILON)[:, None]
    key_scale = lax.rsqrt(squares[1] / width + NORM_EPSILON)[:, None]
    query_gain, key_gain = q_gain.reshape(-1), k_gain.reshape(-1)
    queries = rotate((query_raw * query_scale * query_gain).reshape(row_count, heads, HD), cosine, sine).astype(LOW)
    key_heads = rotate((key_raw * key_scale * key_gain).reshape(row_count, heads, HD), cosine, sine).astype(LOW)
    own_kv = jnp.concatenate([key_heads.reshape(row_count, -1), values], axis=1)
    own_docs = documents.reshape(row_count // 128, 128)
    before_kv, before_docs = halo([own_kv, own_docs], chain, True, 2)
    spot = group % chain
    exists = jnp.stack([spot >= 2, spot >= 1])
    before_kv = jnp.where(exists[:, None, None], before_kv, jnp.zeros((), LOW))
    before_docs = jnp.where(exists[:, None, None], before_docs, -1)
    all_kv = jnp.concatenate([before_kv[0], before_kv[1], own_kv], axis=0)
    all_keys = all_kv[:, : heads * HD].reshape(3 * row_count, heads, HD)
    all_values = all_kv[:, heads * HD :].reshape(3 * row_count, heads, HD)
    all_docs = jnp.concatenate([before_docs[0], before_docs[1], own_docs], axis=0).reshape(-1)
    key_pos = first_row - 2 * row_count + jnp.arange(3 * row_count, dtype=jnp.int32)
    allowed = (
        (all_docs[None, :] == documents[:, None])
        & (key_pos[None, :] <= positions[:, None])
        & (positions[:, None] - key_pos[None, :] < WINDOW)
    )

    def masked_scores():
        raw_scores = jnp.einsum("qhd,khd->hqk", queries, all_keys, preferred_element_type=FULL) * score_scale
        return jnp.where(allowed[None], raw_scores, -1e30)

    scores = masked_scores()
    highest = jnp.max(scores, axis=-1, keepdims=True)
    weights = jnp.where(allowed[None], jnp.exp(scores - highest), 0.0)
    denominator = jnp.sum(weights, axis=-1, keepdims=True)
    log_total = highest + jnp.log(denominator)
    attn_probs = weights / denominator
    attended = jnp.einsum("hqk,khd->qhd", attn_probs.astype(LOW), all_values, preferred_element_type=FULL)
    attended = attended.reshape(row_count, -1).astype(LOW)
    attention = tensor_scatter(dot(attended, w_out).astype(LOW), 3)

    own_inputs = quarter(tokens).astype(FULL)
    own_grad = quarter(out_grad)
    own_grad_float = own_grad.astype(FULL)
    state = own_inputs + attention
    scale_two = lax.rsqrt(jnp.mean(state * state, axis=-1, keepdims=True) + NORM_EPSILON)
    normed_two = (state * scale_two * norm2_gain).astype(LOW)
    router_probs = jax.nn.softmax(dot(normed_two, router_w), axis=-1)
    picked = jnp.any(
        quarter(routes)[:, :, None] == jnp.arange(experts, dtype=jnp.int32)[None, None, :], axis=1
    ).astype(FULL)

    all_grad = gather_rows(own_grad, depth, 4)
    gates = (router_probs * picked).T.reshape(groups, local_experts, rows)
    gates = jnp.concatenate([gates, jnp.zeros((groups, 8 - local_experts, rows), FULL)], axis=1)
    normed_two_grad, gate_cots, all_normed, gated, gate_pre_grad, up_pre_grad, produced = run_experts(
        normed_two, gates, all_grad, w_gate, w_up, w_down, 5
    )
    units = 2 * local_experts * hidden
    all_normed, all_grad = all_normed.reshape(seen, width), all_grad.reshape(seen, width)
    gated, gate_pre_grad, up_pre_grad = (a.reshape(seen, units) for a in (gated, gate_pre_grad, up_pre_grad))
    expert_mix = scatter_rows(produced, 7)

    def expert_grads(left, right):
        return t_dot(left, right)

    gate_wgrad = expert_grads(all_normed, gate_pre_grad).reshape(width, 2, local_experts, hidden).transpose(1, 2, 0, 3)
    up_wgrad = expert_grads(all_normed, up_pre_grad).reshape(width, 2, local_experts, hidden).transpose(1, 2, 0, 3)
    down_wgrad = expert_grads(gated, all_grad).reshape(2, local_experts, hidden, width)
    swaps = pair_swap([gate_wgrad, up_wgrad, down_wgrad], 8)
    w_gate_grad, w_up_grad, w_down_grad = (
        lax.dynamic_index_in_dim(mine, core, 0, keepdims=False) + other
        for mine, other in zip((gate_wgrad, up_wgrad, down_wgrad), swaps)
    )

    output = tensor_gather((state + expert_mix).astype(LOW), 9)

    prob_cot = gate_cots[:, :, :local_experts].reshape(depth, 2, 2, local_experts, rows).sum(axis=2)
    plane = jnp.arange(depth, dtype=jnp.int32) ^ (group // 2)
    prob_cot = prob_cot[plane].reshape(experts, rows).T * picked
    logit_cot = router_probs * (prob_cot - jnp.sum(router_probs * prob_cot, axis=-1, keepdims=True))
    normed_two_grad = normed_two_grad + jnp.einsum(
        "te,de->td", logit_cot, router_w.astype(FULL), precision=HIGHEST_PRECISION
    )
    router_grad = jnp.einsum("td,te->ed", normed_two.astype(FULL), logit_cot, precision=HIGHEST_PRECISION)
    norm2_grad = jnp.sum(normed_two_grad * state * scale_two, axis=0)
    inner_two = jnp.sum(normed_two_grad * norm2_gain * state, axis=-1, keepdims=True)
    state_cot = own_grad_float + scale_two * norm2_gain * normed_two_grad - state * scale_two**3 * inner_two / width
    state_low = tensor_gather(state_cot.astype(LOW), 10)

    w_out_grad = t_dot(state_low, attended)
    attended_cot = dot_t(state_low, w_out).astype(LOW).reshape(row_count, heads, HD)
    scores = masked_scores()
    attn_probs = jnp.where(allowed[None], jnp.exp(scores - log_total), 0.0)
    value_cot_all = jnp.einsum("hqk,qhd->khd", attn_probs.astype(LOW), attended_cot, preferred_element_type=FULL)
    prob_grad = jnp.einsum("qhd,khd->hqk", attended_cot, all_values, preferred_element_type=FULL)
    delta = jnp.sum(attn_probs * prob_grad, axis=-1, keepdims=True)
    score_cot = (attn_probs * (prob_grad - delta)).astype(LOW)
    query_cot = jnp.einsum("hqk,khd->qhd", score_cot, all_keys, preferred_element_type=FULL) * score_scale
    key_cot_all = jnp.einsum("hqk,qhd->khd", score_cot, queries, preferred_element_type=FULL) * score_scale
    kv_cot = jnp.concatenate(
        [key_cot_all.reshape(3, row_count, -1), value_cot_all.reshape(3, row_count, -1)], axis=2
    )
    (after_kv,) = halo([kv_cot[:2].astype(LOW)], chain, False, 11)
    follows = jnp.stack([spot < chain - 2, spot < chain - 1])
    after_kv = jnp.where(follows[:, None, None], after_kv, jnp.zeros((), LOW)).astype(FULL)
    kv_cot = kv_cot[2] + after_kv[0] + after_kv[1]
    key_cot = kv_cot[:, : heads * HD].reshape(row_count, heads, HD)
    value_low = kv_cot[:, heads * HD :].astype(LOW)
    query_norm_cot = rotate_back(query_cot, cosine, sine).reshape(row_count, -1)
    key_norm_cot = rotate_back(key_cot, cosine, sine).reshape(row_count, -1)
    q_gain_local = jnp.sum(query_norm_cot * query_raw * query_scale, axis=0).reshape(heads, HD)
    k_gain_local = jnp.sum(key_norm_cot * key_raw * key_scale, axis=0).reshape(heads, HD)
    inners = lax.psum(
        jnp.stack(
            [
                jnp.sum(query_norm_cot * query_gain * query_raw, axis=-1),
                jnp.sum(key_norm_cot * key_gain * key_raw, axis=-1),
            ]
        ),
        "tensor",
    )
    query_raw_cot = (
        query_scale * query_gain * query_norm_cot - query_raw * query_scale**3 * inners[0][:, None] / width
    ).astype(LOW)
    key_raw_cot = (
        key_scale * key_gain * key_norm_cot - key_raw * key_scale**3 * inners[1][:, None] / width
    ).astype(LOW)
    normed_part = dot_t(query_raw_cot, w_query) + dot_t(key_raw_cot, w_key) + dot_t(value_low, w_value)
    normed_one_grad = tensor_scatter(normed_part.astype(LOW), 12)
    own_scale = quarter(scale_one)
    norm1_grad = jnp.sum(normed_one_grad * own_inputs * own_scale, axis=0)
    inner_one = jnp.sum(normed_one_grad * norm1_gain * own_inputs, axis=-1, keepdims=True)
    input_grad = (
        state_cot + own_scale * norm1_gain * normed_one_grad - own_inputs * own_scale**3 * inner_one / width
    )
    input_grad = tensor_gather(input_grad.astype(LOW), 13).astype(FULL)

    local = jnp.concatenate(
        [
            t_dot(normed_one, query_raw_cot),
            t_dot(normed_one, key_raw_cot),
            t_dot(normed_one, value_low),
            w_out_grad,
        ],
        axis=1,
    ).astype(LOW)
    summed = expert_scatter(local, depth, 14)
    w_query_grad, w_key_grad, w_value_grad, w_out_grad = jnp.split(summed, 4, axis=1)
    vectors = jnp.concatenate([router_grad, norm1_grad[None], norm2_grad[None]], axis=0)
    vectors = lax.psum(lax.psum_scatter(vectors, "expert", scatter_dimension=1, tiled=True), "tensor")
    gains = lax.psum_scatter(
        jnp.concatenate([q_gain_local, k_gain_local], axis=0), "expert", scatter_dimension=1, tiled=True
    )
    return (
        output,
        input_grad,
        vectors[experts],
        gains[:heads],
        gains[heads:],
        w_query_grad,
        w_key_grad,
        w_value_grad,
        w_out_grad.T,
        vectors[experts + 1],
        vectors[:experts].T,
        w_gate_grad,
        w_up_grad,
        w_down_grad,
    )


def solution(mesh):
    placed = (
        P("expert", None),
        P("expert"),
        P("expert", None),
        P(),
        P("tensor", None),
        P("tensor", None),
        P(None, "tensor"),
        P(None, "tensor"),
        P(None, "tensor"),
        P("tensor", None),
        P(),
        P(),
        P("expert", None, "tensor"),
        P("expert", None, "tensor"),
        P("expert", "tensor", None),
        P("expert", None),
    )
    return jax.shard_map(
        functools.partial(body, mesh.shape["expert"], mesh.shape["tensor"]),
        mesh=mesh,
        in_specs=placed,
        out_specs=(
            P("expert", None),
            P("expert", None),
            P("expert"),
            P("tensor", "expert"),
            P("tensor", "expert"),
            P("expert", "tensor"),
            P("expert", "tensor"),
            P("expert", "tensor"),
            P("tensor", "expert"),
            P("expert"),
            P("expert", None),
            P("expert", None, "tensor"),
            P("expert", None, "tensor"),
            P("expert", "tensor", None),
        ),
        check_vma=False,
    )
```

```python
import functools

import jax
import jax.numpy as jnp
from jax import lax
from jax.experimental import pallas as pl
from jax.experimental.pallas import tpu as pltpu
from jax.sharding import PartitionSpec as P

HD = 128
TOP = 8
WINDOW = 1024
LENGTH = 2048


NORM_EPSILON = 1e-05
HIGHEST_PRECISION = lax.Precision.HIGHEST


def for_sending(value):
    return jax.tree.map(lambda a: a.astype(jnp.bfloat16) if a.dtype == jnp.float32 else a, value)


def shifted(value, axis, steps):
    count = lax.axis_size(axis)
    initial, last = (max(0, -steps), min(count, count - steps))
    return lax.ppermute(value, axis, [(source, source + steps) for source in range(initial, last)])


def rope_tables(positions):
    half_width = HD // 2
    frequency = 10000.0 ** (-jnp.arange(half_width, dtype=jnp.float32) * 2.0 / HD)
    angles = positions.astype(jnp.float32)[:, None] * frequency[None, :]
    angles = jnp.concatenate([angles, angles], axis=-1)
    return (jnp.cos(angles)[:, None, :], jnp.sin(angles)[:, None, :])


def rotate(values, cosine, sine):
    half_width = values.shape[-1] // 2
    turned = jnp.concatenate([-values[..., half_width:], values[..., :half_width]], axis=-1)
    return values * cosine + turned * sine


def rotate_back(grads, cosine, sine):
    half_width = grads.shape[-1] // 2
    scaled = grads * sine
    turned = jnp.concatenate([scaled[..., half_width:], -scaled[..., :half_width]], axis=-1)
    return grads * cosine + turned


def previous_block(pieces):
    return jax.tree.map(
        lambda part, own: part.astype(own.dtype), shifted(for_sending(pieces), "expert", 1), pieces
    )


def following_block(pieces):
    return shifted((for_sending(pieces[0]), for_sending(pieces[1])), "expert", -1)


def body_routed(
    tokens,
    documents,
    routes,
    norm1_gain,
    q_gain,
    k_gain,
    w_query,
    w_key,
    w_value,
    w_out,
    norm2_gain,
    router_w,
    w_gate,
    w_up,
    w_down,
    out_grad,
):
    row_count, model_width = tokens.shape
    groups = lax.axis_size("expert")
    local_experts = w_gate.shape[0]
    experts = local_experts * groups
    capacity = 2 * row_count * TOP // experts
    slots_group = local_experts * capacity
    heads = w_query.shape[1] // HD
    score_scale = HD ** (-0.5)
    first_row = lax.axis_index("expert") * row_count
    positions = first_row + jnp.arange(row_count, dtype=jnp.int32)
    cosine, sine = rope_tables(positions % LENGTH)
    inputs = tokens.astype(jnp.float32)
    scale_one = lax.rsqrt(jnp.mean(inputs * inputs, axis=-1, keepdims=True) + NORM_EPSILON)
    normed_one = (inputs * scale_one * norm1_gain).astype(jnp.bfloat16)
    query_raw = jnp.dot(normed_one, w_query, preferred_element_type=jnp.float32)
    key_raw = jnp.dot(normed_one, w_key, preferred_element_type=jnp.float32)
    values = jnp.dot(normed_one, w_value, preferred_element_type=jnp.float32).astype(jnp.bfloat16)
    query_square, key_square = lax.psum(
        (jnp.sum(query_raw * query_raw, axis=-1), jnp.sum(key_raw * key_raw, axis=-1)), "tensor"
    )
    query_scale = lax.rsqrt(query_square / model_width + NORM_EPSILON)[:, None]
    key_scale = lax.rsqrt(key_square / model_width + NORM_EPSILON)[:, None]
    query_gain = q_gain.reshape(-1)
    key_gain = k_gain.reshape(-1)
    queries = rotate(
        (query_raw * query_scale * query_gain).reshape(row_count, heads, HD), cosine, sine
    ).astype(jnp.bfloat16)
    key_heads = rotate(
        (key_raw * key_scale * key_gain).reshape(row_count, heads, HD), cosine, sine
    ).astype(jnp.bfloat16)
    value_heads = values.reshape(row_count, heads, HD)
    labels = jnp.stack([documents // 256, documents % 256]).astype(jnp.bfloat16)
    previous_one = previous_block((key_heads, value_heads, labels))
    previous_two = previous_block(previous_one)
    all_keys = jnp.concatenate([previous_two[0], previous_one[0], key_heads], axis=0)
    all_values = jnp.concatenate([previous_two[1], previous_one[1], value_heads], axis=0)
    all_labels = jnp.concatenate([previous_two[2], previous_one[2], labels], axis=1)
    key_pos = first_row - 2 * row_count + jnp.arange(3 * row_count, dtype=jnp.int32)
    same_doc = (all_labels[0][None, :] == labels[0][:, None]) & (
        all_labels[1][None, :] == labels[1][:, None]
    )
    allowed = (
        same_doc
        & (key_pos[None, :] <= positions[:, None])
        & (positions[:, None] - key_pos[None, :] < WINDOW)
        & (key_pos[None, :] >= 0)
    )

    def masked_scores():
        raw_scores = (
            jnp.einsum("qhd,khd->hqk", queries, all_keys, preferred_element_type=jnp.float32)
            * score_scale
        )
        return jnp.where(allowed[None], raw_scores, -1e30)

    scores = masked_scores()
    highest = jnp.max(scores, axis=-1, keepdims=True)
    weights = jnp.where(allowed[None], jnp.exp(scores - highest), 0.0)
    denominator = jnp.sum(weights, axis=-1, keepdims=True)
    log_total = highest + jnp.log(denominator)
    attn_probs = weights / denominator
    attended = jnp.einsum(
        "hqk,khd->qhd",
        attn_probs.astype(jnp.bfloat16),
        all_values,
        preferred_element_type=jnp.float32,
    )
    attended = attended.reshape(row_count, -1).astype(jnp.bfloat16)
    attention = lax.psum(jnp.dot(attended, w_out, preferred_element_type=jnp.float32), "tensor")
    state = inputs + attention
    scale_two = lax.rsqrt(jnp.mean(state * state, axis=-1, keepdims=True) + NORM_EPSILON)
    normed_two = (state * scale_two * norm2_gain).astype(jnp.bfloat16)
    router_probs = jax.nn.softmax(
        jnp.dot(normed_two, router_w, preferred_element_type=jnp.float32), axis=-1
    )
    chosen = (routes[:, :, None] == jnp.arange(experts, dtype=jnp.int32)[None, None, :]).astype(
        jnp.float32
    )
    gates = jnp.sum(chosen * router_probs[:, None, :], axis=-1)
    flat_routes = routes.reshape(-1)
    onehot = (flat_routes[:, None] == jnp.arange(experts, dtype=jnp.int32)[None, :]).astype(
        jnp.int32
    )
    slot_index = jnp.sum(jnp.cumsum(onehot, axis=0) * onehot, axis=1) - 1
    target = flat_routes * capacity + slot_index
    source = (
        jnp.full((experts * capacity,), -1, jnp.int32)
        .at[target]
        .set(jnp.arange(row_count * TOP, dtype=jnp.int32))
    )
    live_slot = source >= 0
    pick_index = jnp.maximum(source, 0)
    send_rows = jnp.where(
        live_slot[:, None], normed_two[pick_index // TOP], jnp.zeros((), jnp.bfloat16)
    ).reshape(groups, slots_group, model_width)
    grad_float = out_grad.astype(jnp.float32)
    pick_grads = (
        (gates[:, :, None] * grad_float[:, None, :])
        .astype(jnp.bfloat16)
        .reshape(row_count * TOP, model_width)
    )
    send_grads = jnp.where(
        live_slot[:, None], pick_grads[pick_index], jnp.zeros((), jnp.bfloat16)
    ).reshape(groups, slots_group, model_width)
    arrived = lax.all_to_all(send_rows, "expert", split_axis=0, concat_axis=0, tiled=True)
    stacked = arrived.reshape(groups, local_experts, capacity, model_width)
    gate_pre = jnp.einsum("secd,edf->secf", stacked, w_gate, preferred_element_type=jnp.float32)
    up_pre = jnp.einsum("secd,edf->secf", stacked, w_up, preferred_element_type=jnp.float32)
    activated = jax.nn.silu(gate_pre)
    inner_act = (activated * up_pre).astype(jnp.bfloat16)
    produced = jnp.einsum(
        "secf,efd->secd", inner_act, w_down, preferred_element_type=jnp.float32
    ).astype(jnp.bfloat16)
    returned = lax.all_to_all(
        produced.reshape(groups, slots_group, model_width),
        "expert",
        split_axis=0,
        concat_axis=0,
        tiled=True,
    )
    back_rows = (
        returned.reshape(experts * capacity, model_width)[target]
        .reshape(row_count, TOP, model_width)
        .astype(jnp.float32)
    )
    expert_part = jnp.sum(gates[:, :, None] * back_rows, axis=1)
    expert_mix = lax.psum(expert_part.astype(jnp.bfloat16), "tensor").astype(jnp.float32)
    output = (state + expert_mix).astype(jnp.bfloat16)
    gate_part = jnp.sum(grad_float[:, None, :] * back_rows, axis=-1)
    arrived_grad = lax.all_to_all(send_grads, "expert", split_axis=0, concat_axis=0, tiled=True)
    slot_grad = arrived_grad.reshape(groups, local_experts, capacity, model_width)
    w_down_grad = jnp.einsum(
        "secf,secd->efd", inner_act, slot_grad, preferred_element_type=jnp.float32
    )
    inner_grad = jnp.einsum("secd,efd->secf", slot_grad, w_down, preferred_element_type=jnp.float32)
    logistic = jax.nn.sigmoid(gate_pre)
    gate_pre_grad = (inner_grad * up_pre * logistic * (1.0 + gate_pre * (1.0 - logistic))).astype(
        jnp.bfloat16
    )
    up_pre_grad = (inner_grad * activated).astype(jnp.bfloat16)
    w_gate_grad = jnp.einsum(
        "secd,secf->edf", stacked, gate_pre_grad, preferred_element_type=jnp.float32
    )
    w_up_grad = jnp.einsum(
        "secd,secf->edf", stacked, up_pre_grad, preferred_element_type=jnp.float32
    )
    row_grad = jnp.einsum(
        "secf,edf->secd", gate_pre_grad, w_gate, preferred_element_type=jnp.float32
    )
    row_grad = (
        row_grad
        + jnp.einsum("secf,edf->secd", up_pre_grad, w_up, preferred_element_type=jnp.float32)
    ).astype(jnp.bfloat16)
    grad_back = lax.all_to_all(
        row_grad.reshape(groups, slots_group, model_width),
        "expert",
        split_axis=0,
        concat_axis=0,
        tiled=True,
    )
    grad_picks = (
        grad_back.reshape(experts * capacity, model_width)[target]
        .reshape(row_count, TOP, model_width)
        .astype(jnp.float32)
    )
    normed_part = jnp.sum(grad_picks, axis=1)
    normed_two_grad, gate_cot = lax.psum((normed_part, gate_part), "tensor")
    prob_cot = jnp.sum(gate_cot[:, :, None] * chosen, axis=1)
    logit_cot = router_probs * (prob_cot - jnp.sum(router_probs * prob_cot, axis=-1, keepdims=True))
    router_float = router_w.astype(jnp.float32)
    normed_two_grad = normed_two_grad + jnp.einsum(
        "te,de->td", logit_cot, router_float, precision=HIGHEST_PRECISION
    )
    router_grad = jnp.einsum(
        "td,te->de", normed_two.astype(jnp.float32), logit_cot, precision=HIGHEST_PRECISION
    )
    norm2_grad = jnp.sum(normed_two_grad * state * scale_two, axis=0)
    inner_two = jnp.sum(normed_two_grad * norm2_gain * state, axis=-1, keepdims=True)
    state_cot = (
        grad_float
        + scale_two * norm2_gain * normed_two_grad
        - state * scale_two**3 * inner_two / model_width
    )
    state_low = state_cot.astype(jnp.bfloat16)
    w_out_grad = jnp.einsum("tf,td->fd", attended, state_low, preferred_element_type=jnp.float32)
    attended_cot = (
        jnp.einsum("td,fd->tf", state_low, w_out, preferred_element_type=jnp.float32)
        .astype(jnp.bfloat16)
        .reshape(row_count, heads, HD)
    )
    scores = masked_scores()
    attn_probs = jnp.where(allowed[None], jnp.exp(scores - log_total), 0.0)
    value_cot_all = jnp.einsum(
        "hqk,qhd->khd",
        attn_probs.astype(jnp.bfloat16),
        attended_cot,
        preferred_element_type=jnp.float32,
    )
    prob_grad = jnp.einsum(
        "qhd,khd->hqk", attended_cot, all_values, preferred_element_type=jnp.float32
    )
    delta = jnp.sum(attn_probs * prob_grad, axis=-1, keepdims=True)
    score_cot = (attn_probs * (prob_grad - delta)).astype(jnp.bfloat16)
    query_cot = (
        jnp.einsum("hqk,khd->qhd", score_cot, all_keys, preferred_element_type=jnp.float32)
        * score_scale
    )
    key_cot_all = (
        jnp.einsum("hqk,qhd->khd", score_cot, queries, preferred_element_type=jnp.float32)
        * score_scale
    )
    carried = following_block((key_cot_all[:row_count], value_cot_all[:row_count]))
    carried = following_block(
        (
            key_cot_all[row_count : 2 * row_count] + carried[0],
            value_cot_all[row_count : 2 * row_count] + carried[1],
        )
    )
    key_cot = key_cot_all[2 * row_count :] + carried[0]
    value_cot = value_cot_all[2 * row_count :] + carried[1]
    query_norm_cot = rotate_back(query_cot, cosine, sine).reshape(row_count, -1)
    key_norm_cot = rotate_back(key_cot, cosine, sine).reshape(row_count, -1)
    q_gain_local = jnp.sum(query_norm_cot * query_raw * query_scale, axis=0).reshape(heads, HD)
    k_gain_local = jnp.sum(key_norm_cot * key_raw * key_scale, axis=0).reshape(heads, HD)
    query_inner, key_inner = lax.psum(
        (
            jnp.sum(query_norm_cot * query_gain * query_raw, axis=-1),
            jnp.sum(key_norm_cot * key_gain * key_raw, axis=-1),
        ),
        "tensor",
    )
    query_raw_cot = (
        query_scale * query_gain * query_norm_cot
        - query_raw * query_scale**3 * query_inner[:, None] / model_width
    ).astype(jnp.bfloat16)
    key_raw_cot = (
        key_scale * key_gain * key_norm_cot
        - key_raw * key_scale**3 * key_inner[:, None] / model_width
    ).astype(jnp.bfloat16)
    value_low = value_cot.reshape(row_count, -1).astype(jnp.bfloat16)
    w_query_local = jnp.einsum(
        "td,tf->df", normed_one, query_raw_cot, preferred_element_type=jnp.float32
    )
    w_key_local = jnp.einsum(
        "td,tf->df", normed_one, key_raw_cot, preferred_element_type=jnp.float32
    )
    w_value_local = jnp.einsum(
        "td,tf->df", normed_one, value_low, preferred_element_type=jnp.float32
    )
    normed_part_one = jnp.einsum(
        "tf,df->td", query_raw_cot, w_query, preferred_element_type=jnp.float32
    )
    normed_part_one = normed_part_one + jnp.einsum(
        "tf,df->td", key_raw_cot, w_key, preferred_element_type=jnp.float32
    )
    normed_part_one = normed_part_one + jnp.einsum(
        "tf,df->td", value_low, w_value, preferred_element_type=jnp.float32
    )
    normed_one_grad = lax.psum(normed_part_one.astype(jnp.bfloat16), "tensor").astype(jnp.float32)
    norm1_grad = jnp.sum(normed_one_grad * inputs * scale_one, axis=0)
    inner_one = jnp.sum(normed_one_grad * norm1_gain * inputs, axis=-1, keepdims=True)
    input_grad = (
        state_cot
        + scale_one * norm1_gain * normed_one_grad
        - inputs * scale_one**3 * inner_one / model_width
    )
    summed = (
        lax.psum_scatter(
            w_query_local.astype(jnp.bfloat16), "expert", scatter_dimension=0, tiled=True
        ).astype(jnp.float32),
        lax.psum_scatter(
            w_key_local.astype(jnp.bfloat16), "expert", scatter_dimension=0, tiled=True
        ).astype(jnp.float32),
        lax.psum_scatter(
            w_value_local.astype(jnp.bfloat16), "expert", scatter_dimension=0, tiled=True
        ).astype(jnp.float32),
        lax.psum_scatter(
            w_out_grad.astype(jnp.bfloat16), "expert", scatter_dimension=1, tiled=True
        ).astype(jnp.float32),
        lax.psum_scatter(
            router_grad.astype(jnp.bfloat16), "expert", scatter_dimension=0, tiled=True
        ).astype(jnp.float32),
        lax.psum_scatter(
            norm1_grad.astype(jnp.bfloat16), "expert", scatter_dimension=0, tiled=True
        ).astype(jnp.float32),
        lax.psum_scatter(
            norm2_grad.astype(jnp.bfloat16), "expert", scatter_dimension=0, tiled=True
        ).astype(jnp.float32),
        lax.psum_scatter(
            q_gain_local.astype(jnp.bfloat16), "expert", scatter_dimension=1, tiled=True
        ).astype(jnp.float32),
        lax.psum_scatter(
            k_gain_local.astype(jnp.bfloat16), "expert", scatter_dimension=1, tiled=True
        ).astype(jnp.float32),
    )
    return (
        output,
        input_grad,
        summed[5],
        summed[7],
        summed[8],
        summed[0],
        summed[1],
        summed[2],
        summed[3],
        summed[6],
        summed[4],
        w_gate_grad,
        w_up_grad,
        w_down_grad,
    )


MESH = pl.DeviceIdType.MESH
ANY = pl.BlockSpec(memory_space=pl.ANY)
VMEM = pl.BlockSpec(memory_space=pltpu.VMEM)
VMEM_BYTES = 60 * 1024 * 1024
LOW = jnp.bfloat16
FULL = jnp.float32


def place():
    group, part = lax.axis_index("expert"), lax.axis_index("tensor")
    return group // 2, group % 2, part // 2, part % 2


def device(z, x, y, core):
    return (2 * z + x, 2 * y + core)


def swapped(index, step):
    result, bit = index, 1
    while bit <= step:
        if step & bit:
            result = result + bit - 2 * bit * ((index // bit) % 2)
        bit *= 2
    return result


def greet(partners):
    barrier = pltpu.get_barrier_semaphore()
    for partner in partners:
        pl.semaphore_signal(barrier, inc=1, device_id=partner, device_id_type=MESH)
    pl.semaphore_wait(barrier, len(partners))


def remote(source, target, send, arrive, to):
    return pltpu.make_async_remote_copy(
        src_ref=source, dst_ref=target, send_sem=send, recv_sem=arrive, device_id=to, device_id_type=MESH
    )


def dma(*shape):
    return pltpu.SemaphoreType.DMA(shape)


def comm_params(number):
    return pltpu.CompilerParams(collective_id=number, has_side_effects=True, vmem_limit_bytes=VMEM_BYTES)


def add_rows(target, sources, rows, step=16):
    @pl.loop(0, rows // step)
    def _(index):
        part = pl.ds(index * step, step)
        total = sources[0][part].astype(FULL)
        for source in sources[1:]:
            total = total + source[part].astype(FULL)
        target[part] = total.astype(target.dtype)


class Copies:
    def __init__(self):
        self.open = []

    def start(self, copy):
        copy.start()
        self.open.append([copy, True])
        return copy

    def arrived(self, copy):
        copy.wait_recv()
        for entry in self.open:
            if entry[0] is copy:
                entry[1] = False

    def finish(self):
        for copy, receiving in self.open:
            copy.wait_send()
            if receiving:
                copy.wait_recv()


class Gather:
    def __init__(self, copies, block, target, rows, z_send, z_recv, p_send, p_recv):
        self.copies, self.block, self.target, self.rows = copies, block, target, rows
        self.z_send, self.z_recv, self.p_send, self.p_recv = z_send, z_recv, p_send, p_recv
        z, x, y, core = place()
        self.over_x, self.over_y = device(z, 1 - x, y, core), device(z, x, 1 - y, core)
        self.here, self.x_place, self.y_place = 2 * x + y, 2 * (1 - x) + y, 2 * x + 1 - y
        self.column = [device(swapped(z, step), x, y, core) for step in range(target.shape[0])]
        self.along, self.planes, self.diagonals = {}, {}, {}

    def at(self, step, spot, part):
        half = self.rows // 2
        if part is None:
            return self.target.at[step, pl.ds(pl.multiple_of(spot * self.rows, self.rows), self.rows)]
        return self.target.at[step, pl.ds(pl.multiple_of(spot * self.rows + part * half, half), half)]

    def begin(self):
        self.spread(0)
        for step in range(1, len(self.column)):
            self.along[step] = self.copies.start(
                remote(self.block, self.at(step, self.here, None), self.z_send.at[step], self.z_recv.at[step], self.column[step])
            )

    def spread(self, step):
        if step:
            self.copies.arrived(self.along[step])
        half = self.rows // 2
        planes = []
        for number, (to, part) in enumerate([(self.over_x, 0), (self.over_y, 1), (self.over_x, 1), (self.over_y, 0)]):
            here = self.at(step, self.here, part)
            source = here if step else self.block.at[pl.ds(part * half, half)]
            planes.append(self.copies.start(remote(source, here, self.p_send.at[step, number], self.p_recv.at[step, number], to)))
        self.planes[step] = planes

    def turn(self, step):
        self.copies.arrived(self.planes[step][0])
        passed = self.at(step, self.x_place, 0)
        first = self.copies.start(remote(passed, passed, self.p_send.at[step, 4], self.p_recv.at[step, 4], self.over_y))
        self.copies.arrived(self.planes[step][1])
        passed = self.at(step, self.y_place, 1)
        second = self.copies.start(remote(passed, passed, self.p_send.at[step, 5], self.p_recv.at[step, 5], self.over_x))
        self.diagonals[step] = (first, second)

    def complete(self, step):
        for copy in self.planes[step][2:] + list(self.diagonals[step]):
            self.copies.arrived(copy)


class Scatter:
    def __init__(self, copies, work, diagonal, from_x, from_y, from_z, rows, send, recv):
        self.copies, self.work, self.rows, self.send, self.recv = copies, work, rows, send, recv
        self.diagonal, self.from_x, self.from_y, self.from_z = diagonal, from_x, from_y, from_z
        z, x, y, core = place()
        self.over_x, self.over_y = device(z, 1 - x, y, core), device(z, x, 1 - y, core)
        self.here, self.x_place, self.y_place = 2 * x + y, 2 * (1 - x) + y, 2 * x + 1 - y
        self.far = 2 * (1 - x) + 1 - y
        self.column = [device(swapped(z, step), x, y, core) for step in range(work.shape[0])]
        self.corners, self.sides, self.along = {}, {}, {}

    def at(self, step, spot, part=None):
        half = self.rows // 2
        if part is None:
            return self.work.at[step, pl.ds(pl.multiple_of(spot * self.rows, self.rows), self.rows)]
        return self.work.at[step, pl.ds(pl.multiple_of(spot * self.rows + part * half, half), half)]

    def copy(self, step, number, source, target, to):
        return self.copies.start(remote(source, target, self.send.at[step, number], self.recv.at[step, number], to))

    def corner(self, step):
        self.corners[step] = (
            self.copy(step, 0, self.at(step, self.far, 0), self.diagonal.at[step, 0], self.over_y),
            self.copy(step, 1, self.at(step, self.far, 1), self.diagonal.at[step, 1], self.over_x),
        )

    def side(self, step):
        via_y, via_x = self.corners[step]
        self.copies.arrived(via_y)
        add_rows(self.at(step, self.x_place, 0), [self.at(step, self.x_place, 0), self.diagonal.at[step, 0]], self.rows // 2)
        to_x = self.copy(step, 2, self.at(step, self.x_place), self.from_x.at[step], self.over_x)
        self.copies.arrived(via_x)
        add_rows(self.at(step, self.y_place, 1), [self.at(step, self.y_place, 1), self.diagonal.at[step, 1]], self.rows // 2)
        to_y = self.copy(step, 3, self.at(step, self.y_place), self.from_y.at[step], self.over_y)
        self.sides[step] = (to_x, to_y)

    def climb(self, step):
        for copy in self.sides[step]:
            self.copies.arrived(copy)
        if step:
            here = self.at(step, self.here)
            add_rows(here, [here, self.from_x.at[step], self.from_y.at[step]], self.rows)
            self.along[step] = self.copy(step, 4, here, self.from_z.at[step], self.column[step])

    def result(self, target):
        for copy in self.along.values():
            self.copies.arrived(copy)
        terms = [self.at(0, self.here), self.from_x.at[0], self.from_y.at[0]]
        add_rows(target, terms + [self.from_z.at[step] for step in self.along], self.rows)

    @staticmethod
    def scratch(depth, rows, width):
        return [
            pltpu.VMEM((depth, 2, rows // 2, width), LOW),
            pltpu.VMEM((depth, rows, width), LOW),
            pltpu.VMEM((depth, rows, width), LOW),
            pltpu.VMEM((depth, rows, width), LOW),
            dma(depth, 5),
            dma(depth, 5),
        ]


def experts_kernel(
    depth, rows, local, hidden,
    x_ref, gates_ref, grad_ref, gate_ref, up_ref, down_ref,
    sum_ref, cots_ref, normed_ref, gated_ref, gate_grad_ref, up_grad_ref, produced_ref,
    wg, wu, wd, x_all, grads, work, y_out, gated, gate_grad, up_grad, gates, gate_wide, cots, cot_rows,
    diagonal, from_x, from_y, from_z, r_send, r_recv,
    z_send, z_recv, p_send, p_recv, s_send, s_recv, w_send, w_recv, w_load, g_load, saves, local_sem,
):
    z, x, y, core = place()
    here, sibling = 2 * x + y, device(z, x, y, 1 - core)
    others = [
        (step, turn, (swapped(z, step), swapped(x, turn // 2), swapped(y, turn % 2)))
        for step in range(depth)
        for turn in range(4)
        if step or turn
    ]
    greet([device(*other, core) for _, _, other in others] + [sibling])
    copies = Copies()
    gather = Gather(copies, x_ref, x_all, rows, z_send, z_recv, p_send, p_recv)
    gather.begin()
    plain = []

    def fetch(source, target, sem):
        copy = pltpu.make_async_copy(source, target, sem)
        copy.start()
        return copy

    plain.append(fetch(x_ref, gather.at(0, here, None), local_sem.at[0]))
    weights = []
    for index in range(local):
        first = pl.multiple_of((core * local + index) * hidden, hidden)
        columns = pl.ds(first, hidden)
        for number, (source, target) in enumerate(
            [(gate_ref, wg.at[:, columns]), (up_ref, wu.at[:, columns]), (down_ref, wd.at[columns])]
        ):
            weights.append(copies.start(remote(source.at[index], target, w_send.at[number, index], w_recv.at[number, index], sibling)))
            plain.append(fetch(source.at[index], target, w_load.at[number, index]))
    smalls = []
    for step, turn, other in others:
        oz, ox, oy = other
        smalls.append(
            copies.start(
                remote(
                    gates_ref.at[2 * oz + ox], gates.at[step, here], s_send.at[0, step, turn], s_recv.at[0, step, turn],
                    device(oz, ox, oy, core),
                )
            )
        )
    plain.append(fetch(gates_ref.at[2 * z + x], gates.at[0, here], local_sem.at[1]))
    grad_copies = [fetch(grad_ref.at[0], grads.at[0], g_load.at[0])]
    scatter = Scatter(copies, work, diagonal, from_x, from_y, from_z, rows, r_send, r_recv)
    saving, producing, keeping = [], [], []
    wave_rows = 4 * rows
    lanes = lax.broadcasted_iota(jnp.int32, (wave_rows, 128), 1)

    def first_half(step):
        for copy in saving:
            copy.wait()
        saving.clear()
        for spot in range(4):
            padded = jnp.concatenate([gates[step, spot], jnp.zeros((120, 128), FULL)], axis=0)
            gate_wide[pl.ds(spot * rows, rows), :] = padded.T
        cots[...] = jnp.zeros_like(cots)
        grad_copies[step].wait()
        if step + 1 < depth:
            grad_copies.append(fetch(grad_ref.at[step + 1], grads.at[(step + 1) % 2], g_load.at[(step + 1) % 2]))
        grad = grads.at[step % 2]

        @pl.loop(0, 2 * local)
        def _(unit):
            columns = pl.ds(pl.multiple_of(unit * hidden, hidden), hidden)
            expert = lax.rem(unit, local)
            gate_pre = dot(x_all[step], wg[:, columns])
            up_pre = dot(x_all[step], wu[:, columns])
            back = dot_t(grad[...], wd[columns, :])
            logistic = 1.0 / (1.0 + jnp.exp(-gate_pre))
            activated = gate_pre * logistic
            inner = activated * up_pre
            cot = jnp.sum(inner * back, axis=-1, keepdims=True)
            cots[...] += jnp.where(lanes == expert, cot, 0.0)
            gate = jnp.sum(jnp.where(lanes == expert, gate_wide[...], 0.0), axis=-1, keepdims=True)
            gated[:, columns] = (gate * inner).astype(LOW)
            inner_grad = gate * back
            gate_grad[:, columns] = (inner_grad * up_pre * logistic * (1.0 + gate_pre * (1.0 - logistic))).astype(LOW)
            up_grad[:, columns] = (inner_grad * activated).astype(LOW)

        for spot in range(4):
            cot_rows[step, spot] = cots[pl.ds(spot * rows, rows), :].T[:8]
        for number, (source, target) in enumerate([(gated, gated_ref), (gate_grad, gate_grad_ref), (up_grad, up_grad_ref)]):
            saving.append(fetch(source, target.at[step], saves.at[number]))
        keeping.append(fetch(x_all.at[step], normed_ref.at[step], saves.at[4 + step]))

    def second_half(step):
        for copy in producing:
            copy.wait()
        producing.clear()
        tile = 512

        @pl.loop(0, x_all.shape[2] // tile)
        def _(index):
            columns = pl.ds(pl.multiple_of(index * tile, tile), tile)
            y_out[:, columns] = dot(gated[...], wd[:, columns]).astype(LOW)
            work[step, :, columns] = (dot_t(gate_grad[...], wg[columns, :]) + dot_t(up_grad[...], wu[columns, :])).astype(LOW)

        producing.append(fetch(y_out, produced_ref.at[step], saves.at[3]))

    gather.turn(0)
    if depth > 1:
        gather.spread(1)
    gather.complete(0)
    for copy in plain:
        copy.wait()
    for copy in weights + smalls:
        copies.arrived(copy)
    for step in range(depth):
        if step:
            gather.complete(step)
        first_half(step)
        if step + 1 < depth:
            gather.turn(step + 1)
        if step + 2 < depth:
            gather.spread(step + 2)
        if step >= 1:
            scatter.side(step - 1)
        if step >= 2:
            scatter.climb(step - 2)
        second_half(step)
        scatter.corner(step)
    for step, turn, (oz, ox, oy) in others:
        copies.start(
            remote(
                cot_rows.at[step, 2 * ox + oy], cots_ref.at[step, here], s_send.at[1, step, turn], s_recv.at[1, step, turn],
                device(oz, ox, oy, core),
            )
        )
    own_cots = fetch(cot_rows.at[0, here], cots_ref.at[0, here], local_sem.at[2])
    if depth > 1:
        scatter.climb(depth - 2)
    scatter.side(depth - 1)
    scatter.climb(depth - 1)
    scatter.result(sum_ref)
    own_cots.wait()
    for copy in saving + producing + keeping:
        copy.wait()
    copies.finish()


def run_experts(block, gates, grads, w_gate, w_up, w_down, number):
    depth, wave, width = grads.shape
    rows = wave // 4
    local, _, hidden = w_gate.shape
    units = 2 * local * hidden
    kept = jax.ShapeDtypeStruct((depth, wave, units), LOW)
    wide = jax.ShapeDtypeStruct((depth, wave, width), LOW)
    return pl.pallas_call(
        functools.partial(experts_kernel, depth, rows, local, hidden),
        out_shape=(
            jax.ShapeDtypeStruct((rows, width), FULL),
            jax.ShapeDtypeStruct((depth, 4, 8, 128), FULL),
            wide, kept, kept, kept, wide,
        ),
        in_specs=[ANY] * 6,
        out_specs=(VMEM, VMEM, ANY, ANY, ANY, ANY, ANY),
        scratch_shapes=[
            pltpu.VMEM((width, units), LOW), pltpu.VMEM((width, units), LOW), pltpu.VMEM((units, width), LOW),
            pltpu.VMEM((depth, wave, width), LOW), pltpu.VMEM((2, wave, width), LOW),
            pltpu.VMEM((depth, wave, width), LOW), pltpu.VMEM((wave, width), LOW),
            pltpu.VMEM((wave, units), LOW), pltpu.VMEM((wave, units), LOW), pltpu.VMEM((wave, units), LOW),
            pltpu.VMEM((depth, 4, 8, 128), FULL), pltpu.VMEM((wave, 128), FULL), pltpu.VMEM((wave, 128), FULL),
            pltpu.VMEM((depth, 4, 8, 128), FULL),
        ]
        + Scatter.scratch(depth, rows, width)
        + [
            dma(depth), dma(depth), dma(depth, 6), dma(depth, 6), dma(2, depth, 4), dma(2, depth, 4),
            dma(3, local), dma(3, local), dma(3, local), dma(2), dma(4 + depth), dma(3),
        ],
        compiler_params=comm_params(number),
    )(block, gates, grads, w_gate, w_up, w_down)


class TensorScatter:
    def __init__(self, copies, work, from_pair, from_y, send, recv):
        self.copies, self.work, self.from_pair, self.from_y, self.send, self.recv = copies, work, from_pair, from_y, send, recv
        z, x, self.y, self.core = place()
        self.sibling, self.over_y = device(z, x, self.y, 1 - self.core), device(z, x, 1 - self.y, self.core)
        self.rows = work.shape[2]

    def begin(self):
        self.pairs = []
        for turn in (1, 0):
            source = self.work.at[swapped(self.y, turn), 1 - self.core]
            self.pairs.append(
                self.copies.start(remote(source, self.from_pair.at[turn], self.send.at[turn], self.recv.at[turn], self.sibling))
            )

    def cross(self):
        self.copies.arrived(self.pairs[0])
        block = self.work.at[1 - self.y, self.core]
        add_rows(block, [block, self.from_pair.at[1]], self.rows)
        self.across = self.copies.start(remote(block, self.from_y, self.send.at[2], self.recv.at[2], self.over_y))

    def result(self, target):
        self.copies.arrived(self.pairs[1])
        self.copies.arrived(self.across)
        add_rows(target, [self.work.at[self.y, self.core], self.from_pair.at[0], self.from_y], self.rows)

    @staticmethod
    def scratch(rows, width):
        return [
            pltpu.VMEM((2, 2, rows, width), LOW),
            pltpu.VMEM((2, rows, width), LOW),
            pltpu.VMEM((rows, width), LOW),
            dma(3),
            dma(3),
        ]


class TensorGather:
    def __init__(self, copies, block, target, send, recv):
        self.copies, self.target, self.send, self.recv = copies, target, send, recv
        z, x, self.y, self.core = place()
        self.sibling, over_y = device(z, x, self.y, 1 - self.core), device(z, x, 1 - self.y, self.core)
        mine = target.at[self.y, self.core]
        self.across = copies.start(remote(block, mine, send.at[0], recv.at[0], over_y))
        self.near = copies.start(remote(block, mine, send.at[1], recv.at[1], self.sibling))
        self.own = pltpu.make_async_copy(block, mine, send.at[3])
        self.own.start()

    def cross(self):
        self.copies.arrived(self.across)
        block = self.target.at[1 - self.y, self.core]
        self.passed = self.copies.start(remote(block, block, self.send.at[2], self.recv.at[2], self.sibling))

    def finish(self):
        self.own.wait()
        self.copies.arrived(self.near)
        self.copies.arrived(self.passed)


def partners_of(depth):
    z, x, y, core = place()
    return [device(swapped(z, step), x, y, core) for step in range(1, depth)] + [
        device(z, 1 - x, y, core),
        device(z, x, 1 - y, core),
        device(z, x, y, 1 - core),
        device(swapped(z, 1), 1 - x, y, core),
    ]


def mask_bias(bias, key_docs, query_docs, length):
    blocks = bias.shape[0] // length

    @pl.loop(0, bias.shape[0] // 128)
    def _(index):
        part = pl.ds(pl.multiple_of(index * 128, 128), 128)
        key = index * 128 + lax.broadcasted_iota(jnp.int32, (128, length), 0) - (blocks - 1) * length
        query = lax.broadcasted_iota(jnp.int32, (128, length), 1)
        seen = (key_docs[part, :] == query_docs[0:1, :]) & (key <= query) & (query - key < WINDOW)
        bias[part, :] = jnp.where(seen, 0.0, -1e30)


def attention_kernel(
    depth, rows, heads, chain,
    query_ref, kv_ref, key_docs, query_docs, w_out, grad_ref,
    kv_all, attended, logs, sum_ref, all_grad,
    scores, bias, partial, from_pair, from_y, t_send, t_recv,
    z_send, z_recv, p_send, p_recv, h_send, h_recv, local,
):
    z, x, y, core = place()
    group, part = lax.axis_index("expert"), lax.axis_index("tensor")
    spot = group % chain
    greet(partners_of(depth))
    copies = Copies()
    length = kv_ref.shape[0]
    scale = HD ** (-0.5)

    def halo_copy(distance, to):
        return remote(kv_ref, kv_all.at[2 - distance], h_send.at[distance], h_recv.at[distance], (to, part))

    for distance in (1, 2):

        @pl.when(spot < chain - distance)
        def _():
            halo_copy(distance, group + distance).start()

    gather = Gather(copies, grad_ref, all_grad, rows, z_send, z_recv, p_send, p_recv)
    gather.begin()
    own = pltpu.make_async_copy(grad_ref, gather.at(0, gather.here, None), local.at[0])
    own.start()
    kv_all[2] = kv_ref[...]
    mask_bias(bias, key_docs, query_docs, length)

    def score(block):
        @pl.loop(0, heads)
        def _(head):
            columns = pl.ds(pl.multiple_of(head * HD, HD), HD)
            keys = pl.ds(block * length, length)
            scores[head, keys, :] = dot_t(kv_all[block, :, columns], query_ref[:, columns]) * scale + bias[keys, :]

    score(2)
    gather.turn(0)
    for distance in (1, 2):

        @pl.when(spot >= distance)
        def _():
            halo_copy(distance, group - distance).wait_recv()

        @pl.when(spot < distance)
        def _():
            kv_all[2 - distance] = jnp.zeros_like(kv_ref)

        score(2 - distance)
    if depth > 1:
        gather.spread(1)

    @pl.loop(0, heads)
    def _(head):
        columns = pl.ds(pl.multiple_of(head * HD, HD), HD)
        mine = scores.at[head]
        highest = jnp.max(mine[...], axis=0, keepdims=True)
        total = jnp.zeros_like(highest)
        mixed = jnp.zeros((HD, length), FULL)
        for block in range(3):
            weights = jnp.exp(mine[pl.ds(block * length, length), :] - highest)
            total = total + jnp.sum(weights, axis=0, keepdims=True)
            mine[pl.ds(block * length, length), :] = weights
        for block in range(3):
            probs = (mine[pl.ds(block * length, length), :] * (1.0 / total)).astype(LOW)
            values = pl.ds(pl.multiple_of((heads + head) * HD, HD), HD)
            mixed = mixed + t_dot(kv_all[block, :, values], probs)
        attended[:, columns] = mixed.T.astype(LOW)
        logs[head] = jnp.broadcast_to(highest + jnp.log(total), (8, length))

    if depth > 1:
        gather.turn(1)
    if depth > 2:
        gather.spread(2)
    for index in range(4):
        partial[index // 2, index % 2] = dot(attended[pl.ds(index * rows, rows), :], w_out[...]).astype(LOW)
    scatter = TensorScatter(copies, partial, from_pair, from_y, t_send, t_recv)
    scatter.begin()
    scatter.cross()
    if depth > 2:
        gather.turn(2)
    for step in range(3, depth):
        gather.spread(step)
    scatter.result(sum_ref)
    for step in range(3, depth):
        gather.turn(step)
    own.wait()
    for distance in (1, 2):

        @pl.when(spot < chain - distance)
        def _():
            halo_copy(distance, group + distance).wait_send()

    copies.finish()


def run_attention(queries, kv, key_docs, query_docs, w_out, grads, depth, chain, number):
    length, wide = kv.shape
    heads = wide // (2 * HD)
    rows, width = grads.shape
    return pl.pallas_call(
        functools.partial(attention_kernel, depth, rows, heads, chain),
        out_shape=(
            jax.ShapeDtypeStruct((3, length, wide), LOW),
            jax.ShapeDtypeStruct(queries.shape, LOW),
            jax.ShapeDtypeStruct((heads, 8, length), FULL),
            jax.ShapeDtypeStruct((rows, width), FULL),
            jax.ShapeDtypeStruct((depth, 4 * rows, width), LOW),
        ),
        in_specs=[VMEM] * 5 + [ANY],
        out_specs=(VMEM, VMEM, VMEM, VMEM, ANY),
        scratch_shapes=[pltpu.VMEM((heads, 3 * length, length), FULL), pltpu.VMEM((3 * length, length), FULL)]
        + TensorScatter.scratch(rows, width)
        + [dma(depth), dma(depth), dma(depth, 6), dma(depth, 6), dma(3), dma(3), dma(1)],
        compiler_params=comm_params(number),
    )(queries, kv, key_docs, query_docs, w_out, grads)


def attention_back_kernel(
    depth, rows, heads, chain,
    low_ref, query_ref, kv_all, attended, logs, key_docs, query_docs, w_out, produced_ref,
    lows, query_cot, kv_cot, mix_ref,
    bias, cots, deltas, turned, sending, landed, work,
    diagonal, from_x, from_y, from_z, r_send, r_recv, t_send, t_recv, h_send, h_recv, load,
):
    group, part = lax.axis_index("expert"), lax.axis_index("tensor")
    spot = group % chain
    greet(partners_of(depth))
    copies = Copies()
    length = query_ref.shape[0]
    scale = HD ** (-0.5)
    wide = heads * HD
    gather = TensorGather(copies, low_ref, lows, t_send, t_recv)
    order = [step for step in range(1, depth)] + [0]
    loads = {}
    for step in order:
        loads[step] = pltpu.make_async_copy(produced_ref.at[step], work.at[step], load.at[step])
        loads[step].start()
    scatter = Scatter(copies, work, diagonal, from_x, from_y, from_z, rows, r_send, r_recv)
    for step in order:
        loads[step].wait()
        scatter.corner(step)
    mask_bias(bias, key_docs, query_docs, length)
    gather.cross()
    gather.finish()
    for index in range(4):
        cots[pl.ds(index * rows, rows), :] = dot_t(lows[index // 2, index % 2], w_out[...]).astype(LOW)
    for head in range(heads):
        columns = pl.ds(head * HD, HD)
        product = cots[:, columns].astype(FULL) * attended[:, columns].astype(FULL)
        deltas[head] = jnp.broadcast_to(jnp.sum(product.T, axis=0, keepdims=True), (8, length))
    turned[...] = jnp.zeros_like(turned)

    def back(block, target):
        @pl.loop(0, heads)
        def _(head):
            columns = pl.ds(pl.multiple_of(head * HD, HD), HD)
            others = pl.ds(pl.multiple_of((heads + head) * HD, HD), HD)
            query, cot = query_ref[:, columns], cots[:, columns]
            log, delta = logs[head, 0:1, :], deltas[head, 0:1, :]
            tile = 256

            @pl.loop(0, length // tile)
            def _(index):
                keys = pl.ds(pl.multiple_of(index * tile, tile), tile)
                key, value = kv_all[block, keys, columns], kv_all[block, keys, others]
                hidden = bias[pl.ds(pl.multiple_of(block * length + index * tile, tile), tile), :]
                probs = jnp.exp(dot_t(key, query) * scale + hidden - log)
                score_cot = (probs * (dot_t(value, cot) - delta)).astype(LOW)
                turned[head] += t_dot(key, score_cot)
                target[keys, columns] = (dot(score_cot, query) * scale).astype(target.dtype)
                target[keys, others] = dot(probs.astype(LOW), cot).astype(target.dtype)

    def halo_copy(distance, to):
        return remote(sending.at[2 - distance], landed.at[2 - distance], h_send.at[distance], h_recv.at[distance], (to, part))

    def send(distance):
        @pl.when(spot >= distance)
        def _():
            halo_copy(distance, group - distance).start()

    back(1, sending.at[1])
    send(1)
    scatter.side(order[0])
    back(0, sending.at[0])
    send(2)
    for step in order[1:-1]:
        scatter.side(step)
    back(2, kv_cot)
    for head in range(heads):
        query_cot[:, pl.ds(head * HD, HD)] = turned[head].T * scale
    scatter.side(order[-1])
    for step in order[:-1]:
        scatter.climb(step)
    for distance in (1, 2):

        @pl.when(spot < chain - distance)
        def _():
            halo_copy(distance, group + distance).wait_recv()
            add_rows(kv_cot, [kv_cot, landed.at[2 - distance]], length)

    scatter.climb(order[-1])
    scatter.result(mix_ref)
    for distance in (1, 2):

        @pl.when(spot >= distance)
        def _():
            halo_copy(distance, group - distance).wait_send()

    copies.finish()


def run_attention_back(low, queries, kv_all, attended, logs, key_docs, query_docs, w_out, produced, chain, number):
    depth = produced.shape[0]
    rows, width = low.shape
    length, wide = kv_all.shape[1:]
    heads = wide // (2 * HD)
    return pl.pallas_call(
        functools.partial(attention_back_kernel, depth, rows, heads, chain),
        out_shape=(
            jax.ShapeDtypeStruct((2, 2, rows, width), LOW),
            jax.ShapeDtypeStruct(queries.shape, FULL),
            jax.ShapeDtypeStruct((length, wide), FULL),
            jax.ShapeDtypeStruct((rows, width), FULL),
        ),
        in_specs=[VMEM] * 8 + [ANY],
        out_specs=(VMEM,) * 4,
        scratch_shapes=[
            pltpu.VMEM((3 * length, length), FULL), pltpu.VMEM((length, wide // 2), LOW),
            pltpu.VMEM((heads, 8, length), FULL), pltpu.VMEM((heads, HD, length), FULL),
            pltpu.VMEM((2, length, wide), LOW), pltpu.VMEM((2, length, wide), LOW),
            pltpu.VMEM(produced.shape, LOW),
        ]
        + Scatter.scratch(depth, rows, width)
        + [dma(4), dma(3), dma(3), dma(3), dma(depth)],
        compiler_params=comm_params(number),
    )(low, queries, kv_all, attended, logs, key_docs, query_docs, w_out, produced)


def pair_swap_kernel(count, *refs):
    ins, outs, (send, recv) = refs[:count], refs[count : 2 * count], refs[2 * count :]
    z, x, y, core = place()
    sibling = device(z, x, y, 1 - core)
    greet([sibling])
    waits = []
    for index in range(count):
        copy = remote(ins[index].at[1 - core], outs[index], send.at[index], recv.at[index], sibling)
        copy.start()
        waits.append(copy)
    for copy in waits:
        copy.wait()


def pair_swap(arrays, number):
    count = len(arrays)
    return pl.pallas_call(
        functools.partial(pair_swap_kernel, count),
        out_shape=tuple(jax.ShapeDtypeStruct(a.shape[1:], a.dtype) for a in arrays),
        in_specs=[ANY] * count,
        out_specs=(ANY,) * count,
        scratch_shapes=[dma(count), dma(count)],
        compiler_params=comm_params(number),
    )(*arrays)


def tensor_scatter_kernel(rows, p_ref, o_ref, work, from_pair, from_y, load, send, recv):
    z, x, y, core = place()
    sibling, over_y = device(z, x, y, 1 - core), device(z, x, 1 - y, core)
    greet([sibling, over_y])
    fetch = pltpu.make_async_copy(p_ref, work, load.at[0])
    fetch.start()
    pairs = []
    for turn in (1, 0):
        row = swapped(y, turn)
        copy = remote(p_ref.at[row, 1 - core], from_pair.at[turn], send.at[turn], recv.at[turn], sibling)
        copy.start()
        pairs.append(copy)
    fetch.wait()
    pairs[0].wait_recv()
    add_rows(work.at[1 - y, core], [work.at[1 - y, core], from_pair.at[1]], rows)
    across = remote(work.at[1 - y, core], from_y, send.at[2], recv.at[2], over_y)
    across.start()
    pairs[1].wait_recv()
    across.wait_recv()
    add_rows(o_ref, [work.at[y, core], from_pair.at[0], from_y], rows)
    for copy in pairs + [across]:
        copy.wait_send()


def tensor_scatter(parts, number):
    rows, width = parts.shape[0] // 4, parts.shape[1]
    shaped = parts.reshape(2, 2, rows, width)
    return pl.pallas_call(
        functools.partial(tensor_scatter_kernel, rows),
        out_shape=jax.ShapeDtypeStruct((rows, width), FULL),
        in_specs=[ANY],
        out_specs=VMEM,
        scratch_shapes=[
            pltpu.VMEM(shaped.shape, parts.dtype),
            pltpu.VMEM((2, rows, width), parts.dtype),
            pltpu.VMEM((rows, width), parts.dtype),
            dma(1), dma(3), dma(3),
        ],
        compiler_params=comm_params(number),
    )(shaped)


def tensor_gather_kernel(x_ref, o_ref, send, recv, local):
    z, x, y, core = place()
    sibling, over_y = device(z, x, y, 1 - core), device(z, x, 1 - y, core)
    greet([sibling, over_y])
    own = pltpu.make_async_copy(x_ref, o_ref.at[y, core], local.at[0])
    own.start()
    across = remote(x_ref, o_ref.at[y, core], send.at[0], recv.at[0], over_y)
    across.start()
    near = remote(x_ref, o_ref.at[y, core], send.at[1], recv.at[1], sibling)
    near.start()
    across.wait_recv()
    block = o_ref.at[1 - y, core]
    passed = remote(block, block, send.at[2], recv.at[2], sibling)
    passed.start()
    own.wait()
    across.wait_send()
    near.wait()
    passed.wait()


def tensor_gather(block, number):
    rows, width = block.shape
    gathered = pl.pallas_call(
        tensor_gather_kernel,
        out_shape=jax.ShapeDtypeStruct((2, 2, rows, width), block.dtype),
        in_specs=[VMEM],
        out_specs=VMEM,
        scratch_shapes=[dma(3), dma(3), dma(1)],
        compiler_params=comm_params(number),
    )(block)
    return gathered.reshape(4 * rows, width)


def expert_scatter_kernel(depth, rows, p_ref, o_ref, work, from_x, from_z, load, send, recv):
    z, x, y, core = place()
    over_x = device(z, 1 - x, y, core)
    greet([over_x] + [device(swapped(z, step), x, y, core) for step in range(1, depth)])
    order = [step for step in range(1, depth)] + [0]
    sides, along, loads = {}, [], {}
    for step in order:
        at = swapped(z, step)
        sides[step] = remote(p_ref.at[at, 1 - x], from_x.at[step], send.at[0, step], recv.at[0, step], over_x)
        sides[step].start()
        loads[step] = pltpu.make_async_copy(p_ref.at[at, x], work.at[step], load.at[step])
        loads[step].start()
    for step in order:
        loads[step].wait()
        sides[step].wait_recv()
        if step:
            add_rows(work.at[step], [work.at[step], from_x.at[step]], rows)
            copy = remote(work.at[step], from_z.at[step], send.at[1, step], recv.at[1, step], device(swapped(z, step), x, y, core))
            copy.start()
            along.append(copy)
    for copy in along:
        copy.wait_recv()
    add_rows(o_ref, [work.at[0], from_x.at[0]] + [from_z.at[step] for step in range(1, depth)], rows)
    for copy in list(sides.values()) + along:
        copy.wait_send()


def expert_scatter(parts, depth, number):
    rows, width = parts.shape[0] // (2 * depth), parts.shape[1]
    shaped = parts.reshape(depth, 2, rows, width)
    return pl.pallas_call(
        functools.partial(expert_scatter_kernel, depth, rows),
        out_shape=jax.ShapeDtypeStruct((rows, width), FULL),
        in_specs=[ANY],
        out_specs=VMEM,
        scratch_shapes=[
            pltpu.VMEM((depth, rows, width), parts.dtype),
            pltpu.VMEM((depth, rows, width), parts.dtype),
            pltpu.VMEM((depth, rows, width), parts.dtype),
            dma(depth), dma(2, depth), dma(2, depth),
        ],
        compiler_params=comm_params(number),
    )(shaped)


def dot(left, right):
    return jnp.dot(left, right, preferred_element_type=FULL)


def dot_t(left, right):
    return lax.dot_general(left, right, (((1,), (1,)), ((), ())), preferred_element_type=FULL)


def t_dot(left, right):
    return lax.dot_general(left, right, (((0,), (0,)), ((), ())), preferred_element_type=FULL)


def body(
    groups, parts,
    tokens, documents, routes, norm1_gain, q_gain, k_gain, w_query, w_key, w_value, w_out, norm2_gain, router_w,
    w_gate, w_up, w_down, out_grad,
):
    row_count, width = tokens.shape
    local_experts, _, hidden = w_gate.shape
    experts = local_experts * groups
    chain = LENGTH // row_count
    if not (parts == 4 and groups % 2 == 0 and experts <= 2 * TOP and chain == 4 and 4 * row_count == LENGTH and WINDOW == 2 * row_count):
        return body_routed(
            tokens, documents, routes, norm1_gain, q_gain, k_gain, w_query, w_key, w_value, w_out, norm2_gain, router_w,
            w_gate, w_up, w_down, out_grad,
        )
    depth = groups // 2
    rows = row_count // parts
    seen = groups * row_count // 2
    heads = w_query.shape[1] // HD
    group, part = lax.axis_index("expert"), lax.axis_index("tensor")
    core = part % 2

    def quarter(array):
        return lax.dynamic_slice_in_dim(array, part * rows, rows, 0)

    first_row = group * row_count
    positions = first_row + jnp.arange(row_count, dtype=jnp.int32)
    cosine, sine = rope_tables(positions % LENGTH)
    inputs = tokens.astype(FULL)
    scale_one = lax.rsqrt(jnp.mean(inputs * inputs, axis=-1, keepdims=True) + NORM_EPSILON)
    normed_one = (inputs * scale_one * norm1_gain).astype(LOW)
    query_raw = dot(normed_one, w_query)
    key_raw = dot(normed_one, w_key)
    values = dot(normed_one, w_value).astype(LOW)
    squares = lax.psum(
        jnp.stack([jnp.sum(query_raw * query_raw, axis=-1), jnp.sum(key_raw * key_raw, axis=-1)]), "tensor"
    )
    query_scale = lax.rsqrt(squares[0] / width + NORM_EPSILON)[:, None]
    key_scale = lax.rsqrt(squares[1] / width + NORM_EPSILON)[:, None]
    query_gain, key_gain = q_gain.reshape(-1), k_gain.reshape(-1)
    queries = rotate((query_raw * query_scale * query_gain).reshape(row_count, heads, HD), cosine, sine).astype(LOW)
    key_heads = rotate((key_raw * key_scale * key_gain).reshape(row_count, heads, HD), cosine, sine).astype(LOW)
    queries = queries.reshape(row_count, -1)
    own_kv = jnp.concatenate([key_heads.reshape(row_count, -1), values], axis=1)
    every_doc = jnp.concatenate([jnp.full((2 * row_count,), -1, jnp.int32), lax.all_gather(documents, "expert", tiled=True)])
    key_docs = lax.dynamic_slice_in_dim(every_doc, first_row, 3 * row_count, 0)
    spot = group % chain
    block_of = jnp.arange(3 * row_count, dtype=jnp.int32) // row_count
    key_docs = jnp.where(spot + block_of >= 2, key_docs, -1)[:, None]
    query_docs = jnp.broadcast_to(documents[None, :], (8, row_count))
    kv_all, attended, logs, attention, all_grad = run_attention(
        queries, own_kv, key_docs, query_docs, w_out, quarter(out_grad), depth, chain, 3
    )

    own_inputs = quarter(tokens).astype(FULL)
    own_grad = quarter(out_grad)
    own_grad_float = own_grad.astype(FULL)
    state = own_inputs + attention
    scale_two = lax.rsqrt(jnp.mean(state * state, axis=-1, keepdims=True) + NORM_EPSILON)
    normed_two = (state * scale_two * norm2_gain).astype(LOW)
    router_probs = jax.nn.softmax(dot(normed_two, router_w), axis=-1)
    picked = jnp.any(
        quarter(routes)[:, :, None] == jnp.arange(experts, dtype=jnp.int32)[None, None, :], axis=1
    ).astype(FULL)

    gates = (router_probs * picked).T.reshape(groups, local_experts, rows)
    gates = jnp.concatenate([gates, jnp.zeros((groups, 8 - local_experts, rows), FULL)], axis=1)
    normed_two_grad, gate_cots, all_normed, gated, gate_pre_grad, up_pre_grad, produced = run_experts(
        normed_two, gates, all_grad, w_gate, w_up, w_down, 5
    )
    units = 2 * local_experts * hidden
    all_normed, all_grad = all_normed.reshape(seen, width), all_grad.reshape(seen, width)
    gated, gate_pre_grad, up_pre_grad = (a.reshape(seen, units) for a in (gated, gate_pre_grad, up_pre_grad))

    def expert_grads(left, right):
        return t_dot(left, right)

    gate_wgrad = expert_grads(all_normed, gate_pre_grad).reshape(width, 2, local_experts, hidden).transpose(1, 2, 0, 3)
    up_wgrad = expert_grads(all_normed, up_pre_grad).reshape(width, 2, local_experts, hidden).transpose(1, 2, 0, 3)
    down_wgrad = expert_grads(gated, all_grad).reshape(2, local_experts, hidden, width)
    swaps = pair_swap([gate_wgrad, up_wgrad, down_wgrad], 8)
    w_gate_grad, w_up_grad, w_down_grad = (
        lax.dynamic_index_in_dim(mine, core, 0, keepdims=False) + other
        for mine, other in zip((gate_wgrad, up_wgrad, down_wgrad), swaps)
    )

    prob_cot = gate_cots[:, :, :local_experts].reshape(depth, 2, 2, local_experts, rows).sum(axis=2)
    plane = jnp.arange(depth, dtype=jnp.int32) ^ (group // 2)
    prob_cot = prob_cot[plane].reshape(experts, rows).T * picked
    logit_cot = router_probs * (prob_cot - jnp.sum(router_probs * prob_cot, axis=-1, keepdims=True))
    normed_two_grad = normed_two_grad + jnp.einsum(
        "te,de->td", logit_cot, router_w.astype(FULL), precision=HIGHEST_PRECISION
    )
    router_grad = jnp.einsum("td,te->ed", normed_two.astype(FULL), logit_cot, precision=HIGHEST_PRECISION)
    norm2_grad = jnp.sum(normed_two_grad * state * scale_two, axis=0)
    inner_two = jnp.sum(normed_two_grad * norm2_gain * state, axis=-1, keepdims=True)
    state_cot = own_grad_float + scale_two * norm2_gain * normed_two_grad - state * scale_two**3 * inner_two / width
    state_low, query_cot, kv_cot, expert_mix = run_attention_back(
        state_cot.astype(LOW), queries, kv_all, attended, logs, key_docs, query_docs, w_out, produced, chain, 10
    )
    state_low = state_low.reshape(row_count, width)
    output = tensor_gather((state + expert_mix).astype(LOW), 9)
    w_out_grad = t_dot(state_low, attended)
    query_cot = query_cot.reshape(row_count, heads, HD)
    key_cot = kv_cot[:, : heads * HD].reshape(row_count, heads, HD)
    value_low = kv_cot[:, heads * HD :].astype(LOW)
    query_norm_cot = rotate_back(query_cot, cosine, sine).reshape(row_count, -1)
    key_norm_cot = rotate_back(key_cot, cosine, sine).reshape(row_count, -1)
    q_gain_local = jnp.sum(query_norm_cot * query_raw * query_scale, axis=0).reshape(heads, HD)
    k_gain_local = jnp.sum(key_norm_cot * key_raw * key_scale, axis=0).reshape(heads, HD)
    inners = lax.psum(
        jnp.stack(
            [
                jnp.sum(query_norm_cot * query_gain * query_raw, axis=-1),
                jnp.sum(key_norm_cot * key_gain * key_raw, axis=-1),
            ]
        ),
        "tensor",
    )
    query_raw_cot = (
        query_scale * query_gain * query_norm_cot - query_raw * query_scale**3 * inners[0][:, None] / width
    ).astype(LOW)
    key_raw_cot = (
        key_scale * key_gain * key_norm_cot - key_raw * key_scale**3 * inners[1][:, None] / width
    ).astype(LOW)
    normed_part = dot_t(query_raw_cot, w_query) + dot_t(key_raw_cot, w_key) + dot_t(value_low, w_value)
    normed_one_grad = tensor_scatter(normed_part.astype(LOW), 12)
    own_scale = quarter(scale_one)
    norm1_grad = jnp.sum(normed_one_grad * own_inputs * own_scale, axis=0)
    inner_one = jnp.sum(normed_one_grad * norm1_gain * own_inputs, axis=-1, keepdims=True)
    input_grad = (
        state_cot + own_scale * norm1_gain * normed_one_grad - own_inputs * own_scale**3 * inner_one / width
    )
    input_grad = tensor_gather(input_grad.astype(LOW), 13).astype(FULL)

    local = jnp.concatenate(
        [
            t_dot(normed_one, query_raw_cot),
            t_dot(normed_one, key_raw_cot),
            t_dot(normed_one, value_low),
            w_out_grad,
        ],
        axis=1,
    ).astype(LOW)
    summed = expert_scatter(local, depth, 14)
    w_query_grad, w_key_grad, w_value_grad, w_out_grad = jnp.split(summed, 4, axis=1)
    vectors = jnp.concatenate([router_grad, norm1_grad[None], norm2_grad[None]], axis=0)
    vectors = lax.psum(lax.psum_scatter(vectors, "expert", scatter_dimension=1, tiled=True), "tensor")
    gains = lax.psum_scatter(
        jnp.concatenate([q_gain_local, k_gain_local], axis=0), "expert", scatter_dimension=1, tiled=True
    )
    return (
        output,
        input_grad,
        vectors[experts],
        gains[:heads],
        gains[heads:],
        w_query_grad,
        w_key_grad,
        w_value_grad,
        w_out_grad.T,
        vectors[experts + 1],
        vectors[:experts].T,
        w_gate_grad,
        w_up_grad,
        w_down_grad,
    )


def solution(mesh):
    placed = (
        P("expert", None),
        P("expert"),
        P("expert", None),
        P(),
        P("tensor", None),
        P("tensor", None),
        P(None, "tensor"),
        P(None, "tensor"),
        P(None, "tensor"),
        P("tensor", None),
        P(),
        P(),
        P("expert", None, "tensor"),
        P("expert", None, "tensor"),
        P("expert", "tensor", None),
        P("expert", None),
    )
    return jax.shard_map(
        functools.partial(body, mesh.shape["expert"], mesh.shape["tensor"]),
        mesh=mesh,
        in_specs=placed,
        out_specs=(
            P("expert", None),
            P("expert", None),
            P("expert"),
            P("tensor", "expert"),
            P("tensor", "expert"),
            P("expert", "tensor"),
            P("expert", "tensor"),
            P("expert", "tensor"),
            P("tensor", "expert"),
            P("expert"),
            P("expert", None),
            P("expert", None, "tensor"),
            P("expert", None, "tensor"),
            P("expert", "tensor", None),
        ),
        check_vma=False,
    )
```

```python
import functools

import jax
import jax.numpy as jnp
from jax import lax
from jax.experimental import pallas as pl
from jax.experimental.pallas import tpu as pltpu
from jax.sharding import PartitionSpec as P

HD = 128
TOP = 8
WINDOW = 1024
LENGTH = 2048


NORM_EPSILON = 1e-05
HIGHEST_PRECISION = lax.Precision.HIGHEST


def for_sending(value):
    return jax.tree.map(lambda a: a.astype(jnp.bfloat16) if a.dtype == jnp.float32 else a, value)


def shifted(value, axis, steps):
    count = lax.axis_size(axis)
    initial, last = (max(0, -steps), min(count, count - steps))
    return lax.ppermute(value, axis, [(source, source + steps) for source in range(initial, last)])


def rope_tables(positions):
    half_width = HD // 2
    frequency = 10000.0 ** (-jnp.arange(half_width, dtype=jnp.float32) * 2.0 / HD)
    angles = positions.astype(jnp.float32)[:, None] * frequency[None, :]
    angles = jnp.concatenate([angles, angles], axis=-1)
    return (jnp.cos(angles)[:, None, :], jnp.sin(angles)[:, None, :])


def rotate(values, cosine, sine):
    half_width = values.shape[-1] // 2
    turned = jnp.concatenate([-values[..., half_width:], values[..., :half_width]], axis=-1)
    return values * cosine + turned * sine


def rotate_back(grads, cosine, sine):
    half_width = grads.shape[-1] // 2
    scaled = grads * sine
    turned = jnp.concatenate([scaled[..., half_width:], -scaled[..., :half_width]], axis=-1)
    return grads * cosine + turned


def previous_block(pieces):
    return jax.tree.map(
        lambda part, own: part.astype(own.dtype), shifted(for_sending(pieces), "expert", 1), pieces
    )


def following_block(pieces):
    return shifted((for_sending(pieces[0]), for_sending(pieces[1])), "expert", -1)


def body_routed(
    tokens,
    documents,
    routes,
    norm1_gain,
    q_gain,
    k_gain,
    w_query,
    w_key,
    w_value,
    w_out,
    norm2_gain,
    router_w,
    w_gate,
    w_up,
    w_down,
    out_grad,
):
    row_count, model_width = tokens.shape
    groups = lax.axis_size("expert")
    local_experts = w_gate.shape[0]
    experts = local_experts * groups
    capacity = 2 * row_count * TOP // experts
    slots_group = local_experts * capacity
    heads = w_query.shape[1] // HD
    score_scale = HD ** (-0.5)
    first_row = lax.axis_index("expert") * row_count
    positions = first_row + jnp.arange(row_count, dtype=jnp.int32)
    cosine, sine = rope_tables(positions % LENGTH)
    inputs = tokens.astype(jnp.float32)
    scale_one = lax.rsqrt(jnp.mean(inputs * inputs, axis=-1, keepdims=True) + NORM_EPSILON)
    normed_one = (inputs * scale_one * norm1_gain).astype(jnp.bfloat16)
    query_raw = jnp.dot(normed_one, w_query, preferred_element_type=jnp.float32)
    key_raw = jnp.dot(normed_one, w_key, preferred_element_type=jnp.float32)
    values = jnp.dot(normed_one, w_value, preferred_element_type=jnp.float32).astype(jnp.bfloat16)
    query_square, key_square = lax.psum(
        (jnp.sum(query_raw * query_raw, axis=-1), jnp.sum(key_raw * key_raw, axis=-1)), "tensor"
    )
    query_scale = lax.rsqrt(query_square / model_width + NORM_EPSILON)[:, None]
    key_scale = lax.rsqrt(key_square / model_width + NORM_EPSILON)[:, None]
    query_gain = q_gain.reshape(-1)
    key_gain = k_gain.reshape(-1)
    queries = rotate(
        (query_raw * query_scale * query_gain).reshape(row_count, heads, HD), cosine, sine
    ).astype(jnp.bfloat16)
    key_heads = rotate(
        (key_raw * key_scale * key_gain).reshape(row_count, heads, HD), cosine, sine
    ).astype(jnp.bfloat16)
    value_heads = values.reshape(row_count, heads, HD)
    labels = jnp.stack([documents // 256, documents % 256]).astype(jnp.bfloat16)
    previous_one = previous_block((key_heads, value_heads, labels))
    previous_two = previous_block(previous_one)
    all_keys = jnp.concatenate([previous_two[0], previous_one[0], key_heads], axis=0)
    all_values = jnp.concatenate([previous_two[1], previous_one[1], value_heads], axis=0)
    all_labels = jnp.concatenate([previous_two[2], previous_one[2], labels], axis=1)
    key_pos = first_row - 2 * row_count + jnp.arange(3 * row_count, dtype=jnp.int32)
    same_doc = (all_labels[0][None, :] == labels[0][:, None]) & (
        all_labels[1][None, :] == labels[1][:, None]
    )
    allowed = (
        same_doc
        & (key_pos[None, :] <= positions[:, None])
        & (positions[:, None] - key_pos[None, :] < WINDOW)
        & (key_pos[None, :] >= 0)
    )

    def masked_scores():
        raw_scores = (
            jnp.einsum("qhd,khd->hqk", queries, all_keys, preferred_element_type=jnp.float32)
            * score_scale
        )
        return jnp.where(allowed[None], raw_scores, -1e30)

    scores = masked_scores()
    highest = jnp.max(scores, axis=-1, keepdims=True)
    weights = jnp.where(allowed[None], jnp.exp(scores - highest), 0.0)
    denominator = jnp.sum(weights, axis=-1, keepdims=True)
    log_total = highest + jnp.log(denominator)
    attn_probs = weights / denominator
    attended = jnp.einsum(
        "hqk,khd->qhd",
        attn_probs.astype(jnp.bfloat16),
        all_values,
        preferred_element_type=jnp.float32,
    )
    attended = attended.reshape(row_count, -1).astype(jnp.bfloat16)
    attention = lax.psum(jnp.dot(attended, w_out, preferred_element_type=jnp.float32), "tensor")
    state = inputs + attention
    scale_two = lax.rsqrt(jnp.mean(state * state, axis=-1, keepdims=True) + NORM_EPSILON)
    normed_two = (state * scale_two * norm2_gain).astype(jnp.bfloat16)
    router_probs = jax.nn.softmax(
        jnp.dot(normed_two, router_w, preferred_element_type=jnp.float32), axis=-1
    )
    chosen = (routes[:, :, None] == jnp.arange(experts, dtype=jnp.int32)[None, None, :]).astype(
        jnp.float32
    )
    gates = jnp.sum(chosen * router_probs[:, None, :], axis=-1)
    flat_routes = routes.reshape(-1)
    onehot = (flat_routes[:, None] == jnp.arange(experts, dtype=jnp.int32)[None, :]).astype(
        jnp.int32
    )
    slot_index = jnp.sum(jnp.cumsum(onehot, axis=0) * onehot, axis=1) - 1
    target = flat_routes * capacity + slot_index
    source = (
        jnp.full((experts * capacity,), -1, jnp.int32)
        .at[target]
        .set(jnp.arange(row_count * TOP, dtype=jnp.int32))
    )
    live_slot = source >= 0
    pick_index = jnp.maximum(source, 0)
    send_rows = jnp.where(
        live_slot[:, None], normed_two[pick_index // TOP], jnp.zeros((), jnp.bfloat16)
    ).reshape(groups, slots_group, model_width)
    grad_float = out_grad.astype(jnp.float32)
    pick_grads = (
        (gates[:, :, None] * grad_float[:, None, :])
        .astype(jnp.bfloat16)
        .reshape(row_count * TOP, model_width)
    )
    send_grads = jnp.where(
        live_slot[:, None], pick_grads[pick_index], jnp.zeros((), jnp.bfloat16)
    ).reshape(groups, slots_group, model_width)
    arrived = lax.all_to_all(send_rows, "expert", split_axis=0, concat_axis=0, tiled=True)
    stacked = arrived.reshape(groups, local_experts, capacity, model_width)
    gate_pre = jnp.einsum("secd,edf->secf", stacked, w_gate, preferred_element_type=jnp.float32)
    up_pre = jnp.einsum("secd,edf->secf", stacked, w_up, preferred_element_type=jnp.float32)
    activated = jax.nn.silu(gate_pre)
    inner_act = (activated * up_pre).astype(jnp.bfloat16)
    produced = jnp.einsum(
        "secf,efd->secd", inner_act, w_down, preferred_element_type=jnp.float32
    ).astype(jnp.bfloat16)
    returned = lax.all_to_all(
        produced.reshape(groups, slots_group, model_width),
        "expert",
        split_axis=0,
        concat_axis=0,
        tiled=True,
    )
    back_rows = (
        returned.reshape(experts * capacity, model_width)[target]
        .reshape(row_count, TOP, model_width)
        .astype(jnp.float32)
    )
    expert_part = jnp.sum(gates[:, :, None] * back_rows, axis=1)
    expert_mix = lax.psum(expert_part.astype(jnp.bfloat16), "tensor").astype(jnp.float32)
    output = (state + expert_mix).astype(jnp.bfloat16)
    gate_part = jnp.sum(grad_float[:, None, :] * back_rows, axis=-1)
    arrived_grad = lax.all_to_all(send_grads, "expert", split_axis=0, concat_axis=0, tiled=True)
    slot_grad = arrived_grad.reshape(groups, local_experts, capacity, model_width)
    w_down_grad = jnp.einsum(
        "secf,secd->efd", inner_act, slot_grad, preferred_element_type=jnp.float32
    )
    inner_grad = jnp.einsum("secd,efd->secf", slot_grad, w_down, preferred_element_type=jnp.float32)
    logistic = jax.nn.sigmoid(gate_pre)
    gate_pre_grad = (inner_grad * up_pre * logistic * (1.0 + gate_pre * (1.0 - logistic))).astype(
        jnp.bfloat16
    )
    up_pre_grad = (inner_grad * activated).astype(jnp.bfloat16)
    w_gate_grad = jnp.einsum(
        "secd,secf->edf", stacked, gate_pre_grad, preferred_element_type=jnp.float32
    )
    w_up_grad = jnp.einsum(
        "secd,secf->edf", stacked, up_pre_grad, preferred_element_type=jnp.float32
    )
    row_grad = jnp.einsum(
        "secf,edf->secd", gate_pre_grad, w_gate, preferred_element_type=jnp.float32
    )
    row_grad = (
        row_grad
        + jnp.einsum("secf,edf->secd", up_pre_grad, w_up, preferred_element_type=jnp.float32)
    ).astype(jnp.bfloat16)
    grad_back = lax.all_to_all(
        row_grad.reshape(groups, slots_group, model_width),
        "expert",
        split_axis=0,
        concat_axis=0,
        tiled=True,
    )
    grad_picks = (
        grad_back.reshape(experts * capacity, model_width)[target]
        .reshape(row_count, TOP, model_width)
        .astype(jnp.float32)
    )
    normed_part = jnp.sum(grad_picks, axis=1)
    normed_two_grad, gate_cot = lax.psum((normed_part, gate_part), "tensor")
    prob_cot = jnp.sum(gate_cot[:, :, None] * chosen, axis=1)
    logit_cot = router_probs * (prob_cot - jnp.sum(router_probs * prob_cot, axis=-1, keepdims=True))
    router_float = router_w.astype(jnp.float32)
    normed_two_grad = normed_two_grad + jnp.einsum(
        "te,de->td", logit_cot, router_float, precision=HIGHEST_PRECISION
    )
    router_grad = jnp.einsum(
        "td,te->de", normed_two.astype(jnp.float32), logit_cot, precision=HIGHEST_PRECISION
    )
    norm2_grad = jnp.sum(normed_two_grad * state * scale_two, axis=0)
    inner_two = jnp.sum(normed_two_grad * norm2_gain * state, axis=-1, keepdims=True)
    state_cot = (
        grad_float
        + scale_two * norm2_gain * normed_two_grad
        - state * scale_two**3 * inner_two / model_width
    )
    state_low = state_cot.astype(jnp.bfloat16)
    w_out_grad = jnp.einsum("tf,td->fd", attended, state_low, preferred_element_type=jnp.float32)
    attended_cot = (
        jnp.einsum("td,fd->tf", state_low, w_out, preferred_element_type=jnp.float32)
        .astype(jnp.bfloat16)
        .reshape(row_count, heads, HD)
    )
    scores = masked_scores()
    attn_probs = jnp.where(allowed[None], jnp.exp(scores - log_total), 0.0)
    value_cot_all = jnp.einsum(
        "hqk,qhd->khd",
        attn_probs.astype(jnp.bfloat16),
        attended_cot,
        preferred_element_type=jnp.float32,
    )
    prob_grad = jnp.einsum(
        "qhd,khd->hqk", attended_cot, all_values, preferred_element_type=jnp.float32
    )
    delta = jnp.sum(attn_probs * prob_grad, axis=-1, keepdims=True)
    score_cot = (attn_probs * (prob_grad - delta)).astype(jnp.bfloat16)
    query_cot = (
        jnp.einsum("hqk,khd->qhd", score_cot, all_keys, preferred_element_type=jnp.float32)
        * score_scale
    )
    key_cot_all = (
        jnp.einsum("hqk,qhd->khd", score_cot, queries, preferred_element_type=jnp.float32)
        * score_scale
    )
    carried = following_block((key_cot_all[:row_count], value_cot_all[:row_count]))
    carried = following_block(
        (
            key_cot_all[row_count : 2 * row_count] + carried[0],
            value_cot_all[row_count : 2 * row_count] + carried[1],
        )
    )
    key_cot = key_cot_all[2 * row_count :] + carried[0]
    value_cot = value_cot_all[2 * row_count :] + carried[1]
    query_norm_cot = rotate_back(query_cot, cosine, sine).reshape(row_count, -1)
    key_norm_cot = rotate_back(key_cot, cosine, sine).reshape(row_count, -1)
    q_gain_local = jnp.sum(query_norm_cot * query_raw * query_scale, axis=0).reshape(heads, HD)
    k_gain_local = jnp.sum(key_norm_cot * key_raw * key_scale, axis=0).reshape(heads, HD)
    query_inner, key_inner = lax.psum(
        (
            jnp.sum(query_norm_cot * query_gain * query_raw, axis=-1),
            jnp.sum(key_norm_cot * key_gain * key_raw, axis=-1),
        ),
        "tensor",
    )
    query_raw_cot = (
        query_scale * query_gain * query_norm_cot
        - query_raw * query_scale**3 * query_inner[:, None] / model_width
    ).astype(jnp.bfloat16)
    key_raw_cot = (
        key_scale * key_gain * key_norm_cot
        - key_raw * key_scale**3 * key_inner[:, None] / model_width
    ).astype(jnp.bfloat16)
    value_low = value_cot.reshape(row_count, -1).astype(jnp.bfloat16)
    w_query_local = jnp.einsum(
        "td,tf->df", normed_one, query_raw_cot, preferred_element_type=jnp.float32
    )
    w_key_local = jnp.einsum(
        "td,tf->df", normed_one, key_raw_cot, preferred_element_type=jnp.float32
    )
    w_value_local = jnp.einsum(
        "td,tf->df", normed_one, value_low, preferred_element_type=jnp.float32
    )
    normed_part_one = jnp.einsum(
        "tf,df->td", query_raw_cot, w_query, preferred_element_type=jnp.float32
    )
    normed_part_one = normed_part_one + jnp.einsum(
        "tf,df->td", key_raw_cot, w_key, preferred_element_type=jnp.float32
    )
    normed_part_one = normed_part_one + jnp.einsum(
        "tf,df->td", value_low, w_value, preferred_element_type=jnp.float32
    )
    normed_one_grad = lax.psum(normed_part_one.astype(jnp.bfloat16), "tensor").astype(jnp.float32)
    norm1_grad = jnp.sum(normed_one_grad * inputs * scale_one, axis=0)
    inner_one = jnp.sum(normed_one_grad * norm1_gain * inputs, axis=-1, keepdims=True)
    input_grad = (
        state_cot
        + scale_one * norm1_gain * normed_one_grad
        - inputs * scale_one**3 * inner_one / model_width
    )
    summed = (
        lax.psum_scatter(
            w_query_local.astype(jnp.bfloat16), "expert", scatter_dimension=0, tiled=True
        ).astype(jnp.float32),
        lax.psum_scatter(
            w_key_local.astype(jnp.bfloat16), "expert", scatter_dimension=0, tiled=True
        ).astype(jnp.float32),
        lax.psum_scatter(
            w_value_local.astype(jnp.bfloat16), "expert", scatter_dimension=0, tiled=True
        ).astype(jnp.float32),
        lax.psum_scatter(
            w_out_grad.astype(jnp.bfloat16), "expert", scatter_dimension=1, tiled=True
        ).astype(jnp.float32),
        lax.psum_scatter(
            router_grad.astype(jnp.bfloat16), "expert", scatter_dimension=0, tiled=True
        ).astype(jnp.float32),
        lax.psum_scatter(
            norm1_grad.astype(jnp.bfloat16), "expert", scatter_dimension=0, tiled=True
        ).astype(jnp.float32),
        lax.psum_scatter(
            norm2_grad.astype(jnp.bfloat16), "expert", scatter_dimension=0, tiled=True
        ).astype(jnp.float32),
        lax.psum_scatter(
            q_gain_local.astype(jnp.bfloat16), "expert", scatter_dimension=1, tiled=True
        ).astype(jnp.float32),
        lax.psum_scatter(
            k_gain_local.astype(jnp.bfloat16), "expert", scatter_dimension=1, tiled=True
        ).astype(jnp.float32),
    )
    return (
        output,
        input_grad,
        summed[5],
        summed[7],
        summed[8],
        summed[0],
        summed[1],
        summed[2],
        summed[3],
        summed[6],
        summed[4],
        w_gate_grad,
        w_up_grad,
        w_down_grad,
    )


MESH = pl.DeviceIdType.MESH
ANY = pl.BlockSpec(memory_space=pl.ANY)
VMEM = pl.BlockSpec(memory_space=pltpu.VMEM)
VMEM_BYTES = 60 * 1024 * 1024
LOW = jnp.bfloat16
FULL = jnp.float32


def place():
    group, part = lax.axis_index("expert"), lax.axis_index("tensor")
    return group // 2, group % 2, part // 2, part % 2


def device(z, x, y, core):
    return (2 * z + x, 2 * y + core)


def swapped(index, step):
    result, bit = index, 1
    while bit <= step:
        if step & bit:
            result = result + bit - 2 * bit * ((index // bit) % 2)
        bit *= 2
    return result


def greet(partners):
    barrier = pltpu.get_barrier_semaphore()
    for partner in partners:
        pl.semaphore_signal(barrier, inc=1, device_id=partner, device_id_type=MESH)
    pl.semaphore_wait(barrier, len(partners))


def remote(source, target, send, arrive, to):
    return pltpu.make_async_remote_copy(
        src_ref=source, dst_ref=target, send_sem=send, recv_sem=arrive, device_id=to, device_id_type=MESH
    )


def dma(*shape):
    return pltpu.SemaphoreType.DMA(shape)


def comm_params(number):
    return pltpu.CompilerParams(collective_id=number, has_side_effects=True, vmem_limit_bytes=VMEM_BYTES)


def add_rows(target, sources, rows, step=16):
    @pl.loop(0, rows // step)
    def _(index):
        part = pl.ds(index * step, step)
        total = sources[0][part].astype(FULL)
        for source in sources[1:]:
            total = total + source[part].astype(FULL)
        target[part] = total.astype(target.dtype)


class Copies:
    def __init__(self):
        self.open = []

    def start(self, copy):
        copy.start()
        self.open.append((copy, set()))
        return copy

    def mark(self, copy, what):
        for entry, done in self.open:
            if entry is copy:
                done.add(what)

    def arrived(self, copy):
        copy.wait_recv()
        self.mark(copy, "arrived")

    def sent(self, copy):
        copy.wait_send()
        self.mark(copy, "sent")

    def finish(self):
        for copy, done in self.open:
            if "sent" not in done:
                copy.wait_send()
            if "arrived" not in done:
                copy.wait_recv()


class Gather:
    def __init__(self, copies, block, target, rows, z_send, z_recv, p_send, p_recv):
        self.copies, self.block, self.target, self.rows = copies, block, target, rows
        self.z_send, self.z_recv, self.p_send, self.p_recv = z_send, z_recv, p_send, p_recv
        z, x, y, core = place()
        self.over_x, self.over_y = device(z, 1 - x, y, core), device(z, x, 1 - y, core)
        self.here, self.x_place, self.y_place = 2 * x + y, 2 * (1 - x) + y, 2 * x + 1 - y
        self.column = [device(swapped(z, step), x, y, core) for step in range(target.shape[0])]
        self.along, self.planes, self.diagonals = {}, {}, {}

    def at(self, step, spot, part):
        half = self.rows // 2
        if part is None:
            return self.target.at[step, pl.ds(pl.multiple_of(spot * self.rows, self.rows), self.rows)]
        return self.target.at[step, pl.ds(pl.multiple_of(spot * self.rows + part * half, half), half)]

    def begin(self):
        self.spread(0)
        for step in range(1, len(self.column)):
            self.along[step] = self.copies.start(
                remote(self.block, self.at(step, self.here, None), self.z_send.at[step], self.z_recv.at[step], self.column[step])
            )

    def spread(self, step):
        if step:
            self.copies.arrived(self.along[step])
        half = self.rows // 2
        planes = []
        for number, (to, part) in enumerate([(self.over_x, 0), (self.over_y, 1), (self.over_x, 1), (self.over_y, 0)]):
            here = self.at(step, self.here, part)
            source = here if step else self.block.at[pl.ds(part * half, half)]
            planes.append(self.copies.start(remote(source, here, self.p_send.at[step, number], self.p_recv.at[step, number], to)))
        self.planes[step] = planes

    def turn(self, step):
        self.copies.arrived(self.planes[step][0])
        passed = self.at(step, self.x_place, 0)
        first = self.copies.start(remote(passed, passed, self.p_send.at[step, 4], self.p_recv.at[step, 4], self.over_y))
        self.copies.arrived(self.planes[step][1])
        passed = self.at(step, self.y_place, 1)
        second = self.copies.start(remote(passed, passed, self.p_send.at[step, 5], self.p_recv.at[step, 5], self.over_x))
        self.diagonals[step] = (first, second)

    def complete(self, step):
        for copy in self.planes[step][2:] + list(self.diagonals[step]):
            self.copies.arrived(copy)


class Scatter:
    def __init__(self, copies, work, diagonal, from_x, from_y, from_z, rows, send, recv):
        self.copies, self.work, self.rows, self.send, self.recv = copies, work, rows, send, recv
        self.diagonal, self.from_x, self.from_y, self.from_z = diagonal, from_x, from_y, from_z
        z, x, y, core = place()
        self.over_x, self.over_y = device(z, 1 - x, y, core), device(z, x, 1 - y, core)
        self.here, self.x_place, self.y_place = 2 * x + y, 2 * (1 - x) + y, 2 * x + 1 - y
        self.far = 2 * (1 - x) + 1 - y
        self.column = [device(swapped(z, step), x, y, core) for step in range(work.shape[0])]
        self.corners, self.sides, self.along = {}, {}, {}

    def at(self, step, spot, part=None):
        half = self.rows // 2
        if part is None:
            return self.work.at[step, pl.ds(pl.multiple_of(spot * self.rows, self.rows), self.rows)]
        return self.work.at[step, pl.ds(pl.multiple_of(spot * self.rows + part * half, half), half)]

    def copy(self, step, number, source, target, to):
        return self.copies.start(remote(source, target, self.send.at[step, number], self.recv.at[step, number], to))

    def corner(self, step):
        self.corners[step] = (
            self.copy(step, 0, self.at(step, self.far, 0), self.diagonal.at[step, 0], self.over_y),
            self.copy(step, 1, self.at(step, self.far, 1), self.diagonal.at[step, 1], self.over_x),
        )

    def side(self, step):
        via_y, via_x = self.corners[step]
        self.copies.arrived(via_y)
        add_rows(self.at(step, self.x_place, 0), [self.at(step, self.x_place, 0), self.diagonal.at[step, 0]], self.rows // 2)
        to_x = self.copy(step, 2, self.at(step, self.x_place), self.from_x.at[step], self.over_x)
        self.copies.arrived(via_x)
        add_rows(self.at(step, self.y_place, 1), [self.at(step, self.y_place, 1), self.diagonal.at[step, 1]], self.rows // 2)
        to_y = self.copy(step, 3, self.at(step, self.y_place), self.from_y.at[step], self.over_y)
        self.sides[step] = (to_x, to_y)

    def climb(self, step):
        for copy in self.sides[step]:
            self.copies.arrived(copy)
        if step:
            here = self.at(step, self.here)
            add_rows(here, [here, self.from_x.at[step], self.from_y.at[step]], self.rows)
            self.along[step] = self.copy(step, 4, here, self.from_z.at[step], self.column[step])

    def result(self, target):
        for copy in self.along.values():
            self.copies.arrived(copy)
        terms = [self.at(0, self.here), self.from_x.at[0], self.from_y.at[0]]
        add_rows(target, terms + [self.from_z.at[step] for step in self.along], self.rows)

    @staticmethod
    def scratch(depth, rows, width):
        return [
            pltpu.VMEM((depth, 2, rows // 2, width), LOW),
            pltpu.VMEM((depth, rows, width), LOW),
            pltpu.VMEM((depth, rows, width), LOW),
            pltpu.VMEM((depth, rows, width), LOW),
            dma(depth, 5),
            dma(depth, 5),
        ]


def experts_kernel(
    depth, rows, local, hidden,
    x_ref, gates_ref, grad_ref, gate_ref, up_ref, down_ref,
    sum_ref, cots_ref, normed_ref, gated_ref, gate_grad_ref, up_grad_ref, produced_ref,
    wg, wu, wd, x_all, grads, work, y_out, gated, gate_grad, up_grad, gates, gate_wide, cots, cot_rows,
    diagonal, from_x, from_y, from_z, r_send, r_recv,
    z_send, z_recv, p_send, p_recv, s_send, s_recv, w_send, w_recv, w_load, g_load, saves, local_sem,
):
    z, x, y, core = place()
    here, sibling = 2 * x + y, device(z, x, y, 1 - core)
    others = [
        (step, turn, (swapped(z, step), swapped(x, turn // 2), swapped(y, turn % 2)))
        for step in range(depth)
        for turn in range(4)
        if step or turn
    ]
    greet([device(*other, core) for _, _, other in others] + [sibling])
    copies = Copies()
    gather = Gather(copies, x_ref, x_all, rows, z_send, z_recv, p_send, p_recv)
    gather.begin()
    plain = []

    def fetch(source, target, sem):
        copy = pltpu.make_async_copy(source, target, sem)
        copy.start()
        return copy

    plain.append(fetch(x_ref, gather.at(0, here, None), local_sem.at[0]))
    weights = []
    for index in range(local):
        first = pl.multiple_of((core * local + index) * hidden, hidden)
        columns = pl.ds(first, hidden)
        for number, (source, target) in enumerate(
            [(gate_ref, wg.at[:, columns]), (up_ref, wu.at[:, columns]), (down_ref, wd.at[columns])]
        ):
            weights.append(copies.start(remote(source.at[index], target, w_send.at[number, index], w_recv.at[number, index], sibling)))
            plain.append(fetch(source.at[index], target, w_load.at[number, index]))
    smalls = []
    for step, turn, other in others:
        oz, ox, oy = other
        smalls.append(
            copies.start(
                remote(
                    gates_ref.at[2 * oz + ox], gates.at[step, here], s_send.at[0, step, turn], s_recv.at[0, step, turn],
                    device(oz, ox, oy, core),
                )
            )
        )
    plain.append(fetch(gates_ref.at[2 * z + x], gates.at[0, here], local_sem.at[1]))
    grad_copies = [fetch(grad_ref.at[0], grads.at[0], g_load.at[0])]
    scatter = Scatter(copies, work, diagonal, from_x, from_y, from_z, rows, r_send, r_recv)
    saving, producing, keeping = [], [], []
    wave_rows = 4 * rows
    lanes = lax.broadcasted_iota(jnp.int32, (wave_rows, 128), 1)

    def first_half(step):
        for copy in saving:
            copy.wait()
        saving.clear()
        for spot in range(4):
            padded = jnp.concatenate([gates[step, spot], jnp.zeros((120, 128), FULL)], axis=0)
            gate_wide[pl.ds(spot * rows, rows), :] = padded.T
        cots[...] = jnp.zeros_like(cots)
        grad_copies[step].wait()
        if step + 1 < depth:
            grad_copies.append(fetch(grad_ref.at[step + 1], grads.at[(step + 1) % 2], g_load.at[(step + 1) % 2]))
        grad = grads.at[step % 2]

        @pl.loop(0, 2 * local)
        def _(unit):
            columns = pl.ds(pl.multiple_of(unit * hidden, hidden), hidden)
            expert = lax.rem(unit, local)
            gate_pre = dot(x_all[step], wg[:, columns])
            up_pre = dot(x_all[step], wu[:, columns])
            back = dot_t(grad[...], wd[columns, :])
            logistic = 1.0 / (1.0 + jnp.exp(-gate_pre))
            activated = gate_pre * logistic
            inner = activated * up_pre
            cot = jnp.sum(inner * back, axis=-1, keepdims=True)
            cots[...] += jnp.where(lanes == expert, cot, 0.0)
            gate = jnp.sum(jnp.where(lanes == expert, gate_wide[...], 0.0), axis=-1, keepdims=True)
            gated[:, columns] = (gate * inner).astype(LOW)
            inner_grad = gate * back
            gate_grad[:, columns] = (inner_grad * up_pre * logistic * (1.0 + gate_pre * (1.0 - logistic))).astype(LOW)
            up_grad[:, columns] = (inner_grad * activated).astype(LOW)

        for spot in range(4):
            cot_rows[step, spot] = cots[pl.ds(spot * rows, rows), :].T[:8]
        for number, (source, target) in enumerate([(gated, gated_ref), (gate_grad, gate_grad_ref), (up_grad, up_grad_ref)]):
            saving.append(fetch(source, target.at[step], saves.at[number]))
        keeping.append(fetch(x_all.at[step], normed_ref.at[step], saves.at[4 + step]))

    def second_half(step):
        for copy in producing:
            copy.wait()
        producing.clear()
        tile = 512

        @pl.loop(0, x_all.shape[2] // tile)
        def _(index):
            columns = pl.ds(pl.multiple_of(index * tile, tile), tile)
            y_out[:, columns] = dot(gated[...], wd[:, columns]).astype(LOW)
            work[step, :, columns] = (dot_t(gate_grad[...], wg[columns, :]) + dot_t(up_grad[...], wu[columns, :])).astype(LOW)

        producing.append(fetch(y_out, produced_ref.at[step], saves.at[3]))

    gather.turn(0)
    if depth > 1:
        gather.spread(1)
    gather.complete(0)
    for copy in plain:
        copy.wait()
    for copy in weights + smalls:
        copies.arrived(copy)
    for step in range(depth):
        if step:
            gather.complete(step)
        first_half(step)
        if step + 1 < depth:
            gather.turn(step + 1)
        if step + 2 < depth:
            gather.spread(step + 2)
        if step >= 1:
            scatter.side(step - 1)
        if step >= 2:
            scatter.climb(step - 2)
        second_half(step)
        scatter.corner(step)
    for step, turn, (oz, ox, oy) in others:
        copies.start(
            remote(
                cot_rows.at[step, 2 * ox + oy], cots_ref.at[step, here], s_send.at[1, step, turn], s_recv.at[1, step, turn],
                device(oz, ox, oy, core),
            )
        )
    own_cots = fetch(cot_rows.at[0, here], cots_ref.at[0, here], local_sem.at[2])
    if depth > 1:
        scatter.climb(depth - 2)
    scatter.side(depth - 1)
    scatter.climb(depth - 1)
    scatter.result(sum_ref)
    own_cots.wait()
    for copy in saving + producing + keeping:
        copy.wait()
    copies.finish()


def run_experts(block, gates, grads, w_gate, w_up, w_down, number):
    depth, wave, width = grads.shape
    rows = wave // 4
    local, _, hidden = w_gate.shape
    units = 2 * local * hidden
    kept = jax.ShapeDtypeStruct((depth, wave, units), LOW)
    wide = jax.ShapeDtypeStruct((depth, wave, width), LOW)
    return pl.pallas_call(
        functools.partial(experts_kernel, depth, rows, local, hidden),
        out_shape=(
            jax.ShapeDtypeStruct((rows, width), FULL),
            jax.ShapeDtypeStruct((depth, 4, 8, 128), FULL),
            wide, kept, kept, kept, wide,
        ),
        in_specs=[ANY] * 6,
        out_specs=(VMEM, VMEM, ANY, ANY, ANY, ANY, ANY),
        scratch_shapes=[
            pltpu.VMEM((width, units), LOW), pltpu.VMEM((width, units), LOW), pltpu.VMEM((units, width), LOW),
            pltpu.VMEM((depth, wave, width), LOW), pltpu.VMEM((2, wave, width), LOW),
            pltpu.VMEM((depth, wave, width), LOW), pltpu.VMEM((wave, width), LOW),
            pltpu.VMEM((wave, units), LOW), pltpu.VMEM((wave, units), LOW), pltpu.VMEM((wave, units), LOW),
            pltpu.VMEM((depth, 4, 8, 128), FULL), pltpu.VMEM((wave, 128), FULL), pltpu.VMEM((wave, 128), FULL),
            pltpu.VMEM((depth, 4, 8, 128), FULL),
        ]
        + Scatter.scratch(depth, rows, width)
        + [
            dma(depth), dma(depth), dma(depth, 6), dma(depth, 6), dma(2, depth, 4), dma(2, depth, 4),
            dma(3, local), dma(3, local), dma(3, local), dma(2), dma(4 + depth), dma(3),
        ],
        compiler_params=comm_params(number),
    )(block, gates, grads, w_gate, w_up, w_down)


class TensorScatter:
    def __init__(self, copies, work, from_pair, from_y, send, recv):
        self.copies, self.work, self.from_pair, self.from_y, self.send, self.recv = copies, work, from_pair, from_y, send, recv
        z, x, self.y, self.core = place()
        self.sibling, self.over_y = device(z, x, self.y, 1 - self.core), device(z, x, 1 - self.y, self.core)
        self.rows = work.shape[2]

    def begin(self):
        self.pairs = []
        for turn in (1, 0):
            source = self.work.at[swapped(self.y, turn), 1 - self.core]
            self.pairs.append(
                self.copies.start(remote(source, self.from_pair.at[turn], self.send.at[turn], self.recv.at[turn], self.sibling))
            )

    def cross(self):
        self.copies.arrived(self.pairs[0])
        block = self.work.at[1 - self.y, self.core]
        add_rows(block, [block, self.from_pair.at[1]], self.rows)
        self.across = self.copies.start(remote(block, self.from_y, self.send.at[2], self.recv.at[2], self.over_y))

    def result(self, target):
        self.copies.arrived(self.pairs[1])
        self.copies.arrived(self.across)
        add_rows(target, [self.work.at[self.y, self.core], self.from_pair.at[0], self.from_y], self.rows)

    @staticmethod
    def scratch(rows, width):
        return [
            pltpu.VMEM((2, 2, rows, width), LOW),
            pltpu.VMEM((2, rows, width), LOW),
            pltpu.VMEM((rows, width), LOW),
            dma(3),
            dma(3),
        ]


class TensorGather:
    def __init__(self, copies, block, target, send, recv):
        self.copies, self.target, self.send, self.recv = copies, target, send, recv
        z, x, self.y, self.core = place()
        self.sibling, over_y = device(z, x, self.y, 1 - self.core), device(z, x, 1 - self.y, self.core)
        mine = target.at[self.y, self.core]
        self.across = copies.start(remote(block, mine, send.at[0], recv.at[0], over_y))
        self.near = copies.start(remote(block, mine, send.at[1], recv.at[1], self.sibling))
        self.own = pltpu.make_async_copy(block, mine, send.at[3])
        self.own.start()

    def cross(self):
        self.copies.arrived(self.across)
        block = self.target.at[1 - self.y, self.core]
        self.passed = self.copies.start(remote(block, block, self.send.at[2], self.recv.at[2], self.sibling))

    def finish(self):
        self.own.wait()
        self.copies.arrived(self.near)
        self.copies.arrived(self.passed)


def partners_of(depth):
    z, x, y, core = place()
    return [device(swapped(z, step), x, y, core) for step in range(1, depth)] + [
        device(z, 1 - x, y, core),
        device(z, x, 1 - y, core),
        device(z, x, y, 1 - core),
        device(swapped(z, 1), 1 - x, y, core),
    ]


def mask_bias(bias, key_docs, query_docs, length):
    blocks = bias.shape[0] // length

    @pl.loop(0, bias.shape[0] // 128)
    def _(index):
        part = pl.ds(pl.multiple_of(index * 128, 128), 128)
        key = index * 128 + lax.broadcasted_iota(jnp.int32, (128, length), 0) - (blocks - 1) * length
        query = lax.broadcasted_iota(jnp.int32, (128, length), 1)
        seen = (key_docs[part, :] == query_docs[0:1, :]) & (key <= query) & (query - key < WINDOW)
        bias[part, :] = jnp.where(seen, 0.0, -1e30)


def attention_kernel(
    depth, rows, heads, chain,
    query_ref, kv_ref, key_docs, query_docs, w_out, grad_ref,
    kv_all, attended, logs, sum_ref, all_grad,
    scores, bias, partial, from_pair, from_y, t_send, t_recv,
    z_send, z_recv, p_send, p_recv, h_send, h_recv, local,
):
    z, x, y, core = place()
    group, part = lax.axis_index("expert"), lax.axis_index("tensor")
    spot = group % chain
    greet(partners_of(depth))
    copies = Copies()
    length = kv_ref.shape[0]
    scale = HD ** (-0.5)

    def halo_copy(distance, to):
        return remote(kv_ref, kv_all.at[2 - distance], h_send.at[distance], h_recv.at[distance], (to, part))

    for distance in (1, 2):

        @pl.when(spot < chain - distance)
        def _():
            halo_copy(distance, group + distance).start()

    gather = Gather(copies, grad_ref, all_grad, rows, z_send, z_recv, p_send, p_recv)
    gather.begin()
    own = pltpu.make_async_copy(grad_ref, gather.at(0, gather.here, None), local.at[0])
    own.start()
    kv_all[2] = kv_ref[...]
    mask_bias(bias, key_docs, query_docs, length)

    def score(block):
        @pl.loop(0, heads)
        def _(head):
            columns = pl.ds(pl.multiple_of(head * HD, HD), HD)
            keys = pl.ds(block * length, length)
            scores[head, keys, :] = dot_t(kv_all[block, :, columns], query_ref[:, columns]) * scale + bias[keys, :]

    score(2)
    gather.turn(0)
    for distance in (1, 2):

        @pl.when(spot >= distance)
        def _():
            halo_copy(distance, group - distance).wait_recv()

        @pl.when(spot < distance)
        def _():
            kv_all[2 - distance] = jnp.zeros_like(kv_ref)

        score(2 - distance)
    if depth > 1:
        gather.spread(1)

    @pl.loop(0, heads)
    def _(head):
        columns = pl.ds(pl.multiple_of(head * HD, HD), HD)
        mine = scores.at[head]
        highest = jnp.max(mine[...], axis=0, keepdims=True)
        total = jnp.zeros_like(highest)
        mixed = jnp.zeros((HD, length), FULL)
        for block in range(3):
            weights = jnp.exp(mine[pl.ds(block * length, length), :] - highest)
            total = total + jnp.sum(weights, axis=0, keepdims=True)
            mine[pl.ds(block * length, length), :] = weights
        for block in range(3):
            probs = (mine[pl.ds(block * length, length), :] * (1.0 / total)).astype(LOW)
            values = pl.ds(pl.multiple_of((heads + head) * HD, HD), HD)
            mixed = mixed + t_dot(kv_all[block, :, values], probs)
        attended[:, columns] = mixed.T.astype(LOW)
        logs[head] = jnp.broadcast_to(highest + jnp.log(total), (8, length))

    if depth > 1:
        gather.turn(1)
    if depth > 2:
        gather.spread(2)
    for index in range(4):
        partial[index // 2, index % 2] = dot(attended[pl.ds(index * rows, rows), :], w_out[...]).astype(LOW)
    scatter = TensorScatter(copies, partial, from_pair, from_y, t_send, t_recv)
    scatter.begin()
    scatter.cross()
    if depth > 2:
        gather.turn(2)
    for step in range(3, depth):
        gather.spread(step)
    scatter.result(sum_ref)
    for step in range(3, depth):
        gather.turn(step)
    own.wait()
    for distance in (1, 2):

        @pl.when(spot < chain - distance)
        def _():
            halo_copy(distance, group + distance).wait_send()

    copies.finish()


def run_attention(queries, kv, key_docs, query_docs, w_out, grads, depth, chain, number):
    length, wide = kv.shape
    heads = wide // (2 * HD)
    rows, width = grads.shape
    return pl.pallas_call(
        functools.partial(attention_kernel, depth, rows, heads, chain),
        out_shape=(
            jax.ShapeDtypeStruct((3, length, wide), LOW),
            jax.ShapeDtypeStruct(queries.shape, LOW),
            jax.ShapeDtypeStruct((heads, 8, length), FULL),
            jax.ShapeDtypeStruct((rows, width), FULL),
            jax.ShapeDtypeStruct((depth, 4 * rows, width), LOW),
        ),
        in_specs=[VMEM] * 5 + [ANY],
        out_specs=(VMEM, VMEM, VMEM, VMEM, ANY),
        scratch_shapes=[pltpu.VMEM((heads, 3 * length, length), FULL), pltpu.VMEM((3 * length, length), FULL)]
        + TensorScatter.scratch(rows, width)
        + [dma(depth), dma(depth), dma(depth, 6), dma(depth, 6), dma(3), dma(3), dma(1)],
        compiler_params=comm_params(number),
    )(queries, kv, key_docs, query_docs, w_out, grads)


def attention_back_kernel(
    depth, rows, heads, chain,
    low_ref, query_ref, kv_all, attended, logs, key_docs, query_docs, w_out, produced_ref,
    lows, query_cot, kv_cot, mix_ref,
    bias, cots, deltas, turned, sending, landed, work,
    diagonal, from_x, from_y, from_z, r_send, r_recv, t_send, t_recv, h_send, h_recv, load,
):
    group, part = lax.axis_index("expert"), lax.axis_index("tensor")
    spot = group % chain
    greet(partners_of(depth))
    copies = Copies()
    length = query_ref.shape[0]
    scale = HD ** (-0.5)
    wide = heads * HD
    gather = TensorGather(copies, low_ref, lows, t_send, t_recv)
    order = [step for step in range(1, depth)] + [0]
    loads = {}
    for step in order:
        loads[step] = pltpu.make_async_copy(produced_ref.at[step], work.at[step], load.at[step])
        loads[step].start()
    scatter = Scatter(copies, work, diagonal, from_x, from_y, from_z, rows, r_send, r_recv)
    for step in order:
        loads[step].wait()
        scatter.corner(step)
    mask_bias(bias, key_docs, query_docs, length)
    gather.cross()
    gather.finish()
    for index in range(4):
        cots[pl.ds(index * rows, rows), :] = dot_t(lows[index // 2, index % 2], w_out[...]).astype(LOW)
    for head in range(heads):
        columns = pl.ds(head * HD, HD)
        product = cots[:, columns].astype(FULL) * attended[:, columns].astype(FULL)
        deltas[head] = jnp.broadcast_to(jnp.sum(product.T, axis=0, keepdims=True), (8, length))
    turned[...] = jnp.zeros_like(turned)

    def back(block, target):
        @pl.loop(0, heads)
        def _(head):
            columns = pl.ds(pl.multiple_of(head * HD, HD), HD)
            others = pl.ds(pl.multiple_of((heads + head) * HD, HD), HD)
            query, cot = query_ref[:, columns], cots[:, columns]
            log, delta = logs[head, 0:1, :], deltas[head, 0:1, :]
            tile = 256

            @pl.loop(0, length // tile)
            def _(index):
                keys = pl.ds(pl.multiple_of(index * tile, tile), tile)
                key, value = kv_all[block, keys, columns], kv_all[block, keys, others]
                hidden = bias[pl.ds(pl.multiple_of(block * length + index * tile, tile), tile), :]
                probs = jnp.exp(dot_t(key, query) * scale + hidden - log)
                score_cot = (probs * (dot_t(value, cot) - delta)).astype(LOW)
                turned[head] += t_dot(key, score_cot)
                target[keys, columns] = (dot(score_cot, query) * scale).astype(target.dtype)
                target[keys, others] = dot(probs.astype(LOW), cot).astype(target.dtype)

    def halo_copy(distance, to):
        return remote(sending.at[2 - distance], landed.at[2 - distance], h_send.at[distance], h_recv.at[distance], (to, part))

    def send(distance):
        @pl.when(spot >= distance)
        def _():
            halo_copy(distance, group - distance).start()

    back(1, sending.at[1])
    send(1)
    scatter.side(order[0])
    back(0, sending.at[0])
    send(2)
    for step in order[1:-1]:
        scatter.side(step)
    back(2, kv_cot)
    for head in range(heads):
        query_cot[:, pl.ds(head * HD, HD)] = turned[head].T * scale
    scatter.side(order[-1])
    for step in order[:-1]:
        scatter.climb(step)
    for distance in (1, 2):

        @pl.when(spot < chain - distance)
        def _():
            halo_copy(distance, group + distance).wait_recv()
            add_rows(kv_cot, [kv_cot, landed.at[2 - distance]], length)

    scatter.climb(order[-1])
    scatter.result(mix_ref)
    for distance in (1, 2):

        @pl.when(spot >= distance)
        def _():
            halo_copy(distance, group - distance).wait_send()

    copies.finish()


def run_attention_back(low, queries, kv_all, attended, logs, key_docs, query_docs, w_out, produced, chain, number):
    depth = produced.shape[0]
    rows, width = low.shape
    length, wide = kv_all.shape[1:]
    heads = wide // (2 * HD)
    return pl.pallas_call(
        functools.partial(attention_back_kernel, depth, rows, heads, chain),
        out_shape=(
            jax.ShapeDtypeStruct((2, 2, rows, width), LOW),
            jax.ShapeDtypeStruct(queries.shape, FULL),
            jax.ShapeDtypeStruct((length, wide), FULL),
            jax.ShapeDtypeStruct((rows, width), FULL),
        ),
        in_specs=[VMEM] * 8 + [ANY],
        out_specs=(VMEM,) * 4,
        scratch_shapes=[
            pltpu.VMEM((3 * length, length), FULL), pltpu.VMEM((length, wide // 2), LOW),
            pltpu.VMEM((heads, 8, length), FULL), pltpu.VMEM((heads, HD, length), FULL),
            pltpu.VMEM((2, length, wide), LOW), pltpu.VMEM((2, length, wide), LOW),
            pltpu.VMEM(produced.shape, LOW),
        ]
        + Scatter.scratch(depth, rows, width)
        + [dma(4), dma(3), dma(3), dma(3), dma(depth)],
        compiler_params=comm_params(number),
    )(low, queries, kv_all, attended, logs, key_docs, query_docs, w_out, produced)


def dot(left, right):
    return jnp.dot(left, right, preferred_element_type=FULL)


def dot_t(left, right):
    return lax.dot_general(left, right, (((1,), (1,)), ((), ())), preferred_element_type=FULL)


def t_dot(left, right):
    return lax.dot_general(left, right, (((0,), (0,)), ((), ())), preferred_element_type=FULL)


class ExpertScatter:
    def __init__(self, copies, parts, work, from_x, from_z, load, send, recv):
        self.copies, self.parts, self.work, self.from_x, self.from_z = copies, parts, work, from_x, from_z
        self.load, self.send, self.recv = load, send, recv
        self.z, self.x, y, core = place()
        self.depth, self.rows = work.shape[1], work.shape[2]
        self.over_x = device(self.z, 1 - self.x, y, core)
        self.column = [device(swapped(self.z, step), self.x, y, core) for step in range(self.depth)]
        self.order = list(range(self.depth - 1, -1, -1))
        self.loads, self.sides, self.along = {}, {}, {}

    def begin(self, index):
        for step in self.order:
            at = swapped(self.z, step)
            self.sides[index, step] = self.copies.start(
                remote(
                    self.parts[index].at[at, 1 - self.x], self.from_x.at[index, step],
                    self.send.at[0, index, step], self.recv.at[0, index, step], self.over_x,
                )
            )
            load = pltpu.make_async_copy(self.parts[index].at[at, self.x], self.work.at[index, step], self.load.at[index, step])
            load.start()
            self.loads[index, step] = load

    def climb(self, index, step):
        self.loads[index, step].wait()
        self.copies.arrived(self.sides[index, step])
        mine = self.work.at[index, step]
        if step:
            add_rows(mine, [mine, self.from_x.at[index, step]], self.rows)
            self.along[index, step] = self.copies.start(
                remote(
                    mine, self.from_z.at[index, step],
                    self.send.at[1, index, step], self.recv.at[1, index, step], self.column[step],
                )
            )

    def result(self, index, target):
        terms = [self.work.at[index, 0], self.from_x.at[index, 0]]
        for step in range(1, self.depth):
            self.copies.arrived(self.along[index, step])
            terms.append(self.from_z.at[index, step])
        add_rows(target, terms, self.rows)


def gradients_kernel(
    depth, rows, local, hidden, matrices, *refs,
):
    parts, refs = refs[:matrices], refs[matrices:]
    (
        normed_part, tokens_ref, state_cot, scale_ref, gain_ref, out_ref, vector_ref,
        normed_ref, grad_ref, gated_ref, gate_grad_ref, up_grad_ref,
    ) = refs[:12]
    sums, refs = refs[12 : 12 + matrices], refs[12 + matrices :]
    (
        input_grads, outputs, vector_sum,
        gate_own, up_own, down_own, gate_other, up_other, down_other,
        work, from_x, from_z, partial, from_pair, from_y, normed_grad, low, vectors, vector_in, vector_mid, vector_turn,
        tiles, turned, acts, gated_turned, near, far, near_down, far_down,
        e_load, e_send, e_recv, t_send, t_recv, g_send, g_recv, o_send, o_recv, v_send, v_recv, u_send, u_recv,
        tile_load, act_load, save, pair_send, pair_recv, local_sem,
    ) = refs
    z, x, y, core = place()
    group = 2 * z + x
    sibling = device(z, x, y, 1 - core)
    groups = [(step, turn) for step in range(depth) for turn in range(2) if step or turn]
    peers = [device(swapped(z, step), swapped(x, turn), y, core) for step, turn in groups]
    mates = [(z, x, swapped(y, turn // 2), swapped(core, turn % 2)) for turn in range(1, 4)]
    greet(peers + [device(*mate) for mate in mates])
    copies = Copies()
    width = normed_ref.shape[1]
    tile = 512
    count = width // tile

    def fetch(source, target, sem):
        copy = pltpu.make_async_copy(source, target, sem)
        copy.start()
        return copy

    experts = ExpertScatter(copies, parts, work, from_x, from_z, e_load, e_send, e_recv)
    loaded = fetch(normed_part, partial, local_sem.at[0])
    experts.begin(0)
    loaded.wait()
    scatter = TensorScatter(copies, partial, from_pair, from_y, t_send, t_recv)
    scatter.begin()
    out_gather = TensorGather(copies, out_ref, outputs, o_send, o_recv)
    for index in range(1, matrices):
        experts.begin(index)
    act_copies = [fetch(gate_grad_ref, acts.at[0], act_load.at[0]), fetch(up_grad_ref, acts.at[1], act_load.at[1])]

    def fetch_tile(number):
        source = normed_ref if number < count else grad_ref
        columns = pl.ds((number % count) * tile, tile)
        return fetch(source.at[:, columns], tiles.at[number % 2], tile_load.at[number % 2])

    tile_copies = [fetch_tile(0)]
    saving = {}

    def first_unit(owner):
        return owner * local * hidden

    def gate_and_up(number):
        slot = number % 2
        tile_copies[number].wait()
        tile_copies.append(fetch_tile(number + 1))
        turned[...] = tiles[slot].T
        for copy, remote_one in saving.pop(slot, []):
            copies.sent(copy) if remote_one else copy.wait()
        for which in range(2):
            for owner, target in ((1 - core, far), (core, near)):

                @pl.loop(0, local)
                def _(expert):
                    columns = pl.ds(pl.multiple_of(first_unit(owner) + expert * hidden, hidden), hidden)
                    target[which, slot, expert] = dot(turned[...], acts[which, :, columns]).astype(target.dtype)

        saves = []
        place_of = pl.ds(number * tile, tile)
        for which, (own, other) in enumerate(((gate_own, gate_other), (up_own, up_other))):
            away = remote(
                far.at[which, slot], other.at[:, place_of], pair_send.at[which, number], pair_recv.at[which, number], sibling
            )
            copies.start(away)
            saves.append((away, True))
            saves.append((fetch(near.at[which, slot], own.at[:, place_of], save.at[which, slot]), False))
        saving[slot] = saves

    def down(number):
        slot = number % 2
        tile_copies[count + number].wait()
        if number + 1 < count:
            tile_copies.append(fetch_tile(count + number + 1))
        for copy, remote_one in saving.pop(("down", slot), []):
            copies.sent(copy) if remote_one else copy.wait()
        for owner, target in ((1 - core, far_down), (core, near_down)):

            @pl.loop(0, local)
            def _(expert):
                units = pl.ds(pl.multiple_of(first_unit(owner) + expert * hidden, hidden), hidden)
                target[slot, expert] = dot(gated_turned[units, :], tiles[slot]).astype(target.dtype)

        columns = pl.ds(number * tile, tile)
        away = remote(
            far_down.at[slot], down_other.at[:, :, columns], pair_send.at[2, number], pair_recv.at[2, number], sibling
        )
        copies.start(away)
        saving["down", slot] = [
            (away, True), (fetch(near_down.at[slot], down_own.at[:, :, columns], save.at[2, slot]), False)
        ]

    for copy in act_copies:
        copy.wait()
    gate_and_up(0)
    scatter.cross()
    experts.climb(0, experts.order[0])
    gate_and_up(1)
    out_gather.cross()
    experts.climb(0, experts.order[1])
    scatter.result(normed_grad)

    inputs = tokens_ref[...].astype(FULL)
    factor, gain = scale_ref[:, 0:1], gain_ref[0:1, :]
    normed = normed_grad[...]
    inner = jnp.sum(normed * gain * inputs, axis=-1, keepdims=True)
    low[...] = (
        state_cot[...] + factor * gain * normed - inputs * (factor * factor * factor) * inner * (1.0 / width)
    ).astype(LOW)
    gain_grad = jnp.sum(normed * inputs * factor, axis=0, keepdims=True)
    grad_gather = TensorGather(copies, low, input_grads, g_send, g_recv)
    vectors[...] = vector_ref[...]
    slice_width = vectors.shape[2]
    for index in range(vectors.shape[0]):
        vectors[index, 16:17, :] = gain_grad[:, index * slice_width : (index + 1) * slice_width]
    vector_copies = []
    for number, ((step, turn), peer) in enumerate(zip(groups, peers)):
        to = 2 * swapped(z, step) + swapped(x, turn)
        vector_copies.append(
            copies.start(remote(vectors.at[to], vector_in.at[number], v_send.at[number], v_recv.at[number], peer))
        )

    for step in experts.order[2:]:
        experts.climb(0, step)
    gate_and_up(2)
    for step in experts.order[:2]:
        experts.climb(1, step)
    grad_gather.cross()
    gate_and_up(3)
    for copy in vector_copies:
        copies.arrived(copy)
    total = vectors[group]
    for number in range(len(peers)):
        total = total + vector_in[number]
    vector_mid[...] = total
    turn_copies = [
        copies.start(remote(vector_mid, vector_turn.at[number], u_send.at[number], u_recv.at[number], device(*mate)))
        for number, mate in enumerate(mates)
    ]
    for step in experts.order[2:]:
        experts.climb(1, step)
    gated_copy = fetch(gated_ref, acts.at[0], act_load.at[0])
    gated_copy.wait()
    for index in range(2):
        half = pl.ds(index * local * hidden, local * hidden)
        gated_turned[half, :] = acts[0, :, half].T
    experts.result(0, sums[0])
    down(0)
    experts.climb(2, experts.order[0])
    down(1)
    for step in experts.order[1:]:
        experts.climb(2, step)
    down(2)
    experts.result(1, sums[1])
    down(3)
    for copy in turn_copies:
        copies.arrived(copy)
    total = vector_mid[...]
    for number in range(len(mates)):
        total = total + vector_turn[number]
    keep = lax.broadcasted_iota(jnp.int32, total.shape, 0) < 18
    vector_sum[...] = jnp.where(keep, total, vector_mid[...])
    for index in range(3, matrices):
        for step in experts.order:
            experts.climb(index, step)
    for index in range(2, matrices):
        experts.result(index, sums[index])
    out_gather.finish()
    grad_gather.finish()
    for entries in saving.values():
        for copy, remote_one in entries:
            if not remote_one:
                copy.wait()
    copies.finish()


def run_gradients(parts, normed_part, tokens, state_cot, scale, gain, out, vectors, normed, grads, gated, gate_grad, up_grad, local, number):
    matrices = len(parts)
    depth, _, piece, columns = parts[0].shape
    rows, width = tokens.shape
    seen, units = gated.shape
    hidden = units // (2 * local)
    tile = 512
    sum_of = jax.ShapeDtypeStruct((piece, columns), FULL)
    spread = jax.ShapeDtypeStruct((2, 2, rows, width), LOW)
    wide, tall = (local, width, hidden), (local, hidden, width)
    results = pl.pallas_call(
        functools.partial(gradients_kernel, depth, rows, local, hidden, matrices),
        out_shape=(sum_of,) * matrices
        + (
            spread, spread, jax.ShapeDtypeStruct(vectors.shape[1:], FULL),
            jax.ShapeDtypeStruct(wide, FULL), jax.ShapeDtypeStruct(wide, FULL), jax.ShapeDtypeStruct(tall, FULL),
            jax.ShapeDtypeStruct(wide, LOW), jax.ShapeDtypeStruct(wide, LOW), jax.ShapeDtypeStruct(tall, LOW),
        ),
        in_specs=[ANY] * (matrices + 1) + [VMEM] * 6 + [ANY] * 5,
        out_specs=(VMEM,) * (matrices + 3) + (ANY,) * 6,
        scratch_shapes=[pltpu.VMEM((matrices, depth, piece, columns), LOW)] * 3
        + TensorScatter.scratch(rows, width)[:3]
        + [
            pltpu.VMEM((rows, width), FULL), pltpu.VMEM((rows, width), LOW),
            pltpu.VMEM(vectors.shape, FULL), pltpu.VMEM((2 * depth - 1,) + vectors.shape[1:], FULL),
            pltpu.VMEM(vectors.shape[1:], FULL), pltpu.VMEM((3,) + vectors.shape[1:], FULL),
            pltpu.VMEM((2, seen, tile), LOW), pltpu.VMEM((tile, seen), LOW),
            pltpu.VMEM((2, seen, units), LOW), pltpu.VMEM((units, seen), LOW),
            pltpu.VMEM((2, 2, local, tile, hidden), FULL), pltpu.VMEM((2, 2, local, tile, hidden), LOW),
            pltpu.VMEM((2, local, hidden, tile), FULL), pltpu.VMEM((2, local, hidden, tile), LOW),
            dma(matrices, depth), dma(2, matrices, depth), dma(2, matrices, depth),
            dma(3), dma(3), dma(4), dma(3), dma(4), dma(3),
            dma(2 * depth - 1), dma(2 * depth - 1), dma(3), dma(3),
            dma(2), dma(2), dma(3, 2), dma(3, width // tile), dma(3, width // tile), dma(1),
        ],
        compiler_params=comm_params(number),
    )(*parts, normed_part, tokens, state_cot, scale, gain, out, vectors, normed, grads, gated, gate_grad, up_grad)
    return results[:matrices], results[matrices:]


def body(
    groups, parts,
    tokens, documents, routes, norm1_gain, q_gain, k_gain, w_query, w_key, w_value, w_out, norm2_gain, router_w,
    w_gate, w_up, w_down, out_grad,
):
    row_count, width = tokens.shape
    local_experts, _, hidden = w_gate.shape
    experts = local_experts * groups
    chain = LENGTH // row_count
    if not (parts == 4 and groups % 2 == 0 and experts <= min(16, 2 * TOP) and 2 * w_query.shape[1] <= 14 * HD and chain == 4 and 4 * row_count == LENGTH and WINDOW == 2 * row_count):
        return body_routed(
            tokens, documents, routes, norm1_gain, q_gain, k_gain, w_query, w_key, w_value, w_out, norm2_gain, router_w,
            w_gate, w_up, w_down, out_grad,
        )
    depth = groups // 2
    rows = row_count // parts
    seen = groups * row_count // 2
    heads = w_query.shape[1] // HD
    group, part = lax.axis_index("expert"), lax.axis_index("tensor")
    core = part % 2

    def quarter(array):
        return lax.dynamic_slice_in_dim(array, part * rows, rows, 0)

    first_row = group * row_count
    positions = first_row + jnp.arange(row_count, dtype=jnp.int32)
    cosine, sine = rope_tables(positions % LENGTH)
    inputs = tokens.astype(FULL)
    scale_one = lax.rsqrt(jnp.mean(inputs * inputs, axis=-1, keepdims=True) + NORM_EPSILON)
    normed_one = (inputs * scale_one * norm1_gain).astype(LOW)
    query_raw = dot(normed_one, w_query)
    key_raw = dot(normed_one, w_key)
    values = dot(normed_one, w_value).astype(LOW)
    squares = lax.psum(
        jnp.stack([jnp.sum(query_raw * query_raw, axis=-1), jnp.sum(key_raw * key_raw, axis=-1)]), "tensor"
    )
    query_scale = lax.rsqrt(squares[0] / width + NORM_EPSILON)[:, None]
    key_scale = lax.rsqrt(squares[1] / width + NORM_EPSILON)[:, None]
    query_gain, key_gain = q_gain.reshape(-1), k_gain.reshape(-1)
    queries = rotate((query_raw * query_scale * query_gain).reshape(row_count, heads, HD), cosine, sine).astype(LOW)
    key_heads = rotate((key_raw * key_scale * key_gain).reshape(row_count, heads, HD), cosine, sine).astype(LOW)
    queries = queries.reshape(row_count, -1)
    own_kv = jnp.concatenate([key_heads.reshape(row_count, -1), values], axis=1)
    every_doc = jnp.concatenate([jnp.full((2 * row_count,), -1, jnp.int32), lax.all_gather(documents, "expert", tiled=True)])
    key_docs = lax.dynamic_slice_in_dim(every_doc, first_row, 3 * row_count, 0)
    spot = group % chain
    block_of = jnp.arange(3 * row_count, dtype=jnp.int32) // row_count
    key_docs = jnp.where(spot + block_of >= 2, key_docs, -1)[:, None]
    query_docs = jnp.broadcast_to(documents[None, :], (8, row_count))
    kv_all, attended, logs, attention, all_grad = run_attention(
        queries, own_kv, key_docs, query_docs, w_out, quarter(out_grad), depth, chain, 3
    )

    own_inputs = quarter(tokens).astype(FULL)
    own_grad = quarter(out_grad)
    own_grad_float = own_grad.astype(FULL)
    state = own_inputs + attention
    scale_two = lax.rsqrt(jnp.mean(state * state, axis=-1, keepdims=True) + NORM_EPSILON)
    normed_two = (state * scale_two * norm2_gain).astype(LOW)
    router_probs = jax.nn.softmax(dot(normed_two, router_w), axis=-1)
    picked = jnp.any(
        quarter(routes)[:, :, None] == jnp.arange(experts, dtype=jnp.int32)[None, None, :], axis=1
    ).astype(FULL)

    gates = (router_probs * picked).T.reshape(groups, local_experts, rows)
    gates = jnp.concatenate([gates, jnp.zeros((groups, 8 - local_experts, rows), FULL)], axis=1)
    normed_two_grad, gate_cots, all_normed, gated, gate_pre_grad, up_pre_grad, produced = run_experts(
        normed_two, gates, all_grad, w_gate, w_up, w_down, 5
    )
    units = 2 * local_experts * hidden
    all_normed, all_grad = all_normed.reshape(seen, width), all_grad.reshape(seen, width)
    gated, gate_pre_grad, up_pre_grad = (a.reshape(seen, units) for a in (gated, gate_pre_grad, up_pre_grad))

    prob_cot = gate_cots[:, :, :local_experts].reshape(depth, 2, 2, local_experts, rows).sum(axis=2)
    plane = jnp.arange(depth, dtype=jnp.int32) ^ (group // 2)
    prob_cot = prob_cot[plane].reshape(experts, rows).T * picked
    logit_cot = router_probs * (prob_cot - jnp.sum(router_probs * prob_cot, axis=-1, keepdims=True))
    normed_two_grad = normed_two_grad + jnp.einsum(
        "te,de->td", logit_cot, router_w.astype(FULL), precision=HIGHEST_PRECISION
    )
    router_grad = jnp.einsum("td,te->ed", normed_two.astype(FULL), logit_cot, precision=HIGHEST_PRECISION)
    norm2_grad = jnp.sum(normed_two_grad * state * scale_two, axis=0)
    inner_two = jnp.sum(normed_two_grad * norm2_gain * state, axis=-1, keepdims=True)
    state_cot = own_grad_float + scale_two * norm2_gain * normed_two_grad - state * scale_two**3 * inner_two / width
    state_low, query_cot, kv_cot, expert_mix = run_attention_back(
        state_cot.astype(LOW), queries, kv_all, attended, logs, key_docs, query_docs, w_out, produced, chain, 10
    )
    state_low = state_low.reshape(row_count, width)
    query_cot = query_cot.reshape(row_count, heads, HD)
    key_cot = kv_cot[:, : heads * HD].reshape(row_count, heads, HD)
    value_low = kv_cot[:, heads * HD :].astype(LOW)
    query_norm_cot = rotate_back(query_cot, cosine, sine).reshape(row_count, -1)
    key_norm_cot = rotate_back(key_cot, cosine, sine).reshape(row_count, -1)
    q_gain_local = jnp.sum(query_norm_cot * query_raw * query_scale, axis=0).reshape(heads, HD)
    k_gain_local = jnp.sum(key_norm_cot * key_raw * key_scale, axis=0).reshape(heads, HD)
    inners = lax.psum(
        jnp.stack(
            [
                jnp.sum(query_norm_cot * query_gain * query_raw, axis=-1),
                jnp.sum(key_norm_cot * key_gain * key_raw, axis=-1),
            ]
        ),
        "tensor",
    )
    query_raw_cot = (
        query_scale * query_gain * query_norm_cot - query_raw * query_scale**3 * inners[0][:, None] / width
    ).astype(LOW)
    key_raw_cot = (
        key_scale * key_gain * key_norm_cot - key_raw * key_scale**3 * inners[1][:, None] / width
    ).astype(LOW)
    normed_part = dot_t(query_raw_cot, w_query) + dot_t(key_raw_cot, w_key) + dot_t(value_low, w_value)
    pieces = [
        t_dot(left, right).astype(LOW).reshape(depth, 2, width // groups, -1)
        for left, right in (
            (state_low, attended), (normed_one, value_low), (normed_one, query_raw_cot), (normed_one, key_raw_cot)
        )
    ]
    vectors = jnp.concatenate(
        [router_grad, jnp.zeros((17 - experts, width), FULL), norm2_grad[None]], axis=0
    ).reshape(18, groups, width // groups).transpose(1, 0, 2)
    gains = jnp.concatenate([q_gain_local, k_gain_local], axis=0)
    gains = jnp.pad(gains, ((0, 14 - 2 * heads), (0, width // groups - HD)))
    vectors = jnp.concatenate([vectors, jnp.broadcast_to(gains[None], (groups,) + gains.shape)], axis=1)
    sums, (input_grad, output, vector_sum, gate_own, up_own, down_own, gate_other, up_other, down_other) = run_gradients(
        pieces, normed_part.astype(LOW).reshape(2, 2, rows, width), quarter(tokens), state_cot, quarter(scale_one),
        norm1_gain[None], (state + expert_mix).astype(LOW), vectors, all_normed, all_grad, gated, gate_pre_grad, up_pre_grad,
        local_experts, 14,
    )
    own_columns = group * (HD // groups)
    return (
        output.reshape(row_count, width),
        input_grad.reshape(row_count, width).astype(FULL),
        vector_sum[16],
        lax.dynamic_slice(vector_sum, (18, own_columns), (heads, HD // groups)),
        lax.dynamic_slice(vector_sum, (18 + heads, own_columns), (heads, HD // groups)),
        sums[2],
        sums[3],
        sums[1],
        sums[0].T,
        vector_sum[17],
        vector_sum[:experts].T,
        gate_own + gate_other.astype(FULL),
        up_own + up_other.astype(FULL),
        down_own + down_other.astype(FULL),
    )


def solution(mesh):
    placed = (
        P("expert", None),
        P("expert"),
        P("expert", None),
        P(),
        P("tensor", None),
        P("tensor", None),
        P(None, "tensor"),
        P(None, "tensor"),
        P(None, "tensor"),
        P("tensor", None),
        P(),
        P(),
        P("expert", None, "tensor"),
        P("expert", None, "tensor"),
        P("expert", "tensor", None),
        P("expert", None),
    )
    return jax.shard_map(
        functools.partial(body, mesh.shape["expert"], mesh.shape["tensor"]),
        mesh=mesh,
        in_specs=placed,
        out_specs=(
            P("expert", None),
            P("expert", None),
            P("expert"),
            P("tensor", "expert"),
            P("tensor", "expert"),
            P("expert", "tensor"),
            P("expert", "tensor"),
            P("expert", "tensor"),
            P("tensor", "expert"),
            P("expert"),
            P("expert", None),
            P("expert", None, "tensor"),
            P("expert", None, "tensor"),
            P("expert", "tensor", None),
        ),
        check_vma=False,
    )
```

```python
import functools

import jax
import jax.numpy as jnp
from jax import lax
from jax.experimental import pallas as pl
from jax.experimental.pallas import tpu as pltpu
from jax.sharding import PartitionSpec as P

HD = 128
TOP = 8
WINDOW = 1024
LENGTH = 2048


NORM_EPSILON = 1e-05
HIGHEST_PRECISION = lax.Precision.HIGHEST


def for_sending(value):
    return jax.tree.map(lambda a: a.astype(jnp.bfloat16) if a.dtype == jnp.float32 else a, value)


def shifted(value, axis, steps):
    count = lax.axis_size(axis)
    initial, last = (max(0, -steps), min(count, count - steps))
    return lax.ppermute(value, axis, [(source, source + steps) for source in range(initial, last)])


def rope_tables(positions):
    half_width = HD // 2
    frequency = 10000.0 ** (-jnp.arange(half_width, dtype=jnp.float32) * 2.0 / HD)
    angles = positions.astype(jnp.float32)[:, None] * frequency[None, :]
    angles = jnp.concatenate([angles, angles], axis=-1)
    return (jnp.cos(angles)[:, None, :], jnp.sin(angles)[:, None, :])


def rotate(values, cosine, sine):
    half_width = values.shape[-1] // 2
    turned = jnp.concatenate([-values[..., half_width:], values[..., :half_width]], axis=-1)
    return values * cosine + turned * sine


def rotate_back(grads, cosine, sine):
    half_width = grads.shape[-1] // 2
    scaled = grads * sine
    turned = jnp.concatenate([scaled[..., half_width:], -scaled[..., :half_width]], axis=-1)
    return grads * cosine + turned


def previous_block(pieces):
    return jax.tree.map(
        lambda part, own: part.astype(own.dtype), shifted(for_sending(pieces), "expert", 1), pieces
    )


def following_block(pieces):
    return shifted((for_sending(pieces[0]), for_sending(pieces[1])), "expert", -1)


def body_routed(
    tokens,
    documents,
    routes,
    norm1_gain,
    q_gain,
    k_gain,
    w_query,
    w_key,
    w_value,
    w_out,
    norm2_gain,
    router_w,
    w_gate,
    w_up,
    w_down,
    out_grad,
):
    row_count, model_width = tokens.shape
    groups = lax.axis_size("expert")
    local_experts = w_gate.shape[0]
    experts = local_experts * groups
    capacity = 2 * row_count * TOP // experts
    slots_group = local_experts * capacity
    heads = w_query.shape[1] // HD
    score_scale = HD ** (-0.5)
    first_row = lax.axis_index("expert") * row_count
    positions = first_row + jnp.arange(row_count, dtype=jnp.int32)
    cosine, sine = rope_tables(positions % LENGTH)
    inputs = tokens.astype(jnp.float32)
    scale_one = lax.rsqrt(jnp.mean(inputs * inputs, axis=-1, keepdims=True) + NORM_EPSILON)
    normed_one = (inputs * scale_one * norm1_gain).astype(jnp.bfloat16)
    query_raw = jnp.dot(normed_one, w_query, preferred_element_type=jnp.float32)
    key_raw = jnp.dot(normed_one, w_key, preferred_element_type=jnp.float32)
    values = jnp.dot(normed_one, w_value, preferred_element_type=jnp.float32).astype(jnp.bfloat16)
    query_square, key_square = lax.psum(
        (jnp.sum(query_raw * query_raw, axis=-1), jnp.sum(key_raw * key_raw, axis=-1)), "tensor"
    )
    query_scale = lax.rsqrt(query_square / model_width + NORM_EPSILON)[:, None]
    key_scale = lax.rsqrt(key_square / model_width + NORM_EPSILON)[:, None]
    query_gain = q_gain.reshape(-1)
    key_gain = k_gain.reshape(-1)
    queries = rotate(
        (query_raw * query_scale * query_gain).reshape(row_count, heads, HD), cosine, sine
    ).astype(jnp.bfloat16)
    key_heads = rotate(
        (key_raw * key_scale * key_gain).reshape(row_count, heads, HD), cosine, sine
    ).astype(jnp.bfloat16)
    value_heads = values.reshape(row_count, heads, HD)
    labels = jnp.stack([documents // 256, documents % 256]).astype(jnp.bfloat16)
    previous_one = previous_block((key_heads, value_heads, labels))
    previous_two = previous_block(previous_one)
    all_keys = jnp.concatenate([previous_two[0], previous_one[0], key_heads], axis=0)
    all_values = jnp.concatenate([previous_two[1], previous_one[1], value_heads], axis=0)
    all_labels = jnp.concatenate([previous_two[2], previous_one[2], labels], axis=1)
    key_pos = first_row - 2 * row_count + jnp.arange(3 * row_count, dtype=jnp.int32)
    same_doc = (all_labels[0][None, :] == labels[0][:, None]) & (
        all_labels[1][None, :] == labels[1][:, None]
    )
    allowed = (
        same_doc
        & (key_pos[None, :] <= positions[:, None])
        & (positions[:, None] - key_pos[None, :] < WINDOW)
        & (key_pos[None, :] >= 0)
    )

    def masked_scores():
        raw_scores = (
            jnp.einsum("qhd,khd->hqk", queries, all_keys, preferred_element_type=jnp.float32)
            * score_scale
        )
        return jnp.where(allowed[None], raw_scores, -1e30)

    scores = masked_scores()
    highest = jnp.max(scores, axis=-1, keepdims=True)
    weights = jnp.where(allowed[None], jnp.exp(scores - highest), 0.0)
    denominator = jnp.sum(weights, axis=-1, keepdims=True)
    log_total = highest + jnp.log(denominator)
    attn_probs = weights / denominator
    attended = jnp.einsum(
        "hqk,khd->qhd",
        attn_probs.astype(jnp.bfloat16),
        all_values,
        preferred_element_type=jnp.float32,
    )
    attended = attended.reshape(row_count, -1).astype(jnp.bfloat16)
    attention = lax.psum(jnp.dot(attended, w_out, preferred_element_type=jnp.float32), "tensor")
    state = inputs + attention
    scale_two = lax.rsqrt(jnp.mean(state * state, axis=-1, keepdims=True) + NORM_EPSILON)
    normed_two = (state * scale_two * norm2_gain).astype(jnp.bfloat16)
    router_probs = jax.nn.softmax(
        jnp.dot(normed_two, router_w, preferred_element_type=jnp.float32), axis=-1
    )
    chosen = (routes[:, :, None] == jnp.arange(experts, dtype=jnp.int32)[None, None, :]).astype(
        jnp.float32
    )
    gates = jnp.sum(chosen * router_probs[:, None, :], axis=-1)
    flat_routes = routes.reshape(-1)
    onehot = (flat_routes[:, None] == jnp.arange(experts, dtype=jnp.int32)[None, :]).astype(
        jnp.int32
    )
    slot_index = jnp.sum(jnp.cumsum(onehot, axis=0) * onehot, axis=1) - 1
    target = flat_routes * capacity + slot_index
    source = (
        jnp.full((experts * capacity,), -1, jnp.int32)
        .at[target]
        .set(jnp.arange(row_count * TOP, dtype=jnp.int32))
    )
    live_slot = source >= 0
    pick_index = jnp.maximum(source, 0)
    send_rows = jnp.where(
        live_slot[:, None], normed_two[pick_index // TOP], jnp.zeros((), jnp.bfloat16)
    ).reshape(groups, slots_group, model_width)
    grad_float = out_grad.astype(jnp.float32)
    pick_grads = (
        (gates[:, :, None] * grad_float[:, None, :])
        .astype(jnp.bfloat16)
        .reshape(row_count * TOP, model_width)
    )
    send_grads = jnp.where(
        live_slot[:, None], pick_grads[pick_index], jnp.zeros((), jnp.bfloat16)
    ).reshape(groups, slots_group, model_width)
    arrived = lax.all_to_all(send_rows, "expert", split_axis=0, concat_axis=0, tiled=True)
    stacked = arrived.reshape(groups, local_experts, capacity, model_width)
    gate_pre = jnp.einsum("secd,edf->secf", stacked, w_gate, preferred_element_type=jnp.float32)
    up_pre = jnp.einsum("secd,edf->secf", stacked, w_up, preferred_element_type=jnp.float32)
    activated = jax.nn.silu(gate_pre)
    inner_act = (activated * up_pre).astype(jnp.bfloat16)
    produced = jnp.einsum(
        "secf,efd->secd", inner_act, w_down, preferred_element_type=jnp.float32
    ).astype(jnp.bfloat16)
    returned = lax.all_to_all(
        produced.reshape(groups, slots_group, model_width),
        "expert",
        split_axis=0,
        concat_axis=0,
        tiled=True,
    )
    back_rows = (
        returned.reshape(experts * capacity, model_width)[target]
        .reshape(row_count, TOP, model_width)
        .astype(jnp.float32)
    )
    expert_part = jnp.sum(gates[:, :, None] * back_rows, axis=1)
    expert_mix = lax.psum(expert_part.astype(jnp.bfloat16), "tensor").astype(jnp.float32)
    output = (state + expert_mix).astype(jnp.bfloat16)
    gate_part = jnp.sum(grad_float[:, None, :] * back_rows, axis=-1)
    arrived_grad = lax.all_to_all(send_grads, "expert", split_axis=0, concat_axis=0, tiled=True)
    slot_grad = arrived_grad.reshape(groups, local_experts, capacity, model_width)
    w_down_grad = jnp.einsum(
        "secf,secd->efd", inner_act, slot_grad, preferred_element_type=jnp.float32
    )
    inner_grad = jnp.einsum("secd,efd->secf", slot_grad, w_down, preferred_element_type=jnp.float32)
    logistic = jax.nn.sigmoid(gate_pre)
    gate_pre_grad = (inner_grad * up_pre * logistic * (1.0 + gate_pre * (1.0 - logistic))).astype(
        jnp.bfloat16
    )
    up_pre_grad = (inner_grad * activated).astype(jnp.bfloat16)
    w_gate_grad = jnp.einsum(
        "secd,secf->edf", stacked, gate_pre_grad, preferred_element_type=jnp.float32
    )
    w_up_grad = jnp.einsum(
        "secd,secf->edf", stacked, up_pre_grad, preferred_element_type=jnp.float32
    )
    row_grad = jnp.einsum(
        "secf,edf->secd", gate_pre_grad, w_gate, preferred_element_type=jnp.float32
    )
    row_grad = (
        row_grad
        + jnp.einsum("secf,edf->secd", up_pre_grad, w_up, preferred_element_type=jnp.float32)
    ).astype(jnp.bfloat16)
    grad_back = lax.all_to_all(
        row_grad.reshape(groups, slots_group, model_width),
        "expert",
        split_axis=0,
        concat_axis=0,
        tiled=True,
    )
    grad_picks = (
        grad_back.reshape(experts * capacity, model_width)[target]
        .reshape(row_count, TOP, model_width)
        .astype(jnp.float32)
    )
    normed_part = jnp.sum(grad_picks, axis=1)
    normed_two_grad, gate_cot = lax.psum((normed_part, gate_part), "tensor")
    prob_cot = jnp.sum(gate_cot[:, :, None] * chosen, axis=1)
    logit_cot = router_probs * (prob_cot - jnp.sum(router_probs * prob_cot, axis=-1, keepdims=True))
    router_float = router_w.astype(jnp.float32)
    normed_two_grad = normed_two_grad + jnp.einsum(
        "te,de->td", logit_cot, router_float, precision=HIGHEST_PRECISION
    )
    router_grad = jnp.einsum(
        "td,te->de", normed_two.astype(jnp.float32), logit_cot, precision=HIGHEST_PRECISION
    )
    norm2_grad = jnp.sum(normed_two_grad * state * scale_two, axis=0)
    inner_two = jnp.sum(normed_two_grad * norm2_gain * state, axis=-1, keepdims=True)
    state_cot = (
        grad_float
        + scale_two * norm2_gain * normed_two_grad
        - state * scale_two**3 * inner_two / model_width
    )
    state_low = state_cot.astype(jnp.bfloat16)
    w_out_grad = jnp.einsum("tf,td->fd", attended, state_low, preferred_element_type=jnp.float32)
    attended_cot = (
        jnp.einsum("td,fd->tf", state_low, w_out, preferred_element_type=jnp.float32)
        .astype(jnp.bfloat16)
        .reshape(row_count, heads, HD)
    )
    scores = masked_scores()
    attn_probs = jnp.where(allowed[None], jnp.exp(scores - log_total), 0.0)
    value_cot_all = jnp.einsum(
        "hqk,qhd->khd",
        attn_probs.astype(jnp.bfloat16),
        attended_cot,
        preferred_element_type=jnp.float32,
    )
    prob_grad = jnp.einsum(
        "qhd,khd->hqk", attended_cot, all_values, preferred_element_type=jnp.float32
    )
    delta = jnp.sum(attn_probs * prob_grad, axis=-1, keepdims=True)
    score_cot = (attn_probs * (prob_grad - delta)).astype(jnp.bfloat16)
    query_cot = (
        jnp.einsum("hqk,khd->qhd", score_cot, all_keys, preferred_element_type=jnp.float32)
        * score_scale
    )
    key_cot_all = (
        jnp.einsum("hqk,qhd->khd", score_cot, queries, preferred_element_type=jnp.float32)
        * score_scale
    )
    carried = following_block((key_cot_all[:row_count], value_cot_all[:row_count]))
    carried = following_block(
        (
            key_cot_all[row_count : 2 * row_count] + carried[0],
            value_cot_all[row_count : 2 * row_count] + carried[1],
        )
    )
    key_cot = key_cot_all[2 * row_count :] + carried[0]
    value_cot = value_cot_all[2 * row_count :] + carried[1]
    query_norm_cot = rotate_back(query_cot, cosine, sine).reshape(row_count, -1)
    key_norm_cot = rotate_back(key_cot, cosine, sine).reshape(row_count, -1)
    q_gain_local = jnp.sum(query_norm_cot * query_raw * query_scale, axis=0).reshape(heads, HD)
    k_gain_local = jnp.sum(key_norm_cot * key_raw * key_scale, axis=0).reshape(heads, HD)
    query_inner, key_inner = lax.psum(
        (
            jnp.sum(query_norm_cot * query_gain * query_raw, axis=-1),
            jnp.sum(key_norm_cot * key_gain * key_raw, axis=-1),
        ),
        "tensor",
    )
    query_raw_cot = (
        query_scale * query_gain * query_norm_cot
        - query_raw * query_scale**3 * query_inner[:, None] / model_width
    ).astype(jnp.bfloat16)
    key_raw_cot = (
        key_scale * key_gain * key_norm_cot
        - key_raw * key_scale**3 * key_inner[:, None] / model_width
    ).astype(jnp.bfloat16)
    value_low = value_cot.reshape(row_count, -1).astype(jnp.bfloat16)
    w_query_local = jnp.einsum(
        "td,tf->df", normed_one, query_raw_cot, preferred_element_type=jnp.float32
    )
    w_key_local = jnp.einsum(
        "td,tf->df", normed_one, key_raw_cot, preferred_element_type=jnp.float32
    )
    w_value_local = jnp.einsum(
        "td,tf->df", normed_one, value_low, preferred_element_type=jnp.float32
    )
    normed_part_one = jnp.einsum(
        "tf,df->td", query_raw_cot, w_query, preferred_element_type=jnp.float32
    )
    normed_part_one = normed_part_one + jnp.einsum(
        "tf,df->td", key_raw_cot, w_key, preferred_element_type=jnp.float32
    )
    normed_part_one = normed_part_one + jnp.einsum(
        "tf,df->td", value_low, w_value, preferred_element_type=jnp.float32
    )
    normed_one_grad = lax.psum(normed_part_one.astype(jnp.bfloat16), "tensor").astype(jnp.float32)
    norm1_grad = jnp.sum(normed_one_grad * inputs * scale_one, axis=0)
    inner_one = jnp.sum(normed_one_grad * norm1_gain * inputs, axis=-1, keepdims=True)
    input_grad = (
        state_cot
        + scale_one * norm1_gain * normed_one_grad
        - inputs * scale_one**3 * inner_one / model_width
    )
    summed = (
        lax.psum_scatter(
            w_query_local.astype(jnp.bfloat16), "expert", scatter_dimension=0, tiled=True
        ).astype(jnp.float32),
        lax.psum_scatter(
            w_key_local.astype(jnp.bfloat16), "expert", scatter_dimension=0, tiled=True
        ).astype(jnp.float32),
        lax.psum_scatter(
            w_value_local.astype(jnp.bfloat16), "expert", scatter_dimension=0, tiled=True
        ).astype(jnp.float32),
        lax.psum_scatter(
            w_out_grad.astype(jnp.bfloat16), "expert", scatter_dimension=1, tiled=True
        ).astype(jnp.float32),
        lax.psum_scatter(
            router_grad.astype(jnp.bfloat16), "expert", scatter_dimension=0, tiled=True
        ).astype(jnp.float32),
        lax.psum_scatter(
            norm1_grad.astype(jnp.bfloat16), "expert", scatter_dimension=0, tiled=True
        ).astype(jnp.float32),
        lax.psum_scatter(
            norm2_grad.astype(jnp.bfloat16), "expert", scatter_dimension=0, tiled=True
        ).astype(jnp.float32),
        lax.psum_scatter(
            q_gain_local.astype(jnp.bfloat16), "expert", scatter_dimension=1, tiled=True
        ).astype(jnp.float32),
        lax.psum_scatter(
            k_gain_local.astype(jnp.bfloat16), "expert", scatter_dimension=1, tiled=True
        ).astype(jnp.float32),
    )
    return (
        output,
        input_grad,
        summed[5],
        summed[7],
        summed[8],
        summed[0],
        summed[1],
        summed[2],
        summed[3],
        summed[6],
        summed[4],
        w_gate_grad,
        w_up_grad,
        w_down_grad,
    )


MESH = pl.DeviceIdType.MESH
ANY = pl.BlockSpec(memory_space=pl.ANY)
VMEM = pl.BlockSpec(memory_space=pltpu.VMEM)
VMEM_BYTES = 60 * 1024 * 1024
LOW = jnp.bfloat16
FULL = jnp.float32


def place():
    group, part = lax.axis_index("expert"), lax.axis_index("tensor")
    return group // 2, group % 2, part // 2, part % 2


def device(z, x, y, core):
    return (2 * z + x, 2 * y + core)


def swapped(index, step):
    result, bit = index, 1
    while bit <= step:
        if step & bit:
            result = result + bit - 2 * bit * ((index // bit) % 2)
        bit *= 2
    return result


def greet(partners):
    barrier = pltpu.get_barrier_semaphore()
    for partner in partners:
        pl.semaphore_signal(barrier, inc=1, device_id=partner, device_id_type=MESH)
    pl.semaphore_wait(barrier, len(partners))


def remote(source, target, send, arrive, to):
    return pltpu.make_async_remote_copy(
        src_ref=source, dst_ref=target, send_sem=send, recv_sem=arrive, device_id=to, device_id_type=MESH
    )


def dma(*shape):
    return pltpu.SemaphoreType.DMA(shape)


def comm_params(number):
    return pltpu.CompilerParams(collective_id=number, has_side_effects=True, vmem_limit_bytes=VMEM_BYTES)


def add_rows(target, sources, rows, step=16):
    @pl.loop(0, rows // step)
    def _(index):
        part = pl.ds(index * step, step)
        total = sources[0][part].astype(FULL)
        for source in sources[1:]:
            total = total + source[part].astype(FULL)
        target[part] = total.astype(target.dtype)


class Copies:
    def __init__(self):
        self.open = []

    def start(self, copy):
        copy.start()
        self.open.append((copy, set()))
        return copy

    def mark(self, copy, what):
        for entry, done in self.open:
            if entry is copy:
                done.add(what)

    def arrived(self, copy):
        copy.wait_recv()
        self.mark(copy, "arrived")

    def sent(self, copy):
        copy.wait_send()
        self.mark(copy, "sent")

    def finish(self):
        for copy, done in self.open:
            if "sent" not in done:
                copy.wait_send()
            if "arrived" not in done:
                copy.wait_recv()


class Gather:
    def __init__(self, copies, block, target, rows, z_send, z_recv, p_send, p_recv):
        self.copies, self.block, self.target, self.rows = copies, block, target, rows
        self.z_send, self.z_recv, self.p_send, self.p_recv = z_send, z_recv, p_send, p_recv
        z, x, y, core = place()
        self.over_x, self.over_y = device(z, 1 - x, y, core), device(z, x, 1 - y, core)
        self.here, self.x_place, self.y_place = 2 * x + y, 2 * (1 - x) + y, 2 * x + 1 - y
        self.column = [device(swapped(z, step), x, y, core) for step in range(target.shape[0])]
        self.along, self.planes, self.diagonals = {}, {}, {}

    def at(self, step, spot, part):
        half = self.rows // 2
        if part is None:
            return self.target.at[step, pl.ds(pl.multiple_of(spot * self.rows, self.rows), self.rows)]
        return self.target.at[step, pl.ds(pl.multiple_of(spot * self.rows + part * half, half), half)]

    def begin(self):
        self.spread(0)
        for step in range(1, len(self.column)):
            self.lift(step)

    def lift(self, step):
        if 0 < step < len(self.column):
            self.along[step] = self.copies.start(
                remote(self.block, self.at(step, self.here, None), self.z_send.at[step], self.z_recv.at[step], self.column[step])
            )

    def spread(self, step):
        if step:
            self.copies.arrived(self.along[step])
        half = self.rows // 2
        planes = []
        for number, (to, part) in enumerate([(self.over_x, 0), (self.over_y, 1), (self.over_x, 1), (self.over_y, 0)]):
            here = self.at(step, self.here, part)
            source = here if step else self.block.at[pl.ds(part * half, half)]
            planes.append(self.copies.start(remote(source, here, self.p_send.at[step, number], self.p_recv.at[step, number], to)))
        self.planes[step] = planes

    def turn(self, step):
        self.copies.arrived(self.planes[step][0])
        passed = self.at(step, self.x_place, 0)
        first = self.copies.start(remote(passed, passed, self.p_send.at[step, 4], self.p_recv.at[step, 4], self.over_y))
        self.copies.arrived(self.planes[step][1])
        passed = self.at(step, self.y_place, 1)
        second = self.copies.start(remote(passed, passed, self.p_send.at[step, 5], self.p_recv.at[step, 5], self.over_x))
        self.diagonals[step] = (first, second)

    def complete(self, step):
        for copy in self.planes[step][2:] + list(self.diagonals[step]):
            self.copies.arrived(copy)


class Scatter:
    def __init__(self, copies, work, diagonal, from_x, from_y, from_z, rows, send, recv):
        self.copies, self.work, self.rows, self.send, self.recv = copies, work, rows, send, recv
        self.diagonal, self.from_x, self.from_y, self.from_z = diagonal, from_x, from_y, from_z
        z, x, y, core = place()
        self.over_x, self.over_y = device(z, 1 - x, y, core), device(z, x, 1 - y, core)
        self.here, self.x_place, self.y_place = 2 * x + y, 2 * (1 - x) + y, 2 * x + 1 - y
        self.far = 2 * (1 - x) + 1 - y
        self.column = [device(swapped(z, step), x, y, core) for step in range(work.shape[0])]
        self.corners, self.sides, self.along = {}, {}, {}

    def at(self, step, spot, part=None):
        half = self.rows // 2
        if part is None:
            return self.work.at[step, pl.ds(pl.multiple_of(spot * self.rows, self.rows), self.rows)]
        return self.work.at[step, pl.ds(pl.multiple_of(spot * self.rows + part * half, half), half)]

    def copy(self, step, number, source, target, to):
        return self.copies.start(remote(source, target, self.send.at[step, number], self.recv.at[step, number], to))

    def corner(self, step):
        self.corners[step] = (
            self.copy(step, 0, self.at(step, self.far, 0), self.diagonal.at[step, 0], self.over_y),
            self.copy(step, 1, self.at(step, self.far, 1), self.diagonal.at[step, 1], self.over_x),
        )

    def side(self, step):
        via_y, via_x = self.corners[step]
        self.copies.arrived(via_y)
        add_rows(self.at(step, self.x_place, 0), [self.at(step, self.x_place, 0), self.diagonal.at[step, 0]], self.rows // 2)
        to_x = self.copy(step, 2, self.at(step, self.x_place), self.from_x.at[step], self.over_x)
        self.copies.arrived(via_x)
        add_rows(self.at(step, self.y_place, 1), [self.at(step, self.y_place, 1), self.diagonal.at[step, 1]], self.rows // 2)
        to_y = self.copy(step, 3, self.at(step, self.y_place), self.from_y.at[step], self.over_y)
        self.sides[step] = (to_x, to_y)

    def climb(self, step):
        for copy in self.sides[step]:
            self.copies.arrived(copy)
        if step:
            here = self.at(step, self.here)
            add_rows(here, [here, self.from_x.at[step], self.from_y.at[step]], self.rows)
            self.along[step] = self.copy(step, 4, here, self.from_z.at[step], self.column[step])

    def result(self, target):
        for copy in self.along.values():
            self.copies.arrived(copy)
        terms = [self.at(0, self.here), self.from_x.at[0], self.from_y.at[0]]
        add_rows(target, terms + [self.from_z.at[step] for step in self.along], self.rows)

    @staticmethod
    def scratch(depth, rows, width):
        return [
            pltpu.VMEM((depth, 2, rows // 2, width), LOW),
            pltpu.VMEM((depth, rows, width), LOW),
            pltpu.VMEM((depth, rows, width), LOW),
            pltpu.VMEM((depth, rows, width), LOW),
            dma(depth, 5),
            dma(depth, 5),
        ]


def experts_kernel(
    depth, rows, local, hidden,
    x_ref, gates_ref, grad_ref, gate_ref, up_ref, down_ref,
    sum_ref, cots_ref, normed_ref, gated_ref, gate_grad_ref, up_grad_ref, produced_ref,
    wg, wu, wd, x_all, grads, work, y_out, gated, gate_grad, up_grad, gates, gate_wide, cots, cot_rows,
    diagonal, from_x, from_y, from_z, r_send, r_recv,
    z_send, z_recv, p_send, p_recv, s_send, s_recv, w_send, w_recv, w_load, g_load, saves, local_sem,
):
    z, x, y, core = place()
    here, sibling = 2 * x + y, device(z, x, y, 1 - core)
    others = [
        (step, turn, (swapped(z, step), swapped(x, turn // 2), swapped(y, turn % 2)))
        for step in range(depth)
        for turn in range(4)
        if step or turn
    ]
    greet([device(*other, core) for _, _, other in others] + [sibling])
    copies = Copies()
    gather = Gather(copies, x_ref, x_all, rows, z_send, z_recv, p_send, p_recv)
    gather.begin()
    plain = []

    def fetch(source, target, sem):
        copy = pltpu.make_async_copy(source, target, sem)
        copy.start()
        return copy

    plain.append(fetch(x_ref, gather.at(0, here, None), local_sem.at[0]))
    weights = []
    for index in range(local):
        first = pl.multiple_of((core * local + index) * hidden, hidden)
        columns = pl.ds(first, hidden)
        for number, (source, target) in enumerate(
            [(gate_ref, wg.at[:, columns]), (up_ref, wu.at[:, columns]), (down_ref, wd.at[columns])]
        ):
            weights.append(copies.start(remote(source.at[index], target, w_send.at[number, index], w_recv.at[number, index], sibling)))
            plain.append(fetch(source.at[index], target, w_load.at[number, index]))
    smalls = []
    for step, turn, other in others:
        oz, ox, oy = other
        smalls.append(
            copies.start(
                remote(
                    gates_ref.at[2 * oz + ox], gates.at[step, here], s_send.at[0, step, turn], s_recv.at[0, step, turn],
                    device(oz, ox, oy, core),
                )
            )
        )
    plain.append(fetch(gates_ref.at[2 * z + x], gates.at[0, here], local_sem.at[1]))
    grad_copies = [fetch(grad_ref.at[0], grads.at[0], g_load.at[0])]
    scatter = Scatter(copies, work, diagonal, from_x, from_y, from_z, rows, r_send, r_recv)
    saving, producing, keeping = [], [], []
    wave_rows = 4 * rows
    lanes = lax.broadcasted_iota(jnp.int32, (wave_rows, 128), 1)

    def first_half(step):
        for copy in saving:
            copy.wait()
        saving.clear()
        for spot in range(4):
            padded = jnp.concatenate([gates[step, spot], jnp.zeros((120, 128), FULL)], axis=0)
            gate_wide[pl.ds(spot * rows, rows), :] = padded.T
        cots[...] = jnp.zeros_like(cots)
        grad_copies[step].wait()
        if step + 1 < depth:
            grad_copies.append(fetch(grad_ref.at[step + 1], grads.at[(step + 1) % 2], g_load.at[(step + 1) % 2]))
        grad = grads.at[step % 2]

        @pl.loop(0, 2 * local)
        def _(unit):
            columns = pl.ds(pl.multiple_of(unit * hidden, hidden), hidden)
            expert = lax.rem(unit, local)
            gate_pre = dot(x_all[step], wg[:, columns])
            up_pre = dot(x_all[step], wu[:, columns])
            back = dot_t(grad[...], wd[columns, :])
            logistic = 1.0 / (1.0 + jnp.exp(-gate_pre))
            activated = gate_pre * logistic
            inner = activated * up_pre
            cot = jnp.sum(inner * back, axis=-1, keepdims=True)
            cots[...] += jnp.where(lanes == expert, cot, 0.0)
            gate = jnp.sum(jnp.where(lanes == expert, gate_wide[...], 0.0), axis=-1, keepdims=True)
            gated[:, columns] = (gate * inner).astype(LOW)
            inner_grad = gate * back
            gate_grad[:, columns] = (inner_grad * up_pre * logistic * (1.0 + gate_pre * (1.0 - logistic))).astype(LOW)
            up_grad[:, columns] = (inner_grad * activated).astype(LOW)

        for spot in range(4):
            cot_rows[step, spot] = cots[pl.ds(spot * rows, rows), :].T[:8]
        for number, (source, target) in enumerate([(gated, gated_ref), (gate_grad, gate_grad_ref), (up_grad, up_grad_ref)]):
            saving.append(fetch(source, target.at[step], saves.at[number]))
        keeping.append(fetch(x_all.at[step], normed_ref.at[step], saves.at[4 + step]))

    def second_half(step):
        for copy in producing:
            copy.wait()
        producing.clear()
        tile = 512

        @pl.loop(0, x_all.shape[2] // tile)
        def _(index):
            columns = pl.ds(pl.multiple_of(index * tile, tile), tile)
            y_out[:, columns] = dot(gated[...], wd[:, columns]).astype(LOW)
            work[step, :, columns] = (dot_t(gate_grad[...], wg[columns, :]) + dot_t(up_grad[...], wu[columns, :])).astype(LOW)

        producing.append(fetch(y_out, produced_ref.at[step], saves.at[3]))

    gather.turn(0)
    if depth > 1:
        gather.spread(1)
    gather.complete(0)
    for copy in plain:
        copy.wait()
    for copy in weights + smalls:
        copies.arrived(copy)
    for step in range(depth):
        if step:
            gather.complete(step)
        first_half(step)
        if step + 1 < depth:
            gather.turn(step + 1)
        if step + 2 < depth:
            gather.spread(step + 2)
        if step >= 1:
            scatter.side(step - 1)
        if step >= 2:
            scatter.climb(step - 2)
        second_half(step)
        scatter.corner(step)
    for step, turn, (oz, ox, oy) in others:
        copies.start(
            remote(
                cot_rows.at[step, 2 * ox + oy], cots_ref.at[step, here], s_send.at[1, step, turn], s_recv.at[1, step, turn],
                device(oz, ox, oy, core),
            )
        )
    own_cots = fetch(cot_rows.at[0, here], cots_ref.at[0, here], local_sem.at[2])
    if depth > 1:
        scatter.climb(depth - 2)
    scatter.side(depth - 1)
    scatter.climb(depth - 1)
    scatter.result(sum_ref)
    own_cots.wait()
    for copy in saving + producing + keeping:
        copy.wait()
    copies.finish()


def run_experts(block, gates, grads, w_gate, w_up, w_down, number):
    depth, wave, width = grads.shape
    rows = wave // 4
    local, _, hidden = w_gate.shape
    units = 2 * local * hidden
    kept = jax.ShapeDtypeStruct((depth, wave, units), LOW)
    wide = jax.ShapeDtypeStruct((depth, wave, width), LOW)
    return pl.pallas_call(
        functools.partial(experts_kernel, depth, rows, local, hidden),
        out_shape=(
            jax.ShapeDtypeStruct((rows, width), FULL),
            jax.ShapeDtypeStruct((depth, 4, 8, 128), FULL),
            wide, kept, kept, kept, wide,
        ),
        in_specs=[ANY] * 6,
        out_specs=(VMEM, VMEM, ANY, ANY, ANY, ANY, ANY),
        scratch_shapes=[
            pltpu.VMEM((width, units), LOW), pltpu.VMEM((width, units), LOW), pltpu.VMEM((units, width), LOW),
            pltpu.VMEM((depth, wave, width), LOW), pltpu.VMEM((2, wave, width), LOW),
            pltpu.VMEM((depth, wave, width), LOW), pltpu.VMEM((wave, width), LOW),
            pltpu.VMEM((wave, units), LOW), pltpu.VMEM((wave, units), LOW), pltpu.VMEM((wave, units), LOW),
            pltpu.VMEM((depth, 4, 8, 128), FULL), pltpu.VMEM((wave, 128), FULL), pltpu.VMEM((wave, 128), FULL),
            pltpu.VMEM((depth, 4, 8, 128), FULL),
        ]
        + Scatter.scratch(depth, rows, width)
        + [
            dma(depth), dma(depth), dma(depth, 6), dma(depth, 6), dma(2, depth, 4), dma(2, depth, 4),
            dma(3, local), dma(3, local), dma(3, local), dma(2), dma(4 + depth), dma(3),
        ],
        compiler_params=comm_params(number),
    )(block, gates, grads, w_gate, w_up, w_down)


class TensorScatter:
    def __init__(self, copies, work, from_pair, from_y, send, recv):
        self.copies, self.work, self.from_pair, self.from_y, self.send, self.recv = copies, work, from_pair, from_y, send, recv
        z, x, self.y, self.core = place()
        self.sibling, self.over_y = device(z, x, self.y, 1 - self.core), device(z, x, 1 - self.y, self.core)
        self.rows = work.shape[2]

    def begin(self):
        self.pairs = []
        for turn in (1, 0):
            source = self.work.at[swapped(self.y, turn), 1 - self.core]
            self.pairs.append(
                self.copies.start(remote(source, self.from_pair.at[turn], self.send.at[turn], self.recv.at[turn], self.sibling))
            )

    def cross(self):
        self.copies.arrived(self.pairs[0])
        block = self.work.at[1 - self.y, self.core]
        add_rows(block, [block, self.from_pair.at[1]], self.rows)
        self.across = self.copies.start(remote(block, self.from_y, self.send.at[2], self.recv.at[2], self.over_y))

    def result(self, target):
        self.copies.arrived(self.pairs[1])
        self.copies.arrived(self.across)
        add_rows(target, [self.work.at[self.y, self.core], self.from_pair.at[0], self.from_y], self.rows)

    @staticmethod
    def scratch(rows, width):
        return [
            pltpu.VMEM((2, 2, rows, width), LOW),
            pltpu.VMEM((2, rows, width), LOW),
            pltpu.VMEM((rows, width), LOW),
            dma(3),
            dma(3),
        ]


class TensorGather:
    def __init__(self, copies, block, target, send, recv):
        self.copies, self.target, self.send, self.recv = copies, target, send, recv
        z, x, self.y, self.core = place()
        self.sibling, over_y = device(z, x, self.y, 1 - self.core), device(z, x, 1 - self.y, self.core)
        mine = target.at[self.y, self.core]
        self.across = copies.start(remote(block, mine, send.at[0], recv.at[0], over_y))
        self.near = copies.start(remote(block, mine, send.at[1], recv.at[1], self.sibling))
        self.own = pltpu.make_async_copy(block, mine, send.at[3])
        self.own.start()

    def cross(self):
        self.copies.arrived(self.across)
        block = self.target.at[1 - self.y, self.core]
        self.passed = self.copies.start(remote(block, block, self.send.at[2], self.recv.at[2], self.sibling))

    def finish(self):
        self.own.wait()
        self.copies.arrived(self.near)
        self.copies.arrived(self.passed)


def partners_of(depth):
    z, x, y, core = place()
    return [device(swapped(z, step), x, y, core) for step in range(1, depth)] + [
        device(z, 1 - x, y, core),
        device(z, x, 1 - y, core),
        device(z, x, y, 1 - core),
        device(swapped(z, 1), 1 - x, y, core),
    ]


def mask_bias(bias, key_docs, query_docs, length):
    blocks = bias.shape[0] // length

    @pl.loop(0, bias.shape[0] // 128)
    def _(index):
        part = pl.ds(pl.multiple_of(index * 128, 128), 128)
        key = index * 128 + lax.broadcasted_iota(jnp.int32, (128, length), 0) - (blocks - 1) * length
        query = lax.broadcasted_iota(jnp.int32, (128, length), 1)
        seen = (key_docs[part, :] == query_docs[0:1, :]) & (key <= query) & (query - key < WINDOW)
        bias[part, :] = jnp.where(seen, 0.0, -1e30).astype(bias.dtype)


def exchange(copies, mine, landed, send, recv, mates):
    return [
        copies.start(remote(mine, landed.at[number], send.at[number], recv.at[number], device(*mate)))
        for number, mate in enumerate(mates)
    ]


def mates_of():
    z, x, y, core = place()
    return [(z, x, swapped(y, turn // 2), swapped(core, turn % 2)) for turn in range(1, 4)]


def as_rows(columns):
    lanes = lax.broadcasted_iota(jnp.int32, (columns[0].shape[0], 128), 1)
    wide = jnp.zeros(lanes.shape, FULL)
    for index, column in enumerate(columns):
        wide = jnp.where(lanes == index, column, wide)
    return wide.T[:8]


def as_columns(rows_of_eight):
    length = rows_of_eight.shape[1]
    return jnp.concatenate([rows_of_eight, jnp.zeros((120, length), FULL)], axis=0).T


def attention_kernel(
    depth, rows, heads, chain, local,
    tokens_ref, wq_ref, wk_ref, wv_ref, wo_ref, grad_ref,
    gain1_ref, q_gain_ref, k_gain_ref, cosine_ref, sine_ref, docs_ref, gain2_ref, router_ref, picked_ref,
    normed_turned, q_raw, k_raw, queries, kv_all, key_docs, scales, attended, logs, state_ref, normed2_ref, probs_ref, gates_ref,
    all_grad,
    tokens, normed_ref, wq, wk, wv, wo, docs_in, squares, squares_in, scores, bias, partial, from_pair, from_y, sum_ref,
    t_send, t_recv, z_send, z_recv, p_send, p_recv, h_send, h_recv, q_send, q_recv, load,
):
    z, x, y, core = place()
    group, part = lax.axis_index("expert"), lax.axis_index("tensor")
    spot = group % chain
    length, width = tokens.shape
    wide = heads * HD
    scale = HD ** (-0.5)
    loads = []
    for number, (source, target) in enumerate([(tokens_ref, tokens), (wv_ref, wv), (wk_ref, wk), (wq_ref, wq), (wo_ref, wo)]):
        loads.append(pltpu.make_async_copy(source, target, load.at[number]))
        loads[-1].start()
    mates = mates_of()
    z1, x1 = swapped(z, 1), 1 - x
    greet(
        [device(swapped(z, step), x, y, core) for step in range(1, depth)]
        + [device(z, x1, y, core), device(z1, x1, y, core)]
        + [device(*mate) for mate in mates]
    )
    copies = Copies()
    gather = Gather(copies, grad_ref, all_grad, rows, z_send, z_recv, p_send, p_recv)
    gather.spread(0)
    gather.lift(1)
    own = pltpu.make_async_copy(grad_ref, gather.at(0, gather.here, None), load.at[5])
    own.start()
    key_part, value_part = pl.ds(0, wide), pl.ds(wide, wide)

    def halo_copy(kind, distance, to):
        if kind == 2:
            return remote(docs_ref, docs_in.at[2 - distance], h_send.at[kind, distance], h_recv.at[kind, distance], (to, part))
        columns = (key_part, value_part)[kind]
        return remote(
            kv_all.at[2, :, columns], kv_all.at[2 - distance, :, columns],
            h_send.at[kind, distance], h_recv.at[kind, distance], (to, part),
        )

    def halo_start(kind):
        for distance in (1, 2):

            @pl.when(spot < chain - distance)
            def _():
                halo_copy(kind, distance, group + distance).start()

    def halo_arrive(kind, distance):
        @pl.when(spot >= distance)
        def _():
            halo_copy(kind, distance, group - distance).wait_recv()

        @pl.when(spot < distance)
        def _():
            if kind == 2:
                docs_in[2 - distance] = jnp.full_like(docs_ref, -1)
            else:
                columns = (key_part, value_part)[kind]
                kv_all[2 - distance, :, columns] = jnp.zeros((length, wide), LOW)

    halo_start(2)
    loads[0].wait()

    @pl.loop(0, length // 128)
    def _(index):
        part_rows = pl.ds(pl.multiple_of(index * 128, 128), 128)
        values = tokens[part_rows, :].astype(FULL)
        factor = lax.rsqrt(jnp.mean(values * values, axis=-1, keepdims=True) + NORM_EPSILON)
        normed_ref[part_rows, :] = (values * factor * gain1_ref[0:1, :]).astype(LOW)

    def project(weights, store):
        @pl.loop(0, wide // 256)
        def _(index):
            columns = pl.ds(pl.multiple_of(index * 256, 256), 256)
            store(index, columns, dot(normed_ref[...], weights[:, columns]))

    def keep_value(index, columns, result):
        kv_all[2, :, pl.ds(pl.multiple_of(wide + index * 256, 256), 256)] = result.astype(LOW)

    def keep_key(index, columns, result):
        k_raw[:, columns] = result

    def keep_query(index, columns, result):
        q_raw[:, columns] = result

    loads[2].wait()
    project(wk, keep_key)
    loads[3].wait()
    project(wq, keep_query)
    squares[...] = as_rows(
        [jnp.sum(q_raw[...] * q_raw[...], axis=-1, keepdims=True), jnp.sum(k_raw[...] * k_raw[...], axis=-1, keepdims=True)]
    )
    sent = exchange(copies, squares, squares_in, q_send, q_recv, mates)
    loads[1].wait()
    project(wv, keep_value)
    halo_start(1)

    @pl.loop(0, width // 256)
    def _(index):
        columns = pl.ds(pl.multiple_of(index * 256, 256), 256)
        normed_turned[columns, :] = normed_ref[:, columns].T

    for copy in sent:
        copies.arrived(copy)
    total = squares[...]
    for number in range(3):
        total = total + squares_in[number]
    scales[...] = lax.rsqrt(total * (1.0 / width) + NORM_EPSILON)
    factors = as_columns(scales[...])

    def turn_heads(raw, gain_ref, factor, store):
        for head in range(heads):
            columns = pl.ds(head * HD, HD)
            normed = raw[:, columns] * factor * gain_ref[0:1, columns]
            store(head, (normed * cosine_ref[...] + pltpu.roll(normed, HD // 2, 1) * sine_ref[...]).astype(LOW))

    def store_key(head, turned):
        kv_all[2, :, pl.ds(head * HD, HD)] = turned

    def store_query(head, turned):
        queries[:, pl.ds(head * HD, HD)] = turned

    turn_heads(k_raw, k_gain_ref, factors[:, 1:2], store_key)
    halo_start(0)
    gather.turn(0)
    gather.spread(1)
    gather.lift(2)
    turn_heads(q_raw, q_gain_ref, factors[:, 0:1], store_query)
    for distance in (1, 2):
        halo_arrive(2, distance)
    for block in range(3):
        rows_of = docs_in[block] if block < 2 else docs_ref[...]
        key_docs[pl.ds(block * length, length), :] = rows_of.astype(FULL).T[:, 0:1].astype(jnp.int32)
    mask_bias(bias, key_docs, docs_ref, length)

    def score(block):
        @pl.loop(0, heads)
        def _(head):
            columns = pl.ds(pl.multiple_of(head * HD, HD), HD)
            keys = pl.ds(block * length, length)
            scores[head, keys, :] = dot_t(kv_all[block, :, columns], queries[:, columns]) * scale + bias[keys, :]

    score(2)
    gather.turn(1)
    gather.spread(2)
    gather.lift(3)
    for distance in (1, 2):
        halo_arrive(0, distance)
        score(2 - distance)
    for distance in (1, 2):
        halo_arrive(1, distance)

    @pl.loop(0, heads)
    def _(head):
        columns = pl.ds(pl.multiple_of(head * HD, HD), HD)
        mine = scores.at[head]
        highest = jnp.max(mine[...], axis=0, keepdims=True)
        total = jnp.zeros_like(highest)
        mixed = jnp.zeros((HD, length), FULL)
        for block in range(3):
            weights = jnp.exp(mine[pl.ds(block * length, length), :] - highest)
            total = total + jnp.sum(weights, axis=0, keepdims=True)
            mine[pl.ds(block * length, length), :] = weights
        for block in range(3):
            probs = (mine[pl.ds(block * length, length), :] * (1.0 / total)).astype(LOW)
            values = pl.ds(pl.multiple_of((heads + head) * HD, HD), HD)
            mixed = mixed + t_dot(kv_all[block, :, values], probs)
        attended[:, columns] = mixed.T.astype(LOW)
        logs[head] = jnp.broadcast_to(highest + jnp.log(total), (8, length))

    gather.turn(2)
    gather.spread(3)
    loads[4].wait()
    for index in range(4):
        partial[index // 2, index % 2] = dot(attended[pl.ds(index * rows, rows), :], wo[...]).astype(LOW)
    scatter = TensorScatter(copies, partial, from_pair, from_y, t_send, t_recv)
    scatter.begin()
    scatter.cross()
    gather.turn(3)
    scatter.result(sum_ref)
    own_rows = pl.ds(pl.multiple_of(part * rows, rows), rows)
    state = tokens[own_rows, :].astype(FULL) + sum_ref[...]
    state_ref[...] = state
    factor = lax.rsqrt(jnp.mean(state * state, axis=-1, keepdims=True) + NORM_EPSILON)
    normed2_ref[...] = (state * factor * gain2_ref[0:1, :]).astype(LOW)
    logits = dot(normed2_ref[...], router_ref[...])
    experts = gates_ref.shape[0] * local
    lanes = lax.broadcasted_iota(jnp.int32, logits.shape, 1)
    logits = jnp.where(lanes < experts, logits, -1e30)
    weights = jnp.exp(logits - jnp.max(logits, axis=-1, keepdims=True))
    probs = weights / jnp.sum(weights, axis=-1, keepdims=True)
    probs_ref[...] = probs
    gates = (probs * picked_ref[...]).T
    gates_ref[...] = jnp.zeros_like(gates_ref)
    for index in range(gates_ref.shape[0]):
        gates_ref[index, 0:local, :] = gates[index * local : (index + 1) * local]
    own.wait()
    for kind in range(3):
        for distance in (1, 2):

            @pl.when(spot < chain - distance)
            def _():
                halo_copy(kind, distance, group + distance).wait_send()

    copies.finish()


def run_attention(tokens, weights, grads, gains, tables, docs, gain2, router, picked, depth, chain, local, number):
    length, width = tokens.shape
    rows = grads.shape[0]
    wide = weights[0].shape[1]
    heads = wide // HD
    return pl.pallas_call(
        functools.partial(attention_kernel, depth, rows, heads, chain, local),
        out_shape=(
            jax.ShapeDtypeStruct((width, length), LOW),
            jax.ShapeDtypeStruct((length, wide), FULL),
            jax.ShapeDtypeStruct((length, wide), FULL),
            jax.ShapeDtypeStruct((length, wide), LOW),
            jax.ShapeDtypeStruct((3, length, 2 * wide), LOW),
            jax.ShapeDtypeStruct((3 * length, 1), jnp.int32),
            jax.ShapeDtypeStruct((8, length), FULL),
            jax.ShapeDtypeStruct((length, wide), LOW),
            jax.ShapeDtypeStruct((heads, 8, length), FULL),
            jax.ShapeDtypeStruct((rows, width), FULL),
            jax.ShapeDtypeStruct((rows, width), LOW),
            jax.ShapeDtypeStruct((rows, 128), FULL),
            jax.ShapeDtypeStruct((2 * depth, 8, rows), FULL),
            jax.ShapeDtypeStruct((depth, 4 * rows, width), LOW),
        ),
        in_specs=[ANY] * 6 + [VMEM] * 9,
        out_specs=(VMEM,) * 13 + (ANY,),
        scratch_shapes=[
            pltpu.VMEM(tokens.shape, LOW), pltpu.VMEM(tokens.shape, LOW), pltpu.VMEM((width, wide), LOW), pltpu.VMEM((width, wide), LOW),
            pltpu.VMEM((width, wide), LOW), pltpu.VMEM((wide, width), LOW), pltpu.VMEM((2, 8, length), jnp.int32),
            pltpu.VMEM((8, length), FULL), pltpu.VMEM((3, 8, length), FULL),
            pltpu.VMEM((heads, 3 * length, length), FULL), pltpu.VMEM((3 * length, length), FULL),
        ]
        + TensorScatter.scratch(rows, width)[:3]
        + [
            pltpu.VMEM((rows, width), FULL), dma(3), dma(3),
            dma(depth), dma(depth), dma(depth, 6), dma(depth, 6), dma(3, 3), dma(3, 3), dma(3), dma(3), dma(6),
        ],
        compiler_params=comm_params(number),
    )(tokens, *weights, grads, *gains, *tables, docs, gain2, router, picked)


def attention_back_kernel(
    depth, rows, heads, chain, local,
    sum_ref, gate_cots, probs_ref, picked_ref, state_ref, gain2_ref, router_ref, normed2_ref, grad_ref,
    query_ref, kv_all, attended, logs, key_docs, query_docs, q_raw, k_raw, q_gain_ref, k_gain_ref, cosine_ref, sine_ref, scales,
    w_out, produced_ref, normed_ref, wq_ref, wk_ref, wv_ref,
    state_cot_ref, router_grad_ref, norm2_grad_ref, q_grad_ref, k_grad_ref, mix_ref, normed_part, piece0, piece1, piece2, piece3,
    low, lows, by_expert, bias, cots, deltas, turned, query_cot, kv_cot, sending, landed, work, raw_cots, flipped, wq, wk, wv,
    inners, inners_in, staging,
    diagonal, from_x, from_y, from_z, r_send, r_recv, t_send, t_recv, h_send, h_recv, i_send, i_recv, load, saves,
):
    z, x, y, core = place()
    group, part = lax.axis_index("expert"), lax.axis_index("tensor")
    spot = group % chain
    length, width = query_ref.shape[0], w_out.shape[1]
    wide = heads * HD
    scale = HD ** (-0.5)
    order = [step for step in range(depth - 1, 0, -1)] + [0]
    loads = {}
    for step in order:
        loads[step] = pltpu.make_async_copy(produced_ref.at[step], work.at[step], load.at[step])
        loads[step].start()
    others = []
    for number, (source, target) in enumerate([(wq_ref, wq), (wk_ref, wk), (wv_ref, wv)]):
        others.append(pltpu.make_async_copy(source, target, load.at[depth + number]))
        others[-1].start()
    mates = mates_of()
    greet(
        [device(swapped(z, step), x, y, core) for step in range(1, depth)]
        + [device(z, 1 - x, y, core), device(swapped(z, 1), 1 - x, y, core)]
        + [device(*mate) for mate in mates]
    )
    copies = Copies()

    by_expert[...] = jnp.zeros_like(by_expert)
    for plane in range(depth):
        step = swapped(z, plane)
        for column in range(2):
            first = (2 * plane + column) * local
            by_expert[first : first + local, :] = (gate_cots[step, 2 * column] + gate_cots[step, 2 * column + 1])[:local]
    probs = probs_ref[...]
    prob_cot = by_expert[...].T * picked_ref[...]
    logit_cot = probs * (prob_cot - jnp.sum(probs * prob_cot, axis=-1, keepdims=True))
    normed2_cot = sum_ref[...] + lax.dot_general(
        logit_cot, router_ref[...].astype(FULL), (((1,), (1,)), ((), ())),
        precision=HIGHEST_PRECISION, preferred_element_type=FULL,
    )
    state = state_ref[...]
    factor = lax.rsqrt(jnp.mean(state * state, axis=-1, keepdims=True) + NORM_EPSILON)
    norm2_grad_ref[...] = jnp.broadcast_to(jnp.sum(normed2_cot * state * factor, axis=0, keepdims=True), norm2_grad_ref.shape)
    inner = jnp.sum(normed2_cot * gain2_ref[0:1, :] * state, axis=-1, keepdims=True)
    state_cot = (
        grad_ref[...].astype(FULL)
        + factor * gain2_ref[0:1, :] * normed2_cot
        - state * (factor * factor * factor) * inner * (1.0 / width)
    )
    state_cot_ref[...] = state_cot
    low[...] = state_cot.astype(LOW)
    gather = TensorGather(copies, low, lows, t_send, t_recv)
    scatter = Scatter(copies, work, diagonal, from_x, from_y, from_z, rows, r_send, r_recv)
    for step in order[:2]:
        loads[step].wait()
        scatter.corner(step)
    router_grad_ref[...] = jnp.dot(
        logit_cot.T, normed2_ref[...].astype(FULL), precision=HIGHEST_PRECISION, preferred_element_type=FULL
    )[: router_grad_ref.shape[0]]
    mask_bias(bias, key_docs, query_docs, length)
    gather.cross()
    gather.finish()
    for index in range(4):
        cots[pl.ds(index * rows, rows), :] = dot_t(lows[index // 2, index % 2], w_out[...]).astype(LOW)
    for head in range(heads):
        columns = pl.ds(head * HD, HD)
        product = cots[:, columns].astype(FULL) * attended[:, columns].astype(FULL)
        deltas[head] = jnp.broadcast_to(jnp.sum(product.T, axis=0, keepdims=True), (8, length))
    turned[...] = jnp.zeros_like(turned)

    def back(block, target):
        @pl.loop(0, heads)
        def _(head):
            columns = pl.ds(pl.multiple_of(head * HD, HD), HD)
            values = pl.ds(pl.multiple_of((heads + head) * HD, HD), HD)
            query, cot = query_ref[:, columns], cots[:, columns]
            log, delta = logs[head, 0:1, :], deltas[head, 0:1, :]
            tile = 256

            @pl.loop(0, length // tile)
            def _(index):
                keys = pl.ds(pl.multiple_of(index * tile, tile), tile)
                key, value = kv_all[block, keys, columns], kv_all[block, keys, values]
                hidden = bias[pl.ds(pl.multiple_of(block * length + index * tile, tile), tile), :].astype(FULL)
                probs = jnp.exp(dot_t(key, query) * scale + hidden - log)
                score_cot = (probs * (dot_t(value, cot) - delta)).astype(LOW)
                turned[head] += t_dot(key, score_cot)
                target[keys, columns] = (dot(score_cot, query) * scale).astype(target.dtype)
                target[keys, values] = dot(probs.astype(LOW), cot).astype(target.dtype)

    def halo_copy(distance, to):
        return remote(sending.at[2 - distance], landed.at[2 - distance], h_send.at[distance], h_recv.at[distance], (to, part))

    def send(distance):
        @pl.when(spot >= distance)
        def _():
            halo_copy(distance, group - distance).start()

    back(1, sending.at[1])
    send(1)
    scatter.side(order[0])
    back(0, sending.at[0])
    send(2)
    for step in order[2:]:
        loads[step].wait()
        scatter.corner(step)
    scatter.side(order[1])
    back(2, kv_cot)
    for head in range(heads):
        query_cot[:, pl.ds(head * HD, HD)] = turned[head].T * scale
    scatter.climb(order[0])

    saving = {}

    def weight_piece(number, right, target):
        piece = target.shape[2]
        for index in range(2 * depth):
            slot = index % 2
            if slot in saving:
                saving.pop(slot).wait()
            staging[slot] = dot(flipped[pl.ds(index * piece, piece), :], right).astype(LOW)
            saving[slot] = pltpu.make_async_copy(staging.at[slot], target.at[index // 2, index % 2], saves.at[slot])
            saving[slot].start()

    @pl.loop(0, width // 256)
    def _(index):
        columns = pl.ds(pl.multiple_of(index * 256, 256), 256)
        flipped[columns, :] = jnp.concatenate([lows[block // 2, block % 2, :, columns] for block in range(4)], axis=0).T

    weight_piece(0, attended[...], piece0)
    normed_copy = pltpu.make_async_copy(normed_ref, flipped, load.at[depth + 3])
    normed_copy.start()
    for step in order[2:]:
        scatter.side(step)
    factors = as_columns(scales[...])

    def turn_back(cot, raw, gain_ref, factor, grad_out):
        total = jnp.zeros((length, 1), FULL)
        for head in range(heads):
            columns = pl.ds(head * HD, HD)
            mine = cot[:, columns]
            mine = mine * cosine_ref[...] - pltpu.roll(mine, HD // 2, 1) * sine_ref[...]
            cot[:, columns] = mine
            mine = mine * raw[:, columns]
            grad_out[:, columns] = jnp.broadcast_to(jnp.sum(mine * factor, axis=0, keepdims=True), (8, HD))
            total = total + jnp.sum(mine * gain_ref[0:1, columns], axis=-1, keepdims=True)
        return total

    query_inner = turn_back(query_cot, q_raw, q_gain_ref, factors[:, 0:1], q_grad_ref)
    scatter.climb(order[1])
    for distance in (1, 2):

        @pl.when(spot < chain - distance)
        def _():
            halo_copy(distance, group + distance).wait_recv()
            add_rows(kv_cot, [kv_cot, landed.at[2 - distance]], length)

    key_inner = turn_back(kv_cot, k_raw, k_gain_ref, factors[:, 1:2], k_grad_ref)
    inners[...] = as_rows([query_inner, key_inner])
    sent = exchange(copies, inners, inners_in, i_send, i_recv, mates)
    raw_cots[2] = kv_cot[:, pl.ds(wide, wide)].astype(LOW)
    normed_copy.wait()
    weight_piece(1, raw_cots[2], piece1)
    for copy in sent:
        copies.arrived(copy)
    total = inners[...]
    for number in range(3):
        total = total + inners_in[number]
    totals = as_columns(total * (1.0 / width))

    def raw_cot(number, cot, raw, gain_ref):
        factor = factors[:, number : number + 1]
        shrink = (factor * factor * factor) * totals[:, number : number + 1]
        for head in range(heads):
            columns = pl.ds(head * HD, HD)
            raw_cots[number, :, columns] = (
                factor * gain_ref[0:1, columns] * cot[:, columns] - raw[:, columns] * shrink
            ).astype(LOW)

    raw_cot(0, query_cot, q_raw, q_gain_ref)
    raw_cot(1, kv_cot, k_raw, k_gain_ref)
    for copy in others:
        copy.wait()

    @pl.loop(0, width // 256)
    def _(index):
        columns = pl.ds(pl.multiple_of(index * 256, 256), 256)
        result = (
            dot_t(raw_cots[0], wq[columns, :]) + dot_t(raw_cots[1], wk[columns, :]) + dot_t(raw_cots[2], wv[columns, :])
        ).astype(LOW)
        for block in range(4):
            normed_part[block // 2, block % 2, :, columns] = result[block * rows : (block + 1) * rows]

    weight_piece(2, raw_cots[0], piece2)
    weight_piece(3, raw_cots[1], piece3)
    for step in order[2:]:
        scatter.climb(step)
    scatter.result(mix_ref)
    for distance in (1, 2):

        @pl.when(spot >= distance)
        def _():
            halo_copy(distance, group - distance).wait_send()

    for copy in saving.values():
        copy.wait()
    copies.finish()


def run_attention_back(rows_of, attention, sources, produced, normed, weights, chain, local, experts, number):
    depth = produced.shape[0]
    rows, width = rows_of[0].shape
    queries, kv_all = attention[0], attention[1]
    length, wide2 = kv_all.shape[1:]
    wide = wide2 // 2
    heads = wide // HD
    piece = jax.ShapeDtypeStruct((depth, 2, width // (2 * depth), wide), LOW)
    return pl.pallas_call(
        functools.partial(attention_back_kernel, depth, rows, heads, chain, local),
        out_shape=(
            jax.ShapeDtypeStruct((rows, width), FULL),
            jax.ShapeDtypeStruct((experts, width), FULL),
            jax.ShapeDtypeStruct((8, width), FULL),
            jax.ShapeDtypeStruct((8, wide), FULL),
            jax.ShapeDtypeStruct((8, wide), FULL),
            jax.ShapeDtypeStruct((rows, width), FULL),
            jax.ShapeDtypeStruct((2, 2, rows, width), LOW),
            piece, piece, piece, piece,
        ),
        in_specs=[VMEM] * 23 + [ANY] * 5,
        out_specs=(VMEM,) * 7 + (ANY,) * 4,
        scratch_shapes=[
            pltpu.VMEM((rows, width), LOW), pltpu.VMEM((2, 2, rows, width), LOW), pltpu.VMEM((128, rows), FULL),
            pltpu.VMEM((3 * length, length), LOW), pltpu.VMEM((length, wide), LOW),
            pltpu.VMEM((heads, 8, length), FULL), pltpu.VMEM((heads, HD, length), FULL),
            pltpu.VMEM((length, wide), FULL), pltpu.VMEM((length, wide2), FULL),
            pltpu.VMEM((2, length, wide2), LOW), pltpu.VMEM((2, length, wide2), LOW),
            pltpu.VMEM(produced.shape, LOW), pltpu.VMEM((3, length, wide), LOW), pltpu.VMEM((width, length), LOW),
            pltpu.VMEM((width, wide), LOW), pltpu.VMEM((width, wide), LOW), pltpu.VMEM((width, wide), LOW),
            pltpu.VMEM((8, length), FULL), pltpu.VMEM((3, 8, length), FULL), pltpu.VMEM((2,) + piece.shape[2:], LOW),
        ]
        + Scatter.scratch(depth, rows, width)
        + [dma(4), dma(3), dma(3), dma(3), dma(3), dma(3), dma(depth + 4), dma(2)],
        compiler_params=comm_params(number),
    )(*rows_of, *attention, *sources, produced, normed, *weights)


def dot(left, right):
    return jnp.dot(left, right, preferred_element_type=FULL)


def dot_t(left, right):
    return lax.dot_general(left, right, (((1,), (1,)), ((), ())), preferred_element_type=FULL)


def t_dot(left, right):
    return lax.dot_general(left, right, (((0,), (0,)), ((), ())), preferred_element_type=FULL)


class ExpertScatter:
    def __init__(self, copies, parts, work, from_x, from_z, load, send, recv):
        self.copies, self.parts, self.work, self.from_x, self.from_z = copies, parts, work, from_x, from_z
        self.load, self.send, self.recv = load, send, recv
        self.z, self.x, y, core = place()
        self.depth, self.rows = work.shape[1], work.shape[2]
        self.over_x = device(self.z, 1 - self.x, y, core)
        self.column = [device(swapped(self.z, step), self.x, y, core) for step in range(self.depth)]
        self.order = list(range(self.depth - 1, -1, -1))
        self.loads, self.sides, self.along = {}, {}, {}

    def begin(self, index):
        for step in self.order:
            at = swapped(self.z, step)
            self.sides[index, step] = self.copies.start(
                remote(
                    self.parts[index].at[at, 1 - self.x], self.from_x.at[index, step],
                    self.send.at[0, index, step], self.recv.at[0, index, step], self.over_x,
                )
            )
            load = pltpu.make_async_copy(self.parts[index].at[at, self.x], self.work.at[index, step], self.load.at[index, step])
            load.start()
            self.loads[index, step] = load

    def climb(self, index, step):
        self.loads[index, step].wait()
        self.copies.arrived(self.sides[index, step])
        mine = self.work.at[index, step]
        if step:
            add_rows(mine, [mine, self.from_x.at[index, step]], self.rows)
            self.along[index, step] = self.copies.start(
                remote(
                    mine, self.from_z.at[index, step],
                    self.send.at[1, index, step], self.recv.at[1, index, step], self.column[step],
                )
            )

    def result(self, index, target):
        terms = [self.work.at[index, 0], self.from_x.at[index, 0]]
        for step in range(1, self.depth):
            self.copies.arrived(self.along[index, step])
            terms.append(self.from_z.at[index, step])
        add_rows(target, terms, self.rows)


def gradients_kernel(
    depth, rows, local, hidden, matrices, *refs,
):
    parts, refs = refs[:matrices], refs[matrices:]
    (
        normed_part, tokens_ref, state_cot, scale_ref, gain_ref, out_ref, vector_ref,
        normed_ref, grad_ref, gated_ref, gate_grad_ref, up_grad_ref,
    ) = refs[:12]
    sums, refs = refs[12 : 12 + matrices], refs[12 + matrices :]
    (
        input_grads, outputs, vector_sum,
        gate_own, up_own, down_own, gate_other, up_other, down_other,
        work, from_x, from_z, partial, from_pair, from_y, normed_grad, low, vectors, vector_in, vector_mid, vector_turn,
        tiles, turned, acts, gated_turned, near, far, near_down, far_down,
        e_load, e_send, e_recv, t_send, t_recv, g_send, g_recv, o_send, o_recv, v_send, v_recv, u_send, u_recv,
        tile_load, act_load, save, pair_send, pair_recv, local_sem,
    ) = refs
    z, x, y, core = place()
    group = 2 * z + x
    sibling = device(z, x, y, 1 - core)
    groups = [(step, turn) for step in range(depth) for turn in range(2) if step or turn]
    peers = [device(swapped(z, step), swapped(x, turn), y, core) for step, turn in groups]
    mates = [(z, x, swapped(y, turn // 2), swapped(core, turn % 2)) for turn in range(1, 4)]
    greet(peers + [device(*mate) for mate in mates])
    copies = Copies()
    width = normed_ref.shape[1]
    tile = 512
    count = width // tile

    def fetch(source, target, sem):
        copy = pltpu.make_async_copy(source, target, sem)
        copy.start()
        return copy

    experts = ExpertScatter(copies, parts, work, from_x, from_z, e_load, e_send, e_recv)
    loaded = fetch(normed_part, partial, local_sem.at[0])
    experts.begin(0)
    loaded.wait()
    scatter = TensorScatter(copies, partial, from_pair, from_y, t_send, t_recv)
    scatter.begin()
    out_gather = TensorGather(copies, out_ref, outputs, o_send, o_recv)
    for index in range(1, matrices):
        experts.begin(index)
    act_copies = [fetch(gate_grad_ref, acts.at[0], act_load.at[0]), fetch(up_grad_ref, acts.at[1], act_load.at[1])]

    def fetch_tile(number):
        source = normed_ref if number < count else grad_ref
        columns = pl.ds((number % count) * tile, tile)
        return fetch(source.at[:, columns], tiles.at[number % 2], tile_load.at[number % 2])

    tile_copies = [fetch_tile(0)]
    saving = {}

    def first_unit(owner):
        return owner * local * hidden

    def gate_and_up(number):
        slot = number % 2
        tile_copies[number].wait()
        tile_copies.append(fetch_tile(number + 1))
        turned[...] = tiles[slot].T
        for copy, remote_one in saving.pop(slot, []):
            copies.sent(copy) if remote_one else copy.wait()
        for which in range(2):
            for owner, target in ((1 - core, far), (core, near)):

                @pl.loop(0, local)
                def _(expert):
                    columns = pl.ds(pl.multiple_of(first_unit(owner) + expert * hidden, hidden), hidden)
                    target[which, slot, expert] = dot(turned[...], acts[which, :, columns]).astype(target.dtype)

        saves = []
        place_of = pl.ds(number * tile, tile)
        for which, (own, other) in enumerate(((gate_own, gate_other), (up_own, up_other))):
            away = remote(
                far.at[which, slot], other.at[:, place_of], pair_send.at[which, number], pair_recv.at[which, number], sibling
            )
            copies.start(away)
            saves.append((away, True))
            saves.append((fetch(near.at[which, slot], own.at[:, place_of], save.at[which, slot]), False))
        saving[slot] = saves

    def down(number):
        slot = number % 2
        tile_copies[count + number].wait()
        if number + 1 < count:
            tile_copies.append(fetch_tile(count + number + 1))
        for copy, remote_one in saving.pop(("down", slot), []):
            copies.sent(copy) if remote_one else copy.wait()
        for owner, target in ((1 - core, far_down), (core, near_down)):

            @pl.loop(0, local)
            def _(expert):
                units = pl.ds(pl.multiple_of(first_unit(owner) + expert * hidden, hidden), hidden)
                target[slot, expert] = dot(gated_turned[units, :], tiles[slot]).astype(target.dtype)

        columns = pl.ds(number * tile, tile)
        away = remote(
            far_down.at[slot], down_other.at[:, :, columns], pair_send.at[2, number], pair_recv.at[2, number], sibling
        )
        copies.start(away)
        saving["down", slot] = [
            (away, True), (fetch(near_down.at[slot], down_own.at[:, :, columns], save.at[2, slot]), False)
        ]

    for copy in act_copies:
        copy.wait()
    gate_and_up(0)
    scatter.cross()
    experts.climb(0, experts.order[0])
    gate_and_up(1)
    out_gather.cross()
    experts.climb(0, experts.order[1])
    scatter.result(normed_grad)

    inputs = tokens_ref[...].astype(FULL)
    factor, gain = scale_ref[:, 0:1], gain_ref[0:1, :]
    normed = normed_grad[...]
    inner = jnp.sum(normed * gain * inputs, axis=-1, keepdims=True)
    low[...] = (
        state_cot[...] + factor * gain * normed - inputs * (factor * factor * factor) * inner * (1.0 / width)
    ).astype(LOW)
    gain_grad = jnp.sum(normed * inputs * factor, axis=0, keepdims=True)
    grad_gather = TensorGather(copies, low, input_grads, g_send, g_recv)
    vectors[...] = vector_ref[...]
    slice_width = vectors.shape[2]
    for index in range(vectors.shape[0]):
        vectors[index, 16:17, :] = gain_grad[:, index * slice_width : (index + 1) * slice_width]
    vector_copies = []
    for number, ((step, turn), peer) in enumerate(zip(groups, peers)):
        to = 2 * swapped(z, step) + swapped(x, turn)
        vector_copies.append(
            copies.start(remote(vectors.at[to], vector_in.at[number], v_send.at[number], v_recv.at[number], peer))
        )

    for step in experts.order[2:]:
        experts.climb(0, step)
    gate_and_up(2)
    for step in experts.order[:2]:
        experts.climb(1, step)
    grad_gather.cross()
    gate_and_up(3)
    for copy in vector_copies:
        copies.arrived(copy)
    total = vectors[group]
    for number in range(len(peers)):
        total = total + vector_in[number]
    vector_mid[...] = total
    turn_copies = [
        copies.start(remote(vector_mid, vector_turn.at[number], u_send.at[number], u_recv.at[number], device(*mate)))
        for number, mate in enumerate(mates)
    ]
    for step in experts.order[2:]:
        experts.climb(1, step)
    gated_copy = fetch(gated_ref, acts.at[0], act_load.at[0])
    gated_copy.wait()
    for index in range(2):
        half = pl.ds(index * local * hidden, local * hidden)
        gated_turned[half, :] = acts[0, :, half].T
    experts.result(0, sums[0])
    down(0)
    experts.climb(2, experts.order[0])
    down(1)
    for step in experts.order[1:]:
        experts.climb(2, step)
    down(2)
    experts.result(1, sums[1])
    down(3)
    for copy in turn_copies:
        copies.arrived(copy)
    total = vector_mid[...]
    for number in range(len(mates)):
        total = total + vector_turn[number]
    keep = lax.broadcasted_iota(jnp.int32, total.shape, 0) < 18
    vector_sum[...] = jnp.where(keep, total, vector_mid[...])
    for index in range(3, matrices):
        for step in experts.order:
            experts.climb(index, step)
    for index in range(2, matrices):
        experts.result(index, sums[index])
    out_gather.finish()
    grad_gather.finish()
    for entries in saving.values():
        for copy, remote_one in entries:
            if not remote_one:
                copy.wait()
    copies.finish()


def run_gradients(parts, normed_part, tokens, state_cot, scale, gain, out, vectors, normed, grads, gated, gate_grad, up_grad, local, number):
    matrices = len(parts)
    depth, _, piece, columns = parts[0].shape
    rows, width = tokens.shape
    seen, units = gated.shape
    hidden = units // (2 * local)
    tile = 512
    sum_of = jax.ShapeDtypeStruct((piece, columns), FULL)
    spread = jax.ShapeDtypeStruct((2, 2, rows, width), LOW)
    wide, tall = (local, width, hidden), (local, hidden, width)
    results = pl.pallas_call(
        functools.partial(gradients_kernel, depth, rows, local, hidden, matrices),
        out_shape=(sum_of,) * matrices
        + (
            spread, spread, jax.ShapeDtypeStruct(vectors.shape[1:], FULL),
            jax.ShapeDtypeStruct(wide, FULL), jax.ShapeDtypeStruct(wide, FULL), jax.ShapeDtypeStruct(tall, FULL),
            jax.ShapeDtypeStruct(wide, LOW), jax.ShapeDtypeStruct(wide, LOW), jax.ShapeDtypeStruct(tall, LOW),
        ),
        in_specs=[ANY] * (matrices + 1) + [VMEM] * 6 + [ANY] * 5,
        out_specs=(VMEM,) * (matrices + 3) + (ANY,) * 6,
        scratch_shapes=[pltpu.VMEM((matrices, depth, piece, columns), LOW)] * 3
        + TensorScatter.scratch(rows, width)[:3]
        + [
            pltpu.VMEM((rows, width), FULL), pltpu.VMEM((rows, width), LOW),
            pltpu.VMEM(vectors.shape, FULL), pltpu.VMEM((2 * depth - 1,) + vectors.shape[1:], FULL),
            pltpu.VMEM(vectors.shape[1:], FULL), pltpu.VMEM((3,) + vectors.shape[1:], FULL),
            pltpu.VMEM((2, seen, tile), LOW), pltpu.VMEM((tile, seen), LOW),
            pltpu.VMEM((2, seen, units), LOW), pltpu.VMEM((units, seen), LOW),
            pltpu.VMEM((2, 2, local, tile, hidden), FULL), pltpu.VMEM((2, 2, local, tile, hidden), LOW),
            pltpu.VMEM((2, local, hidden, tile), FULL), pltpu.VMEM((2, local, hidden, tile), LOW),
            dma(matrices, depth), dma(2, matrices, depth), dma(2, matrices, depth),
            dma(3), dma(3), dma(4), dma(3), dma(4), dma(3),
            dma(2 * depth - 1), dma(2 * depth - 1), dma(3), dma(3),
            dma(2), dma(2), dma(3, 2), dma(3, width // tile), dma(3, width // tile), dma(1),
        ],
        compiler_params=comm_params(number),
    )(*parts, normed_part, tokens, state_cot, scale, gain, out, vectors, normed, grads, gated, gate_grad, up_grad)
    return results[:matrices], results[matrices:]


def body(
    groups, parts,
    tokens, documents, routes, norm1_gain, q_gain, k_gain, w_query, w_key, w_value, w_out, norm2_gain, router_w,
    w_gate, w_up, w_down, out_grad,
):
    row_count, width = tokens.shape
    local_experts, _, hidden = w_gate.shape
    experts = local_experts * groups
    chain = LENGTH // row_count
    if not (parts == 4 and groups % 2 == 0 and experts <= min(16, 2 * TOP) and 2 * w_query.shape[1] <= 14 * HD and chain == 4 and 4 * row_count == LENGTH and WINDOW == 2 * row_count):
        return body_routed(
            tokens, documents, routes, norm1_gain, q_gain, k_gain, w_query, w_key, w_value, w_out, norm2_gain, router_w,
            w_gate, w_up, w_down, out_grad,
        )
    depth = groups // 2
    rows = row_count // parts
    seen = groups * row_count // 2
    heads = w_query.shape[1] // HD
    group, part = lax.axis_index("expert"), lax.axis_index("tensor")
    core = part % 2

    def quarter(array):
        return lax.dynamic_slice_in_dim(array, part * rows, rows, 0)

    def across(vector):
        return vector.reshape(1, -1)

    positions = group * row_count + jnp.arange(row_count, dtype=jnp.int32)
    cosine, sine = (table[:, 0, :] for table in rope_tables(positions % LENGTH))
    sine = jnp.concatenate([-sine[:, : HD // 2], sine[:, HD // 2 :]], axis=1)
    docs = jnp.broadcast_to(documents[None, :], (8, row_count))
    picked = jnp.any(quarter(routes)[:, :, None] == jnp.arange(128, dtype=jnp.int32)[None, None, :], axis=1).astype(FULL)
    router_wide = jnp.pad(router_w, ((0, 0), (0, 128 - experts)))
    own_grad = quarter(out_grad)
    query_gain, key_gain = across(q_gain), across(k_gain)
    (
        normed_one, query_raw, key_raw, queries, kv_all, key_docs, scales, attended, logs, state, normed_two, router_probs, gates,
        all_grad,
    ) = run_attention(
        tokens, (w_query, w_key, w_value, w_out), own_grad, (across(norm1_gain), query_gain, key_gain), (cosine, sine), docs,
        across(norm2_gain), router_wide, picked, depth, chain, local_experts, 3,
    )

    normed_two_grad, gate_cots, all_normed, gated, gate_pre_grad, up_pre_grad, produced = run_experts(
        normed_two, gates, all_grad, w_gate, w_up, w_down, 5
    )
    units = 2 * local_experts * hidden
    all_normed, all_grad = all_normed.reshape(seen, width), all_grad.reshape(seen, width)
    gated, gate_pre_grad, up_pre_grad = (a.reshape(seen, units) for a in (gated, gate_pre_grad, up_pre_grad))

    (
        state_cot, router_grad, norm2_grad, q_gain_local, k_gain_local, expert_mix, normed_part, *pieces
    ) = run_attention_back(
        (normed_two_grad, gate_cots, router_probs, picked, state, across(norm2_gain), router_wide, normed_two, own_grad),
        (queries, kv_all, attended, logs, key_docs, docs, query_raw, key_raw, query_gain, key_gain, cosine, sine, scales),
        (w_out,), produced, normed_one, (w_query, w_key, w_value), chain, local_experts, experts, 10,
    )
    own_inputs = quarter(tokens).astype(FULL)
    own_scale = lax.rsqrt(jnp.mean(own_inputs * own_inputs, axis=-1, keepdims=True) + NORM_EPSILON)

    vectors = jnp.concatenate(
        [router_grad, jnp.zeros((17 - experts, width), FULL), norm2_grad[:1]], axis=0
    ).reshape(18, groups, width // groups).transpose(1, 0, 2)
    gains = jnp.concatenate([q_gain_local[0].reshape(heads, HD), k_gain_local[0].reshape(heads, HD)], axis=0)
    gains = jnp.pad(gains, ((0, 14 - 2 * heads), (0, width // groups - HD)))
    vectors = jnp.concatenate([vectors, jnp.broadcast_to(gains[None], (groups,) + gains.shape)], axis=1)
    sums, (input_grad, output, vector_sum, gate_own, up_own, down_own, gate_other, up_other, down_other) = run_gradients(
        pieces, normed_part, quarter(tokens), state_cot, own_scale,
        norm1_gain[None], (state + expert_mix).astype(LOW), vectors, all_normed, all_grad, gated, gate_pre_grad, up_pre_grad,
        local_experts, 14,
    )
    own_columns = group * (HD // groups)
    return (
        output.reshape(row_count, width),
        input_grad.reshape(row_count, width).astype(FULL),
        vector_sum[16],
        lax.dynamic_slice(vector_sum, (18, own_columns), (heads, HD // groups)),
        lax.dynamic_slice(vector_sum, (18 + heads, own_columns), (heads, HD // groups)),
        sums[2],
        sums[3],
        sums[1],
        sums[0].T,
        vector_sum[17],
        vector_sum[:experts].T,
        gate_own + gate_other.astype(FULL),
        up_own + up_other.astype(FULL),
        down_own + down_other.astype(FULL),
    )


def solution(mesh):
    placed = (
        P("expert", None),
        P("expert"),
        P("expert", None),
        P(),
        P("tensor", None),
        P("tensor", None),
        P(None, "tensor"),
        P(None, "tensor"),
        P(None, "tensor"),
        P("tensor", None),
        P(),
        P(),
        P("expert", None, "tensor"),
        P("expert", None, "tensor"),
        P("expert", "tensor", None),
        P("expert", None),
    )
    return jax.shard_map(
        functools.partial(body, mesh.shape["expert"], mesh.shape["tensor"]),
        mesh=mesh,
        in_specs=placed,
        out_specs=(
            P("expert", None),
            P("expert", None),
            P("expert"),
            P("tensor", "expert"),
            P("tensor", "expert"),
            P("expert", "tensor"),
            P("expert", "tensor"),
            P("expert", "tensor"),
            P("tensor", "expert"),
            P("expert"),
            P("expert", None),
            P("expert", None, "tensor"),
            P("expert", None, "tensor"),
            P("expert", "tensor", None),
        ),
        check_vma=False,
    )
```

```python
import functools

import jax
import jax.numpy as jnp
from jax import lax
from jax.experimental import pallas as pl
from jax.experimental.pallas import tpu as pltpu
from jax.sharding import PartitionSpec as P

HD = 128
TOP = 8
WINDOW = 1024
LENGTH = 2048


NORM_EPSILON = 1e-05
HIGHEST_PRECISION = lax.Precision.HIGHEST


def for_sending(value):
    return jax.tree.map(lambda a: a.astype(jnp.bfloat16) if a.dtype == jnp.float32 else a, value)


def shifted(value, axis, steps):
    count = lax.axis_size(axis)
    initial, last = (max(0, -steps), min(count, count - steps))
    return lax.ppermute(value, axis, [(source, source + steps) for source in range(initial, last)])


def rope_tables(positions):
    half_width = HD // 2
    frequency = 10000.0 ** (-jnp.arange(half_width, dtype=jnp.float32) * 2.0 / HD)
    angles = positions.astype(jnp.float32)[:, None] * frequency[None, :]
    angles = jnp.concatenate([angles, angles], axis=-1)
    return (jnp.cos(angles)[:, None, :], jnp.sin(angles)[:, None, :])


def rotate(values, cosine, sine):
    half_width = values.shape[-1] // 2
    turned = jnp.concatenate([-values[..., half_width:], values[..., :half_width]], axis=-1)
    return values * cosine + turned * sine


def rotate_back(grads, cosine, sine):
    half_width = grads.shape[-1] // 2
    scaled = grads * sine
    turned = jnp.concatenate([scaled[..., half_width:], -scaled[..., :half_width]], axis=-1)
    return grads * cosine + turned


def previous_block(pieces):
    return jax.tree.map(
        lambda part, own: part.astype(own.dtype), shifted(for_sending(pieces), "expert", 1), pieces
    )


def following_block(pieces):
    return shifted((for_sending(pieces[0]), for_sending(pieces[1])), "expert", -1)


def body_routed(
    tokens,
    documents,
    routes,
    norm1_gain,
    q_gain,
    k_gain,
    w_query,
    w_key,
    w_value,
    w_out,
    norm2_gain,
    router_w,
    w_gate,
    w_up,
    w_down,
    out_grad,
):
    row_count, model_width = tokens.shape
    groups = lax.axis_size("expert")
    local_experts = w_gate.shape[0]
    experts = local_experts * groups
    capacity = 2 * row_count * TOP // experts
    slots_group = local_experts * capacity
    heads = w_query.shape[1] // HD
    score_scale = HD ** (-0.5)
    first_row = lax.axis_index("expert") * row_count
    positions = first_row + jnp.arange(row_count, dtype=jnp.int32)
    cosine, sine = rope_tables(positions % LENGTH)
    inputs = tokens.astype(jnp.float32)
    scale_one = lax.rsqrt(jnp.mean(inputs * inputs, axis=-1, keepdims=True) + NORM_EPSILON)
    normed_one = (inputs * scale_one * norm1_gain).astype(jnp.bfloat16)
    query_raw = jnp.dot(normed_one, w_query, preferred_element_type=jnp.float32)
    key_raw = jnp.dot(normed_one, w_key, preferred_element_type=jnp.float32)
    values = jnp.dot(normed_one, w_value, preferred_element_type=jnp.float32).astype(jnp.bfloat16)
    query_square, key_square = lax.psum(
        (jnp.sum(query_raw * query_raw, axis=-1), jnp.sum(key_raw * key_raw, axis=-1)), "tensor"
    )
    query_scale = lax.rsqrt(query_square / model_width + NORM_EPSILON)[:, None]
    key_scale = lax.rsqrt(key_square / model_width + NORM_EPSILON)[:, None]
    query_gain = q_gain.reshape(-1)
    key_gain = k_gain.reshape(-1)
    queries = rotate(
        (query_raw * query_scale * query_gain).reshape(row_count, heads, HD), cosine, sine
    ).astype(jnp.bfloat16)
    key_heads = rotate(
        (key_raw * key_scale * key_gain).reshape(row_count, heads, HD), cosine, sine
    ).astype(jnp.bfloat16)
    value_heads = values.reshape(row_count, heads, HD)
    labels = jnp.stack([documents // 256, documents % 256]).astype(jnp.bfloat16)
    previous_one = previous_block((key_heads, value_heads, labels))
    previous_two = previous_block(previous_one)
    all_keys = jnp.concatenate([previous_two[0], previous_one[0], key_heads], axis=0)
    all_values = jnp.concatenate([previous_two[1], previous_one[1], value_heads], axis=0)
    all_labels = jnp.concatenate([previous_two[2], previous_one[2], labels], axis=1)
    key_pos = first_row - 2 * row_count + jnp.arange(3 * row_count, dtype=jnp.int32)
    same_doc = (all_labels[0][None, :] == labels[0][:, None]) & (
        all_labels[1][None, :] == labels[1][:, None]
    )
    allowed = (
        same_doc
        & (key_pos[None, :] <= positions[:, None])
        & (positions[:, None] - key_pos[None, :] < WINDOW)
        & (key_pos[None, :] >= 0)
    )

    def masked_scores():
        raw_scores = (
            jnp.einsum("qhd,khd->hqk", queries, all_keys, preferred_element_type=jnp.float32)
            * score_scale
        )
        return jnp.where(allowed[None], raw_scores, -1e30)

    scores = masked_scores()
    highest = jnp.max(scores, axis=-1, keepdims=True)
    weights = jnp.where(allowed[None], jnp.exp(scores - highest), 0.0)
    denominator = jnp.sum(weights, axis=-1, keepdims=True)
    log_total = highest + jnp.log(denominator)
    attn_probs = weights / denominator
    attended = jnp.einsum(
        "hqk,khd->qhd",
        attn_probs.astype(jnp.bfloat16),
        all_values,
        preferred_element_type=jnp.float32,
    )
    attended = attended.reshape(row_count, -1).astype(jnp.bfloat16)
    attention = lax.psum(jnp.dot(attended, w_out, preferred_element_type=jnp.float32), "tensor")
    state = inputs + attention
    scale_two = lax.rsqrt(jnp.mean(state * state, axis=-1, keepdims=True) + NORM_EPSILON)
    normed_two = (state * scale_two * norm2_gain).astype(jnp.bfloat16)
    router_probs = jax.nn.softmax(
        jnp.dot(normed_two, router_w, preferred_element_type=jnp.float32), axis=-1
    )
    chosen = (routes[:, :, None] == jnp.arange(experts, dtype=jnp.int32)[None, None, :]).astype(
        jnp.float32
    )
    gates = jnp.sum(chosen * router_probs[:, None, :], axis=-1)
    flat_routes = routes.reshape(-1)
    onehot = (flat_routes[:, None] == jnp.arange(experts, dtype=jnp.int32)[None, :]).astype(
        jnp.int32
    )
    slot_index = jnp.sum(jnp.cumsum(onehot, axis=0) * onehot, axis=1) - 1
    target = flat_routes * capacity + slot_index
    source = (
        jnp.full((experts * capacity,), -1, jnp.int32)
        .at[target]
        .set(jnp.arange(row_count * TOP, dtype=jnp.int32))
    )
    live_slot = source >= 0
    pick_index = jnp.maximum(source, 0)
    send_rows = jnp.where(
        live_slot[:, None], normed_two[pick_index // TOP], jnp.zeros((), jnp.bfloat16)
    ).reshape(groups, slots_group, model_width)
    grad_float = out_grad.astype(jnp.float32)
    pick_grads = (
        (gates[:, :, None] * grad_float[:, None, :])
        .astype(jnp.bfloat16)
        .reshape(row_count * TOP, model_width)
    )
    send_grads = jnp.where(
        live_slot[:, None], pick_grads[pick_index], jnp.zeros((), jnp.bfloat16)
    ).reshape(groups, slots_group, model_width)
    arrived = lax.all_to_all(send_rows, "expert", split_axis=0, concat_axis=0, tiled=True)
    stacked = arrived.reshape(groups, local_experts, capacity, model_width)
    gate_pre = jnp.einsum("secd,edf->secf", stacked, w_gate, preferred_element_type=jnp.float32)
    up_pre = jnp.einsum("secd,edf->secf", stacked, w_up, preferred_element_type=jnp.float32)
    activated = jax.nn.silu(gate_pre)
    inner_act = (activated * up_pre).astype(jnp.bfloat16)
    produced = jnp.einsum(
        "secf,efd->secd", inner_act, w_down, preferred_element_type=jnp.float32
    ).astype(jnp.bfloat16)
    returned = lax.all_to_all(
        produced.reshape(groups, slots_group, model_width),
        "expert",
        split_axis=0,
        concat_axis=0,
        tiled=True,
    )
    back_rows = (
        returned.reshape(experts * capacity, model_width)[target]
        .reshape(row_count, TOP, model_width)
        .astype(jnp.float32)
    )
    expert_part = jnp.sum(gates[:, :, None] * back_rows, axis=1)
    expert_mix = lax.psum(expert_part.astype(jnp.bfloat16), "tensor").astype(jnp.float32)
    output = (state + expert_mix).astype(jnp.bfloat16)
    gate_part = jnp.sum(grad_float[:, None, :] * back_rows, axis=-1)
    arrived_grad = lax.all_to_all(send_grads, "expert", split_axis=0, concat_axis=0, tiled=True)
    slot_grad = arrived_grad.reshape(groups, local_experts, capacity, model_width)
    w_down_grad = jnp.einsum(
        "secf,secd->efd", inner_act, slot_grad, preferred_element_type=jnp.float32
    )
    inner_grad = jnp.einsum("secd,efd->secf", slot_grad, w_down, preferred_element_type=jnp.float32)
    logistic = jax.nn.sigmoid(gate_pre)
    gate_pre_grad = (inner_grad * up_pre * logistic * (1.0 + gate_pre * (1.0 - logistic))).astype(
        jnp.bfloat16
    )
    up_pre_grad = (inner_grad * activated).astype(jnp.bfloat16)
    w_gate_grad = jnp.einsum(
        "secd,secf->edf", stacked, gate_pre_grad, preferred_element_type=jnp.float32
    )
    w_up_grad = jnp.einsum(
        "secd,secf->edf", stacked, up_pre_grad, preferred_element_type=jnp.float32
    )
    row_grad = jnp.einsum(
        "secf,edf->secd", gate_pre_grad, w_gate, preferred_element_type=jnp.float32
    )
    row_grad = (
        row_grad
        + jnp.einsum("secf,edf->secd", up_pre_grad, w_up, preferred_element_type=jnp.float32)
    ).astype(jnp.bfloat16)
    grad_back = lax.all_to_all(
        row_grad.reshape(groups, slots_group, model_width),
        "expert",
        split_axis=0,
        concat_axis=0,
        tiled=True,
    )
    grad_picks = (
        grad_back.reshape(experts * capacity, model_width)[target]
        .reshape(row_count, TOP, model_width)
        .astype(jnp.float32)
    )
    normed_part = jnp.sum(grad_picks, axis=1)
    normed_two_grad, gate_cot = lax.psum((normed_part, gate_part), "tensor")
    prob_cot = jnp.sum(gate_cot[:, :, None] * chosen, axis=1)
    logit_cot = router_probs * (prob_cot - jnp.sum(router_probs * prob_cot, axis=-1, keepdims=True))
    router_float = router_w.astype(jnp.float32)
    normed_two_grad = normed_two_grad + jnp.einsum(
        "te,de->td", logit_cot, router_float, precision=HIGHEST_PRECISION
    )
    router_grad = jnp.einsum(
        "td,te->de", normed_two.astype(jnp.float32), logit_cot, precision=HIGHEST_PRECISION
    )
    norm2_grad = jnp.sum(normed_two_grad * state * scale_two, axis=0)
    inner_two = jnp.sum(normed_two_grad * norm2_gain * state, axis=-1, keepdims=True)
    state_cot = (
        grad_float
        + scale_two * norm2_gain * normed_two_grad
        - state * scale_two**3 * inner_two / model_width
    )
    state_low = state_cot.astype(jnp.bfloat16)
    w_out_grad = jnp.einsum("tf,td->fd", attended, state_low, preferred_element_type=jnp.float32)
    attended_cot = (
        jnp.einsum("td,fd->tf", state_low, w_out, preferred_element_type=jnp.float32)
        .astype(jnp.bfloat16)
        .reshape(row_count, heads, HD)
    )
    scores = masked_scores()
    attn_probs = jnp.where(allowed[None], jnp.exp(scores - log_total), 0.0)
    value_cot_all = jnp.einsum(
        "hqk,qhd->khd",
        attn_probs.astype(jnp.bfloat16),
        attended_cot,
        preferred_element_type=jnp.float32,
    )
    prob_grad = jnp.einsum(
        "qhd,khd->hqk", attended_cot, all_values, preferred_element_type=jnp.float32
    )
    delta = jnp.sum(attn_probs * prob_grad, axis=-1, keepdims=True)
    score_cot = (attn_probs * (prob_grad - delta)).astype(jnp.bfloat16)
    query_cot = (
        jnp.einsum("hqk,khd->qhd", score_cot, all_keys, preferred_element_type=jnp.float32)
        * score_scale
    )
    key_cot_all = (
        jnp.einsum("hqk,qhd->khd", score_cot, queries, preferred_element_type=jnp.float32)
        * score_scale
    )
    carried = following_block((key_cot_all[:row_count], value_cot_all[:row_count]))
    carried = following_block(
        (
            key_cot_all[row_count : 2 * row_count] + carried[0],
            value_cot_all[row_count : 2 * row_count] + carried[1],
        )
    )
    key_cot = key_cot_all[2 * row_count :] + carried[0]
    value_cot = value_cot_all[2 * row_count :] + carried[1]
    query_norm_cot = rotate_back(query_cot, cosine, sine).reshape(row_count, -1)
    key_norm_cot = rotate_back(key_cot, cosine, sine).reshape(row_count, -1)
    q_gain_local = jnp.sum(query_norm_cot * query_raw * query_scale, axis=0).reshape(heads, HD)
    k_gain_local = jnp.sum(key_norm_cot * key_raw * key_scale, axis=0).reshape(heads, HD)
    query_inner, key_inner = lax.psum(
        (
            jnp.sum(query_norm_cot * query_gain * query_raw, axis=-1),
            jnp.sum(key_norm_cot * key_gain * key_raw, axis=-1),
        ),
        "tensor",
    )
    query_raw_cot = (
        query_scale * query_gain * query_norm_cot
        - query_raw * query_scale**3 * query_inner[:, None] / model_width
    ).astype(jnp.bfloat16)
    key_raw_cot = (
        key_scale * key_gain * key_norm_cot
        - key_raw * key_scale**3 * key_inner[:, None] / model_width
    ).astype(jnp.bfloat16)
    value_low = value_cot.reshape(row_count, -1).astype(jnp.bfloat16)
    w_query_local = jnp.einsum(
        "td,tf->df", normed_one, query_raw_cot, preferred_element_type=jnp.float32
    )
    w_key_local = jnp.einsum(
        "td,tf->df", normed_one, key_raw_cot, preferred_element_type=jnp.float32
    )
    w_value_local = jnp.einsum(
        "td,tf->df", normed_one, value_low, preferred_element_type=jnp.float32
    )
    normed_part_one = jnp.einsum(
        "tf,df->td", query_raw_cot, w_query, preferred_element_type=jnp.float32
    )
    normed_part_one = normed_part_one + jnp.einsum(
        "tf,df->td", key_raw_cot, w_key, preferred_element_type=jnp.float32
    )
    normed_part_one = normed_part_one + jnp.einsum(
        "tf,df->td", value_low, w_value, preferred_element_type=jnp.float32
    )
    normed_one_grad = lax.psum(normed_part_one.astype(jnp.bfloat16), "tensor").astype(jnp.float32)
    norm1_grad = jnp.sum(normed_one_grad * inputs * scale_one, axis=0)
    inner_one = jnp.sum(normed_one_grad * norm1_gain * inputs, axis=-1, keepdims=True)
    input_grad = (
        state_cot
        + scale_one * norm1_gain * normed_one_grad
        - inputs * scale_one**3 * inner_one / model_width
    )
    summed = (
        lax.psum_scatter(
            w_query_local.astype(jnp.bfloat16), "expert", scatter_dimension=0, tiled=True
        ).astype(jnp.float32),
        lax.psum_scatter(
            w_key_local.astype(jnp.bfloat16), "expert", scatter_dimension=0, tiled=True
        ).astype(jnp.float32),
        lax.psum_scatter(
            w_value_local.astype(jnp.bfloat16), "expert", scatter_dimension=0, tiled=True
        ).astype(jnp.float32),
        lax.psum_scatter(
            w_out_grad.astype(jnp.bfloat16), "expert", scatter_dimension=1, tiled=True
        ).astype(jnp.float32),
        lax.psum_scatter(
            router_grad.astype(jnp.bfloat16), "expert", scatter_dimension=0, tiled=True
        ).astype(jnp.float32),
        lax.psum_scatter(
            norm1_grad.astype(jnp.bfloat16), "expert", scatter_dimension=0, tiled=True
        ).astype(jnp.float32),
        lax.psum_scatter(
            norm2_grad.astype(jnp.bfloat16), "expert", scatter_dimension=0, tiled=True
        ).astype(jnp.float32),
        lax.psum_scatter(
            q_gain_local.astype(jnp.bfloat16), "expert", scatter_dimension=1, tiled=True
        ).astype(jnp.float32),
        lax.psum_scatter(
            k_gain_local.astype(jnp.bfloat16), "expert", scatter_dimension=1, tiled=True
        ).astype(jnp.float32),
    )
    return (
        output,
        input_grad,
        summed[5],
        summed[7],
        summed[8],
        summed[0],
        summed[1],
        summed[2],
        summed[3],
        summed[6],
        summed[4],
        w_gate_grad,
        w_up_grad,
        w_down_grad,
    )


MESH = pl.DeviceIdType.MESH
ANY = pl.BlockSpec(memory_space=pl.ANY)
VMEM = pl.BlockSpec(memory_space=pltpu.VMEM)
VMEM_BYTES = 60 * 1024 * 1024
LOW = jnp.bfloat16
FULL = jnp.float32


def place():
    group, part = lax.axis_index("expert"), lax.axis_index("tensor")
    return group // 2, group % 2, part // 2, part % 2


def device(z, x, y, core):
    return (2 * z + x, 2 * y + core)


def swapped(index, step):
    result, bit = index, 1
    while bit <= step:
        if step & bit:
            result = result + bit - 2 * bit * ((index // bit) % 2)
        bit *= 2
    return result


def greet(partners):
    barrier = pltpu.get_barrier_semaphore()
    for partner in partners:
        pl.semaphore_signal(barrier, inc=1, device_id=partner, device_id_type=MESH)
    pl.semaphore_wait(barrier, len(partners))


def remote(source, target, send, arrive, to):
    return pltpu.make_async_remote_copy(
        src_ref=source, dst_ref=target, send_sem=send, recv_sem=arrive, device_id=to, device_id_type=MESH
    )


def dma(*shape):
    return pltpu.SemaphoreType.DMA(shape)


def comm_params(number):
    return pltpu.CompilerParams(collective_id=number, has_side_effects=True, vmem_limit_bytes=VMEM_BYTES)


def add_rows(target, sources, rows, step=16):
    @pl.loop(0, rows // step)
    def _(index):
        part = pl.ds(index * step, step)
        total = sources[0][part].astype(FULL)
        for source in sources[1:]:
            total = total + source[part].astype(FULL)
        target[part] = total.astype(target.dtype)


class Copies:
    def __init__(self):
        self.open = []

    def start(self, copy):
        copy.start()
        self.open.append((copy, set()))
        return copy

    def mark(self, copy, what):
        for entry, done in self.open:
            if entry is copy:
                done.add(what)

    def arrived(self, copy):
        copy.wait_recv()
        self.mark(copy, "arrived")

    def sent(self, copy):
        copy.wait_send()
        self.mark(copy, "sent")

    def finish(self):
        for copy, done in self.open:
            if "sent" not in done:
                copy.wait_send()
            if "arrived" not in done:
                copy.wait_recv()


class Gather:
    def __init__(self, copies, block, target, rows, z_send, z_recv, p_send, p_recv):
        self.copies, self.block, self.target, self.rows = copies, block, target, rows
        self.z_send, self.z_recv, self.p_send, self.p_recv = z_send, z_recv, p_send, p_recv
        z, x, y, core = place()
        self.over_x, self.over_y = device(z, 1 - x, y, core), device(z, x, 1 - y, core)
        self.here, self.x_place, self.y_place = 2 * x + y, 2 * (1 - x) + y, 2 * x + 1 - y
        self.column = [device(swapped(z, step), x, y, core) for step in range(target.shape[0])]
        self.along, self.planes, self.diagonals = {}, {}, {}

    def at(self, step, spot, part):
        half = self.rows // 2
        if part is None:
            return self.target.at[step, pl.ds(pl.multiple_of(spot * self.rows, self.rows), self.rows)]
        return self.target.at[step, pl.ds(pl.multiple_of(spot * self.rows + part * half, half), half)]

    def begin(self):
        self.spread(0)
        for step in range(1, len(self.column)):
            self.lift(step)

    def lift(self, step):
        if 0 < step < len(self.column):
            self.along[step] = self.copies.start(
                remote(self.block, self.at(step, self.here, None), self.z_send.at[step], self.z_recv.at[step], self.column[step])
            )

    def spread(self, step):
        if step:
            self.copies.arrived(self.along[step])
        half = self.rows // 2
        planes = []
        for number, (to, part) in enumerate([(self.over_x, 0), (self.over_y, 1), (self.over_x, 1), (self.over_y, 0)]):
            here = self.at(step, self.here, part)
            source = here if step else self.block.at[pl.ds(part * half, half)]
            planes.append(self.copies.start(remote(source, here, self.p_send.at[step, number], self.p_recv.at[step, number], to)))
        self.planes[step] = planes

    def turn(self, step):
        self.copies.arrived(self.planes[step][0])
        passed = self.at(step, self.x_place, 0)
        first = self.copies.start(remote(passed, passed, self.p_send.at[step, 4], self.p_recv.at[step, 4], self.over_y))
        self.copies.arrived(self.planes[step][1])
        passed = self.at(step, self.y_place, 1)
        second = self.copies.start(remote(passed, passed, self.p_send.at[step, 5], self.p_recv.at[step, 5], self.over_x))
        self.diagonals[step] = (first, second)

    def complete(self, step):
        for copy in self.planes[step][2:] + list(self.diagonals[step]):
            self.copies.arrived(copy)


class Scatter:
    def __init__(self, copies, work, diagonal, from_x, from_y, from_z, rows, send, recv):
        self.copies, self.work, self.rows, self.send, self.recv = copies, work, rows, send, recv
        self.diagonal, self.from_x, self.from_y, self.from_z = diagonal, from_x, from_y, from_z
        z, x, y, core = place()
        self.over_x, self.over_y = device(z, 1 - x, y, core), device(z, x, 1 - y, core)
        self.here, self.x_place, self.y_place = 2 * x + y, 2 * (1 - x) + y, 2 * x + 1 - y
        self.far = 2 * (1 - x) + 1 - y
        self.column = [device(swapped(z, step), x, y, core) for step in range(work.shape[0])]
        self.corners, self.sides, self.along = {}, {}, {}

    def at(self, step, spot, part=None):
        half = self.rows // 2
        if part is None:
            return self.work.at[step, pl.ds(pl.multiple_of(spot * self.rows, self.rows), self.rows)]
        return self.work.at[step, pl.ds(pl.multiple_of(spot * self.rows + part * half, half), half)]

    def copy(self, step, number, source, target, to):
        return self.copies.start(remote(source, target, self.send.at[step, number], self.recv.at[step, number], to))

    def corner(self, step):
        self.corners[step] = (
            self.copy(step, 0, self.at(step, self.far, 0), self.diagonal.at[step, 0], self.over_y),
            self.copy(step, 1, self.at(step, self.far, 1), self.diagonal.at[step, 1], self.over_x),
        )

    def side(self, step):
        via_y, via_x = self.corners[step]
        self.copies.arrived(via_y)
        add_rows(self.at(step, self.x_place, 0), [self.at(step, self.x_place, 0), self.diagonal.at[step, 0]], self.rows // 2)
        to_x = self.copy(step, 2, self.at(step, self.x_place), self.from_x.at[step], self.over_x)
        self.copies.arrived(via_x)
        add_rows(self.at(step, self.y_place, 1), [self.at(step, self.y_place, 1), self.diagonal.at[step, 1]], self.rows // 2)
        to_y = self.copy(step, 3, self.at(step, self.y_place), self.from_y.at[step], self.over_y)
        self.sides[step] = (to_x, to_y)

    def climb(self, step):
        for copy in self.sides[step]:
            self.copies.arrived(copy)
        if step:
            here = self.at(step, self.here)
            add_rows(here, [here, self.from_x.at[step], self.from_y.at[step]], self.rows)
            self.along[step] = self.copy(step, 4, here, self.from_z.at[step], self.column[step])

    def result(self, target):
        for copy in self.along.values():
            self.copies.arrived(copy)
        terms = [self.at(0, self.here), self.from_x.at[0], self.from_y.at[0]]
        add_rows(target, terms + [self.from_z.at[step] for step in self.along], self.rows)

    @staticmethod
    def scratch(depth, rows, width):
        return [
            pltpu.VMEM((depth, 2, rows // 2, width), LOW),
            pltpu.VMEM((depth, rows, width), LOW),
            pltpu.VMEM((depth, rows, width), LOW),
            pltpu.VMEM((depth, rows, width), LOW),
            dma(depth, 5),
            dma(depth, 5),
        ]


def experts_kernel(
    depth, rows, local, hidden,
    x_ref, gates_ref, grad_ref, gate_ref, up_ref, down_ref,
    sum_ref, cots_ref, normed_ref, gated_ref, gate_grad_ref, up_grad_ref, produced_ref,
    wg, wu, wd, x_all, grads, work, y_out, gated, gate_grad, up_grad, gates, gate_wide, cots, cot_rows,
    diagonal, from_x, from_y, from_z, r_send, r_recv,
    z_send, z_recv, p_send, p_recv, s_send, s_recv, w_send, w_recv, w_load, g_load, saves, local_sem,
):
    z, x, y, core = place()
    here, sibling = 2 * x + y, device(z, x, y, 1 - core)
    others = [
        (step, turn, (swapped(z, step), swapped(x, turn // 2), swapped(y, turn % 2)))
        for step in range(depth)
        for turn in range(4)
        if step or turn
    ]
    greet([device(*other, core) for _, _, other in others] + [sibling])
    copies = Copies()
    smalls = []
    for step, turn, other in others:
        oz, ox, oy = other
        smalls.append(
            copies.start(
                remote(
                    gates_ref.at[2 * oz + ox], gates.at[step, here], s_send.at[0, step, turn], s_recv.at[0, step, turn],
                    device(oz, ox, oy, core),
                )
            )
        )
    gather = Gather(copies, x_ref, x_all, rows, z_send, z_recv, p_send, p_recv)
    gather.begin()
    plain = []

    def fetch(source, target, sem):
        copy = pltpu.make_async_copy(source, target, sem)
        copy.start()
        return copy

    plain.append(fetch(x_ref, gather.at(0, here, None), local_sem.at[0]))
    weights = []
    for index in range(local):
        first = pl.multiple_of((core * local + index) * hidden, hidden)
        columns = pl.ds(first, hidden)
        for number, (source, target) in enumerate(
            [(gate_ref, wg.at[:, columns]), (up_ref, wu.at[:, columns]), (down_ref, wd.at[columns])]
        ):
            weights.append(copies.start(remote(source.at[index], target, w_send.at[number, index], w_recv.at[number, index], sibling)))
            plain.append(fetch(source.at[index], target, w_load.at[number, index]))
    plain.append(fetch(gates_ref.at[2 * z + x], gates.at[0, here], local_sem.at[1]))
    grad_copies = [fetch(grad_ref.at[0], grads.at[0], g_load.at[0])]
    scatter = Scatter(copies, work, diagonal, from_x, from_y, from_z, rows, r_send, r_recv)
    saving, producing, keeping = [], [], []
    wave_rows = 4 * rows
    lanes = lax.broadcasted_iota(jnp.int32, (wave_rows, 128), 1)

    def first_half(step):
        for copy in saving:
            copy.wait()
        saving.clear()
        for spot in range(4):
            padded = jnp.concatenate([gates[step, spot], jnp.zeros((120, 128), FULL)], axis=0)
            gate_wide[pl.ds(spot * rows, rows), :] = padded.T
        cots[...] = jnp.zeros_like(cots)
        grad_copies[step].wait()
        if step + 1 < depth:
            grad_copies.append(fetch(grad_ref.at[step + 1], grads.at[(step + 1) % 2], g_load.at[(step + 1) % 2]))
        grad = grads.at[step % 2]

        @pl.loop(0, 2 * local)
        def _(unit):
            columns = pl.ds(pl.multiple_of(unit * hidden, hidden), hidden)
            expert = lax.rem(unit, local)
            gate_pre = dot(x_all[step], wg[:, columns])
            up_pre = dot(x_all[step], wu[:, columns])
            back = dot_t(grad[...], wd[columns, :])
            logistic = 1.0 / (1.0 + jnp.exp(-gate_pre))
            activated = gate_pre * logistic
            inner = activated * up_pre
            cot = jnp.sum(inner * back, axis=-1, keepdims=True)
            cots[...] += jnp.where(lanes == expert, cot, 0.0)
            gate = jnp.sum(jnp.where(lanes == expert, gate_wide[...], 0.0), axis=-1, keepdims=True)
            gated[:, columns] = (gate * inner).astype(LOW)
            inner_grad = gate * back
            gate_grad[:, columns] = (inner_grad * up_pre * logistic * (1.0 + gate_pre * (1.0 - logistic))).astype(LOW)
            up_grad[:, columns] = (inner_grad * activated).astype(LOW)

        for spot in range(4):
            cot_rows[step, spot] = cots[pl.ds(spot * rows, rows), :].T[:8]
        for other_step, turn, (oz, ox, oy) in others:
            if other_step == step:
                copies.start(
                    remote(
                        cot_rows.at[step, 2 * ox + oy], cots_ref.at[step, here], s_send.at[1, step, turn], s_recv.at[1, step, turn],
                        device(oz, ox, oy, core),
                    )
                )
        for number, (source, target) in enumerate([(gated, gated_ref), (gate_grad, gate_grad_ref), (up_grad, up_grad_ref)]):
            saving.append(fetch(source, target.at[step], saves.at[number]))
        keeping.append(fetch(x_all.at[step], normed_ref.at[step], saves.at[4 + step]))

    def second_half(step):
        for copy in producing:
            copy.wait()
        producing.clear()
        tile = 512

        @pl.loop(0, x_all.shape[2] // tile)
        def _(index):
            columns = pl.ds(pl.multiple_of(index * tile, tile), tile)
            y_out[:, columns] = dot(gated[...], wd[:, columns]).astype(LOW)
            work[step, :, columns] = (dot_t(gate_grad[...], wg[columns, :]) + dot_t(up_grad[...], wu[columns, :])).astype(LOW)

        producing.append(fetch(y_out, produced_ref.at[step], saves.at[3]))

    gather.turn(0)
    if depth > 1:
        gather.spread(1)
    gather.complete(0)
    for copy in plain:
        copy.wait()
    for copy in weights + smalls:
        copies.arrived(copy)
    for step in range(depth):
        if step:
            gather.complete(step)
        first_half(step)
        if step + 1 < depth:
            gather.turn(step + 1)
        if step + 2 < depth:
            gather.spread(step + 2)
        if step >= 1:
            scatter.side(step - 1)
        if step >= 2:
            scatter.climb(step - 2)
        second_half(step)
        scatter.corner(step)
    own_cots = fetch(cot_rows.at[0, here], cots_ref.at[0, here], local_sem.at[2])
    if depth > 1:
        scatter.climb(depth - 2)
    scatter.side(depth - 1)
    scatter.climb(depth - 1)
    scatter.result(sum_ref)
    own_cots.wait()
    for copy in saving + producing + keeping:
        copy.wait()
    copies.finish()


def run_experts(block, gates, grads, w_gate, w_up, w_down, number):
    depth, wave, width = grads.shape
    rows = wave // 4
    local, _, hidden = w_gate.shape
    units = 2 * local * hidden
    kept = jax.ShapeDtypeStruct((depth, wave, units), LOW)
    wide = jax.ShapeDtypeStruct((depth, wave, width), LOW)
    return pl.pallas_call(
        functools.partial(experts_kernel, depth, rows, local, hidden),
        out_shape=(
            jax.ShapeDtypeStruct((rows, width), FULL),
            jax.ShapeDtypeStruct((depth, 4, 8, 128), FULL),
            wide, kept, kept, kept, wide,
        ),
        in_specs=[ANY] * 6,
        out_specs=(VMEM, VMEM, ANY, ANY, ANY, ANY, ANY),
        scratch_shapes=[
            pltpu.VMEM((width, units), LOW), pltpu.VMEM((width, units), LOW), pltpu.VMEM((units, width), LOW),
            pltpu.VMEM((depth, wave, width), LOW), pltpu.VMEM((2, wave, width), LOW),
            pltpu.VMEM((depth, wave, width), LOW), pltpu.VMEM((wave, width), LOW),
            pltpu.VMEM((wave, units), LOW), pltpu.VMEM((wave, units), LOW), pltpu.VMEM((wave, units), LOW),
            pltpu.VMEM((depth, 4, 8, 128), FULL), pltpu.VMEM((wave, 128), FULL), pltpu.VMEM((wave, 128), FULL),
            pltpu.VMEM((depth, 4, 8, 128), FULL),
        ]
        + Scatter.scratch(depth, rows, width)
        + [
            dma(depth), dma(depth), dma(depth, 6), dma(depth, 6), dma(2, depth, 4), dma(2, depth, 4),
            dma(3, local), dma(3, local), dma(3, local), dma(2), dma(4 + depth), dma(3),
        ],
        compiler_params=comm_params(number),
    )(block, gates, grads, w_gate, w_up, w_down)


class TensorScatter:
    def __init__(self, copies, work, from_pair, from_y, send, recv):
        self.copies, self.work, self.from_pair, self.from_y, self.send, self.recv = copies, work, from_pair, from_y, send, recv
        z, x, self.y, self.core = place()
        self.sibling, self.over_y = device(z, x, self.y, 1 - self.core), device(z, x, 1 - self.y, self.core)
        self.rows = work.shape[2]

    def begin(self):
        self.pairs = []
        for turn in (1, 0):
            source = self.work.at[swapped(self.y, turn), 1 - self.core]
            self.pairs.append(
                self.copies.start(remote(source, self.from_pair.at[turn], self.send.at[turn], self.recv.at[turn], self.sibling))
            )

    def cross(self):
        self.copies.arrived(self.pairs[0])
        block = self.work.at[1 - self.y, self.core]
        add_rows(block, [block, self.from_pair.at[1]], self.rows)
        self.across = self.copies.start(remote(block, self.from_y, self.send.at[2], self.recv.at[2], self.over_y))

    def result(self, target):
        self.copies.arrived(self.pairs[1])
        self.copies.arrived(self.across)
        add_rows(target, [self.work.at[self.y, self.core], self.from_pair.at[0], self.from_y], self.rows)

    @staticmethod
    def scratch(rows, width):
        return [
            pltpu.VMEM((2, 2, rows, width), LOW),
            pltpu.VMEM((2, rows, width), LOW),
            pltpu.VMEM((rows, width), LOW),
            dma(3),
            dma(3),
        ]


class TensorGather:
    def __init__(self, copies, block, target, send, recv):
        self.copies, self.target, self.send, self.recv = copies, target, send, recv
        z, x, self.y, self.core = place()
        self.sibling, over_y = device(z, x, self.y, 1 - self.core), device(z, x, 1 - self.y, self.core)
        mine = target.at[self.y, self.core]
        self.across = copies.start(remote(block, mine, send.at[0], recv.at[0], over_y))
        self.near = copies.start(remote(block, mine, send.at[1], recv.at[1], self.sibling))
        self.own = pltpu.make_async_copy(block, mine, send.at[3])
        self.own.start()

    def cross(self):
        self.copies.arrived(self.across)
        block = self.target.at[1 - self.y, self.core]
        self.passed = self.copies.start(remote(block, block, self.send.at[2], self.recv.at[2], self.sibling))

    def finish(self):
        self.own.wait()
        self.copies.arrived(self.near)
        self.copies.arrived(self.passed)


def partners_of(depth):
    z, x, y, core = place()
    return [device(swapped(z, step), x, y, core) for step in range(1, depth)] + [
        device(z, 1 - x, y, core),
        device(z, x, 1 - y, core),
        device(z, x, y, 1 - core),
        device(swapped(z, 1), 1 - x, y, core),
    ]


def mask_bias(bias, key_docs, query_docs, length):
    blocks = bias.shape[0] // length

    @pl.loop(0, bias.shape[0] // 128)
    def _(index):
        part = pl.ds(pl.multiple_of(index * 128, 128), 128)
        key = index * 128 + lax.broadcasted_iota(jnp.int32, (128, length), 0) - (blocks - 1) * length
        query = lax.broadcasted_iota(jnp.int32, (128, length), 1)
        seen = (key_docs[part, :] == query_docs[0:1, :]) & (key <= query) & (query - key < WINDOW)
        bias[part, :] = jnp.where(seen, 0.0, -1e30).astype(bias.dtype)


def exchange(copies, mine, landed, send, recv, mates):
    return [
        copies.start(remote(mine, landed.at[number], send.at[number], recv.at[number], device(*mate)))
        for number, mate in enumerate(mates)
    ]


def mates_of():
    z, x, y, core = place()
    return [(z, x, swapped(y, turn // 2), swapped(core, turn % 2)) for turn in range(1, 4)]


def as_rows(columns):
    lanes = lax.broadcasted_iota(jnp.int32, (columns[0].shape[0], 128), 1)
    wide = jnp.zeros(lanes.shape, FULL)
    for index, column in enumerate(columns):
        wide = jnp.where(lanes == index, column, wide)
    return wide.T[:8]


def as_columns(rows_of_eight):
    length = rows_of_eight.shape[1]
    return jnp.concatenate([rows_of_eight, jnp.zeros((120, length), FULL)], axis=0).T


def attention_kernel(
    depth, rows, heads, chain, local,
    tokens_ref, wq_ref, wk_ref, wv_ref, wo_ref, grad_ref,
    gain1_ref, q_gain_ref, k_gain_ref, cosine_ref, sine_ref, docs_ref, gain2_ref, router_ref, picked_ref,
    normed_turned, q_raw, k_raw, queries, kv_all, key_docs, scales, attended, logs, state_ref, normed2_ref, probs_ref, gates_ref,
    all_grad,
    tokens, normed_ref, wq, wk, wv, wo, docs_in, squares, squares_in, scores, bias, partial, from_pair, from_y, sum_ref,
    t_send, t_recv, z_send, z_recv, p_send, p_recv, h_send, h_recv, d_send, d_recv, q_send, q_recv, load,
):
    z, x, y, core = place()
    group, part = lax.axis_index("expert"), lax.axis_index("tensor")
    spot = group % chain
    length, width = tokens.shape
    wide = heads * HD
    scale = HD ** (-0.5)
    loads = []
    for number, (source, target) in enumerate([(tokens_ref, tokens), (wv_ref, wv), (wk_ref, wk), (wq_ref, wq), (wo_ref, wo)]):
        loads.append(pltpu.make_async_copy(source, target, load.at[number]))
        loads[-1].start()
    mates = mates_of()
    z1, x1 = swapped(z, 1), 1 - x
    greet(
        [device(swapped(z, step), x, y, core) for step in range(1, depth)]
        + [device(z, x1, y, core), device(z1, x1, y, core)]
        + [device(*mate) for mate in mates]
    )
    copies = Copies()
    for distance in (1, 2):

        @pl.when(spot < chain - distance)
        def _():
            remote(
                docs_ref, docs_in.at[2 - distance], d_send.at[distance], d_recv.at[distance], (group + distance, part)
            ).start()

    gather = Gather(copies, grad_ref, all_grad, rows, z_send, z_recv, p_send, p_recv)
    gather.spread(0)
    gather.lift(1)
    own = pltpu.make_async_copy(grad_ref, gather.at(0, gather.here, None), load.at[5])
    own.start()
    key_part, value_part = pl.ds(0, wide), pl.ds(wide, wide)

    high = lax.rem(z, 2)
    over_x, over_z = device(z, x1, y, core), device(z1, x, y, core)

    def docs_copy(distance, to):
        return remote(docs_ref, docs_in.at[2 - distance], d_send.at[distance], d_recv.at[distance], (to, part))

    def halo_copy(kind, source, slot, number, to):
        columns = (key_part, value_part)[kind]
        return remote(
            kv_all.at[source, :, columns], kv_all.at[slot, :, columns], h_send.at[kind, number], h_recv.at[kind, number], to
        )

    def x_copy(kind):
        return halo_copy(kind, 2, 1, 0, over_x)

    def z_copy(kind):
        return halo_copy(kind, 2, 0, 1, over_z)

    def relay_copy(kind):
        return halo_copy(kind, 0, 1, 2, over_x)

    def halo_start(kind):
        pl.when(x == 0)(lambda: x_copy(kind).start())
        pl.when(high == 0)(lambda: z_copy(kind).start())

    def halo_relay(kind):
        pl.when(high == 1)(lambda: z_copy(kind).wait_recv())
        pl.when(spot == 3)(lambda: relay_copy(kind).start())

    def halo_arrive(kind):
        columns = (key_part, value_part)[kind]
        pl.when(x == 1)(lambda: x_copy(kind).wait_recv())
        pl.when(spot == 2)(lambda: relay_copy(kind).wait_recv())

        def clear(slot):
            kv_all[slot, :, columns] = jnp.zeros((length, wide), LOW)

        pl.when(spot == 0)(lambda: clear(1))
        pl.when(high == 0)(lambda: clear(0))

    def halo_sent(kind):
        pl.when(x == 0)(lambda: x_copy(kind).wait_send())
        pl.when(high == 0)(lambda: z_copy(kind).wait_send())
        pl.when(spot == 3)(lambda: relay_copy(kind).wait_send())

    loads[0].wait()

    @pl.loop(0, length // 128)
    def _(index):
        part_rows = pl.ds(pl.multiple_of(index * 128, 128), 128)
        values = tokens[part_rows, :].astype(FULL)
        factor = lax.rsqrt(jnp.mean(values * values, axis=-1, keepdims=True) + NORM_EPSILON)
        normed_ref[part_rows, :] = (values * factor * gain1_ref[0:1, :]).astype(LOW)

    def project(weights, store):
        @pl.loop(0, wide // 256)
        def _(index):
            columns = pl.ds(pl.multiple_of(index * 256, 256), 256)
            store(index, columns, dot(normed_ref[...], weights[:, columns]))

    def keep_value(index, columns, result):
        kv_all[2, :, pl.ds(pl.multiple_of(wide + index * 256, 256), 256)] = result.astype(LOW)

    def keep_key(index, columns, result):
        k_raw[:, columns] = result

    def keep_query(index, columns, result):
        q_raw[:, columns] = result

    loads[2].wait()
    project(wk, keep_key)
    loads[3].wait()
    project(wq, keep_query)
    squares[...] = as_rows(
        [jnp.sum(q_raw[...] * q_raw[...], axis=-1, keepdims=True), jnp.sum(k_raw[...] * k_raw[...], axis=-1, keepdims=True)]
    )
    sent = exchange(copies, squares, squares_in, q_send, q_recv, mates)
    loads[1].wait()
    project(wv, keep_value)
    halo_start(1)
    gather.turn(0)

    @pl.loop(0, width // 256)
    def _(index):
        columns = pl.ds(pl.multiple_of(index * 256, 256), 256)
        normed_turned[columns, :] = normed_ref[:, columns].T

    for copy in sent:
        copies.arrived(copy)
    total = squares[...]
    for number in range(3):
        total = total + squares_in[number]
    scales[...] = lax.rsqrt(total * (1.0 / width) + NORM_EPSILON)
    factors = as_columns(scales[...])

    def turn_heads(raw, gain_ref, factor, store):
        for head in range(heads):
            columns = pl.ds(head * HD, HD)
            normed = raw[:, columns] * factor * gain_ref[0:1, columns]
            store(head, (normed * cosine_ref[...] + pltpu.roll(normed, HD // 2, 1) * sine_ref[...]).astype(LOW))

    def store_key(head, turned):
        kv_all[2, :, pl.ds(head * HD, HD)] = turned

    def store_query(head, turned):
        queries[:, pl.ds(head * HD, HD)] = turned

    turn_heads(k_raw, k_gain_ref, factors[:, 1:2], store_key)
    halo_start(0)
    gather.spread(1)
    gather.lift(2)
    turn_heads(q_raw, q_gain_ref, factors[:, 0:1], store_query)
    for distance in (1, 2):

        @pl.when(spot >= distance)
        def _():
            docs_copy(distance, group - distance).wait_recv()

        @pl.when(spot < distance)
        def _():
            docs_in[2 - distance] = jnp.full_like(docs_ref, -1)

    for block in range(3):
        rows_of = docs_in[block] if block < 2 else docs_ref[...]
        key_docs[pl.ds(block * length, length), :] = rows_of.astype(FULL).T[:, 0:1].astype(jnp.int32)
    mask_bias(bias, key_docs, docs_ref, length)

    def score(block):
        @pl.loop(0, heads)
        def _(head):
            columns = pl.ds(pl.multiple_of(head * HD, HD), HD)
            keys = pl.ds(block * length, length)
            scores[head, keys, :] = dot_t(kv_all[block, :, columns], queries[:, columns]) * scale + bias[keys, :]

    score(2)
    halo_relay(1)
    gather.turn(1)
    halo_relay(0)
    gather.spread(2)
    gather.lift(3)
    halo_arrive(0)
    score(0)
    score(1)
    gather.turn(2)
    halo_arrive(1)

    @pl.loop(0, heads)
    def _(head):
        columns = pl.ds(pl.multiple_of(head * HD, HD), HD)
        mine = scores.at[head]
        highest = jnp.max(mine[...], axis=0, keepdims=True)
        total = jnp.zeros_like(highest)
        mixed = jnp.zeros((HD, length), FULL)
        for block in range(3):
            weights = jnp.exp(mine[pl.ds(block * length, length), :] - highest)
            total = total + jnp.sum(weights, axis=0, keepdims=True)
            mine[pl.ds(block * length, length), :] = weights
        for block in range(3):
            probs = (mine[pl.ds(block * length, length), :] * (1.0 / total)).astype(LOW)
            values = pl.ds(pl.multiple_of((heads + head) * HD, HD), HD)
            mixed = mixed + t_dot(kv_all[block, :, values], probs)
        attended[:, columns] = mixed.T.astype(LOW)
        logs[head] = jnp.broadcast_to(highest + jnp.log(total), (8, length))

    gather.spread(3)
    loads[4].wait()
    for index in range(4):
        partial[index // 2, index % 2] = dot(attended[pl.ds(index * rows, rows), :], wo[...]).astype(LOW)
    scatter = TensorScatter(copies, partial, from_pair, from_y, t_send, t_recv)
    scatter.begin()
    scatter.cross()
    gather.turn(3)
    scatter.result(sum_ref)
    own_rows = pl.ds(pl.multiple_of(part * rows, rows), rows)
    state = tokens[own_rows, :].astype(FULL) + sum_ref[...]
    state_ref[...] = state
    factor = lax.rsqrt(jnp.mean(state * state, axis=-1, keepdims=True) + NORM_EPSILON)
    normed2_ref[...] = (state * factor * gain2_ref[0:1, :]).astype(LOW)
    logits = dot(normed2_ref[...], router_ref[...])
    experts = gates_ref.shape[0] * local
    lanes = lax.broadcasted_iota(jnp.int32, logits.shape, 1)
    logits = jnp.where(lanes < experts, logits, -1e30)
    weights = jnp.exp(logits - jnp.max(logits, axis=-1, keepdims=True))
    probs = weights / jnp.sum(weights, axis=-1, keepdims=True)
    probs_ref[...] = probs
    gates = (probs * picked_ref[...]).T
    gates_ref[...] = jnp.zeros_like(gates_ref)
    for index in range(gates_ref.shape[0]):
        gates_ref[index, 0:local, :] = gates[index * local : (index + 1) * local]
    own.wait()
    for kind in range(2):
        halo_sent(kind)
    for distance in (1, 2):

        @pl.when(spot < chain - distance)
        def _():
            docs_copy(distance, group + distance).wait_send()

    copies.finish()


def run_attention(tokens, weights, grads, gains, tables, docs, gain2, router, picked, depth, chain, local, number):
    length, width = tokens.shape
    rows = grads.shape[0]
    wide = weights[0].shape[1]
    heads = wide // HD
    return pl.pallas_call(
        functools.partial(attention_kernel, depth, rows, heads, chain, local),
        out_shape=(
            jax.ShapeDtypeStruct((width, length), LOW),
            jax.ShapeDtypeStruct((length, wide), FULL),
            jax.ShapeDtypeStruct((length, wide), FULL),
            jax.ShapeDtypeStruct((length, wide), LOW),
            jax.ShapeDtypeStruct((3, length, 2 * wide), LOW),
            jax.ShapeDtypeStruct((3 * length, 1), jnp.int32),
            jax.ShapeDtypeStruct((8, length), FULL),
            jax.ShapeDtypeStruct((length, wide), LOW),
            jax.ShapeDtypeStruct((heads, 8, length), FULL),
            jax.ShapeDtypeStruct((rows, width), FULL),
            jax.ShapeDtypeStruct((rows, width), LOW),
            jax.ShapeDtypeStruct((rows, 128), FULL),
            jax.ShapeDtypeStruct((2 * depth, 8, rows), FULL),
            jax.ShapeDtypeStruct((depth, 4 * rows, width), LOW),
        ),
        in_specs=[ANY] * 6 + [VMEM] * 9,
        out_specs=(VMEM,) * 13 + (ANY,),
        scratch_shapes=[
            pltpu.VMEM(tokens.shape, LOW), pltpu.VMEM(tokens.shape, LOW), pltpu.VMEM((width, wide), LOW), pltpu.VMEM((width, wide), LOW),
            pltpu.VMEM((width, wide), LOW), pltpu.VMEM((wide, width), LOW), pltpu.VMEM((2, 8, length), jnp.int32),
            pltpu.VMEM((8, length), FULL), pltpu.VMEM((3, 8, length), FULL),
            pltpu.VMEM((heads, 3 * length, length), FULL), pltpu.VMEM((3 * length, length), FULL),
        ]
        + TensorScatter.scratch(rows, width)[:3]
        + [
            pltpu.VMEM((rows, width), FULL), dma(3), dma(3),
            dma(depth), dma(depth), dma(depth, 6), dma(depth, 6), dma(2, 3), dma(2, 3), dma(3), dma(3), dma(3), dma(3), dma(6),
        ],
        compiler_params=comm_params(number),
    )(tokens, *weights, grads, *gains, *tables, docs, gain2, router, picked)


def attention_back_kernel(
    depth, rows, heads, chain, local,
    sum_ref, gate_cots, probs_ref, picked_ref, state_ref, gain2_ref, router_ref, normed2_ref, grad_ref,
    query_ref, kv_all, attended, logs, key_docs, query_docs, q_raw, k_raw, q_gain_ref, k_gain_ref, cosine_ref, sine_ref, scales,
    w_out, produced_ref, normed_ref, wq_ref, wk_ref, wv_ref,
    state_cot_ref, router_grad_ref, norm2_grad_ref, q_grad_ref, k_grad_ref, mix_ref, normed_part, piece0, piece1, piece2, piece3,
    low, lows, by_expert, bias, cots, deltas, turned, query_cot, kv_cot, sending, landed, work, raw_cots, flipped, wq, wk, wv,
    inners, inners_in, staging,
    diagonal, from_x, from_y, from_z, r_send, r_recv, t_send, t_recv, h_send, h_recv, i_send, i_recv, load, saves,
):
    z, x, y, core = place()
    group, part = lax.axis_index("expert"), lax.axis_index("tensor")
    spot = group % chain
    length, width = query_ref.shape[0], w_out.shape[1]
    wide = heads * HD
    scale = HD ** (-0.5)
    order = [step for step in range(depth - 1, 0, -1)] + [0]
    loads = {}
    for step in order:
        loads[step] = pltpu.make_async_copy(produced_ref.at[step], work.at[step], load.at[step])
        loads[step].start()
    others = []
    for number, (source, target) in enumerate([(wq_ref, wq), (wk_ref, wk), (wv_ref, wv)]):
        others.append(pltpu.make_async_copy(source, target, load.at[depth + number]))
        others[-1].start()
    mates = mates_of()
    greet(
        [device(swapped(z, step), x, y, core) for step in range(1, depth)]
        + [device(z, 1 - x, y, core)]
        + [device(*mate) for mate in mates]
    )
    copies = Copies()
    scatter = Scatter(copies, work, diagonal, from_x, from_y, from_z, rows, r_send, r_recv)

    def corner(step):
        loads[step].wait()
        scatter.corner(step)

    for step in order[:2]:
        corner(step)

    by_expert[...] = jnp.zeros_like(by_expert)
    for plane in range(depth):
        step = swapped(z, plane)
        for column in range(2):
            first = (2 * plane + column) * local
            by_expert[first : first + local, :] = (gate_cots[step, 2 * column] + gate_cots[step, 2 * column + 1])[:local]
    probs = probs_ref[...]
    prob_cot = by_expert[...].T * picked_ref[...]
    logit_cot = probs * (prob_cot - jnp.sum(probs * prob_cot, axis=-1, keepdims=True))
    normed2_cot = sum_ref[...] + lax.dot_general(
        logit_cot, router_ref[...].astype(FULL), (((1,), (1,)), ((), ())),
        precision=HIGHEST_PRECISION, preferred_element_type=FULL,
    )
    state = state_ref[...]
    factor = lax.rsqrt(jnp.mean(state * state, axis=-1, keepdims=True) + NORM_EPSILON)
    norm2_grad_ref[...] = jnp.broadcast_to(jnp.sum(normed2_cot * state * factor, axis=0, keepdims=True), norm2_grad_ref.shape)
    inner = jnp.sum(normed2_cot * gain2_ref[0:1, :] * state, axis=-1, keepdims=True)
    state_cot = (
        grad_ref[...].astype(FULL)
        + factor * gain2_ref[0:1, :] * normed2_cot
        - state * (factor * factor * factor) * inner * (1.0 / width)
    )
    state_cot_ref[...] = state_cot
    low[...] = state_cot.astype(LOW)
    gather = TensorGather(copies, low, lows, t_send, t_recv)
    scatter.side(order[0])
    router_grad_ref[...] = jnp.dot(
        logit_cot.T, normed2_ref[...].astype(FULL), precision=HIGHEST_PRECISION, preferred_element_type=FULL
    )[: router_grad_ref.shape[0]]
    mask_bias(bias, key_docs, query_docs, length)
    gather.cross()
    gather.finish()
    for index in range(4):
        cots[pl.ds(index * rows, rows), :] = dot_t(lows[index // 2, index % 2], w_out[...]).astype(LOW)
    for head in range(heads):
        columns = pl.ds(head * HD, HD)
        product = cots[:, columns].astype(FULL) * attended[:, columns].astype(FULL)
        deltas[head] = jnp.broadcast_to(jnp.sum(product.T, axis=0, keepdims=True), (8, length))
    turned[...] = jnp.zeros_like(turned)

    def back(block, target):
        @pl.loop(0, heads)
        def _(head):
            columns = pl.ds(pl.multiple_of(head * HD, HD), HD)
            values = pl.ds(pl.multiple_of((heads + head) * HD, HD), HD)
            query, cot = query_ref[:, columns], cots[:, columns]
            log, delta = logs[head, 0:1, :], deltas[head, 0:1, :]
            tile = 256

            @pl.loop(0, length // tile)
            def _(index):
                keys = pl.ds(pl.multiple_of(index * tile, tile), tile)
                key, value = kv_all[block, keys, columns], kv_all[block, keys, values]
                hidden = bias[pl.ds(pl.multiple_of(block * length + index * tile, tile), tile), :].astype(FULL)
                probs = jnp.exp(dot_t(key, query) * scale + hidden - log)
                score_cot = (probs * (dot_t(value, cot) - delta)).astype(LOW)
                turned[head] += t_dot(key, score_cot)
                target[keys, columns] = (dot(score_cot, query) * scale).astype(target.dtype)
                target[keys, values] = dot(probs.astype(LOW), cot).astype(target.dtype)

    high = lax.rem(z, 2)
    over_x, over_z = device(z, 1 - x, y, core), device(swapped(z, 1), x, y, core)

    def x_copy():
        return remote(sending.at[1], landed.at[1], h_send.at[0], h_recv.at[0], over_x)

    def z_copy():
        return remote(sending.at[0], landed.at[0], h_send.at[1], h_recv.at[1], over_z)

    back(1, sending.at[1])
    pl.when(spot >= 1)(lambda: x_copy().start())
    corner(1)
    scatter.side(order[1])
    back(0, sending.at[0])
    pl.when(spot == 2)(lambda: z_copy().start())
    scatter.climb(order[0])
    back(2, kv_cot)

    @pl.when(spot == 3)
    def _():
        x_copy().wait_recv()
        add_rows(sending.at[0], [sending.at[0], landed.at[1]], length)
        z_copy().start()

    corner(0)
    for head in range(heads):
        query_cot[:, pl.ds(head * HD, HD)] = turned[head].T * scale
    scatter.side(order[2])
    scatter.climb(order[1])

    saving = {}

    def weight_piece(number, right, target):
        piece = target.shape[2]
        for index in range(2 * depth):
            slot = index % 2
            if slot in saving:
                saving.pop(slot).wait()
            staging[slot] = dot(flipped[pl.ds(index * piece, piece), :], right).astype(LOW)
            saving[slot] = pltpu.make_async_copy(staging.at[slot], target.at[index // 2, index % 2], saves.at[slot])
            saving[slot].start()

    @pl.loop(0, width // 256)
    def _(index):
        columns = pl.ds(pl.multiple_of(index * 256, 256), 256)
        flipped[columns, :] = jnp.concatenate([lows[block // 2, block % 2, :, columns] for block in range(4)], axis=0).T

    weight_piece(0, attended[...], piece0)
    normed_copy = pltpu.make_async_copy(normed_ref, flipped, load.at[depth + 3])
    normed_copy.start()
    scatter.side(order[3])
    factors = as_columns(scales[...])

    def turn_back(cot, raw, gain_ref, factor, grad_out):
        total = jnp.zeros((length, 1), FULL)
        for head in range(heads):
            columns = pl.ds(head * HD, HD)
            mine = cot[:, columns]
            mine = mine * cosine_ref[...] - pltpu.roll(mine, HD // 2, 1) * sine_ref[...]
            cot[:, columns] = mine
            mine = mine * raw[:, columns]
            grad_out[:, columns] = jnp.broadcast_to(jnp.sum(mine * factor, axis=0, keepdims=True), (8, HD))
            total = total + jnp.sum(mine * gain_ref[0:1, columns], axis=-1, keepdims=True)
        return total

    query_inner = turn_back(query_cot, q_raw, q_gain_ref, factors[:, 0:1], q_grad_ref)
    scatter.climb(order[2])

    @pl.when(x == 0)
    def _():
        x_copy().wait_recv()
        add_rows(kv_cot, [kv_cot, landed.at[1]], length)

    @pl.when(high == 0)
    def _():
        z_copy().wait_recv()
        add_rows(kv_cot, [kv_cot, landed.at[0]], length)

    key_inner = turn_back(kv_cot, k_raw, k_gain_ref, factors[:, 1:2], k_grad_ref)
    inners[...] = as_rows([query_inner, key_inner])
    sent = exchange(copies, inners, inners_in, i_send, i_recv, mates)
    raw_cots[2] = kv_cot[:, pl.ds(wide, wide)].astype(LOW)
    normed_copy.wait()
    weight_piece(1, raw_cots[2], piece1)
    for copy in sent:
        copies.arrived(copy)
    total = inners[...]
    for number in range(3):
        total = total + inners_in[number]
    totals = as_columns(total * (1.0 / width))

    def raw_cot(number, cot, raw, gain_ref):
        factor = factors[:, number : number + 1]
        shrink = (factor * factor * factor) * totals[:, number : number + 1]
        for head in range(heads):
            columns = pl.ds(head * HD, HD)
            raw_cots[number, :, columns] = (
                factor * gain_ref[0:1, columns] * cot[:, columns] - raw[:, columns] * shrink
            ).astype(LOW)

    raw_cot(0, query_cot, q_raw, q_gain_ref)
    raw_cot(1, kv_cot, k_raw, k_gain_ref)
    for copy in others:
        copy.wait()

    @pl.loop(0, width // 256)
    def _(index):
        columns = pl.ds(pl.multiple_of(index * 256, 256), 256)
        result = (
            dot_t(raw_cots[0], wq[columns, :]) + dot_t(raw_cots[1], wk[columns, :]) + dot_t(raw_cots[2], wv[columns, :])
        ).astype(LOW)
        for block in range(4):
            normed_part[block // 2, block % 2, :, columns] = result[block * rows : (block + 1) * rows]

    weight_piece(2, raw_cots[0], piece2)
    weight_piece(3, raw_cots[1], piece3)
    scatter.climb(order[3])
    scatter.result(mix_ref)
    pl.when(spot >= 1)(lambda: x_copy().wait_send())
    pl.when(spot >= 2)(lambda: z_copy().wait_send())

    for copy in saving.values():
        copy.wait()
    copies.finish()


def run_attention_back(rows_of, attention, sources, produced, normed, weights, chain, local, experts, number):
    depth = produced.shape[0]
    rows, width = rows_of[0].shape
    queries, kv_all = attention[0], attention[1]
    length, wide2 = kv_all.shape[1:]
    wide = wide2 // 2
    heads = wide // HD
    piece = jax.ShapeDtypeStruct((depth, 2, width // (2 * depth), wide), LOW)
    return pl.pallas_call(
        functools.partial(attention_back_kernel, depth, rows, heads, chain, local),
        out_shape=(
            jax.ShapeDtypeStruct((rows, width), FULL),
            jax.ShapeDtypeStruct((experts, width), FULL),
            jax.ShapeDtypeStruct((8, width), FULL),
            jax.ShapeDtypeStruct((8, wide), FULL),
            jax.ShapeDtypeStruct((8, wide), FULL),
            jax.ShapeDtypeStruct((rows, width), FULL),
            jax.ShapeDtypeStruct((2, 2, rows, width), LOW),
            piece, piece, piece, piece,
        ),
        in_specs=[VMEM] * 23 + [ANY] * 5,
        out_specs=(VMEM,) * 7 + (ANY,) * 4,
        scratch_shapes=[
            pltpu.VMEM((rows, width), LOW), pltpu.VMEM((2, 2, rows, width), LOW), pltpu.VMEM((128, rows), FULL),
            pltpu.VMEM((3 * length, length), LOW), pltpu.VMEM((length, wide), LOW),
            pltpu.VMEM((heads, 8, length), FULL), pltpu.VMEM((heads, HD, length), FULL),
            pltpu.VMEM((length, wide), FULL), pltpu.VMEM((length, wide2), FULL),
            pltpu.VMEM((2, length, wide2), LOW), pltpu.VMEM((2, length, wide2), LOW),
            pltpu.VMEM(produced.shape, LOW), pltpu.VMEM((3, length, wide), LOW), pltpu.VMEM((width, length), LOW),
            pltpu.VMEM((width, wide), LOW), pltpu.VMEM((width, wide), LOW), pltpu.VMEM((width, wide), LOW),
            pltpu.VMEM((8, length), FULL), pltpu.VMEM((3, 8, length), FULL), pltpu.VMEM((2,) + piece.shape[2:], LOW),
        ]
        + Scatter.scratch(depth, rows, width)
        + [dma(4), dma(3), dma(3), dma(3), dma(3), dma(3), dma(depth + 4), dma(2)],
        compiler_params=comm_params(number),
    )(*rows_of, *attention, *sources, produced, normed, *weights)


def dot(left, right):
    return jnp.dot(left, right, preferred_element_type=FULL)


def dot_t(left, right):
    return lax.dot_general(left, right, (((1,), (1,)), ((), ())), preferred_element_type=FULL)


def t_dot(left, right):
    return lax.dot_general(left, right, (((0,), (0,)), ((), ())), preferred_element_type=FULL)


class ExpertScatter:
    def __init__(self, copies, parts, work, from_x, from_z, load, send, recv):
        self.copies, self.parts, self.work, self.from_x, self.from_z = copies, parts, work, from_x, from_z
        self.load, self.send, self.recv = load, send, recv
        self.z, self.x, y, core = place()
        self.depth, self.rows = work.shape[1], work.shape[2]
        self.over_x = device(self.z, 1 - self.x, y, core)
        self.column = [device(swapped(self.z, step), self.x, y, core) for step in range(self.depth)]
        self.order = list(range(self.depth - 1, -1, -1))
        self.loads, self.sides, self.along = {}, {}, {}

    def begin(self, index):
        for step in self.order:
            at = swapped(self.z, step)
            self.sides[index, step] = self.copies.start(
                remote(
                    self.parts[index].at[at, 1 - self.x], self.from_x.at[index, step],
                    self.send.at[0, index, step], self.recv.at[0, index, step], self.over_x,
                )
            )
            load = pltpu.make_async_copy(self.parts[index].at[at, self.x], self.work.at[index, step], self.load.at[index, step])
            load.start()
            self.loads[index, step] = load

    def climb(self, index, step):
        self.loads[index, step].wait()
        self.copies.arrived(self.sides[index, step])
        mine = self.work.at[index, step]
        if step:
            add_rows(mine, [mine, self.from_x.at[index, step]], self.rows)
            self.along[index, step] = self.copies.start(
                remote(
                    mine, self.from_z.at[index, step],
                    self.send.at[1, index, step], self.recv.at[1, index, step], self.column[step],
                )
            )

    def result(self, index, target):
        terms = [self.work.at[index, 0], self.from_x.at[index, 0]]
        for step in range(1, self.depth):
            self.copies.arrived(self.along[index, step])
            terms.append(self.from_z.at[index, step])
        add_rows(target, terms, self.rows)


def gradients_kernel(
    depth, rows, local, hidden, matrices, *refs,
):
    parts, refs = refs[:matrices], refs[matrices:]
    (
        normed_part, tokens_ref, state_cot, scale_ref, gain_ref, out_ref, vector_ref,
        normed_ref, grad_ref, gated_ref, gate_grad_ref, up_grad_ref,
    ) = refs[:12]
    sums, refs = refs[12 : 12 + matrices], refs[12 + matrices :]
    (
        input_grads, outputs, vector_sum,
        gate_own, up_own, down_own, gate_other, up_other, down_other,
        work, from_x, from_z, partial, from_pair, from_y, normed_grad, low, vectors, vector_in, vector_mid, vector_turn,
        tiles, turned, acts, gated_turned, near, far, near_down, far_down,
        e_load, e_send, e_recv, t_send, t_recv, g_send, g_recv, o_send, o_recv, v_send, v_recv, u_send, u_recv,
        tile_load, act_load, save, pair_send, pair_recv, local_sem,
    ) = refs
    z, x, y, core = place()
    group = 2 * z + x
    sibling = device(z, x, y, 1 - core)
    groups = [(step, turn) for step in range(depth) for turn in range(2) if step or turn]
    peers = [device(swapped(z, step), swapped(x, turn), y, core) for step, turn in groups]
    mates = [(z, x, swapped(y, turn // 2), swapped(core, turn % 2)) for turn in range(1, 4)]
    greet(peers + [device(*mate) for mate in mates])
    copies = Copies()
    width = normed_ref.shape[1]
    tile = 512
    count = width // tile

    def fetch(source, target, sem):
        copy = pltpu.make_async_copy(source, target, sem)
        copy.start()
        return copy

    experts = ExpertScatter(copies, parts, work, from_x, from_z, e_load, e_send, e_recv)
    loaded = fetch(normed_part, partial, local_sem.at[0])
    experts.begin(0)
    loaded.wait()
    scatter = TensorScatter(copies, partial, from_pair, from_y, t_send, t_recv)
    scatter.begin()
    out_gather = TensorGather(copies, out_ref, outputs, o_send, o_recv)
    for index in range(1, matrices):
        experts.begin(index)
    act_copies = [fetch(gate_grad_ref, acts.at[0], act_load.at[0]), fetch(up_grad_ref, acts.at[1], act_load.at[1])]

    def fetch_tile(number):
        source = normed_ref if number < count else grad_ref
        columns = pl.ds((number % count) * tile, tile)
        return fetch(source.at[:, columns], tiles.at[number % 2], tile_load.at[number % 2])

    tile_copies = [fetch_tile(0)]
    saving = {}

    def first_unit(owner):
        return owner * local * hidden

    def gate_and_up(number):
        slot = number % 2
        tile_copies[number].wait()
        tile_copies.append(fetch_tile(number + 1))
        turned[...] = tiles[slot].T
        for copy, remote_one in saving.pop(slot, []):
            copies.sent(copy) if remote_one else copy.wait()
        for which in range(2):
            for owner, target in ((1 - core, far), (core, near)):

                @pl.loop(0, local)
                def _(expert):
                    columns = pl.ds(pl.multiple_of(first_unit(owner) + expert * hidden, hidden), hidden)
                    target[which, slot, expert] = dot(turned[...], acts[which, :, columns]).astype(target.dtype)

        saves = []
        place_of = pl.ds(number * tile, tile)
        for which, (own, other) in enumerate(((gate_own, gate_other), (up_own, up_other))):
            away = remote(
                far.at[which, slot], other.at[:, place_of], pair_send.at[which, number], pair_recv.at[which, number], sibling
            )
            copies.start(away)
            saves.append((away, True))
            saves.append((fetch(near.at[which, slot], own.at[:, place_of], save.at[which, slot]), False))
        saving[slot] = saves

    def down(number):
        slot = number % 2
        tile_copies[count + number].wait()
        if number + 1 < count:
            tile_copies.append(fetch_tile(count + number + 1))
        for copy, remote_one in saving.pop(("down", slot), []):
            copies.sent(copy) if remote_one else copy.wait()
        for owner, target in ((1 - core, far_down), (core, near_down)):

            @pl.loop(0, local)
            def _(expert):
                units = pl.ds(pl.multiple_of(first_unit(owner) + expert * hidden, hidden), hidden)
                target[slot, expert] = dot(gated_turned[units, :], tiles[slot]).astype(target.dtype)

        columns = pl.ds(number * tile, tile)
        away = remote(
            far_down.at[slot], down_other.at[:, :, columns], pair_send.at[2, number], pair_recv.at[2, number], sibling
        )
        copies.start(away)
        saving["down", slot] = [
            (away, True), (fetch(near_down.at[slot], down_own.at[:, :, columns], save.at[2, slot]), False)
        ]

    for copy in act_copies:
        copy.wait()
    gate_and_up(0)
    scatter.cross()
    experts.climb(0, experts.order[0])
    gate_and_up(1)
    out_gather.cross()
    experts.climb(0, experts.order[1])
    scatter.result(normed_grad)

    inputs = tokens_ref[...].astype(FULL)
    factor, gain = scale_ref[:, 0:1], gain_ref[0:1, :]
    normed = normed_grad[...]
    inner = jnp.sum(normed * gain * inputs, axis=-1, keepdims=True)
    low[...] = (
        state_cot[...] + factor * gain * normed - inputs * (factor * factor * factor) * inner * (1.0 / width)
    ).astype(LOW)
    gain_grad = jnp.sum(normed * inputs * factor, axis=0, keepdims=True)
    grad_gather = TensorGather(copies, low, input_grads, g_send, g_recv)
    vectors[...] = vector_ref[...]
    slice_width = vectors.shape[2]
    for index in range(vectors.shape[0]):
        vectors[index, 16:17, :] = gain_grad[:, index * slice_width : (index + 1) * slice_width]
    vector_copies = []
    for number, ((step, turn), peer) in enumerate(zip(groups, peers)):
        to = 2 * swapped(z, step) + swapped(x, turn)
        vector_copies.append(
            copies.start(remote(vectors.at[to], vector_in.at[number], v_send.at[number], v_recv.at[number], peer))
        )

    for step in experts.order[2:]:
        experts.climb(0, step)
    gate_and_up(2)
    for step in experts.order[:2]:
        experts.climb(1, step)
    grad_gather.cross()
    gate_and_up(3)
    for step in experts.order[2:]:
        experts.climb(1, step)
    gated_copy = fetch(gated_ref, acts.at[0], act_load.at[0])
    gated_copy.wait()
    for index in range(2):
        half = pl.ds(index * local * hidden, local * hidden)
        gated_turned[half, :] = acts[0, :, half].T
    experts.result(0, sums[0])
    down(0)
    experts.climb(2, experts.order[0])
    down(1)
    for step in experts.order[1:]:
        experts.climb(2, step)
    down(2)
    experts.result(1, sums[1])
    down(3)
    for index in range(3, matrices):
        for step in experts.order:
            experts.climb(index, step)
    for copy in vector_copies:
        copies.arrived(copy)
    total = vectors[group]
    for number in range(len(peers)):
        total = total + vector_in[number]
    vector_mid[...] = total
    turn_copies = [
        copies.start(remote(vector_mid, vector_turn.at[number], u_send.at[number], u_recv.at[number], device(*mate)))
        for number, mate in enumerate(mates)
    ]
    for index in range(2, matrices):
        experts.result(index, sums[index])
    out_gather.finish()
    grad_gather.finish()
    for copy in turn_copies:
        copies.arrived(copy)
    total = vector_mid[...]
    for number in range(len(mates)):
        total = total + vector_turn[number]
    keep = lax.broadcasted_iota(jnp.int32, total.shape, 0) < 18
    vector_sum[...] = jnp.where(keep, total, vector_mid[...])
    for entries in saving.values():
        for copy, remote_one in entries:
            if not remote_one:
                copy.wait()
    copies.finish()


def run_gradients(parts, normed_part, tokens, state_cot, scale, gain, out, vectors, normed, grads, gated, gate_grad, up_grad, local, number):
    matrices = len(parts)
    depth, _, piece, columns = parts[0].shape
    rows, width = tokens.shape
    seen, units = gated.shape
    hidden = units // (2 * local)
    tile = 512
    sum_of = jax.ShapeDtypeStruct((piece, columns), FULL)
    spread = jax.ShapeDtypeStruct((2, 2, rows, width), LOW)
    wide, tall = (local, width, hidden), (local, hidden, width)
    results = pl.pallas_call(
        functools.partial(gradients_kernel, depth, rows, local, hidden, matrices),
        out_shape=(sum_of,) * matrices
        + (
            spread, spread, jax.ShapeDtypeStruct(vectors.shape[1:], FULL),
            jax.ShapeDtypeStruct(wide, FULL), jax.ShapeDtypeStruct(wide, FULL), jax.ShapeDtypeStruct(tall, FULL),
            jax.ShapeDtypeStruct(wide, LOW), jax.ShapeDtypeStruct(wide, LOW), jax.ShapeDtypeStruct(tall, LOW),
        ),
        in_specs=[ANY] * (matrices + 1) + [VMEM] * 6 + [ANY] * 5,
        out_specs=(VMEM,) * (matrices + 3) + (ANY,) * 6,
        scratch_shapes=[pltpu.VMEM((matrices, depth, piece, columns), LOW)] * 3
        + TensorScatter.scratch(rows, width)[:3]
        + [
            pltpu.VMEM((rows, width), FULL), pltpu.VMEM((rows, width), LOW),
            pltpu.VMEM(vectors.shape, FULL), pltpu.VMEM((2 * depth - 1,) + vectors.shape[1:], FULL),
            pltpu.VMEM(vectors.shape[1:], FULL), pltpu.VMEM((3,) + vectors.shape[1:], FULL),
            pltpu.VMEM((2, seen, tile), LOW), pltpu.VMEM((tile, seen), LOW),
            pltpu.VMEM((2, seen, units), LOW), pltpu.VMEM((units, seen), LOW),
            pltpu.VMEM((2, 2, local, tile, hidden), FULL), pltpu.VMEM((2, 2, local, tile, hidden), LOW),
            pltpu.VMEM((2, local, hidden, tile), FULL), pltpu.VMEM((2, local, hidden, tile), LOW),
            dma(matrices, depth), dma(2, matrices, depth), dma(2, matrices, depth),
            dma(3), dma(3), dma(4), dma(3), dma(4), dma(3),
            dma(2 * depth - 1), dma(2 * depth - 1), dma(3), dma(3),
            dma(2), dma(2), dma(3, 2), dma(3, width // tile), dma(3, width // tile), dma(1),
        ],
        compiler_params=comm_params(number),
    )(*parts, normed_part, tokens, state_cot, scale, gain, out, vectors, normed, grads, gated, gate_grad, up_grad)
    return results[:matrices], results[matrices:]


def body(
    groups, parts,
    tokens, documents, routes, norm1_gain, q_gain, k_gain, w_query, w_key, w_value, w_out, norm2_gain, router_w,
    w_gate, w_up, w_down, out_grad,
):
    row_count, width = tokens.shape
    local_experts, _, hidden = w_gate.shape
    experts = local_experts * groups
    chain = LENGTH // row_count
    if not (parts == 4 and groups % 2 == 0 and experts <= min(16, 2 * TOP) and 2 * w_query.shape[1] <= 14 * HD and chain == 4 and 4 * row_count == LENGTH and WINDOW == 2 * row_count):
        return body_routed(
            tokens, documents, routes, norm1_gain, q_gain, k_gain, w_query, w_key, w_value, w_out, norm2_gain, router_w,
            w_gate, w_up, w_down, out_grad,
        )
    depth = groups // 2
    rows = row_count // parts
    seen = groups * row_count // 2
    heads = w_query.shape[1] // HD
    group, part = lax.axis_index("expert"), lax.axis_index("tensor")
    core = part % 2

    def quarter(array):
        return lax.dynamic_slice_in_dim(array, part * rows, rows, 0)

    def across(vector):
        return vector.reshape(1, -1)

    positions = group * row_count + jnp.arange(row_count, dtype=jnp.int32)
    cosine, sine = (table[:, 0, :] for table in rope_tables(positions % LENGTH))
    sine = jnp.concatenate([-sine[:, : HD // 2], sine[:, HD // 2 :]], axis=1)
    docs = jnp.broadcast_to(documents[None, :], (8, row_count))
    picked = jnp.any(quarter(routes)[:, :, None] == jnp.arange(128, dtype=jnp.int32)[None, None, :], axis=1).astype(FULL)
    router_wide = jnp.pad(router_w, ((0, 0), (0, 128 - experts)))
    own_grad = quarter(out_grad)
    query_gain, key_gain = across(q_gain), across(k_gain)
    (
        normed_one, query_raw, key_raw, queries, kv_all, key_docs, scales, attended, logs, state, normed_two, router_probs, gates,
        all_grad,
    ) = run_attention(
        tokens, (w_query, w_key, w_value, w_out), own_grad, (across(norm1_gain), query_gain, key_gain), (cosine, sine), docs,
        across(norm2_gain), router_wide, picked, depth, chain, local_experts, 3,
    )

    normed_two_grad, gate_cots, all_normed, gated, gate_pre_grad, up_pre_grad, produced = run_experts(
        normed_two, gates, all_grad, w_gate, w_up, w_down, 5
    )
    units = 2 * local_experts * hidden
    all_normed, all_grad = all_normed.reshape(seen, width), all_grad.reshape(seen, width)
    gated, gate_pre_grad, up_pre_grad = (a.reshape(seen, units) for a in (gated, gate_pre_grad, up_pre_grad))

    (
        state_cot, router_grad, norm2_grad, q_gain_local, k_gain_local, expert_mix, normed_part, *pieces
    ) = run_attention_back(
        (normed_two_grad, gate_cots, router_probs, picked, state, across(norm2_gain), router_wide, normed_two, own_grad),
        (queries, kv_all, attended, logs, key_docs, docs, query_raw, key_raw, query_gain, key_gain, cosine, sine, scales),
        (w_out,), produced, normed_one, (w_query, w_key, w_value), chain, local_experts, experts, 10,
    )
    own_inputs = quarter(tokens).astype(FULL)
    own_scale = lax.rsqrt(jnp.mean(own_inputs * own_inputs, axis=-1, keepdims=True) + NORM_EPSILON)

    vectors = jnp.concatenate(
        [router_grad, jnp.zeros((17 - experts, width), FULL), norm2_grad[:1]], axis=0
    ).reshape(18, groups, width // groups).transpose(1, 0, 2)
    gains = jnp.concatenate([q_gain_local[0].reshape(heads, HD), k_gain_local[0].reshape(heads, HD)], axis=0)
    gains = jnp.pad(gains, ((0, 14 - 2 * heads), (0, width // groups - HD)))
    vectors = jnp.concatenate([vectors, jnp.broadcast_to(gains[None], (groups,) + gains.shape)], axis=1)
    sums, (input_grad, output, vector_sum, gate_own, up_own, down_own, gate_other, up_other, down_other) = run_gradients(
        pieces, normed_part, quarter(tokens), state_cot, own_scale,
        norm1_gain[None], (state + expert_mix).astype(LOW), vectors, all_normed, all_grad, gated, gate_pre_grad, up_pre_grad,
        local_experts, 14,
    )
    own_columns = group * (HD // groups)
    return (
        output.reshape(row_count, width),
        input_grad.reshape(row_count, width).astype(FULL),
        vector_sum[16],
        lax.dynamic_slice(vector_sum, (18, own_columns), (heads, HD // groups)),
        lax.dynamic_slice(vector_sum, (18 + heads, own_columns), (heads, HD // groups)),
        sums[2],
        sums[3],
        sums[1],
        sums[0].T,
        vector_sum[17],
        vector_sum[:experts].T,
        gate_own + gate_other.astype(FULL),
        up_own + up_other.astype(FULL),
        down_own + down_other.astype(FULL),
    )


def solution(mesh):
    placed = (
        P("expert", None),
        P("expert"),
        P("expert", None),
        P(),
        P("tensor", None),
        P("tensor", None),
        P(None, "tensor"),
        P(None, "tensor"),
        P(None, "tensor"),
        P("tensor", None),
        P(),
        P(),
        P("expert", None, "tensor"),
        P("expert", None, "tensor"),
        P("expert", "tensor", None),
        P("expert", None),
    )
    return jax.shard_map(
        functools.partial(body, mesh.shape["expert"], mesh.shape["tensor"]),
        mesh=mesh,
        in_specs=placed,
        out_specs=(
            P("expert", None),
            P("expert", None),
            P("expert"),
            P("tensor", "expert"),
            P("tensor", "expert"),
            P("expert", "tensor"),
            P("expert", "tensor"),
            P("expert", "tensor"),
            P("tensor", "expert"),
            P("expert"),
            P("expert", None),
            P("expert", None, "tensor"),
            P("expert", None, "tensor"),
            P("expert", "tensor", None),
        ),
        check_vma=False,
    )
```

```python
import functools

import jax
import jax.numpy as jnp
from jax import lax
from jax.experimental import pallas as pl
from jax.experimental.pallas import tpu as pltpu
from jax.sharding import PartitionSpec as P

HD = 128
TOP = 8
WINDOW = 1024
LENGTH = 2048


NORM_EPSILON = 1e-05
HIGHEST_PRECISION = lax.Precision.HIGHEST


def for_sending(value):
    return jax.tree.map(lambda a: a.astype(jnp.bfloat16) if a.dtype == jnp.float32 else a, value)


def shifted(value, axis, steps):
    count = lax.axis_size(axis)
    initial, last = (max(0, -steps), min(count, count - steps))
    return lax.ppermute(value, axis, [(source, source + steps) for source in range(initial, last)])


def rope_tables(positions):
    half_width = HD // 2
    frequency = 10000.0 ** (-jnp.arange(half_width, dtype=jnp.float32) * 2.0 / HD)
    angles = positions.astype(jnp.float32)[:, None] * frequency[None, :]
    angles = jnp.concatenate([angles, angles], axis=-1)
    return (jnp.cos(angles)[:, None, :], jnp.sin(angles)[:, None, :])


def rotate(values, cosine, sine):
    half_width = values.shape[-1] // 2
    turned = jnp.concatenate([-values[..., half_width:], values[..., :half_width]], axis=-1)
    return values * cosine + turned * sine


def rotate_back(grads, cosine, sine):
    half_width = grads.shape[-1] // 2
    scaled = grads * sine
    turned = jnp.concatenate([scaled[..., half_width:], -scaled[..., :half_width]], axis=-1)
    return grads * cosine + turned


def previous_block(pieces):
    return jax.tree.map(
        lambda part, own: part.astype(own.dtype), shifted(for_sending(pieces), "expert", 1), pieces
    )


def following_block(pieces):
    return shifted((for_sending(pieces[0]), for_sending(pieces[1])), "expert", -1)


def body_routed(
    tokens,
    documents,
    routes,
    norm1_gain,
    q_gain,
    k_gain,
    w_query,
    w_key,
    w_value,
    w_out,
    norm2_gain,
    router_w,
    w_gate,
    w_up,
    w_down,
    out_grad,
):
    row_count, model_width = tokens.shape
    groups = lax.axis_size("expert")
    local_experts = w_gate.shape[0]
    experts = local_experts * groups
    capacity = 2 * row_count * TOP // experts
    slots_group = local_experts * capacity
    heads = w_query.shape[1] // HD
    score_scale = HD ** (-0.5)
    first_row = lax.axis_index("expert") * row_count
    positions = first_row + jnp.arange(row_count, dtype=jnp.int32)
    cosine, sine = rope_tables(positions % LENGTH)
    inputs = tokens.astype(jnp.float32)
    scale_one = lax.rsqrt(jnp.mean(inputs * inputs, axis=-1, keepdims=True) + NORM_EPSILON)
    normed_one = (inputs * scale_one * norm1_gain).astype(jnp.bfloat16)
    query_raw = jnp.dot(normed_one, w_query, preferred_element_type=jnp.float32)
    key_raw = jnp.dot(normed_one, w_key, preferred_element_type=jnp.float32)
    values = jnp.dot(normed_one, w_value, preferred_element_type=jnp.float32).astype(jnp.bfloat16)
    query_square, key_square = lax.psum(
        (jnp.sum(query_raw * query_raw, axis=-1), jnp.sum(key_raw * key_raw, axis=-1)), "tensor"
    )
    query_scale = lax.rsqrt(query_square / model_width + NORM_EPSILON)[:, None]
    key_scale = lax.rsqrt(key_square / model_width + NORM_EPSILON)[:, None]
    query_gain = q_gain.reshape(-1)
    key_gain = k_gain.reshape(-1)
    queries = rotate(
        (query_raw * query_scale * query_gain).reshape(row_count, heads, HD), cosine, sine
    ).astype(jnp.bfloat16)
    key_heads = rotate(
        (key_raw * key_scale * key_gain).reshape(row_count, heads, HD), cosine, sine
    ).astype(jnp.bfloat16)
    value_heads = values.reshape(row_count, heads, HD)
    labels = jnp.stack([documents // 256, documents % 256]).astype(jnp.bfloat16)
    previous_one = previous_block((key_heads, value_heads, labels))
    previous_two = previous_block(previous_one)
    all_keys = jnp.concatenate([previous_two[0], previous_one[0], key_heads], axis=0)
    all_values = jnp.concatenate([previous_two[1], previous_one[1], value_heads], axis=0)
    all_labels = jnp.concatenate([previous_two[2], previous_one[2], labels], axis=1)
    key_pos = first_row - 2 * row_count + jnp.arange(3 * row_count, dtype=jnp.int32)
    same_doc = (all_labels[0][None, :] == labels[0][:, None]) & (
        all_labels[1][None, :] == labels[1][:, None]
    )
    allowed = (
        same_doc
        & (key_pos[None, :] <= positions[:, None])
        & (positions[:, None] - key_pos[None, :] < WINDOW)
        & (key_pos[None, :] >= 0)
    )

    def masked_scores():
        raw_scores = (
            jnp.einsum("qhd,khd->hqk", queries, all_keys, preferred_element_type=jnp.float32)
            * score_scale
        )
        return jnp.where(allowed[None], raw_scores, -1e30)

    scores = masked_scores()
    highest = jnp.max(scores, axis=-1, keepdims=True)
    weights = jnp.where(allowed[None], jnp.exp(scores - highest), 0.0)
    denominator = jnp.sum(weights, axis=-1, keepdims=True)
    log_total = highest + jnp.log(denominator)
    attn_probs = weights / denominator
    attended = jnp.einsum(
        "hqk,khd->qhd",
        attn_probs.astype(jnp.bfloat16),
        all_values,
        preferred_element_type=jnp.float32,
    )
    attended = attended.reshape(row_count, -1).astype(jnp.bfloat16)
    attention = lax.psum(jnp.dot(attended, w_out, preferred_element_type=jnp.float32), "tensor")
    state = inputs + attention
    scale_two = lax.rsqrt(jnp.mean(state * state, axis=-1, keepdims=True) + NORM_EPSILON)
    normed_two = (state * scale_two * norm2_gain).astype(jnp.bfloat16)
    router_probs = jax.nn.softmax(
        jnp.dot(normed_two, router_w, preferred_element_type=jnp.float32), axis=-1
    )
    chosen = (routes[:, :, None] == jnp.arange(experts, dtype=jnp.int32)[None, None, :]).astype(
        jnp.float32
    )
    gates = jnp.sum(chosen * router_probs[:, None, :], axis=-1)
    flat_routes = routes.reshape(-1)
    onehot = (flat_routes[:, None] == jnp.arange(experts, dtype=jnp.int32)[None, :]).astype(
        jnp.int32
    )
    slot_index = jnp.sum(jnp.cumsum(onehot, axis=0) * onehot, axis=1) - 1
    target = flat_routes * capacity + slot_index
    source = (
        jnp.full((experts * capacity,), -1, jnp.int32)
        .at[target]
        .set(jnp.arange(row_count * TOP, dtype=jnp.int32))
    )
    live_slot = source >= 0
    pick_index = jnp.maximum(source, 0)
    send_rows = jnp.where(
        live_slot[:, None], normed_two[pick_index // TOP], jnp.zeros((), jnp.bfloat16)
    ).reshape(groups, slots_group, model_width)
    grad_float = out_grad.astype(jnp.float32)
    pick_grads = (
        (gates[:, :, None] * grad_float[:, None, :])
        .astype(jnp.bfloat16)
        .reshape(row_count * TOP, model_width)
    )
    send_grads = jnp.where(
        live_slot[:, None], pick_grads[pick_index], jnp.zeros((), jnp.bfloat16)
    ).reshape(groups, slots_group, model_width)
    arrived = lax.all_to_all(send_rows, "expert", split_axis=0, concat_axis=0, tiled=True)
    stacked = arrived.reshape(groups, local_experts, capacity, model_width)
    gate_pre = jnp.einsum("secd,edf->secf", stacked, w_gate, preferred_element_type=jnp.float32)
    up_pre = jnp.einsum("secd,edf->secf", stacked, w_up, preferred_element_type=jnp.float32)
    activated = jax.nn.silu(gate_pre)
    inner_act = (activated * up_pre).astype(jnp.bfloat16)
    produced = jnp.einsum(
        "secf,efd->secd", inner_act, w_down, preferred_element_type=jnp.float32
    ).astype(jnp.bfloat16)
    returned = lax.all_to_all(
        produced.reshape(groups, slots_group, model_width),
        "expert",
        split_axis=0,
        concat_axis=0,
        tiled=True,
    )
    back_rows = (
        returned.reshape(experts * capacity, model_width)[target]
        .reshape(row_count, TOP, model_width)
        .astype(jnp.float32)
    )
    expert_part = jnp.sum(gates[:, :, None] * back_rows, axis=1)
    expert_mix = lax.psum(expert_part.astype(jnp.bfloat16), "tensor").astype(jnp.float32)
    output = (state + expert_mix).astype(jnp.bfloat16)
    gate_part = jnp.sum(grad_float[:, None, :] * back_rows, axis=-1)
    arrived_grad = lax.all_to_all(send_grads, "expert", split_axis=0, concat_axis=0, tiled=True)
    slot_grad = arrived_grad.reshape(groups, local_experts, capacity, model_width)
    w_down_grad = jnp.einsum(
        "secf,secd->efd", inner_act, slot_grad, preferred_element_type=jnp.float32
    )
    inner_grad = jnp.einsum("secd,efd->secf", slot_grad, w_down, preferred_element_type=jnp.float32)
    logistic = jax.nn.sigmoid(gate_pre)
    gate_pre_grad = (inner_grad * up_pre * logistic * (1.0 + gate_pre * (1.0 - logistic))).astype(
        jnp.bfloat16
    )
    up_pre_grad = (inner_grad * activated).astype(jnp.bfloat16)
    w_gate_grad = jnp.einsum(
        "secd,secf->edf", stacked, gate_pre_grad, preferred_element_type=jnp.float32
    )
    w_up_grad = jnp.einsum(
        "secd,secf->edf", stacked, up_pre_grad, preferred_element_type=jnp.float32
    )
    row_grad = jnp.einsum(
        "secf,edf->secd", gate_pre_grad, w_gate, preferred_element_type=jnp.float32
    )
    row_grad = (
        row_grad
        + jnp.einsum("secf,edf->secd", up_pre_grad, w_up, preferred_element_type=jnp.float32)
    ).astype(jnp.bfloat16)
    grad_back = lax.all_to_all(
        row_grad.reshape(groups, slots_group, model_width),
        "expert",
        split_axis=0,
        concat_axis=0,
        tiled=True,
    )
    grad_picks = (
        grad_back.reshape(experts * capacity, model_width)[target]
        .reshape(row_count, TOP, model_width)
        .astype(jnp.float32)
    )
    normed_part = jnp.sum(grad_picks, axis=1)
    normed_two_grad, gate_cot = lax.psum((normed_part, gate_part), "tensor")
    prob_cot = jnp.sum(gate_cot[:, :, None] * chosen, axis=1)
    logit_cot = router_probs * (prob_cot - jnp.sum(router_probs * prob_cot, axis=-1, keepdims=True))
    router_float = router_w.astype(jnp.float32)
    normed_two_grad = normed_two_grad + jnp.einsum(
        "te,de->td", logit_cot, router_float, precision=HIGHEST_PRECISION
    )
    router_grad = jnp.einsum(
        "td,te->de", normed_two.astype(jnp.float32), logit_cot, precision=HIGHEST_PRECISION
    )
    norm2_grad = jnp.sum(normed_two_grad * state * scale_two, axis=0)
    inner_two = jnp.sum(normed_two_grad * norm2_gain * state, axis=-1, keepdims=True)
    state_cot = (
        grad_float
        + scale_two * norm2_gain * normed_two_grad
        - state * scale_two**3 * inner_two / model_width
    )
    state_low = state_cot.astype(jnp.bfloat16)
    w_out_grad = jnp.einsum("tf,td->fd", attended, state_low, preferred_element_type=jnp.float32)
    attended_cot = (
        jnp.einsum("td,fd->tf", state_low, w_out, preferred_element_type=jnp.float32)
        .astype(jnp.bfloat16)
        .reshape(row_count, heads, HD)
    )
    scores = masked_scores()
    attn_probs = jnp.where(allowed[None], jnp.exp(scores - log_total), 0.0)
    value_cot_all = jnp.einsum(
        "hqk,qhd->khd",
        attn_probs.astype(jnp.bfloat16),
        attended_cot,
        preferred_element_type=jnp.float32,
    )
    prob_grad = jnp.einsum(
        "qhd,khd->hqk", attended_cot, all_values, preferred_element_type=jnp.float32
    )
    delta = jnp.sum(attn_probs * prob_grad, axis=-1, keepdims=True)
    score_cot = (attn_probs * (prob_grad - delta)).astype(jnp.bfloat16)
    query_cot = (
        jnp.einsum("hqk,khd->qhd", score_cot, all_keys, preferred_element_type=jnp.float32)
        * score_scale
    )
    key_cot_all = (
        jnp.einsum("hqk,qhd->khd", score_cot, queries, preferred_element_type=jnp.float32)
        * score_scale
    )
    carried = following_block((key_cot_all[:row_count], value_cot_all[:row_count]))
    carried = following_block(
        (
            key_cot_all[row_count : 2 * row_count] + carried[0],
            value_cot_all[row_count : 2 * row_count] + carried[1],
        )
    )
    key_cot = key_cot_all[2 * row_count :] + carried[0]
    value_cot = value_cot_all[2 * row_count :] + carried[1]
    query_norm_cot = rotate_back(query_cot, cosine, sine).reshape(row_count, -1)
    key_norm_cot = rotate_back(key_cot, cosine, sine).reshape(row_count, -1)
    q_gain_local = jnp.sum(query_norm_cot * query_raw * query_scale, axis=0).reshape(heads, HD)
    k_gain_local = jnp.sum(key_norm_cot * key_raw * key_scale, axis=0).reshape(heads, HD)
    query_inner, key_inner = lax.psum(
        (
            jnp.sum(query_norm_cot * query_gain * query_raw, axis=-1),
            jnp.sum(key_norm_cot * key_gain * key_raw, axis=-1),
        ),
        "tensor",
    )
    query_raw_cot = (
        query_scale * query_gain * query_norm_cot
        - query_raw * query_scale**3 * query_inner[:, None] / model_width
    ).astype(jnp.bfloat16)
    key_raw_cot = (
        key_scale * key_gain * key_norm_cot
        - key_raw * key_scale**3 * key_inner[:, None] / model_width
    ).astype(jnp.bfloat16)
    value_low = value_cot.reshape(row_count, -1).astype(jnp.bfloat16)
    w_query_local = jnp.einsum(
        "td,tf->df", normed_one, query_raw_cot, preferred_element_type=jnp.float32
    )
    w_key_local = jnp.einsum(
        "td,tf->df", normed_one, key_raw_cot, preferred_element_type=jnp.float32
    )
    w_value_local = jnp.einsum(
        "td,tf->df", normed_one, value_low, preferred_element_type=jnp.float32
    )
    normed_part_one = jnp.einsum(
        "tf,df->td", query_raw_cot, w_query, preferred_element_type=jnp.float32
    )
    normed_part_one = normed_part_one + jnp.einsum(
        "tf,df->td", key_raw_cot, w_key, preferred_element_type=jnp.float32
    )
    normed_part_one = normed_part_one + jnp.einsum(
        "tf,df->td", value_low, w_value, preferred_element_type=jnp.float32
    )
    normed_one_grad = lax.psum(normed_part_one.astype(jnp.bfloat16), "tensor").astype(jnp.float32)
    norm1_grad = jnp.sum(normed_one_grad * inputs * scale_one, axis=0)
    inner_one = jnp.sum(normed_one_grad * norm1_gain * inputs, axis=-1, keepdims=True)
    input_grad = (
        state_cot
        + scale_one * norm1_gain * normed_one_grad
        - inputs * scale_one**3 * inner_one / model_width
    )
    summed = (
        lax.psum_scatter(
            w_query_local.astype(jnp.bfloat16), "expert", scatter_dimension=0, tiled=True
        ).astype(jnp.float32),
        lax.psum_scatter(
            w_key_local.astype(jnp.bfloat16), "expert", scatter_dimension=0, tiled=True
        ).astype(jnp.float32),
        lax.psum_scatter(
            w_value_local.astype(jnp.bfloat16), "expert", scatter_dimension=0, tiled=True
        ).astype(jnp.float32),
        lax.psum_scatter(
            w_out_grad.astype(jnp.bfloat16), "expert", scatter_dimension=1, tiled=True
        ).astype(jnp.float32),
        lax.psum_scatter(
            router_grad.astype(jnp.bfloat16), "expert", scatter_dimension=0, tiled=True
        ).astype(jnp.float32),
        lax.psum_scatter(
            norm1_grad.astype(jnp.bfloat16), "expert", scatter_dimension=0, tiled=True
        ).astype(jnp.float32),
        lax.psum_scatter(
            norm2_grad.astype(jnp.bfloat16), "expert", scatter_dimension=0, tiled=True
        ).astype(jnp.float32),
        lax.psum_scatter(
            q_gain_local.astype(jnp.bfloat16), "expert", scatter_dimension=1, tiled=True
        ).astype(jnp.float32),
        lax.psum_scatter(
            k_gain_local.astype(jnp.bfloat16), "expert", scatter_dimension=1, tiled=True
        ).astype(jnp.float32),
    )
    return (
        output,
        input_grad,
        summed[5],
        summed[7],
        summed[8],
        summed[0],
        summed[1],
        summed[2],
        summed[3],
        summed[6],
        summed[4],
        w_gate_grad,
        w_up_grad,
        w_down_grad,
    )


MESH = pl.DeviceIdType.MESH
ANY = pl.BlockSpec(memory_space=pl.ANY)
VMEM = pl.BlockSpec(memory_space=pltpu.VMEM)
VMEM_BYTES = 62 * 1024 * 1024
LOW = jnp.bfloat16
FULL = jnp.float32


def place():
    group, part = lax.axis_index("expert"), lax.axis_index("tensor")
    return group // 2, group % 2, part // 2, part % 2


def device(z, x, y, core):
    return (2 * z + x, 2 * y + core)


def swapped(index, step):
    result, bit = index, 1
    while bit <= step:
        if step & bit:
            result = result + bit - 2 * bit * ((index // bit) % 2)
        bit *= 2
    return result


def greet(partners):
    barrier = pltpu.get_barrier_semaphore()
    for partner in partners:
        pl.semaphore_signal(barrier, inc=1, device_id=partner, device_id_type=MESH)
    pl.semaphore_wait(barrier, len(partners))


def remote(source, target, send, arrive, to):
    return pltpu.make_async_remote_copy(
        src_ref=source, dst_ref=target, send_sem=send, recv_sem=arrive, device_id=to, device_id_type=MESH
    )


def dma(*shape):
    return pltpu.SemaphoreType.DMA(shape)


def comm_params(number):
    return pltpu.CompilerParams(collective_id=number, has_side_effects=True, vmem_limit_bytes=VMEM_BYTES)


def add_rows(target, sources, rows, step=16):
    @pl.loop(0, rows // step)
    def _(index):
        part = pl.ds(index * step, step)
        total = sources[0][part].astype(FULL)
        for source in sources[1:]:
            total = total + source[part].astype(FULL)
        target[part] = total.astype(target.dtype)


class Copies:
    def __init__(self):
        self.open = []

    def start(self, copy):
        copy.start()
        self.open.append((copy, set()))
        return copy

    def once(self, copy, what):
        done = next(done for entry, done in self.open if entry is copy)
        new = what not in done
        done.add(what)
        return new

    def arrived(self, copy):
        if self.once(copy, "arrived"):
            copy.wait_recv()

    def sent(self, copy):
        if self.once(copy, "sent"):
            copy.wait_send()

    def finish(self):
        for copy, done in self.open:
            if "sent" not in done:
                copy.wait_send()
            if "arrived" not in done:
                copy.wait_recv()


class Gather:
    def __init__(self, copies, block, target, rows, z_send, z_recv, p_send, p_recv, c_send, c_recv):
        self.copies, self.block, self.target, self.rows = copies, block, target, rows
        self.z_send, self.z_recv, self.p_send, self.p_recv = z_send, z_recv, p_send, p_recv
        self.c_send, self.c_recv = c_send, c_recv
        z, x, y, core = place()
        self.over_x, self.over_y = device(z, 1 - x, y, core), device(z, x, 1 - y, core)
        self.here, self.x_place, self.y_place = 2 * x + y, 2 * (1 - x) + y, 2 * x + 1 - y
        self.far = 2 * (1 - x) + 1 - y
        self.column = [device(swapped(z, step), x, y, core) for step in range(target.shape[0])]
        self.along, self.planes, self.diagonals, self.shared = {}, {}, {}, {}
        edge = rows * 3 // 8
        self.middle = (edge, rows - 2 * edge)
        self.halves = {0: ((0, rows // 2), (rows // 2, rows // 2)), 1: ((0, edge), (rows - edge, edge))}

    def at(self, step, spot, span):
        first, count = span
        return self.target.at[step, pl.ds(pl.multiple_of(spot * self.rows + first, 16), count)]

    def lift(self, step):
        low, whole = step & -step, (0, self.rows)
        source = self.block if step == low else self.at(step - low, self.here, whole)
        self.along[step] = self.copies.start(
            remote(source, self.at(step, self.here, whole), self.z_send.at[step], self.z_recv.at[step], self.column[low])
        )

    def spread(self, step):
        if step:
            self.copies.arrived(self.along[step])
            bit = 1
            while bit < step & -step:
                self.lift(step | bit)
                bit *= 2
        planes = []
        for number, (to, part) in enumerate([(self.over_x, 0), (self.over_y, 1), (self.over_x, 1), (self.over_y, 0)]):
            span = self.halves[step % 2][part]
            here = self.at(step, self.here, span)
            source = here if step else self.block.at[pl.ds(*span)]
            planes.append(self.copies.start(remote(source, here, self.p_send.at[step, number], self.p_recv.at[step, number], to)))
        self.planes[step] = planes

    def turn(self, step):
        passed = []
        for part, spot, to in ((0, self.x_place, self.over_y), (1, self.y_place, self.over_x)):
            self.copies.arrived(self.planes[step][part])
            here = self.at(step, spot, self.halves[step % 2][part])
            passed.append(
                self.copies.start(remote(here, here, self.p_send.at[step, 4 + part], self.p_recv.at[step, 4 + part], to))
            )
        self.diagonals[step] = passed

    def share(self, step):
        self.complete(step)
        copies = []
        for number, spot in enumerate((self.x_place, self.y_place, self.far)):
            copies.append(
                self.copies.start(
                    remote(
                        self.at(step, spot, self.middle), self.at(step + 1, spot, self.middle),
                        self.c_send.at[step // 2, number], self.c_recv.at[step // 2, number], self.column[1],
                    )
                )
            )
        self.shared[step + 1] = copies

    def complete(self, step):
        for copy in self.planes[step] + self.diagonals[step] + self.shared.get(step, []):
            self.copies.arrived(copy)

    @staticmethod
    def scratch(depth):
        return [dma(depth), dma(depth), dma(depth, 6), dma(depth, 6), dma(depth // 2, 3), dma(depth // 2, 3)]


class Scatter:
    def __init__(self, copies, work, diagonal, from_x, from_y, from_z, rows, send, recv, middle=None):
        self.copies, self.work, self.rows, self.send, self.recv = copies, work, rows, send, recv
        self.diagonal, self.from_x, self.from_y, self.from_z = diagonal, from_x, from_y, from_z
        z, x, y, core = place()
        self.over_x, self.over_y = device(z, 1 - x, y, core), device(z, x, 1 - y, core)
        self.here, self.x_place, self.y_place = 2 * x + y, 2 * (1 - x) + y, 2 * x + 1 - y
        self.far = 2 * (1 - x) + 1 - y
        self.column = [device(swapped(z, step), x, y, core) for step in range(work.shape[0])]
        self.corners, self.sides, self.along, self.shared, self.middle = {}, {}, {}, {}, middle
        edge, half = rows * 3 // 8, rows // 2
        self.center = (edge, rows - 2 * edge)
        self.halves = {0: ((0, half), (half, half)), 1: ((0, half), (half, half))}
        self.pieces = {0: ((0, rows),), 1: ((0, rows),)}
        if middle:
            self.halves[1] = self.pieces[1] = ((0, edge), (rows - edge, edge))

    def at(self, step, spot, span):
        first, count = span
        return self.work.at[step, pl.ds(pl.multiple_of(spot * self.rows + first, 16), count)]

    def copy(self, step, number, source, target, to):
        return self.copies.start(remote(source, target, self.send.at[step, number], self.recv.at[step, number], to))

    def share(self, step):
        landed, send, recv = self.middle
        self.shared[step - 1] = [
            self.copies.start(
                remote(
                    self.at(step, spot, self.center), landed.at[step // 2, spot],
                    send.at[step // 2, spot], recv.at[step // 2, spot], self.column[1],
                )
            )
            for spot in range(4)
        ]

    def corner(self, step):
        for spot, copy in enumerate(self.shared.get(step, [])):
            self.copies.arrived(copy)
            mine = self.at(step, spot, self.center)
            add_rows(mine, [mine, self.middle[0].at[step // 2, spot]], self.center[1])
        first, second = self.halves[step % 2]
        self.corners[step] = (
            self.copy(step, 0, self.at(step, self.far, first), self.diagonal.at[step, pl.ds(*first)], self.over_y),
            self.copy(step, 1, self.at(step, self.far, second), self.diagonal.at[step, pl.ds(*second)], self.over_x),
        )

    def side(self, step):
        first, second = self.halves[step % 2]
        via_y, via_x = self.corners[step]

        def to_x(number, span):
            return self.copy(step, number, self.at(step, self.x_place, span), self.from_x.at[step, pl.ds(*span)], self.over_x)

        def to_y(number, span):
            return self.copy(step, number, self.at(step, self.y_place, span), self.from_y.at[step, pl.ds(*span)], self.over_y)

        sides = [to_x(2, second), to_y(3, first)]
        self.copies.arrived(via_y)
        mine = self.at(step, self.x_place, first)
        add_rows(mine, [mine, self.diagonal.at[step, pl.ds(*first)]], first[1])
        sides.append(to_x(4, first))
        self.copies.arrived(via_x)
        mine = self.at(step, self.y_place, second)
        add_rows(mine, [mine, self.diagonal.at[step, pl.ds(*second)]], second[1])
        sides.append(to_y(5, second))
        self.sides[step] = sides

    def climb(self, step):
        for copy in self.sides[step]:
            self.copies.arrived(copy)
        if step:
            self.along[step] = []
            for number, span in enumerate(self.pieces[step % 2]):
                mine, part = self.at(step, self.here, span), pl.ds(*span)
                add_rows(mine, [mine, self.from_x.at[step, part], self.from_y.at[step, part]], span[1])
                self.along[step].append(self.copy(step, 6 + number, mine, self.from_z.at[step, part], self.column[step]))

    def result(self, target, more=()):
        for copies in self.along.values():
            for copy in copies:
                self.copies.arrived(copy)
        for span in [*self.halves[1], self.center] if self.middle else self.pieces[0]:
            part = pl.ds(*span)
            steps = [step for step in self.along if not (self.middle and span is self.center and step % 2)]
            terms = [self.at(0, self.here, span), self.from_x.at[0, part], self.from_y.at[0, part]]
            terms += [self.from_z.at[step, part] for step in steps] + [term.at[part] for term in more]
            add_rows(target.at[part], terms, span[1])

    @staticmethod
    def scratch(depth, rows, width):
        return [pltpu.VMEM((depth, rows, width), LOW)] * 4 + [dma(depth, 8), dma(depth, 8)]


def experts_kernel(
    depth, rows, local, hidden,
    x_ref, gates_ref, grad_ref, gate_ref, up_ref, down_ref,
    sum_ref, cots_ref, normed_ref, gated_ref, gate_grad_ref, up_grad_ref, produced_ref,
    wg, wu, wd, x_all, grads, work, y_out, gated, gate_grad, up_grad, gates, gate_wide, cots, cot_rows,
    diagonal, from_x, from_y, from_z, r_send, r_recv,
    z_send, z_recv, p_send, p_recv, c_send, c_recv, s_send, s_recv, w_send, w_recv, w_load, g_load, saves, local_sem,
):
    z, x, y, core = place()
    here, sibling = 2 * x + y, device(z, x, y, 1 - core)
    others = [
        (step, turn, (swapped(z, step), swapped(x, turn // 2), swapped(y, turn % 2)))
        for step in range(depth)
        for turn in range(4)
        if step or turn
    ]
    greet([device(*other, core) for _, _, other in others] + [sibling])
    copies = Copies()
    smalls = []
    for step, turn, other in others:
        oz, ox, oy = other
        smalls.append(
            copies.start(
                remote(
                    gates_ref.at[2 * oz + ox], gates.at[step, here], s_send.at[0, step, turn], s_recv.at[0, step, turn],
                    device(oz, ox, oy, core),
                )
            )
        )
    gather = Gather(copies, x_ref, x_all, rows, z_send, z_recv, p_send, p_recv, c_send, c_recv)
    gather.spread(0)
    gather.lift(1)
    gather.lift(2)
    plain = []

    def fetch(source, target, sem):
        copy = pltpu.make_async_copy(source, target, sem)
        copy.start()
        return copy

    plain.append(fetch(x_ref, gather.at(0, here, (0, rows)), local_sem.at[0]))
    weights = []
    for index in range(local):
        first = pl.multiple_of((core * local + index) * hidden, hidden)
        columns = pl.ds(first, hidden)
        for number, (source, target) in enumerate(
            [(gate_ref, wg.at[:, columns]), (up_ref, wu.at[:, columns]), (down_ref, wd.at[columns])]
        ):
            weights.append(copies.start(remote(source.at[index], target, w_send.at[number, index], w_recv.at[number, index], sibling)))
            plain.append(fetch(source.at[index], target, w_load.at[number, index]))
    plain.append(fetch(gates_ref.at[2 * z + x], gates.at[0, here], local_sem.at[1]))
    grad_copies = [fetch(grad_ref.at[0], grads.at[0], g_load.at[0])]
    scatter = Scatter(copies, work, diagonal, from_x, from_y, from_z, rows, r_send, r_recv)
    saving, producing, keeping = [], [], []
    wave_rows = 4 * rows
    lanes = lax.broadcasted_iota(jnp.int32, (wave_rows, 128), 1)

    def first_half(step):
        for copy in saving:
            copy.wait()
        saving.clear()
        for spot in range(4):
            padded = jnp.concatenate([gates[step, spot], jnp.zeros((120, 128), FULL)], axis=0)
            gate_wide[pl.ds(spot * rows, rows), :] = padded.T
        cots[...] = jnp.zeros_like(cots)
        grad_copies[step].wait()
        if step + 1 < depth:
            grad_copies.append(fetch(grad_ref.at[step + 1], grads.at[(step + 1) % 2], g_load.at[(step + 1) % 2]))
        grad = grads.at[step % 2]

        @pl.loop(0, 2 * local)
        def _(unit):
            columns = pl.ds(pl.multiple_of(unit * hidden, hidden), hidden)
            expert = lax.rem(unit, local)
            gate_pre = dot(x_all[step], wg[:, columns])
            up_pre = dot(x_all[step], wu[:, columns])
            back = dot_t(grad[...], wd[columns, :])
            logistic = 1.0 / (1.0 + jnp.exp(-gate_pre))
            activated = gate_pre * logistic
            inner = activated * up_pre
            cot = jnp.sum(inner * back, axis=-1, keepdims=True)
            cots[...] += jnp.where(lanes == expert, cot, 0.0)
            gate = jnp.sum(jnp.where(lanes == expert, gate_wide[...], 0.0), axis=-1, keepdims=True)
            gated[:, columns] = (gate * inner).astype(LOW)
            inner_grad = gate * back
            gate_grad[:, columns] = (inner_grad * up_pre * logistic * (1.0 + gate_pre * (1.0 - logistic))).astype(LOW)
            up_grad[:, columns] = (inner_grad * activated).astype(LOW)

        for spot in range(4):
            cot_rows[step, spot] = cots[pl.ds(spot * rows, rows), :].T[:8]
        for other_step, turn, (oz, ox, oy) in others:
            if other_step == step:
                copies.start(
                    remote(
                        cot_rows.at[step, 2 * ox + oy], cots_ref.at[step, here], s_send.at[1, step, turn], s_recv.at[1, step, turn],
                        device(oz, ox, oy, core),
                    )
                )
        for number, (source, target) in enumerate([(gated, gated_ref), (gate_grad, gate_grad_ref), (up_grad, up_grad_ref)]):
            saving.append(fetch(source, target.at[step], saves.at[number]))
        keeping.append(fetch(x_all.at[step], normed_ref.at[step], saves.at[4 + step]))

    def second_half(step):
        for copy in producing:
            copy.wait()
        producing.clear()
        tile = 512

        @pl.loop(0, x_all.shape[2] // tile)
        def _(index):
            columns = pl.ds(pl.multiple_of(index * tile, tile), tile)
            y_out[:, columns] = dot(gated[...], wd[:, columns]).astype(LOW)
            work[step, :, columns] = (dot_t(gate_grad[...], wg[columns, :]) + dot_t(up_grad[...], wu[columns, :])).astype(LOW)

        producing.append(fetch(y_out, produced_ref.at[step], saves.at[3]))

    gather.turn(0)
    gather.spread(1)
    gather.share(0)
    for copy in plain:
        copy.wait()
    for copy in weights + smalls:
        copies.arrived(copy)
    for step in range(depth):
        if step:
            gather.complete(step)
        first_half(step)
        if step + 1 < depth:
            gather.turn(step + 1)
        if step + 2 < depth:
            gather.spread(step + 2)
        if step == 1:
            gather.share(2)
        if step >= 2:
            scatter.side(step - 1)
        if step >= 3:
            scatter.climb(step - 2)
        second_half(step)
        if step:
            scatter.corner(step)
    scatter.corner(0)
    own_cots = fetch(cot_rows.at[0, here], cots_ref.at[0, here], local_sem.at[2])
    scatter.side(depth - 1)
    scatter.climb(depth - 2)
    scatter.side(0)
    scatter.climb(depth - 1)
    scatter.climb(0)
    scatter.result(sum_ref)
    own_cots.wait()
    for copy in saving + producing + keeping:
        copy.wait()
    copies.finish()


def run_experts(block, gates, grads, w_gate, w_up, w_down, number):
    depth, wave, width = grads.shape
    rows = wave // 4
    local, _, hidden = w_gate.shape
    units = 2 * local * hidden
    kept = jax.ShapeDtypeStruct((depth, wave, units), LOW)
    wide = jax.ShapeDtypeStruct((depth, wave, width), LOW)
    return pl.pallas_call(
        functools.partial(experts_kernel, depth, rows, local, hidden),
        out_shape=(
            jax.ShapeDtypeStruct((rows, width), FULL),
            jax.ShapeDtypeStruct((depth, 4, 8, 128), FULL),
            wide, kept, kept, kept, wide,
        ),
        in_specs=[ANY] * 6,
        out_specs=(VMEM, VMEM, ANY, ANY, ANY, ANY, ANY),
        scratch_shapes=[
            pltpu.VMEM((width, units), LOW), pltpu.VMEM((width, units), LOW), pltpu.VMEM((units, width), LOW),
            pltpu.VMEM((depth, wave, width), LOW), pltpu.VMEM((2, wave, width), LOW),
            pltpu.VMEM((depth, wave, width), LOW), pltpu.VMEM((wave, width), LOW),
            pltpu.VMEM((wave, units), LOW), pltpu.VMEM((wave, units), LOW), pltpu.VMEM((wave, units), LOW),
            pltpu.VMEM((depth, 4, 8, 128), FULL), pltpu.VMEM((wave, 128), FULL), pltpu.VMEM((wave, 128), FULL),
            pltpu.VMEM((depth, 4, 8, 128), FULL),
        ]
        + Scatter.scratch(depth, rows, width)
        + [
            *Gather.scratch(depth), dma(2, depth, 4), dma(2, depth, 4),
            dma(3, local), dma(3, local), dma(3, local), dma(2), dma(4 + depth), dma(3),
        ],
        compiler_params=comm_params(number),
    )(block, gates, grads, w_gate, w_up, w_down)


class TensorScatter:
    def __init__(self, copies, work, from_pair, from_y, send, recv):
        self.copies, self.work, self.from_pair, self.from_y, self.send, self.recv = copies, work, from_pair, from_y, send, recv
        z, x, self.y, self.core = place()
        self.sibling, self.over_y = device(z, x, self.y, 1 - self.core), device(z, x, 1 - self.y, self.core)
        self.rows = work.shape[2]

    def begin(self):
        self.pairs = []
        for turn in (1, 0):
            source = self.work.at[swapped(self.y, turn), 1 - self.core]
            self.pairs.append(
                self.copies.start(remote(source, self.from_pair.at[turn], self.send.at[turn], self.recv.at[turn], self.sibling))
            )

    def cross(self):
        self.copies.arrived(self.pairs[0])
        block = self.work.at[1 - self.y, self.core]
        add_rows(block, [block, self.from_pair.at[1]], self.rows)
        self.across = self.copies.start(remote(block, self.from_y, self.send.at[2], self.recv.at[2], self.over_y))

    def result(self, target):
        self.copies.arrived(self.pairs[1])
        self.copies.arrived(self.across)
        add_rows(target, [self.work.at[self.y, self.core], self.from_pair.at[0], self.from_y], self.rows)

    @staticmethod
    def scratch(rows, width):
        return [
            pltpu.VMEM((2, 2, rows, width), LOW),
            pltpu.VMEM((2, rows, width), LOW),
            pltpu.VMEM((rows, width), LOW),
            dma(3),
            dma(3),
        ]


class TensorGather:
    def __init__(self, copies, block, target, send, recv):
        self.copies, self.target, self.send, self.recv = copies, target, send, recv
        z, x, self.y, self.core = place()
        self.sibling, over_y = device(z, x, self.y, 1 - self.core), device(z, x, 1 - self.y, self.core)
        mine = target.at[self.y, self.core]
        self.across = copies.start(remote(block, mine, send.at[0], recv.at[0], over_y))
        self.near = copies.start(remote(block, mine, send.at[1], recv.at[1], self.sibling))
        self.own = pltpu.make_async_copy(block, mine, send.at[3])
        self.own.start()

    def cross(self):
        self.copies.arrived(self.across)
        block = self.target.at[1 - self.y, self.core]
        self.passed = self.copies.start(remote(block, block, self.send.at[2], self.recv.at[2], self.sibling))

    def finish(self):
        self.own.wait()
        self.copies.arrived(self.near)
        self.copies.arrived(self.passed)


def partners_of(depth):
    z, x, y, core = place()
    return [device(swapped(z, step), x, y, core) for step in range(1, depth)] + [
        device(z, 1 - x, y, core),
        device(z, x, 1 - y, core),
        device(z, x, y, 1 - core),
        device(swapped(z, 1), 1 - x, y, core),
    ]


def mask_bias(bias, key_docs, query_docs, length):
    blocks = bias.shape[0] // length

    @pl.loop(0, bias.shape[0] // 128)
    def _(index):
        part = pl.ds(pl.multiple_of(index * 128, 128), 128)
        key = index * 128 + lax.broadcasted_iota(jnp.int32, (128, length), 0) - (blocks - 1) * length
        query = lax.broadcasted_iota(jnp.int32, (128, length), 1)
        seen = (key_docs[part, :] == query_docs[0:1, :]) & (key <= query) & (query - key < WINDOW)
        bias[part, :] = jnp.where(seen, 0.0, -1e30).astype(bias.dtype)


def exchange(copies, mine, landed, send, recv, mates):
    return [
        copies.start(remote(mine, landed.at[number], send.at[number], recv.at[number], device(*mate)))
        for number, mate in enumerate(mates)
    ]


def mates_of():
    z, x, y, core = place()
    return [(z, x, swapped(y, turn // 2), swapped(core, turn % 2)) for turn in range(1, 4)]


def as_rows(columns):
    lanes = lax.broadcasted_iota(jnp.int32, (columns[0].shape[0], 128), 1)
    wide = jnp.zeros(lanes.shape, FULL)
    for index, column in enumerate(columns):
        wide = jnp.where(lanes == index, column, wide)
    return wide.T[:8]


def as_columns(rows_of_eight):
    length = rows_of_eight.shape[1]
    return jnp.concatenate([rows_of_eight, jnp.zeros((120, length), FULL)], axis=0).T


def attention_kernel(
    depth, rows, heads, chain, local,
    tokens_ref, wq_ref, wk_ref, wv_ref, wo_ref, grad_ref,
    gain1_ref, q_gain_ref, k_gain_ref, cosine_ref, sine_ref, docs_ref, gain2_ref, router_ref, picked_ref,
    normed_turned, q_raw, k_raw, queries, kv_all, key_docs, scales, attended, logs, state_ref, normed2_ref, probs_ref, gates_ref,
    all_grad,
    tokens, normed_ref, wq, wk, wv, wo, docs_in, squares, squares_in, scores, totals, bias, partial, from_pair, from_y, sum_ref,
    t_send, t_recv, z_send, z_recv, p_send, p_recv, c_send, c_recv, h_send, h_recv, d_send, d_recv, q_send, q_recv, load,
):
    z, x, y, core = place()
    group, part = lax.axis_index("expert"), lax.axis_index("tensor")
    spot = group % chain
    length, width = tokens.shape
    wide = heads * HD
    scale = HD ** (-0.5)
    loads = []
    for number, (source, target) in enumerate([(tokens_ref, tokens), (wv_ref, wv), (wk_ref, wk), (wq_ref, wq), (wo_ref, wo)]):
        loads.append(pltpu.make_async_copy(source, target, load.at[number]))
        loads[-1].start()
    mates = mates_of()
    z1, x1 = swapped(z, 1), 1 - x
    greet(
        [device(swapped(z, step), x, y, core) for step in range(1, depth)]
        + [device(z, x1, y, core), device(z1, x1, y, core)]
        + [device(*mate) for mate in mates]
    )
    copies = Copies()
    for distance in (1, 2):

        @pl.when(spot < chain - distance)
        def _():
            remote(
                docs_ref, docs_in.at[2 - distance], d_send.at[distance], d_recv.at[distance], (group + distance, part)
            ).start()

    gather = Gather(copies, grad_ref, all_grad, rows, z_send, z_recv, p_send, p_recv, c_send, c_recv)
    gather.spread(0)
    gather.lift(1)
    own = pltpu.make_async_copy(grad_ref, gather.at(0, gather.here, (0, rows)), load.at[5])
    own.start()
    key_part, value_part = pl.ds(0, wide), pl.ds(wide, wide)

    high = lax.rem(z, 2)
    over_x, over_z = device(z, x1, y, core), device(z1, x, y, core)

    def docs_copy(distance, to):
        return remote(docs_ref, docs_in.at[2 - distance], d_send.at[distance], d_recv.at[distance], (to, part))

    def halo_copy(kind, source, slot, number, to):
        columns = (key_part, value_part)[kind]
        return remote(
            kv_all.at[source, :, columns], kv_all.at[slot, :, columns], h_send.at[kind, number], h_recv.at[kind, number], to
        )

    def x_copy(kind):
        return halo_copy(kind, 2, 1, 0, over_x)

    def z_copy(kind):
        return halo_copy(kind, 2, 0, 1, over_z)

    def relay_copy(kind):
        return halo_copy(kind, 0, 1, 2, over_x)

    def halo_start(kind):
        pl.when(x == 0)(lambda: x_copy(kind).start())
        pl.when(high == 0)(lambda: z_copy(kind).start())

    def halo_relay(kind):
        pl.when(high == 1)(lambda: z_copy(kind).wait_recv())
        pl.when(spot == 3)(lambda: relay_copy(kind).start())

    def halo_arrive(kind):
        columns = (key_part, value_part)[kind]
        pl.when(x == 1)(lambda: x_copy(kind).wait_recv())
        pl.when(spot == 2)(lambda: relay_copy(kind).wait_recv())

        def clear(slot):
            kv_all[slot, :, columns] = jnp.zeros((length, wide), LOW)

        pl.when(spot == 0)(lambda: clear(1))
        pl.when(high == 0)(lambda: clear(0))

    def halo_sent(kind):
        pl.when(x == 0)(lambda: x_copy(kind).wait_send())
        pl.when(high == 0)(lambda: z_copy(kind).wait_send())
        pl.when(spot == 3)(lambda: relay_copy(kind).wait_send())

    loads[0].wait()

    @pl.loop(0, length // 128)
    def _(index):
        part_rows = pl.ds(pl.multiple_of(index * 128, 128), 128)
        values = tokens[part_rows, :].astype(FULL)
        factor = lax.rsqrt(jnp.mean(values * values, axis=-1, keepdims=True) + NORM_EPSILON)
        normed_ref[part_rows, :] = (values * factor * gain1_ref[0:1, :]).astype(LOW)

    def project(weights, store):
        @pl.loop(0, wide // 256)
        def _(index):
            columns = pl.ds(pl.multiple_of(index * 256, 256), 256)
            store(index, columns, dot(normed_ref[...], weights[:, columns]))

    def keep_value(index, columns, result):
        kv_all[2, :, pl.ds(pl.multiple_of(wide + index * 256, 256), 256)] = result.astype(LOW)

    def keep_key(index, columns, result):
        k_raw[:, columns] = result

    def keep_query(index, columns, result):
        q_raw[:, columns] = result

    loads[2].wait()
    project(wk, keep_key)
    loads[3].wait()
    project(wq, keep_query)
    squares[...] = as_rows(
        [jnp.sum(q_raw[...] * q_raw[...], axis=-1, keepdims=True), jnp.sum(k_raw[...] * k_raw[...], axis=-1, keepdims=True)]
    )
    sent = exchange(copies, squares, squares_in, q_send, q_recv, mates)
    loads[1].wait()
    project(wv, keep_value)
    halo_start(1)
    gather.turn(0)

    @pl.loop(0, width // 256)
    def _(index):
        columns = pl.ds(pl.multiple_of(index * 256, 256), 256)
        normed_turned[columns, :] = normed_ref[:, columns].T

    for copy in sent:
        copies.arrived(copy)
    total = squares[...]
    for number in range(3):
        total = total + squares_in[number]
    scales[...] = lax.rsqrt(total * (1.0 / width) + NORM_EPSILON)
    factors = as_columns(scales[...])

    def turn_heads(raw, gain_ref, factor, store):
        for head in range(heads):
            columns = pl.ds(head * HD, HD)
            normed = raw[:, columns] * factor * gain_ref[0:1, columns]
            store(head, (normed * cosine_ref[...] + pltpu.roll(normed, HD // 2, 1) * sine_ref[...]).astype(LOW))

    def store_key(head, turned):
        kv_all[2, :, pl.ds(head * HD, HD)] = turned

    def store_query(head, turned):
        queries[:, pl.ds(head * HD, HD)] = turned

    turn_heads(k_raw, k_gain_ref, factors[:, 1:2], store_key)
    halo_start(0)
    gather.spread(1)
    gather.lift(2)
    turn_heads(q_raw, q_gain_ref, factors[:, 0:1], store_query)
    for distance in (1, 2):

        @pl.when(spot >= distance)
        def _():
            docs_copy(distance, group - distance).wait_recv()

        @pl.when(spot < distance)
        def _():
            docs_in[2 - distance] = jnp.full_like(docs_ref, -1)

    for block in range(3):
        rows_of = docs_in[block] if block < 2 else docs_ref[...]
        key_docs[pl.ds(block * length, length), :] = rows_of.astype(FULL).T[:, 0:1].astype(jnp.int32)
    mask_bias(bias, key_docs, docs_ref, length)

    def score(block):
        @pl.loop(0, heads)
        def _(head):
            columns = pl.ds(pl.multiple_of(head * HD, HD), HD)
            keys = pl.ds(block * length, length)
            scores[head, keys, :] = dot_t(kv_all[block, :, columns], queries[:, columns]) * scale + bias[keys, :]
    score(2)
    halo_relay(1)
    halo_relay(0)
    gather.share(0)
    gather.spread(2)
    halo_arrive(0)
    gather.turn(1)
    score(1)
    score(0)

    @pl.loop(0, heads)
    def _(head):
        mine = scores.at[head]
        highest = jnp.max(mine[...], axis=0, keepdims=True)
        total = jnp.zeros_like(highest)
        for block in range(3):
            weights = jnp.exp(mine[pl.ds(block * length, length), :] - highest)
            total = total + jnp.sum(weights, axis=0, keepdims=True)
            mine[pl.ds(block * length, length), :] = weights
        logs[head] = jnp.broadcast_to(highest + jnp.log(total), (8, length))
        totals[head] = jnp.broadcast_to(1.0 / total, (8, length))

    halo_arrive(1)

    @pl.loop(0, heads)
    def _(head):
        columns = pl.ds(pl.multiple_of(head * HD, HD), HD)
        values = pl.ds(pl.multiple_of((heads + head) * HD, HD), HD)
        mixed = jnp.zeros((HD, length), FULL)
        for block in range(3):
            probs = (scores[head, pl.ds(block * length, length), :] * totals[head, 0:1, :]).astype(LOW)
            mixed = mixed + t_dot(kv_all[block, :, values], probs)
        attended[:, columns] = mixed.T.astype(LOW)

    gather.turn(2)
    gather.spread(3)
    loads[4].wait()
    for index in range(4):
        partial[index // 2, index % 2] = dot(attended[pl.ds(index * rows, rows), :], wo[...]).astype(LOW)
    scatter = TensorScatter(copies, partial, from_pair, from_y, t_send, t_recv)
    scatter.begin()
    scatter.cross()
    gather.share(2)
    gather.turn(3)
    scatter.result(sum_ref)
    own_rows = pl.ds(pl.multiple_of(part * rows, rows), rows)
    state = tokens[own_rows, :].astype(FULL) + sum_ref[...]
    state_ref[...] = state
    factor = lax.rsqrt(jnp.mean(state * state, axis=-1, keepdims=True) + NORM_EPSILON)
    normed2_ref[...] = (state * factor * gain2_ref[0:1, :]).astype(LOW)
    logits = dot(normed2_ref[...], router_ref[...])
    experts = gates_ref.shape[0] * local
    lanes = lax.broadcasted_iota(jnp.int32, logits.shape, 1)
    logits = jnp.where(lanes < experts, logits, -1e30)
    weights = jnp.exp(logits - jnp.max(logits, axis=-1, keepdims=True))
    probs = weights / jnp.sum(weights, axis=-1, keepdims=True)
    probs_ref[...] = probs
    gates = (probs * picked_ref[...]).T
    gates_ref[...] = jnp.zeros_like(gates_ref)
    for index in range(gates_ref.shape[0]):
        gates_ref[index, 0:local, :] = gates[index * local : (index + 1) * local]
    own.wait()
    for kind in range(2):
        halo_sent(kind)
    for distance in (1, 2):

        @pl.when(spot < chain - distance)
        def _():
            docs_copy(distance, group + distance).wait_send()

    copies.finish()


def run_attention(tokens, weights, grads, gains, tables, docs, gain2, router, picked, depth, chain, local, number):
    length, width = tokens.shape
    rows = grads.shape[0]
    wide = weights[0].shape[1]
    heads = wide // HD
    return pl.pallas_call(
        functools.partial(attention_kernel, depth, rows, heads, chain, local),
        out_shape=(
            jax.ShapeDtypeStruct((width, length), LOW),
            jax.ShapeDtypeStruct((length, wide), FULL),
            jax.ShapeDtypeStruct((length, wide), FULL),
            jax.ShapeDtypeStruct((length, wide), LOW),
            jax.ShapeDtypeStruct((3, length, 2 * wide), LOW),
            jax.ShapeDtypeStruct((3 * length, 1), jnp.int32),
            jax.ShapeDtypeStruct((8, length), FULL),
            jax.ShapeDtypeStruct((length, wide), LOW),
            jax.ShapeDtypeStruct((heads, 8, length), FULL),
            jax.ShapeDtypeStruct((rows, width), FULL),
            jax.ShapeDtypeStruct((rows, width), LOW),
            jax.ShapeDtypeStruct((rows, 128), FULL),
            jax.ShapeDtypeStruct((2 * depth, 8, rows), FULL),
            jax.ShapeDtypeStruct((depth, 4 * rows, width), LOW),
        ),
        in_specs=[ANY] * 6 + [VMEM] * 9,
        out_specs=(VMEM,) * 13 + (ANY,),
        scratch_shapes=[
            pltpu.VMEM(tokens.shape, LOW), pltpu.VMEM(tokens.shape, LOW), pltpu.VMEM((width, wide), LOW), pltpu.VMEM((width, wide), LOW),
            pltpu.VMEM((width, wide), LOW), pltpu.VMEM((wide, width), LOW), pltpu.VMEM((2, 8, length), jnp.int32),
            pltpu.VMEM((8, length), FULL), pltpu.VMEM((3, 8, length), FULL),
            pltpu.VMEM((heads, 3 * length, length), FULL), pltpu.VMEM((heads, 8, length), FULL),
            pltpu.VMEM((3 * length, length), FULL),
        ]
        + TensorScatter.scratch(rows, width)[:3]
        + [
            pltpu.VMEM((rows, width), FULL), dma(3), dma(3),
            *Gather.scratch(depth), dma(2, 3), dma(2, 3), dma(3), dma(3), dma(3), dma(3), dma(6),
        ],
        compiler_params=comm_params(number),
    )(tokens, *weights, grads, *gains, *tables, docs, gain2, router, picked)


def attention_back_kernel(
    depth, rows, heads, chain, local,
    sum_ref, gate_cots, probs_ref, picked_ref, state_ref, gain2_ref, router_ref, normed2_ref, grad_ref,
    query_ref, kv_all, attended, logs, key_docs, query_docs, q_raw, k_raw, q_gain_ref, k_gain_ref, cosine_ref, sine_ref, scales,
    w_out, produced_ref, normed_ref, wq_ref, wk_ref, wv_ref,
    state_cot_ref, vectors, out_ref, normed_part, piece0, piece1, piece2, piece3,
    low, lows, by_expert, bias, cots, deltas, turned, query_cot, kv_cot, sending, landed, work, raw_cots, flipped, wq, wk, wv,
    inners, inners_in, staging,
    diagonal, from_x, from_y, from_z, r_send, r_recv, middle, m_send, m_recv,
    t_send, t_recv, h_send, h_recv, i_send, i_recv, load, saves,
):
    z, x, y, core = place()
    group, part = lax.axis_index("expert"), lax.axis_index("tensor")
    spot = group % chain
    length, width = query_ref.shape[0], w_out.shape[1]
    wide = heads * HD
    scale = HD ** (-0.5)
    order = [step for step in range(depth - 1, 0, -2)] + [step for step in range(depth - 2, -1, -2)]
    loads = {}
    for step in order:
        loads[step] = pltpu.make_async_copy(produced_ref.at[step], work.at[step], load.at[step])
        loads[step].start()
    others = []
    for number, (source, target) in enumerate([(wq_ref, wq), (wk_ref, wk), (wv_ref, wv)]):
        others.append(pltpu.make_async_copy(source, target, load.at[depth + number]))
        others[-1].start()
    mates = mates_of()
    greet(
        [device(swapped(z, step), x, y, core) for step in range(1, depth)]
        + [device(z, 1 - x, y, core)]
        + [device(*mate) for mate in mates]
    )
    copies = Copies()
    scatter = Scatter(
        copies, work, diagonal, from_x, from_y, from_z, rows, r_send, r_recv, (middle, m_send, m_recv)
    )

    def corner(step):
        if step % 2 == 0:
            loads[step].wait()
        scatter.corner(step)

    for step in order[:2]:
        loads[step].wait()
        scatter.share(step)
    for step in order[:2]:
        corner(step)

    by_expert[...] = jnp.zeros_like(by_expert)
    for plane in range(depth):
        step = swapped(z, plane)
        for column in range(2):
            first = (2 * plane + column) * local
            by_expert[first : first + local, :] = (gate_cots[step, 2 * column] + gate_cots[step, 2 * column + 1])[:local]
    probs = probs_ref[...]
    prob_cot = by_expert[...].T * picked_ref[...]
    logit_cot = probs * (prob_cot - jnp.sum(probs * prob_cot, axis=-1, keepdims=True))
    normed2_cot = sum_ref[...] + lax.dot_general(
        logit_cot, router_ref[...].astype(FULL), (((1,), (1,)), ((), ())),
        precision=HIGHEST_PRECISION, preferred_element_type=FULL,
    )
    state = state_ref[...]
    factor = lax.rsqrt(jnp.mean(state * state, axis=-1, keepdims=True) + NORM_EPSILON)
    groups, _, slice_width = vectors.shape
    vectors[...] = jnp.zeros_like(vectors)
    gain_grad = jnp.sum(normed2_cot * state * factor, axis=0, keepdims=True)
    for index in range(groups):
        vectors[index, 17:18, :] = gain_grad[:, index * slice_width : (index + 1) * slice_width]
    inner = jnp.sum(normed2_cot * gain2_ref[0:1, :] * state, axis=-1, keepdims=True)
    state_cot = (
        grad_ref[...].astype(FULL)
        + factor * gain2_ref[0:1, :] * normed2_cot
        - state * (factor * factor * factor) * inner * (1.0 / width)
    )
    state_cot_ref[...] = state_cot
    low[...] = state_cot.astype(LOW)
    gather = TensorGather(copies, low, lows, t_send, t_recv)
    scatter.side(order[0])
    router_grad = jnp.dot(
        logit_cot.T, normed2_ref[...].astype(FULL), precision=HIGHEST_PRECISION, preferred_element_type=FULL
    )[:16]
    for index in range(groups):
        vectors[index, 0:16, :] = router_grad[:, index * slice_width : (index + 1) * slice_width]
    mask_bias(bias, key_docs, query_docs, length)
    gather.cross()
    gather.finish()
    for index in range(4):
        cots[pl.ds(index * rows, rows), :] = dot_t(lows[index // 2, index % 2], w_out[...]).astype(LOW)
    for head in range(heads):
        columns = pl.ds(head * HD, HD)
        product = cots[:, columns].astype(FULL) * attended[:, columns].astype(FULL)
        deltas[head] = jnp.broadcast_to(jnp.sum(product.T, axis=0, keepdims=True), (8, length))
    turned[...] = jnp.zeros_like(turned)

    def back(block, store, after):
        @pl.loop(0, heads)
        def _(head):
            columns = pl.ds(pl.multiple_of(head * HD, HD), HD)
            values = pl.ds(pl.multiple_of((heads + head) * HD, HD), HD)
            query, cot = query_ref[:, columns], cots[:, columns]
            log, delta = logs[head, 0:1, :], deltas[head, 0:1, :]
            tile = 256

            @pl.loop(0, length // tile)
            def _(index):
                keys = pl.ds(pl.multiple_of(index * tile, tile), tile)
                key, value = kv_all[block, keys, columns], kv_all[block, keys, values]
                hidden = bias[pl.ds(pl.multiple_of(block * length + index * tile, tile), tile), :].astype(FULL)
                probs = jnp.exp(dot_t(key, query) * scale + hidden - log)
                score_cot = (probs * (dot_t(value, cot) - delta)).astype(LOW)
                turned[head] += t_dot(key, score_cot)
                store(head, keys, dot(score_cot, query) * scale, dot(probs.astype(LOW), cot))

            after(head)

    def store_in(slot):
        def store(head, keys, key_part, value_part):
            sending[slot, head, keys, 0:HD] = key_part.astype(LOW)
            sending[slot, head, keys, HD : 2 * HD] = value_part.astype(LOW)

        return store

    def store_own(head, keys, key_part, value_part):
        kv_cot[keys, pl.ds(pl.multiple_of(head * HD, HD), HD)] = key_part
        kv_cot[keys, pl.ds(pl.multiple_of((heads + head) * HD, HD), HD)] = value_part

    high = lax.rem(z, 2)
    over_x, over_z = device(z, 1 - x, y, core), device(swapped(z, 1), x, y, core)

    def x_copy(head):
        return remote(sending.at[1, head], landed.at[1, head], h_send.at[0, head], h_recv.at[0, head], over_x)

    def z_copy(head):
        return remote(sending.at[0, head], landed.at[0, head], h_send.at[1, head], h_recv.at[1, head], over_z)

    def relay(head):
        @pl.when(spot == 3)
        def _():
            x_copy(head).wait_recv()
            add_rows(sending.at[0, head], [sending.at[0, head], landed.at[1, head]], length, 64)
            z_copy(head).start()

    back(1, store_in(1), lambda head: pl.when(spot >= 1)(lambda: x_copy(head).start()))
    corner(order[2])
    scatter.side(order[1])
    back(0, store_in(0), lambda head: pl.when(spot == 2)(lambda: z_copy(head).start()))
    scatter.climb(order[0])
    back(2, store_own, relay)
    corner(order[3])
    for head in range(heads):
        query_cot[:, pl.ds(head * HD, HD)] = turned[head].T * scale
    scatter.side(order[2])
    scatter.climb(order[1])

    saving = {}

    def weight_piece(number, right, target):
        piece = target.shape[2]
        for index in range(2 * depth):
            slot = index % 2
            if slot in saving:
                saving.pop(slot).wait()
            staging[slot] = dot(flipped[pl.ds(index * piece, piece), :], right).astype(LOW)
            saving[slot] = pltpu.make_async_copy(staging.at[slot], target.at[index // 2, index % 2], saves.at[slot])
            saving[slot].start()

    @pl.loop(0, width // 256)
    def _(index):
        columns = pl.ds(pl.multiple_of(index * 256, 256), 256)
        flipped[columns, :] = jnp.concatenate([lows[block // 2, block % 2, :, columns] for block in range(4)], axis=0).T

    weight_piece(0, attended[...], piece0)
    normed_copy = pltpu.make_async_copy(normed_ref, flipped, load.at[depth + 3])
    normed_copy.start()
    scatter.side(order[3])
    factors = as_columns(scales[...])

    def turn_back(cot, raw, gain_ref, factor, first):
        total = jnp.zeros((length, 1), FULL)
        for head in range(heads):
            columns = pl.ds(head * HD, HD)
            mine = cot[:, columns]
            mine = mine * cosine_ref[...] - pltpu.roll(mine, HD // 2, 1) * sine_ref[...]
            cot[:, columns] = mine
            mine = mine * raw[:, columns]
            grad = jnp.sum(mine * factor, axis=0, keepdims=True)
            for index in range(groups):
                vectors[index, first + head : first + head + 1, 0:HD] = grad
            total = total + jnp.sum(mine * gain_ref[0:1, columns], axis=-1, keepdims=True)
        return total

    query_inner = turn_back(query_cot, q_raw, q_gain_ref, factors[:, 0:1], 18)
    scatter.climb(order[2])

    def take(slot, head):
        (z_copy, x_copy)[slot](head).wait_recv()
        for part in range(2):
            mine = kv_cot.at[:, pl.ds((part * heads + head) * HD, HD)]
            add_rows(mine, [mine, landed.at[slot, head, :, pl.ds(part * HD, HD)]], length, 64)

    for head in range(heads):
        pl.when(x == 0)(functools.partial(take, 1, head))
    for head in range(heads):
        pl.when(high == 0)(functools.partial(take, 0, head))

    key_inner = turn_back(kv_cot, k_raw, k_gain_ref, factors[:, 1:2], 18 + heads)
    inners[...] = as_rows([query_inner, key_inner])
    sent = exchange(copies, inners, inners_in, i_send, i_recv, mates)
    raw_cots[2] = kv_cot[:, pl.ds(wide, wide)].astype(LOW)
    normed_copy.wait()
    weight_piece(1, raw_cots[2], piece1)
    for copy in sent:
        copies.arrived(copy)
    total = inners[...]
    for number in range(3):
        total = total + inners_in[number]
    totals = as_columns(total * (1.0 / width))

    def raw_cot(number, cot, raw, gain_ref):
        factor = factors[:, number : number + 1]
        shrink = (factor * factor * factor) * totals[:, number : number + 1]
        for head in range(heads):
            columns = pl.ds(head * HD, HD)
            raw_cots[number, :, columns] = (
                factor * gain_ref[0:1, columns] * cot[:, columns] - raw[:, columns] * shrink
            ).astype(LOW)

    raw_cot(0, query_cot, q_raw, q_gain_ref)
    raw_cot(1, kv_cot, k_raw, k_gain_ref)
    for copy in others:
        copy.wait()

    @pl.loop(0, width // 256)
    def _(index):
        columns = pl.ds(pl.multiple_of(index * 256, 256), 256)
        result = (
            dot_t(raw_cots[0], wq[columns, :]) + dot_t(raw_cots[1], wk[columns, :]) + dot_t(raw_cots[2], wv[columns, :])
        ).astype(LOW)
        for block in range(4):
            normed_part[block // 2, block % 2, :, columns] = result[block * rows : (block + 1) * rows]

    weight_piece(2, raw_cots[0], piece2)
    weight_piece(3, raw_cots[1], piece3)
    scatter.climb(order[3])
    scatter.result(out_ref, [state_ref])
    for head in range(heads):
        pl.when(spot >= 1)(lambda: x_copy(head).wait_send())
        pl.when(spot >= 2)(lambda: z_copy(head).wait_send())

    for copy in saving.values():
        copy.wait()
    copies.finish()


def run_attention_back(rows_of, attention, sources, produced, normed, weights, chain, local, number):
    depth = produced.shape[0]
    rows, width = rows_of[0].shape
    queries, kv_all = attention[0], attention[1]
    length, wide2 = kv_all.shape[1:]
    wide = wide2 // 2
    heads = wide // HD
    piece = jax.ShapeDtypeStruct((depth, 2, width // (2 * depth), wide), LOW)
    return pl.pallas_call(
        functools.partial(attention_back_kernel, depth, rows, heads, chain, local),
        out_shape=(
            jax.ShapeDtypeStruct((rows, width), FULL),
            jax.ShapeDtypeStruct((2 * depth, 32, width // (2 * depth)), FULL),
            jax.ShapeDtypeStruct((rows, width), LOW),
            jax.ShapeDtypeStruct((2, 2, rows, width), LOW),
            piece, piece, piece, piece,
        ),
        in_specs=[VMEM] * 23 + [ANY] * 5,
        out_specs=(VMEM,) * 4 + (ANY,) * 4,
        scratch_shapes=[
            pltpu.VMEM((rows, width), LOW), pltpu.VMEM((2, 2, rows, width), LOW), pltpu.VMEM((128, rows), FULL),
            pltpu.VMEM((3 * length, length), LOW), pltpu.VMEM((length, wide), LOW),
            pltpu.VMEM((heads, 8, length), FULL), pltpu.VMEM((heads, HD, length), FULL),
            pltpu.VMEM((length, wide), FULL), pltpu.VMEM((length, wide2), FULL),
            pltpu.VMEM((2, heads, length, 2 * HD), LOW), pltpu.VMEM((2, heads, length, 2 * HD), LOW),
            pltpu.VMEM(produced.shape, LOW), pltpu.VMEM((3, length, wide), LOW), pltpu.VMEM((width, length), LOW),
            pltpu.VMEM((width, wide), LOW), pltpu.VMEM((width, wide), LOW), pltpu.VMEM((width, wide), LOW),
            pltpu.VMEM((8, length), FULL), pltpu.VMEM((3, 8, length), FULL), pltpu.VMEM((2,) + piece.shape[2:], LOW),
        ]
        + Scatter.scratch(depth, rows, width)
        + [pltpu.VMEM((depth // 2, 4, rows // 4, width), LOW), dma(depth // 2, 4), dma(depth // 2, 4)]
        + [dma(4), dma(3), dma(2, heads), dma(2, heads), dma(3), dma(3), dma(depth + 4), dma(2)],
        compiler_params=comm_params(number),
    )(*rows_of, *attention, *sources, produced, normed, *weights)


def dot(left, right):
    return jnp.dot(left, right, preferred_element_type=FULL)


def dot_t(left, right):
    return lax.dot_general(left, right, (((1,), (1,)), ((), ())), preferred_element_type=FULL)


def t_dot(left, right):
    return lax.dot_general(left, right, (((0,), (0,)), ((), ())), preferred_element_type=FULL)


class ExpertScatter:
    def __init__(self, copies, parts, widths, work, from_x, from_z, load, send, recv):
        self.widths = widths
        self.copies, self.parts, self.work, self.from_x, self.from_z = copies, parts, work, from_x, from_z
        self.load, self.send, self.recv = load, send, recv
        self.z, self.x, y, core = place()
        self.depth, self.rows = work.shape[1], work.shape[2]
        self.over_x = device(self.z, 1 - self.x, y, core)
        self.column = [device(swapped(self.z, step), self.x, y, core) for step in range(self.depth)]
        self.order = sorted(range(self.depth), key=lambda step: (step == 0, step & -step, -step))
        self.steps = self.order[:-1]
        self.loads, self.sides, self.along = {}, {}, {}

    def begin(self, index):
        for step in self.order:
            at = swapped(self.z, step)
            columns = pl.ds(0, self.widths[index])
            self.sides[index, step] = self.copies.start(
                remote(
                    self.parts[index].at[at, 1 - self.x, :, columns], self.from_x.at[index, step, :, columns],
                    self.send.at[0, index, step], self.recv.at[0, index, step], self.over_x,
                )
            )
            load = pltpu.make_async_copy(
                self.parts[index].at[at, self.x, :, columns], self.work.at[index, step, :, columns], self.load.at[index, step]
            )
            load.start()
            self.loads[index, step] = load

    def climb(self, index, step):
        self.loads[index, step].wait()
        self.copies.arrived(self.sides[index, step])
        columns = pl.ds(0, self.widths[index])
        mine = self.work.at[index, step, :, columns]
        low = step & -step
        terms = [mine, self.from_x.at[index, step, :, columns]] + self.below(index, step)
        add_rows(mine, terms, self.rows)
        self.along[index, step] = self.copies.start(
            remote(
                mine, self.from_z.at[index, step, :, columns],
                self.send.at[1, index, step], self.recv.at[1, index, step], self.column[low],
            )
        )

    def below(self, index, step):
        terms, bit = [], 1
        while bit < (step & -step if step else self.depth):
            self.copies.arrived(self.along[index, step | bit])
            terms.append(self.from_z.at[index, step | bit, :, pl.ds(0, self.widths[index])])
            bit *= 2
        return terms

    def result(self, index, target):
        self.loads[index, 0].wait()
        self.copies.arrived(self.sides[index, 0])
        columns = pl.ds(0, self.widths[index])
        terms = [self.work.at[index, 0, :, columns], self.from_x.at[index, 0, :, columns]] + self.below(index, 0)
        add_rows(target.at[:, columns], terms, self.rows)


class ZScatter:
    def __init__(self, copies, part, columns, work, from_z, from_x, load, send, recv):
        self.copies, self.part, self.columns = copies, part, columns
        self.work, self.from_z, self.from_x, self.load, self.send, self.recv = work, from_z, from_x, load, send, recv
        self.z, self.x, y, core = place()
        self.depth, self.rows = work.shape[0], work.shape[2]
        self.over_x = device(self.z, 1 - self.x, y, core)
        self.column = [device(swapped(self.z, step), self.x, y, core) for step in range(self.depth)]
        self.loads, self.along = {}, {}

    def begin(self):
        for step in range(self.depth):
            source = self.part.at[swapped(self.z, step), :, :, self.columns]
            self.loads[step] = pltpu.make_async_copy(source, self.work.at[step], self.load.at[step])
            self.loads[step].start()

    def climb(self, step):
        self.loads[step].wait()
        low = step & -step if step else self.depth
        bit = 1
        while bit < low:
            self.copies.arrived(self.along[step | bit])
            for column in range(2):
                mine = self.work.at[step, column]
                add_rows(mine, [mine, self.from_z.at[step | bit, column]], self.rows, 32)
            bit *= 2
        if step:
            copy = remote(self.work.at[step], self.from_z.at[step], self.send.at[step], self.recv.at[step], self.column[low])
        else:
            copy = remote(self.work.at[0, 1 - self.x], self.from_x, self.send.at[0], self.recv.at[0], self.over_x)
        self.along[step] = self.copies.start(copy)

    def result(self, target):
        self.copies.arrived(self.along[0])
        add_rows(target, [self.work.at[0, self.x], self.from_x], self.rows)


def gradients_kernel(
    depth, rows, local, hidden, matrices, *refs,
):
    parts, refs = refs[:matrices], refs[matrices:]
    (
        normed_part, tokens_ref, state_cot, gain_ref, out_ref, vector_ref,
        normed_ref, grad_ref, gated_ref, gate_grad_ref, up_grad_ref,
    ) = refs[:11]
    sums, refs = refs[11 : 11 + matrices], refs[11 + matrices :]
    (
        input_grads, outputs, vector_sum,
        gate_own, up_own, down_own,
        work, from_x, from_z, partial, from_pair, from_y, normed_grad, low, vectors, vector_in, vector_mid, vector_turn,
        tiles, turned, acts, gated_turned, near, far, near_down, far_down, other, other_down,
        f_work, f_from_z, f_from_x, f_load, f_send, f_recv,
        e_load, e_send, e_recv, t_send, t_recv, g_send, g_recv, o_send, o_recv, v_send, v_recv, u_send, u_recv,
        tile_load, act_load, save, pair_send, pair_recv, local_sem,
    ) = refs
    z, x, y, core = place()
    group = 2 * z + x
    sibling = device(z, x, y, 1 - core)
    groups = [(step, turn) for step in range(depth) for turn in range(2) if step or turn]
    peers = [device(swapped(z, step), swapped(x, turn), y, core) for step, turn in groups]
    mates = [(z, x, swapped(y, turn // 2), swapped(core, turn % 2)) for turn in range(1, 4)]
    greet(peers + [device(*mate) for mate in mates])
    copies = Copies()
    width = normed_ref.shape[1]
    tile = local * hidden
    count = width // tile

    def fetch(source, target, sem):
        copy = pltpu.make_async_copy(source, target, sem)
        copy.start()
        return copy

    wide = work.shape[3]
    widths = [wide] * (matrices - 1) + [wide // 2]
    experts = ExpertScatter(copies, parts, widths, work, from_x, from_z, e_load, e_send, e_recv)
    eighth = pl.ds(wide // 2, wide // 2)
    z_first = ZScatter(copies, parts[-1], eighth, f_work, f_from_z, f_from_x, f_load, f_send, f_recv)
    loaded = fetch(normed_part, partial, local_sem.at[0])
    experts.begin(0)
    z_first.begin()
    loaded.wait()
    scatter = TensorScatter(copies, partial, from_pair, from_y, t_send, t_recv)
    scatter.begin()
    out_gather = TensorGather(copies, out_ref, outputs, o_send, o_recv)
    for index in range(1, matrices):
        experts.begin(index)
    act_copies = [fetch(gate_grad_ref, acts.at[0], act_load.at[0]), fetch(up_grad_ref, acts.at[1], act_load.at[1])]

    def fetch_tile(number):
        source = normed_ref if number < count else grad_ref
        columns = pl.ds((number % count) * tile, tile)
        return fetch(source.at[:, columns], tiles.at[number % 2], tile_load.at[number % 2])

    tile_copies = [fetch_tile(0)]
    saving = {}

    def first_unit(owner):
        return owner * local * hidden

    def gate_and_up(number):
        slot = number % 2
        tile_copies[number].wait()
        tile_copies.append(fetch_tile(number + 1))
        turned[...] = tiles[slot].T
        for copy, remote_one in saving.pop(slot, []):
            copies.sent(copy) if remote_one else copy.wait()
        for which in range(2):
            for owner, target in ((1 - core, far), (core, near)):

                @pl.loop(0, local)
                def _(expert):
                    columns = pl.ds(pl.multiple_of(first_unit(owner) + expert * hidden, hidden), hidden)
                    target[which, slot, expert] = dot(turned[...], acts[which, :, columns]).astype(target.dtype)

        saves = []
        for which in range(2):
            away = remote(
                far.at[which, slot], other.at[which, :, pl.ds(number * tile, tile)],
                pair_send.at[which, number], pair_recv.at[which, number], sibling,
            )
            copies.start(away)
            saves.append((away, True))
        saving[slot] = saves
        if number:
            settle(number - 1)

    def settle(number):
        slot, place_of = number % 2, pl.ds(number * tile, tile)
        for which, own in enumerate((gate_own, up_own)):
            copies.arrived(saving[slot][which][0])
            for expert in range(local):
                mine = near.at[which, slot, expert]
                add_rows(mine, [mine, other.at[which, expert, place_of]], tile, 64)
        for which, own in enumerate((gate_own, up_own)):
            saving[slot].append((fetch(near.at[which, slot], own.at[:, place_of], save.at[which, slot]), False))

    def down(number):
        slot = number % 2
        tile_copies[count + number].wait()
        if number + 1 < count:
            tile_copies.append(fetch_tile(count + number + 1))
        for copy, remote_one in saving.pop(("down", slot), []):
            copies.sent(copy) if remote_one else copy.wait()
        for source, target in ((turned, far_down), (gated_turned, near_down)):

            @pl.loop(0, local)
            def _(expert):
                units = pl.ds(pl.multiple_of(expert * hidden, hidden), hidden)
                target[slot, expert] = dot(source[units, :], tiles[slot]).astype(target.dtype)

        away = remote(
            far_down.at[slot], other_down.at[number], pair_send.at[2, number], pair_recv.at[2, number], sibling
        )
        copies.start(away)
        saving["down", slot] = [(away, True)]
        settle(count - 1) if number == 0 else settle_down(number - 1)

    def settle_down(number):
        slot = number % 2
        copies.arrived(saving["down", slot][0][0])
        for expert in range(local):
            mine = near_down.at[slot, expert]
            add_rows(mine, [mine, other_down.at[number, expert]], hidden, 64)
        target = down_own.at[:, :, pl.ds(number * tile, tile)]
        saving["down", slot].append((fetch(near_down.at[slot], target, save.at[2, slot]), False))

    for copy in act_copies:
        copy.wait()
    z_first.climb(3)
    z_first.climb(1)
    gate_and_up(0)
    scatter.cross()
    experts.climb(0, experts.steps[0])
    gate_and_up(1)
    out_gather.cross()
    experts.climb(0, experts.steps[1])
    z_first.climb(2)
    scatter.result(normed_grad)

    inputs = tokens_ref[...].astype(FULL)
    factor = lax.rsqrt(jnp.mean(inputs * inputs, axis=-1, keepdims=True) + NORM_EPSILON)
    gain = gain_ref[0:1, :]
    normed = normed_grad[...]
    inner = jnp.sum(normed * gain * inputs, axis=-1, keepdims=True)
    low[...] = (
        state_cot[...] + factor * gain * normed - inputs * (factor * factor * factor) * inner * (1.0 / width)
    ).astype(LOW)
    gain_grad = jnp.sum(normed * inputs * factor, axis=0, keepdims=True)
    grad_gather = TensorGather(copies, low, input_grads, g_send, g_recv)
    vectors[...] = vector_ref[...]
    slice_width = vectors.shape[2]
    for index in range(vectors.shape[0]):
        vectors[index, 16:17, :] = gain_grad[:, index * slice_width : (index + 1) * slice_width]
    vector_copies = []
    for number, ((step, turn), peer) in enumerate(zip(groups, peers)):
        to = 2 * swapped(z, step) + swapped(x, turn)
        vector_copies.append(
            copies.start(remote(vectors.at[to], vector_in.at[number], v_send.at[number], v_recv.at[number], peer))
        )

    for step in experts.steps[2:]:
        experts.climb(0, step)
    gate_and_up(2)
    for step in experts.steps[:2]:
        experts.climb(1, step)
    grad_gather.cross()
    z_first.climb(0)
    gate_and_up(3)
    for step in experts.steps[2:]:
        experts.climb(1, step)
    gated_copy = fetch(gated_ref, acts.at[0], act_load.at[0])
    gated_copy.wait()
    for owner, target in ((1 - core, turned), (core, gated_turned)):
        target[...] = acts[0, :, pl.ds(pl.multiple_of(first_unit(owner), hidden), local * hidden)].T
    experts.result(0, sums[0])
    down(0)
    experts.climb(2, experts.steps[0])
    down(1)
    for step in experts.steps[1:]:
        experts.climb(2, step)
    down(2)
    experts.result(1, sums[1])
    down(3)
    settle_down(3)
    for index in range(3, matrices):
        for step in experts.steps:
            experts.climb(index, step)
    for copy in vector_copies:
        copies.arrived(copy)
    total = vectors[group]
    for number in range(len(peers)):
        total = total + vector_in[number]
    vector_mid[...] = total
    turn_copies = [
        copies.start(remote(vector_mid, vector_turn.at[number], u_send.at[number], u_recv.at[number], device(*mate)))
        for number, mate in enumerate(mates)
    ]
    for index in range(2, matrices):
        experts.result(index, sums[index])
    z_first.result(sums[-1].at[:, eighth])
    out_gather.finish()
    grad_gather.finish()
    for copy in turn_copies:
        copies.arrived(copy)
    total = vector_mid[...]
    for number in range(len(mates)):
        total = total + vector_turn[number]
    keep = lax.broadcasted_iota(jnp.int32, total.shape, 0) < 18
    vector_sum[...] = jnp.where(keep, total, vector_mid[...])
    for entries in saving.values():
        for copy, remote_one in entries:
            if not remote_one:
                copy.wait()
    copies.finish()


def run_gradients(parts, normed_part, tokens, state_cot, gain, out, vectors, normed, grads, gated, gate_grad, up_grad, local, number):
    matrices = len(parts)
    depth, _, piece, columns = parts[0].shape
    rows, width = tokens.shape
    seen, units = gated.shape
    hidden = units // (2 * local)
    tile = units // 2
    sum_of = jax.ShapeDtypeStruct((piece, columns), FULL)
    spread = jax.ShapeDtypeStruct((2, 2, rows, width), LOW)
    wide, tall = (local, width, hidden), (local, hidden, width)
    results = pl.pallas_call(
        functools.partial(gradients_kernel, depth, rows, local, hidden, matrices),
        out_shape=(sum_of,) * matrices
        + (
            spread, spread, jax.ShapeDtypeStruct(vectors.shape[1:], FULL),
            jax.ShapeDtypeStruct(wide, FULL), jax.ShapeDtypeStruct(wide, FULL), jax.ShapeDtypeStruct(tall, FULL),
        ),
        in_specs=[ANY] * (matrices + 1) + [VMEM] * 5 + [ANY] * 5,
        out_specs=(VMEM,) * (matrices + 3) + (ANY,) * 3,
        scratch_shapes=[pltpu.VMEM((matrices, depth, piece, columns), LOW)] * 3
        + TensorScatter.scratch(rows, width)[:3]
        + [
            pltpu.VMEM((rows, width), FULL), pltpu.VMEM((rows, width), LOW),
            pltpu.VMEM(vectors.shape, FULL), pltpu.VMEM((2 * depth - 1,) + vectors.shape[1:], FULL),
            pltpu.VMEM(vectors.shape[1:], FULL), pltpu.VMEM((3,) + vectors.shape[1:], FULL),
            pltpu.VMEM((2, seen, tile), LOW), pltpu.VMEM((tile, seen), LOW),
            pltpu.VMEM((2, seen, units), LOW), pltpu.VMEM((units // 2, seen), LOW),
            pltpu.VMEM((2, 2, local, tile, hidden), FULL), pltpu.VMEM((2, 2, local, tile, hidden), LOW),
            pltpu.VMEM((2, local, hidden, tile), FULL), pltpu.VMEM((2, local, hidden, tile), LOW),
            pltpu.VMEM((2, local, width, hidden), LOW), pltpu.VMEM((width // tile, local, hidden, tile), LOW),
            pltpu.VMEM((depth, 2, piece, columns // 2), LOW), pltpu.VMEM((depth, 2, piece, columns // 2), LOW),
            pltpu.VMEM((piece, columns // 2), LOW), dma(depth), dma(depth), dma(depth),
            dma(matrices, depth), dma(2, matrices, depth), dma(2, matrices, depth),
            dma(3), dma(3), dma(4), dma(3), dma(4), dma(3),
            dma(2 * depth - 1), dma(2 * depth - 1), dma(3), dma(3),
            dma(2), dma(2), dma(3, 2), dma(3, width // tile), dma(3, width // tile), dma(1),
        ],
        compiler_params=comm_params(number),
    )(*parts, normed_part, tokens, state_cot, gain, out, vectors, normed, grads, gated, gate_grad, up_grad)
    return results[:matrices], results[matrices:]


def body(
    groups, parts,
    tokens, documents, routes, norm1_gain, q_gain, k_gain, w_query, w_key, w_value, w_out, norm2_gain, router_w,
    w_gate, w_up, w_down, out_grad,
):
    row_count, width = tokens.shape
    local_experts, _, hidden = w_gate.shape
    experts = local_experts * groups
    chain = LENGTH // row_count
    if not (parts == 4 and groups % 2 == 0 and experts <= min(16, 2 * TOP) and 2 * w_query.shape[1] <= 14 * HD and chain == 4 and groups == 8 and 4 * row_count == LENGTH and WINDOW == 2 * row_count):
        return body_routed(
            tokens, documents, routes, norm1_gain, q_gain, k_gain, w_query, w_key, w_value, w_out, norm2_gain, router_w,
            w_gate, w_up, w_down, out_grad,
        )
    depth = groups // 2
    rows = row_count // parts
    seen = groups * row_count // 2
    heads = w_query.shape[1] // HD
    group, part = lax.axis_index("expert"), lax.axis_index("tensor")
    core = part % 2

    def quarter(array):
        return lax.dynamic_slice_in_dim(array, part * rows, rows, 0)

    def across(vector):
        return vector.reshape(1, -1)

    positions = group * row_count + jnp.arange(row_count, dtype=jnp.int32)
    cosine, sine = (table[:, 0, :] for table in rope_tables(positions % LENGTH))
    sine = jnp.concatenate([-sine[:, : HD // 2], sine[:, HD // 2 :]], axis=1)
    docs = jnp.broadcast_to(documents[None, :], (8, row_count))
    picked = jnp.any(quarter(routes)[:, :, None] == jnp.arange(128, dtype=jnp.int32)[None, None, :], axis=1).astype(FULL)
    router_wide = jnp.pad(router_w, ((0, 0), (0, 128 - experts)))
    own_grad = quarter(out_grad)
    query_gain, key_gain = across(q_gain), across(k_gain)
    (
        normed_one, query_raw, key_raw, queries, kv_all, key_docs, scales, attended, logs, state, normed_two, router_probs, gates,
        all_grad,
    ) = run_attention(
        tokens, (w_query, w_key, w_value, w_out), own_grad, (across(norm1_gain), query_gain, key_gain), (cosine, sine), docs,
        across(norm2_gain), router_wide, picked, depth, chain, local_experts, 3,
    )

    normed_two_grad, gate_cots, all_normed, gated, gate_pre_grad, up_pre_grad, produced = run_experts(
        normed_two, gates, all_grad, w_gate, w_up, w_down, 5
    )
    units = 2 * local_experts * hidden
    all_normed, all_grad = all_normed.reshape(seen, width), all_grad.reshape(seen, width)
    gated, gate_pre_grad, up_pre_grad = (a.reshape(seen, units) for a in (gated, gate_pre_grad, up_pre_grad))

    state_cot, vectors, output_rows, normed_part, *pieces = run_attention_back(
        (normed_two_grad, gate_cots, router_probs, picked, state, across(norm2_gain), router_wide, normed_two, own_grad),
        (queries, kv_all, attended, logs, key_docs, docs, query_raw, key_raw, query_gain, key_gain, cosine, sine, scales),
        (w_out,), produced, normed_one, (w_query, w_key, w_value), chain, local_experts, 10,
    )
    sums, (input_grad, output, vector_sum, *expert_grads) = run_gradients(
        pieces, normed_part, quarter(tokens), state_cot, norm1_gain[None], output_rows, vectors, all_normed, all_grad, gated, gate_pre_grad, up_pre_grad,
        local_experts, 14,
    )
    own_columns = group * (HD // groups)
    return (
        output.reshape(row_count, width),
        input_grad.reshape(row_count, width).astype(FULL),
        vector_sum[16],
        lax.dynamic_slice(vector_sum, (18, own_columns), (heads, HD // groups)),
        lax.dynamic_slice(vector_sum, (18 + heads, own_columns), (heads, HD // groups)),
        sums[2],
        sums[3],
        sums[1],
        sums[0].T,
        vector_sum[17],
        vector_sum[:experts].T,
        *expert_grads,
    )


def solution(mesh):
    placed = (
        P("expert", None),
        P("expert"),
        P("expert", None),
        P(),
        P("tensor", None),
        P("tensor", None),
        P(None, "tensor"),
        P(None, "tensor"),
        P(None, "tensor"),
        P("tensor", None),
        P(),
        P(),
        P("expert", None, "tensor"),
        P("expert", None, "tensor"),
        P("expert", "tensor", None),
        P("expert", None),
    )
    return jax.shard_map(
        functools.partial(body, mesh.shape["expert"], mesh.shape["tensor"]),
        mesh=mesh,
        in_specs=placed,
        out_specs=(
            P("expert", None),
            P("expert", None),
            P("expert"),
            P("tensor", "expert"),
            P("tensor", "expert"),
            P("expert", "tensor"),
            P("expert", "tensor"),
            P("expert", "tensor"),
            P("tensor", "expert"),
            P("expert"),
            P("expert", None),
            P("expert", None, "tensor"),
            P("expert", None, "tensor"),
            P("expert", "tensor", None),
        ),
        check_vma=False,
    )
```

```python
import functools

import jax
import jax.numpy as jnp
from jax import lax
from jax.experimental import pallas as pl
from jax.experimental.pallas import tpu as pltpu
from jax.sharding import PartitionSpec as P

HD = 128
TOP = 8
WINDOW = 1024
LENGTH = 2048


NORM_EPSILON = 1e-05
HIGHEST_PRECISION = lax.Precision.HIGHEST


def for_sending(value):
    return jax.tree.map(lambda a: a.astype(jnp.bfloat16) if a.dtype == jnp.float32 else a, value)


def shifted(value, axis, steps):
    count = lax.axis_size(axis)
    initial, last = (max(0, -steps), min(count, count - steps))
    return lax.ppermute(value, axis, [(source, source + steps) for source in range(initial, last)])


def rope_tables(positions):
    half_width = HD // 2
    frequency = 10000.0 ** (-jnp.arange(half_width, dtype=jnp.float32) * 2.0 / HD)
    angles = positions.astype(jnp.float32)[:, None] * frequency[None, :]
    angles = jnp.concatenate([angles, angles], axis=-1)
    return (jnp.cos(angles)[:, None, :], jnp.sin(angles)[:, None, :])


def rotate(values, cosine, sine):
    half_width = values.shape[-1] // 2
    turned = jnp.concatenate([-values[..., half_width:], values[..., :half_width]], axis=-1)
    return values * cosine + turned * sine


def rotate_back(grads, cosine, sine):
    half_width = grads.shape[-1] // 2
    scaled = grads * sine
    turned = jnp.concatenate([scaled[..., half_width:], -scaled[..., :half_width]], axis=-1)
    return grads * cosine + turned


def previous_block(pieces):
    return jax.tree.map(
        lambda part, own: part.astype(own.dtype), shifted(for_sending(pieces), "expert", 1), pieces
    )


def following_block(pieces):
    return shifted((for_sending(pieces[0]), for_sending(pieces[1])), "expert", -1)


def body_routed(
    tokens,
    documents,
    routes,
    norm1_gain,
    q_gain,
    k_gain,
    w_query,
    w_key,
    w_value,
    w_out,
    norm2_gain,
    router_w,
    w_gate,
    w_up,
    w_down,
    out_grad,
):
    row_count, model_width = tokens.shape
    groups = lax.axis_size("expert")
    local_experts = w_gate.shape[0]
    experts = local_experts * groups
    capacity = 2 * row_count * TOP // experts
    slots_group = local_experts * capacity
    heads = w_query.shape[1] // HD
    score_scale = HD ** (-0.5)
    first_row = lax.axis_index("expert") * row_count
    positions = first_row + jnp.arange(row_count, dtype=jnp.int32)
    cosine, sine = rope_tables(positions % LENGTH)
    inputs = tokens.astype(jnp.float32)
    scale_one = lax.rsqrt(jnp.mean(inputs * inputs, axis=-1, keepdims=True) + NORM_EPSILON)
    normed_one = (inputs * scale_one * norm1_gain).astype(jnp.bfloat16)
    query_raw = jnp.dot(normed_one, w_query, preferred_element_type=jnp.float32)
    key_raw = jnp.dot(normed_one, w_key, preferred_element_type=jnp.float32)
    values = jnp.dot(normed_one, w_value, preferred_element_type=jnp.float32).astype(jnp.bfloat16)
    query_square, key_square = lax.psum(
        (jnp.sum(query_raw * query_raw, axis=-1), jnp.sum(key_raw * key_raw, axis=-1)), "tensor"
    )
    query_scale = lax.rsqrt(query_square / model_width + NORM_EPSILON)[:, None]
    key_scale = lax.rsqrt(key_square / model_width + NORM_EPSILON)[:, None]
    query_gain = q_gain.reshape(-1)
    key_gain = k_gain.reshape(-1)
    queries = rotate(
        (query_raw * query_scale * query_gain).reshape(row_count, heads, HD), cosine, sine
    ).astype(jnp.bfloat16)
    key_heads = rotate(
        (key_raw * key_scale * key_gain).reshape(row_count, heads, HD), cosine, sine
    ).astype(jnp.bfloat16)
    value_heads = values.reshape(row_count, heads, HD)
    labels = jnp.stack([documents // 256, documents % 256]).astype(jnp.bfloat16)
    previous_one = previous_block((key_heads, value_heads, labels))
    previous_two = previous_block(previous_one)
    all_keys = jnp.concatenate([previous_two[0], previous_one[0], key_heads], axis=0)
    all_values = jnp.concatenate([previous_two[1], previous_one[1], value_heads], axis=0)
    all_labels = jnp.concatenate([previous_two[2], previous_one[2], labels], axis=1)
    key_pos = first_row - 2 * row_count + jnp.arange(3 * row_count, dtype=jnp.int32)
    same_doc = (all_labels[0][None, :] == labels[0][:, None]) & (
        all_labels[1][None, :] == labels[1][:, None]
    )
    allowed = (
        same_doc
        & (key_pos[None, :] <= positions[:, None])
        & (positions[:, None] - key_pos[None, :] < WINDOW)
        & (key_pos[None, :] >= 0)
    )

    def masked_scores():
        raw_scores = (
            jnp.einsum("qhd,khd->hqk", queries, all_keys, preferred_element_type=jnp.float32)
            * score_scale
        )
        return jnp.where(allowed[None], raw_scores, -1e30)

    scores = masked_scores()
    highest = jnp.max(scores, axis=-1, keepdims=True)
    weights = jnp.where(allowed[None], jnp.exp(scores - highest), 0.0)
    denominator = jnp.sum(weights, axis=-1, keepdims=True)
    log_total = highest + jnp.log(denominator)
    attn_probs = weights / denominator
    attended = jnp.einsum(
        "hqk,khd->qhd",
        attn_probs.astype(jnp.bfloat16),
        all_values,
        preferred_element_type=jnp.float32,
    )
    attended = attended.reshape(row_count, -1).astype(jnp.bfloat16)
    attention = lax.psum(jnp.dot(attended, w_out, preferred_element_type=jnp.float32), "tensor")
    state = inputs + attention
    scale_two = lax.rsqrt(jnp.mean(state * state, axis=-1, keepdims=True) + NORM_EPSILON)
    normed_two = (state * scale_two * norm2_gain).astype(jnp.bfloat16)
    router_probs = jax.nn.softmax(
        jnp.dot(normed_two, router_w, preferred_element_type=jnp.float32), axis=-1
    )
    chosen = (routes[:, :, None] == jnp.arange(experts, dtype=jnp.int32)[None, None, :]).astype(
        jnp.float32
    )
    gates = jnp.sum(chosen * router_probs[:, None, :], axis=-1)
    flat_routes = routes.reshape(-1)
    onehot = (flat_routes[:, None] == jnp.arange(experts, dtype=jnp.int32)[None, :]).astype(
        jnp.int32
    )
    slot_index = jnp.sum(jnp.cumsum(onehot, axis=0) * onehot, axis=1) - 1
    target = flat_routes * capacity + slot_index
    source = (
        jnp.full((experts * capacity,), -1, jnp.int32)
        .at[target]
        .set(jnp.arange(row_count * TOP, dtype=jnp.int32))
    )
    live_slot = source >= 0
    pick_index = jnp.maximum(source, 0)
    send_rows = jnp.where(
        live_slot[:, None], normed_two[pick_index // TOP], jnp.zeros((), jnp.bfloat16)
    ).reshape(groups, slots_group, model_width)
    grad_float = out_grad.astype(jnp.float32)
    pick_grads = (
        (gates[:, :, None] * grad_float[:, None, :])
        .astype(jnp.bfloat16)
        .reshape(row_count * TOP, model_width)
    )
    send_grads = jnp.where(
        live_slot[:, None], pick_grads[pick_index], jnp.zeros((), jnp.bfloat16)
    ).reshape(groups, slots_group, model_width)
    arrived = lax.all_to_all(send_rows, "expert", split_axis=0, concat_axis=0, tiled=True)
    stacked = arrived.reshape(groups, local_experts, capacity, model_width)
    gate_pre = jnp.einsum("secd,edf->secf", stacked, w_gate, preferred_element_type=jnp.float32)
    up_pre = jnp.einsum("secd,edf->secf", stacked, w_up, preferred_element_type=jnp.float32)
    activated = jax.nn.silu(gate_pre)
    inner_act = (activated * up_pre).astype(jnp.bfloat16)
    produced = jnp.einsum(
        "secf,efd->secd", inner_act, w_down, preferred_element_type=jnp.float32
    ).astype(jnp.bfloat16)
    returned = lax.all_to_all(
        produced.reshape(groups, slots_group, model_width),
        "expert",
        split_axis=0,
        concat_axis=0,
        tiled=True,
    )
    back_rows = (
        returned.reshape(experts * capacity, model_width)[target]
        .reshape(row_count, TOP, model_width)
        .astype(jnp.float32)
    )
    expert_part = jnp.sum(gates[:, :, None] * back_rows, axis=1)
    expert_mix = lax.psum(expert_part.astype(jnp.bfloat16), "tensor").astype(jnp.float32)
    output = (state + expert_mix).astype(jnp.bfloat16)
    gate_part = jnp.sum(grad_float[:, None, :] * back_rows, axis=-1)
    arrived_grad = lax.all_to_all(send_grads, "expert", split_axis=0, concat_axis=0, tiled=True)
    slot_grad = arrived_grad.reshape(groups, local_experts, capacity, model_width)
    w_down_grad = jnp.einsum(
        "secf,secd->efd", inner_act, slot_grad, preferred_element_type=jnp.float32
    )
    inner_grad = jnp.einsum("secd,efd->secf", slot_grad, w_down, preferred_element_type=jnp.float32)
    logistic = jax.nn.sigmoid(gate_pre)
    gate_pre_grad = (inner_grad * up_pre * logistic * (1.0 + gate_pre * (1.0 - logistic))).astype(
        jnp.bfloat16
    )
    up_pre_grad = (inner_grad * activated).astype(jnp.bfloat16)
    w_gate_grad = jnp.einsum(
        "secd,secf->edf", stacked, gate_pre_grad, preferred_element_type=jnp.float32
    )
    w_up_grad = jnp.einsum(
        "secd,secf->edf", stacked, up_pre_grad, preferred_element_type=jnp.float32
    )
    row_grad = jnp.einsum(
        "secf,edf->secd", gate_pre_grad, w_gate, preferred_element_type=jnp.float32
    )
    row_grad = (
        row_grad
        + jnp.einsum("secf,edf->secd", up_pre_grad, w_up, preferred_element_type=jnp.float32)
    ).astype(jnp.bfloat16)
    grad_back = lax.all_to_all(
        row_grad.reshape(groups, slots_group, model_width),
        "expert",
        split_axis=0,
        concat_axis=0,
        tiled=True,
    )
    grad_picks = (
        grad_back.reshape(experts * capacity, model_width)[target]
        .reshape(row_count, TOP, model_width)
        .astype(jnp.float32)
    )
    normed_part = jnp.sum(grad_picks, axis=1)
    normed_two_grad, gate_cot = lax.psum((normed_part, gate_part), "tensor")
    prob_cot = jnp.sum(gate_cot[:, :, None] * chosen, axis=1)
    logit_cot = router_probs * (prob_cot - jnp.sum(router_probs * prob_cot, axis=-1, keepdims=True))
    router_float = router_w.astype(jnp.float32)
    normed_two_grad = normed_two_grad + jnp.einsum(
        "te,de->td", logit_cot, router_float, precision=HIGHEST_PRECISION
    )
    router_grad = jnp.einsum(
        "td,te->de", normed_two.astype(jnp.float32), logit_cot, precision=HIGHEST_PRECISION
    )
    norm2_grad = jnp.sum(normed_two_grad * state * scale_two, axis=0)
    inner_two = jnp.sum(normed_two_grad * norm2_gain * state, axis=-1, keepdims=True)
    state_cot = (
        grad_float
        + scale_two * norm2_gain * normed_two_grad
        - state * scale_two**3 * inner_two / model_width
    )
    state_low = state_cot.astype(jnp.bfloat16)
    w_out_grad = jnp.einsum("tf,td->fd", attended, state_low, preferred_element_type=jnp.float32)
    attended_cot = (
        jnp.einsum("td,fd->tf", state_low, w_out, preferred_element_type=jnp.float32)
        .astype(jnp.bfloat16)
        .reshape(row_count, heads, HD)
    )
    scores = masked_scores()
    attn_probs = jnp.where(allowed[None], jnp.exp(scores - log_total), 0.0)
    value_cot_all = jnp.einsum(
        "hqk,qhd->khd",
        attn_probs.astype(jnp.bfloat16),
        attended_cot,
        preferred_element_type=jnp.float32,
    )
    prob_grad = jnp.einsum(
        "qhd,khd->hqk", attended_cot, all_values, preferred_element_type=jnp.float32
    )
    delta = jnp.sum(attn_probs * prob_grad, axis=-1, keepdims=True)
    score_cot = (attn_probs * (prob_grad - delta)).astype(jnp.bfloat16)
    query_cot = (
        jnp.einsum("hqk,khd->qhd", score_cot, all_keys, preferred_element_type=jnp.float32)
        * score_scale
    )
    key_cot_all = (
        jnp.einsum("hqk,qhd->khd", score_cot, queries, preferred_element_type=jnp.float32)
        * score_scale
    )
    carried = following_block((key_cot_all[:row_count], value_cot_all[:row_count]))
    carried = following_block(
        (
            key_cot_all[row_count : 2 * row_count] + carried[0],
            value_cot_all[row_count : 2 * row_count] + carried[1],
        )
    )
    key_cot = key_cot_all[2 * row_count :] + carried[0]
    value_cot = value_cot_all[2 * row_count :] + carried[1]
    query_norm_cot = rotate_back(query_cot, cosine, sine).reshape(row_count, -1)
    key_norm_cot = rotate_back(key_cot, cosine, sine).reshape(row_count, -1)
    q_gain_local = jnp.sum(query_norm_cot * query_raw * query_scale, axis=0).reshape(heads, HD)
    k_gain_local = jnp.sum(key_norm_cot * key_raw * key_scale, axis=0).reshape(heads, HD)
    query_inner, key_inner = lax.psum(
        (
            jnp.sum(query_norm_cot * query_gain * query_raw, axis=-1),
            jnp.sum(key_norm_cot * key_gain * key_raw, axis=-1),
        ),
        "tensor",
    )
    query_raw_cot = (
        query_scale * query_gain * query_norm_cot
        - query_raw * query_scale**3 * query_inner[:, None] / model_width
    ).astype(jnp.bfloat16)
    key_raw_cot = (
        key_scale * key_gain * key_norm_cot
        - key_raw * key_scale**3 * key_inner[:, None] / model_width
    ).astype(jnp.bfloat16)
    value_low = value_cot.reshape(row_count, -1).astype(jnp.bfloat16)
    w_query_local = jnp.einsum(
        "td,tf->df", normed_one, query_raw_cot, preferred_element_type=jnp.float32
    )
    w_key_local = jnp.einsum(
        "td,tf->df", normed_one, key_raw_cot, preferred_element_type=jnp.float32
    )
    w_value_local = jnp.einsum(
        "td,tf->df", normed_one, value_low, preferred_element_type=jnp.float32
    )
    normed_part_one = jnp.einsum(
        "tf,df->td", query_raw_cot, w_query, preferred_element_type=jnp.float32
    )
    normed_part_one = normed_part_one + jnp.einsum(
        "tf,df->td", key_raw_cot, w_key, preferred_element_type=jnp.float32
    )
    normed_part_one = normed_part_one + jnp.einsum(
        "tf,df->td", value_low, w_value, preferred_element_type=jnp.float32
    )
    normed_one_grad = lax.psum(normed_part_one.astype(jnp.bfloat16), "tensor").astype(jnp.float32)
    norm1_grad = jnp.sum(normed_one_grad * inputs * scale_one, axis=0)
    inner_one = jnp.sum(normed_one_grad * norm1_gain * inputs, axis=-1, keepdims=True)
    input_grad = (
        state_cot
        + scale_one * norm1_gain * normed_one_grad
        - inputs * scale_one**3 * inner_one / model_width
    )
    summed = (
        lax.psum_scatter(
            w_query_local.astype(jnp.bfloat16), "expert", scatter_dimension=0, tiled=True
        ).astype(jnp.float32),
        lax.psum_scatter(
            w_key_local.astype(jnp.bfloat16), "expert", scatter_dimension=0, tiled=True
        ).astype(jnp.float32),
        lax.psum_scatter(
            w_value_local.astype(jnp.bfloat16), "expert", scatter_dimension=0, tiled=True
        ).astype(jnp.float32),
        lax.psum_scatter(
            w_out_grad.astype(jnp.bfloat16), "expert", scatter_dimension=1, tiled=True
        ).astype(jnp.float32),
        lax.psum_scatter(
            router_grad.astype(jnp.bfloat16), "expert", scatter_dimension=0, tiled=True
        ).astype(jnp.float32),
        lax.psum_scatter(
            norm1_grad.astype(jnp.bfloat16), "expert", scatter_dimension=0, tiled=True
        ).astype(jnp.float32),
        lax.psum_scatter(
            norm2_grad.astype(jnp.bfloat16), "expert", scatter_dimension=0, tiled=True
        ).astype(jnp.float32),
        lax.psum_scatter(
            q_gain_local.astype(jnp.bfloat16), "expert", scatter_dimension=1, tiled=True
        ).astype(jnp.float32),
        lax.psum_scatter(
            k_gain_local.astype(jnp.bfloat16), "expert", scatter_dimension=1, tiled=True
        ).astype(jnp.float32),
    )
    return (
        output,
        input_grad,
        summed[5],
        summed[7],
        summed[8],
        summed[0],
        summed[1],
        summed[2],
        summed[3],
        summed[6],
        summed[4],
        w_gate_grad,
        w_up_grad,
        w_down_grad,
    )


MESH = pl.DeviceIdType.MESH
ANY = pl.BlockSpec(memory_space=pl.ANY)
VMEM = pl.BlockSpec(memory_space=pltpu.VMEM)
VMEM_BYTES = 62 * 1024 * 1024
LOW = jnp.bfloat16
FULL = jnp.float32


def place():
    group, part = lax.axis_index("expert"), lax.axis_index("tensor")
    return group // 2, group % 2, part // 2, part % 2


def device(z, x, y, core):
    return (2 * z + x, 2 * y + core)


def swapped(index, step):
    result, bit = index, 1
    while bit <= step:
        if step & bit:
            result = result + bit - 2 * bit * ((index // bit) % 2)
        bit *= 2
    return result


def greet(partners):
    barrier = pltpu.get_barrier_semaphore()
    for partner in partners:
        pl.semaphore_signal(barrier, inc=1, device_id=partner, device_id_type=MESH)
    pl.semaphore_wait(barrier, len(partners))


def remote(source, target, send, arrive, to):
    return pltpu.make_async_remote_copy(
        src_ref=source, dst_ref=target, send_sem=send, recv_sem=arrive, device_id=to, device_id_type=MESH
    )


def dma(*shape):
    return pltpu.SemaphoreType.DMA(shape)


def comm_params(number):
    return pltpu.CompilerParams(collective_id=number, has_side_effects=True, vmem_limit_bytes=VMEM_BYTES)


def add_rows(target, sources, rows, step=16):
    @pl.loop(0, rows // step)
    def _(index):
        part = pl.ds(index * step, step)
        total = sources[0][part].astype(FULL)
        for source in sources[1:]:
            total = total + source[part].astype(FULL)
        target[part] = total.astype(target.dtype)


class Copies:
    def __init__(self):
        self.open = []

    def start(self, copy):
        copy.start()
        self.open.append((copy, set()))
        return copy

    def once(self, copy, what):
        done = next(done for entry, done in self.open if entry is copy)
        new = what not in done
        done.add(what)
        return new

    def arrived(self, copy):
        if self.once(copy, "arrived"):
            copy.wait_recv()

    def sent(self, copy):
        if self.once(copy, "sent"):
            copy.wait_send()

    def finish(self):
        for copy, done in self.open:
            if "sent" not in done:
                copy.wait_send()
            if "arrived" not in done:
                copy.wait_recv()


class Gather:
    def __init__(self, copies, block, target, rows, z_send, z_recv, p_send, p_recv, c_send, c_recv):
        self.copies, self.block, self.target, self.rows = copies, block, target, rows
        self.z_send, self.z_recv, self.p_send, self.p_recv = z_send, z_recv, p_send, p_recv
        self.c_send, self.c_recv = c_send, c_recv
        z, x, y, core = place()
        self.over_x, self.over_y = device(z, 1 - x, y, core), device(z, x, 1 - y, core)
        self.here, self.x_place, self.y_place = 2 * x + y, 2 * (1 - x) + y, 2 * x + 1 - y
        self.far = 2 * (1 - x) + 1 - y
        self.column = [device(swapped(z, step), x, y, core) for step in range(target.shape[0])]
        self.along, self.planes, self.diagonals, self.shared = {}, {}, {}, {}
        edge = rows * 3 // 8
        self.middle = (edge, rows - 2 * edge)
        self.halves = {0: ((0, rows // 2), (rows // 2, rows // 2)), 1: ((0, edge), (rows - edge, edge))}

    def at(self, step, spot, span):
        first, count = span
        return self.target.at[step, pl.ds(pl.multiple_of(spot * self.rows + first, 16), count)]

    def lift(self, step):
        low, whole = step & -step, (0, self.rows)
        source = self.block if step == low else self.at(step - low, self.here, whole)
        self.along[step] = self.copies.start(
            remote(source, self.at(step, self.here, whole), self.z_send.at[step], self.z_recv.at[step], self.column[low])
        )

    def spread(self, step):
        if step:
            self.copies.arrived(self.along[step])
            bit = 1
            while bit < step & -step:
                self.lift(step | bit)
                bit *= 2
        planes = []
        for number, (to, part) in enumerate([(self.over_x, 0), (self.over_y, 1), (self.over_x, 1), (self.over_y, 0)]):
            span = self.halves[step % 2][part]
            here = self.at(step, self.here, span)
            source = here if step else self.block.at[pl.ds(*span)]
            planes.append(self.copies.start(remote(source, here, self.p_send.at[step, number], self.p_recv.at[step, number], to)))
        self.planes[step] = planes

    def turn(self, step):
        passed = []
        for part, spot, to in ((0, self.x_place, self.over_y), (1, self.y_place, self.over_x)):
            self.copies.arrived(self.planes[step][part])
            here = self.at(step, spot, self.halves[step % 2][part])
            passed.append(
                self.copies.start(remote(here, here, self.p_send.at[step, 4 + part], self.p_recv.at[step, 4 + part], to))
            )
        self.diagonals[step] = passed

    def share(self, step):
        self.complete(step)
        copies = []
        for number, spot in enumerate((self.x_place, self.y_place, self.far)):
            copies.append(
                self.copies.start(
                    remote(
                        self.at(step, spot, self.middle), self.at(step + 1, spot, self.middle),
                        self.c_send.at[step // 2, number], self.c_recv.at[step // 2, number], self.column[1],
                    )
                )
            )
        self.shared[step + 1] = copies

    def complete(self, step):
        for copy in self.planes[step] + self.diagonals[step] + self.shared.get(step, []):
            self.copies.arrived(copy)

    @staticmethod
    def scratch(depth):
        return [dma(depth), dma(depth), dma(depth, 6), dma(depth, 6), dma(depth // 2, 3), dma(depth // 2, 3)]


class Scatter:
    def __init__(self, copies, work, diagonal, from_x, from_y, from_z, rows, send, recv, middle=None):
        self.copies, self.work, self.rows, self.send, self.recv = copies, work, rows, send, recv
        self.diagonal, self.from_x, self.from_y, self.from_z = diagonal, from_x, from_y, from_z
        z, x, y, core = place()
        self.over_x, self.over_y = device(z, 1 - x, y, core), device(z, x, 1 - y, core)
        self.here, self.x_place, self.y_place = 2 * x + y, 2 * (1 - x) + y, 2 * x + 1 - y
        self.far = 2 * (1 - x) + 1 - y
        self.column = [device(swapped(z, step), x, y, core) for step in range(work.shape[0])]
        self.corners, self.sides, self.along, self.shared, self.middle = {}, {}, {}, {}, middle
        edge, half = rows * 3 // 8, rows // 2
        self.center = (edge, rows - 2 * edge)
        self.halves = {0: ((0, half), (half, half)), 1: ((0, half), (half, half))}
        self.pieces = {0: ((0, rows),), 1: ((0, rows),)}
        if middle:
            self.halves[1] = self.pieces[1] = ((0, edge), (rows - edge, edge))

    def at(self, step, spot, span):
        first, count = span
        return self.work.at[step, pl.ds(pl.multiple_of(spot * self.rows + first, 16), count)]

    def copy(self, step, number, source, target, to):
        return self.copies.start(remote(source, target, self.send.at[step, number], self.recv.at[step, number], to))

    def share(self, step):
        landed, send, recv = self.middle
        self.shared[step - 1] = [
            self.copies.start(
                remote(
                    self.at(step, spot, self.center), landed.at[step // 2, spot],
                    send.at[step // 2, spot], recv.at[step // 2, spot], self.column[1],
                )
            )
            for spot in range(4)
        ]

    def corner(self, step):
        for spot, copy in enumerate(self.shared.get(step, [])):
            self.copies.arrived(copy)
            mine = self.at(step, spot, self.center)
            add_rows(mine, [mine, self.middle[0].at[step // 2, spot]], self.center[1])
        first, second = self.halves[step % 2]
        self.corners[step] = (
            self.copy(step, 0, self.at(step, self.far, first), self.diagonal.at[step, pl.ds(*first)], self.over_y),
            self.copy(step, 1, self.at(step, self.far, second), self.diagonal.at[step, pl.ds(*second)], self.over_x),
        )

    def side(self, step):
        first, second = self.halves[step % 2]
        via_y, via_x = self.corners[step]

        def to_x(number, span):
            return self.copy(step, number, self.at(step, self.x_place, span), self.from_x.at[step, pl.ds(*span)], self.over_x)

        def to_y(number, span):
            return self.copy(step, number, self.at(step, self.y_place, span), self.from_y.at[step, pl.ds(*span)], self.over_y)

        sides = [to_x(2, second), to_y(3, first)]
        self.copies.arrived(via_y)
        mine = self.at(step, self.x_place, first)
        add_rows(mine, [mine, self.diagonal.at[step, pl.ds(*first)]], first[1])
        sides.append(to_x(4, first))
        self.copies.arrived(via_x)
        mine = self.at(step, self.y_place, second)
        add_rows(mine, [mine, self.diagonal.at[step, pl.ds(*second)]], second[1])
        sides.append(to_y(5, second))
        self.sides[step] = sides

    def below(self, step, odd_rows):
        terms, bit = [], 1
        while bit < (step & -step if step else len(self.column)):
            if odd_rows or (step | bit) % 2 == 0:
                for copy in self.along[step | bit]:
                    self.copies.arrived(copy)
                terms.append(self.from_z.at[step | bit])
            bit *= 2
        return terms

    def spans(self):
        return [(span, True) for span in self.pieces[1]] + ([(self.center, False)] if self.middle else [])

    def climb(self, step):
        for copy in self.sides[step]:
            self.copies.arrived(copy)
        if step:
            for span, odd_rows in self.spans():
                if odd_rows or step % 2 == 0:
                    mine, part = self.at(step, self.here, span), pl.ds(*span)
                    terms = [mine, self.from_x.at[step, part], self.from_y.at[step, part]]
                    terms += [term.at[part] for term in self.below(step, odd_rows)]
                    add_rows(mine, terms, span[1])
            self.along[step] = []
            for number, span in enumerate(self.pieces[step % 2]):
                mine, part = self.at(step, self.here, span), pl.ds(*span)
                self.along[step].append(
                    self.copy(step, 6 + number, mine, self.from_z.at[step, part], self.column[step & -step])
                )

    def result(self, target, more=()):
        for span, odd_rows in self.spans():
            part = pl.ds(*span)
            terms = [self.at(0, self.here, span), self.from_x.at[0, part], self.from_y.at[0, part]]
            terms += [term.at[part] for term in self.below(0, odd_rows)] + [term.at[part] for term in more]
            add_rows(target.at[part], terms, span[1])

    @staticmethod
    def scratch(depth, rows, width):
        return [pltpu.VMEM((depth, rows, width), LOW)] * 4 + [dma(depth, 8), dma(depth, 8)]


def experts_kernel(
    depth, rows, local, hidden,
    x_ref, gates_ref, grad_ref, gate_ref, up_ref, down_ref,
    sum_ref, cots_ref, normed_ref, gated_ref, gate_grad_ref, up_grad_ref, produced_ref,
    wg, wu, wd, x_all, grads, work, y_out, gated, gate_grad, up_grad, gates, gate_wide, cots, cot_rows,
    diagonal, from_x, from_y, from_z, r_send, r_recv,
    z_send, z_recv, p_send, p_recv, c_send, c_recv, s_send, s_recv, w_send, w_recv, w_load, g_load, saves, local_sem,
):
    z, x, y, core = place()
    here, sibling = 2 * x + y, device(z, x, y, 1 - core)
    others = [
        (step, turn, (swapped(z, step), swapped(x, turn // 2), swapped(y, turn % 2)))
        for step in range(depth)
        for turn in range(4)
        if step or turn
    ]
    greet([device(*other, core) for _, _, other in others] + [sibling])
    copies = Copies()
    smalls = []
    for step, turn, other in others:
        oz, ox, oy = other
        smalls.append(
            copies.start(
                remote(
                    gates_ref.at[2 * oz + ox], gates.at[step, here], s_send.at[0, step, turn], s_recv.at[0, step, turn],
                    device(oz, ox, oy, core),
                )
            )
        )
    gather = Gather(copies, x_ref, x_all, rows, z_send, z_recv, p_send, p_recv, c_send, c_recv)
    gather.spread(0)
    gather.lift(1)
    gather.lift(2)
    plain = []

    def fetch(source, target, sem):
        copy = pltpu.make_async_copy(source, target, sem)
        copy.start()
        return copy

    plain.append(fetch(x_ref, gather.at(0, here, (0, rows)), local_sem.at[0]))
    weights = []
    for index in range(local):
        first = pl.multiple_of((core * local + index) * hidden, hidden)
        columns = pl.ds(first, hidden)
        for number, (source, target) in enumerate(
            [(gate_ref, wg.at[:, columns]), (up_ref, wu.at[:, columns]), (down_ref, wd.at[columns])]
        ):
            weights.append(copies.start(remote(source.at[index], target, w_send.at[number, index], w_recv.at[number, index], sibling)))
            plain.append(fetch(source.at[index], target, w_load.at[number, index]))
    plain.append(fetch(gates_ref.at[2 * z + x], gates.at[0, here], local_sem.at[1]))
    sequence = (0, 2, 3, 1)
    grad_copies = [fetch(grad_ref.at[0], grads.at[0], g_load.at[0])]
    scatter = Scatter(copies, work, diagonal, from_x, from_y, from_z, rows, r_send, r_recv)
    saving, producing, keeping = [], [], []
    wave_rows = 4 * rows
    lanes = lax.broadcasted_iota(jnp.int32, (wave_rows, 128), 1)

    def first_half(step):
        for copy in saving:
            copy.wait()
        saving.clear()
        for spot in range(4):
            padded = jnp.concatenate([gates[step, spot], jnp.zeros((120, 128), FULL)], axis=0)
            gate_wide[pl.ds(spot * rows, rows), :] = padded.T
        cots[...] = jnp.zeros_like(cots)
        turn = sequence.index(step)
        grad_copies[turn].wait()
        if turn + 1 < depth:
            slot = (turn + 1) % 2
            grad_copies.append(fetch(grad_ref.at[sequence[turn + 1]], grads.at[slot], g_load.at[slot]))
        grad = grads.at[turn % 2]

        @pl.loop(0, 2 * local)
        def _(unit):
            columns = pl.ds(pl.multiple_of(unit * hidden, hidden), hidden)
            expert = lax.rem(unit, local)
            gate_pre = dot(x_all[step], wg[:, columns])
            up_pre = dot(x_all[step], wu[:, columns])
            back = dot_t(grad[...], wd[columns, :])
            logistic = 1.0 / (1.0 + jnp.exp(-gate_pre))
            activated = gate_pre * logistic
            inner = activated * up_pre
            cot = jnp.sum(inner * back, axis=-1, keepdims=True)
            cots[...] += jnp.where(lanes == expert, cot, 0.0)
            gate = jnp.sum(jnp.where(lanes == expert, gate_wide[...], 0.0), axis=-1, keepdims=True)
            gated[:, columns] = (gate * inner).astype(LOW)
            inner_grad = gate * back
            gate_grad[:, columns] = (inner_grad * up_pre * logistic * (1.0 + gate_pre * (1.0 - logistic))).astype(LOW)
            up_grad[:, columns] = (inner_grad * activated).astype(LOW)

        for spot in range(4):
            cot_rows[step, spot] = cots[pl.ds(spot * rows, rows), :].T[:8]
        for other_step, turn, (oz, ox, oy) in others:
            if other_step == step:
                copies.start(
                    remote(
                        cot_rows.at[step, 2 * ox + oy], cots_ref.at[step, here], s_send.at[1, step, turn], s_recv.at[1, step, turn],
                        device(oz, ox, oy, core),
                    )
                )
        for number, (source, target) in enumerate([(gated, gated_ref), (gate_grad, gate_grad_ref), (up_grad, up_grad_ref)]):
            saving.append(fetch(source, target.at[step], saves.at[number]))
        keeping.append(fetch(x_all.at[step], normed_ref.at[step], saves.at[4 + step]))

    def second_half(step):
        for copy in producing:
            copy.wait()
        producing.clear()
        tile = 512

        @pl.loop(0, x_all.shape[2] // tile)
        def _(index):
            columns = pl.ds(pl.multiple_of(index * tile, tile), tile)
            y_out[:, columns] = dot(gated[...], wd[:, columns]).astype(LOW)
            work[step, :, columns] = (dot_t(gate_grad[...], wg[columns, :]) + dot_t(up_grad[...], wu[columns, :])).astype(LOW)

        producing.append(fetch(y_out, produced_ref.at[step], saves.at[3]))

    gather.turn(0)
    gather.spread(1)
    gather.share(0)
    for copy in plain:
        copy.wait()
    for copy in weights + smalls:
        copies.arrived(copy)
    first_half(0)
    gather.turn(1)
    gather.spread(2)
    second_half(0)
    gather.turn(2)
    gather.spread(3)
    gather.share(2)
    first_half(2)
    gather.turn(3)
    second_half(2)
    scatter.corner(2)
    gather.complete(3)
    first_half(3)
    scatter.side(2)
    second_half(3)
    scatter.corner(3)
    gather.complete(1)
    first_half(1)
    scatter.side(3)
    second_half(1)
    scatter.corner(1)
    scatter.corner(0)
    scatter.climb(3)
    scatter.side(1)
    scatter.climb(2)
    scatter.side(0)
    scatter.climb(1)
    scatter.climb(0)
    scatter.result(sum_ref)
    own_cots = fetch(cot_rows.at[0, here], cots_ref.at[0, here], local_sem.at[2])
    own_cots.wait()
    for copy in saving + producing + keeping:
        copy.wait()
    copies.finish()


def run_experts(block, gates, grads, w_gate, w_up, w_down, number):
    depth, wave, width = grads.shape
    rows = wave // 4
    local, _, hidden = w_gate.shape
    units = 2 * local * hidden
    kept = jax.ShapeDtypeStruct((depth, wave, units), LOW)
    wide = jax.ShapeDtypeStruct((depth, wave, width), LOW)
    return pl.pallas_call(
        functools.partial(experts_kernel, depth, rows, local, hidden),
        out_shape=(
            jax.ShapeDtypeStruct((rows, width), FULL),
            jax.ShapeDtypeStruct((depth, 4, 8, 128), FULL),
            wide, kept, kept, kept, wide,
        ),
        in_specs=[ANY] * 6,
        out_specs=(VMEM, VMEM, ANY, ANY, ANY, ANY, ANY),
        scratch_shapes=[
            pltpu.VMEM((width, units), LOW), pltpu.VMEM((width, units), LOW), pltpu.VMEM((units, width), LOW),
            pltpu.VMEM((depth, wave, width), LOW), pltpu.VMEM((2, wave, width), LOW),
            pltpu.VMEM((depth, wave, width), LOW), pltpu.VMEM((wave, width), LOW),
            pltpu.VMEM((wave, units), LOW), pltpu.VMEM((wave, units), LOW), pltpu.VMEM((wave, units), LOW),
            pltpu.VMEM((depth, 4, 8, 128), FULL), pltpu.VMEM((wave, 128), FULL), pltpu.VMEM((wave, 128), FULL),
            pltpu.VMEM((depth, 4, 8, 128), FULL),
        ]
        + Scatter.scratch(depth, rows, width)
        + [
            *Gather.scratch(depth), dma(2, depth, 4), dma(2, depth, 4),
            dma(3, local), dma(3, local), dma(3, local), dma(2), dma(4 + depth), dma(3),
        ],
        compiler_params=comm_params(number),
    )(block, gates, grads, w_gate, w_up, w_down)


class TensorScatter:
    def __init__(self, copies, work, from_pair, from_y, send, recv):
        self.copies, self.work, self.from_pair, self.from_y, self.send, self.recv = copies, work, from_pair, from_y, send, recv
        z, x, self.y, self.core = place()
        self.sibling, self.over_y = device(z, x, self.y, 1 - self.core), device(z, x, 1 - self.y, self.core)
        self.rows = work.shape[2]

    def begin(self):
        self.pairs = []
        for turn in (1, 0):
            source = self.work.at[swapped(self.y, turn), 1 - self.core]
            self.pairs.append(
                self.copies.start(remote(source, self.from_pair.at[turn], self.send.at[turn], self.recv.at[turn], self.sibling))
            )

    def cross(self):
        self.copies.arrived(self.pairs[0])
        block = self.work.at[1 - self.y, self.core]
        add_rows(block, [block, self.from_pair.at[1]], self.rows)
        self.across = self.copies.start(remote(block, self.from_y, self.send.at[2], self.recv.at[2], self.over_y))

    def result(self, target):
        self.copies.arrived(self.pairs[1])
        self.copies.arrived(self.across)
        add_rows(target, [self.work.at[self.y, self.core], self.from_pair.at[0], self.from_y], self.rows)

    @staticmethod
    def scratch(rows, width):
        return [
            pltpu.VMEM((2, 2, rows, width), LOW),
            pltpu.VMEM((2, rows, width), LOW),
            pltpu.VMEM((rows, width), LOW),
            dma(3),
            dma(3),
        ]


class TensorGather:
    def __init__(self, copies, block, target, send, recv):
        self.copies, self.target, self.send, self.recv = copies, target, send, recv
        z, x, self.y, self.core = place()
        self.sibling, over_y = device(z, x, self.y, 1 - self.core), device(z, x, 1 - self.y, self.core)
        mine = target.at[self.y, self.core]
        self.across = copies.start(remote(block, mine, send.at[0], recv.at[0], over_y))
        self.near = copies.start(remote(block, mine, send.at[1], recv.at[1], self.sibling))
        self.own = pltpu.make_async_copy(block, mine, send.at[3])
        self.own.start()

    def cross(self):
        self.copies.arrived(self.across)
        block = self.target.at[1 - self.y, self.core]
        self.passed = self.copies.start(remote(block, block, self.send.at[2], self.recv.at[2], self.sibling))

    def finish(self):
        self.own.wait()
        self.copies.arrived(self.near)
        self.copies.arrived(self.passed)


def partners_of(depth):
    z, x, y, core = place()
    return [device(swapped(z, step), x, y, core) for step in range(1, depth)] + [
        device(z, 1 - x, y, core),
        device(z, x, 1 - y, core),
        device(z, x, y, 1 - core),
        device(swapped(z, 1), 1 - x, y, core),
    ]


def mask_bias(bias, key_docs, query_docs, length):
    blocks = bias.shape[0] // length

    @pl.loop(0, bias.shape[0] // 128)
    def _(index):
        part = pl.ds(pl.multiple_of(index * 128, 128), 128)
        key = index * 128 + lax.broadcasted_iota(jnp.int32, (128, length), 0) - (blocks - 1) * length
        query = lax.broadcasted_iota(jnp.int32, (128, length), 1)
        seen = (key_docs[part, :] == query_docs[0:1, :]) & (key <= query) & (query - key < WINDOW)
        bias[part, :] = jnp.where(seen, 0.0, -1e30).astype(bias.dtype)


def exchange(copies, mine, landed, send, recv, mates):
    return [
        copies.start(remote(mine, landed.at[number], send.at[number], recv.at[number], device(*mate)))
        for number, mate in enumerate(mates)
    ]


def mates_of():
    z, x, y, core = place()
    return [(z, x, swapped(y, turn // 2), swapped(core, turn % 2)) for turn in range(1, 4)]


def as_rows(columns):
    lanes = lax.broadcasted_iota(jnp.int32, (columns[0].shape[0], 128), 1)
    wide = jnp.zeros(lanes.shape, FULL)
    for index, column in enumerate(columns):
        wide = jnp.where(lanes == index, column, wide)
    return wide.T[:8]


def as_columns(rows_of_eight):
    length = rows_of_eight.shape[1]
    return jnp.concatenate([rows_of_eight, jnp.zeros((120, length), FULL)], axis=0).T


def attention_kernel(
    depth, rows, heads, chain, local,
    tokens_ref, wq_ref, wk_ref, wv_ref, wo_ref, grads_ref,
    gain1_ref, q_gain_ref, k_gain_ref, cosine_ref, sine_ref, docs_row, gain2_ref, router_ref, picked_ref,
    normed_turned, q_raw, k_raw, queries, kv_all, key_docs, scales, attended, logs, state_ref, normed2_ref, probs_ref, gates_ref, own_tokens, own_grads,
    all_grad,
    tokens, normed_ref, wq, wk, wv, wo, docs_ref, logits_ref, docs_in, squares, squares_in, scores, totals, bias, partial, from_pair, from_y, sum_ref,
    t_send, t_recv, z_send, z_recv, p_send, p_recv, c_send, c_recv, h_send, h_recv, d_send, d_recv, q_send, q_recv, load,
):
    z, x, y, core = place()
    group, part = lax.axis_index("expert"), lax.axis_index("tensor")
    spot = group % chain
    length, width = tokens.shape
    wide = heads * HD
    scale = HD ** (-0.5)
    own_rows = pl.ds(pl.multiple_of(part * rows, rows), rows)
    grad_ref = grads_ref.at[own_rows]
    docs_ref[...] = jnp.broadcast_to(docs_row[...], docs_ref.shape)
    own_copy = pltpu.make_async_copy(grad_ref, own_grads, load.at[6])
    own_copy.start()
    loads = []
    for number, (source, target) in enumerate([(tokens_ref, tokens), (wv_ref, wv), (wk_ref, wk), (wq_ref, wq), (wo_ref, wo)]):
        loads.append(pltpu.make_async_copy(source, target, load.at[number]))
        loads[-1].start()
    mates = mates_of()
    z1, x1 = swapped(z, 1), 1 - x
    greet(
        [device(swapped(z, step), x, y, core) for step in range(1, depth)]
        + [device(z, x1, y, core), device(z1, x1, y, core)]
        + [device(*mate) for mate in mates]
    )
    copies = Copies()
    for distance in (1, 2):

        @pl.when(spot < chain - distance)
        def _():
            remote(
                docs_ref, docs_in.at[2 - distance], d_send.at[distance], d_recv.at[distance], (group + distance, part)
            ).start()

    gather = Gather(copies, grad_ref, all_grad, rows, z_send, z_recv, p_send, p_recv, c_send, c_recv)
    gather.spread(0)
    gather.lift(1)
    own = pltpu.make_async_copy(grad_ref, gather.at(0, gather.here, (0, rows)), load.at[5])
    own.start()
    key_part, value_part = pl.ds(0, wide), pl.ds(wide, wide)

    high = lax.rem(z, 2)
    over_x, over_z = device(z, x1, y, core), device(z1, x, y, core)

    def docs_copy(distance, to):
        return remote(docs_ref, docs_in.at[2 - distance], d_send.at[distance], d_recv.at[distance], (to, part))

    def halo_copy(kind, source, slot, number, to):
        columns = (key_part, value_part)[kind]
        return remote(
            kv_all.at[source, :, columns], kv_all.at[slot, :, columns], h_send.at[kind, number], h_recv.at[kind, number], to
        )

    def x_copy(kind):
        return halo_copy(kind, 2, 1, 0, over_x)

    def z_copy(kind):
        return halo_copy(kind, 2, 0, 1, over_z)

    def relay_copy(kind):
        return halo_copy(kind, 0, 1, 2, over_x)

    def halo_start(kind):
        pl.when(x == 0)(lambda: x_copy(kind).start())
        pl.when(high == 0)(lambda: z_copy(kind).start())

    def halo_relay(kind):
        pl.when(high == 1)(lambda: z_copy(kind).wait_recv())
        pl.when(spot == 3)(lambda: relay_copy(kind).start())

    def halo_arrive(kind):
        columns = (key_part, value_part)[kind]
        pl.when(x == 1)(lambda: x_copy(kind).wait_recv())
        pl.when(spot == 2)(lambda: relay_copy(kind).wait_recv())

        def clear(slot):
            kv_all[slot, :, columns] = jnp.zeros((length, wide), LOW)

        pl.when(spot == 0)(lambda: clear(1))
        pl.when(high == 0)(lambda: clear(0))

    def halo_sent(kind):
        pl.when(x == 0)(lambda: x_copy(kind).wait_send())
        pl.when(high == 0)(lambda: z_copy(kind).wait_send())
        pl.when(spot == 3)(lambda: relay_copy(kind).wait_send())

    loads[0].wait()

    @pl.loop(0, length // 128)
    def _(index):
        part_rows = pl.ds(pl.multiple_of(index * 128, 128), 128)
        values = tokens[part_rows, :].astype(FULL)
        factor = lax.rsqrt(jnp.mean(values * values, axis=-1, keepdims=True) + NORM_EPSILON)
        normed_ref[part_rows, :] = (values * factor * gain1_ref[0:1, :]).astype(LOW)

    def project(weights, store):
        @pl.loop(0, wide // 256)
        def _(index):
            columns = pl.ds(pl.multiple_of(index * 256, 256), 256)
            store(index, columns, dot(normed_ref[...], weights[:, columns]))

    def keep_value(index, columns, result):
        kv_all[2, :, pl.ds(pl.multiple_of(wide + index * 256, 256), 256)] = result.astype(LOW)

    def keep_key(index, columns, result):
        k_raw[:, columns] = result

    def keep_query(index, columns, result):
        q_raw[:, columns] = result

    loads[2].wait()
    project(wk, keep_key)
    loads[3].wait()
    project(wq, keep_query)
    squares[...] = as_rows(
        [jnp.sum(q_raw[...] * q_raw[...], axis=-1, keepdims=True), jnp.sum(k_raw[...] * k_raw[...], axis=-1, keepdims=True)]
    )
    sent = exchange(copies, squares, squares_in, q_send, q_recv, mates)
    loads[1].wait()
    project(wv, keep_value)
    halo_start(1)
    gather.turn(0)

    @pl.loop(0, width // 256)
    def _(index):
        columns = pl.ds(pl.multiple_of(index * 256, 256), 256)
        normed_turned[columns, :] = normed_ref[:, columns].T

    for copy in sent:
        copies.arrived(copy)
    total = squares[...]
    for number in range(3):
        total = total + squares_in[number]
    scales[...] = lax.rsqrt(total * (1.0 / width) + NORM_EPSILON)
    factors = as_columns(scales[...])

    def turn_heads(raw, gain_ref, factor, store):
        for head in range(heads):
            columns = pl.ds(head * HD, HD)
            normed = raw[:, columns] * factor * gain_ref[0:1, columns]
            store(head, (normed * cosine_ref[...] + pltpu.roll(normed, HD // 2, 1) * sine_ref[...]).astype(LOW))

    def store_key(head, turned):
        kv_all[2, :, pl.ds(head * HD, HD)] = turned

    def store_query(head, turned):
        queries[:, pl.ds(head * HD, HD)] = turned

    turn_heads(k_raw, k_gain_ref, factors[:, 1:2], store_key)
    halo_start(0)
    gather.spread(1)
    gather.lift(2)
    turn_heads(q_raw, q_gain_ref, factors[:, 0:1], store_query)
    for distance in (1, 2):

        @pl.when(spot >= distance)
        def _():
            docs_copy(distance, group - distance).wait_recv()

        @pl.when(spot < distance)
        def _():
            docs_in[2 - distance] = jnp.full_like(docs_ref, -1)

    for block in range(3):
        rows_of = docs_in[block] if block < 2 else docs_ref[...]
        key_docs[pl.ds(block * length, length), :] = rows_of.astype(FULL).T[:, 0:1].astype(jnp.int32)
    mask_bias(bias, key_docs, docs_ref, length)

    def score(block):
        @pl.loop(0, heads)
        def _(head):
            columns = pl.ds(pl.multiple_of(head * HD, HD), HD)
            keys = pl.ds(block * length, length)
            scores[head, keys, :] = dot_t(kv_all[block, :, columns], queries[:, columns]) * scale + bias[keys, :]
    score(2)
    halo_relay(1)
    halo_relay(0)
    gather.share(0)
    gather.spread(2)
    halo_arrive(0)
    gather.turn(1)
    score(1)
    score(0)

    @pl.loop(0, heads)
    def _(head):
        mine = scores.at[head]
        highest = jnp.max(mine[...], axis=0, keepdims=True)
        total = jnp.zeros_like(highest)
        for block in range(3):
            weights = jnp.exp(mine[pl.ds(block * length, length), :] - highest)
            total = total + jnp.sum(weights, axis=0, keepdims=True)
            mine[pl.ds(block * length, length), :] = weights
        logs[head] = jnp.broadcast_to(highest + jnp.log(total), (8, length))
        totals[head] = jnp.broadcast_to(1.0 / total, (8, length))

    halo_arrive(1)

    @pl.loop(0, heads)
    def _(head):
        columns = pl.ds(pl.multiple_of(head * HD, HD), HD)
        values = pl.ds(pl.multiple_of((heads + head) * HD, HD), HD)
        mixed = jnp.zeros((HD, length), FULL)
        for block in range(3):
            probs = (scores[head, pl.ds(block * length, length), :] * totals[head, 0:1, :]).astype(LOW)
            mixed = mixed + t_dot(kv_all[block, :, values], probs)
        attended[:, columns] = mixed.T.astype(LOW)

    gather.turn(2)
    gather.spread(3)
    loads[4].wait()
    for index in range(4):
        partial[index // 2, index % 2] = dot(attended[pl.ds(index * rows, rows), :], wo[...]).astype(LOW)
    scatter = TensorScatter(copies, partial, from_pair, from_y, t_send, t_recv)
    scatter.begin()
    scatter.cross()
    gather.share(2)
    gather.turn(3)
    scatter.result(sum_ref)
    own_tokens[...] = tokens[own_rows, :]
    state = own_tokens[...].astype(FULL) + sum_ref[...]
    state_ref[...] = state
    factor = lax.rsqrt(jnp.mean(state * state, axis=-1, keepdims=True) + NORM_EPSILON)
    normed2_ref[...] = (state * factor * gain2_ref[0:1, :]).astype(LOW)
    experts = gates_ref.shape[0] * local
    logits_ref[...] = jnp.full_like(logits_ref, -1e30)
    logits_ref[:, :experts] = dot_t(normed2_ref[...], router_ref[...])
    logits = logits_ref[...]
    weights = jnp.exp(logits - jnp.max(logits, axis=-1, keepdims=True))
    probs = weights / jnp.sum(weights, axis=-1, keepdims=True)
    probs_ref[...] = probs
    gates = (probs * picked_ref[...]).T
    gates_ref[...] = jnp.zeros_like(gates_ref)
    for index in range(gates_ref.shape[0]):
        gates_ref[index, 0:local, :] = gates[index * local : (index + 1) * local]
    own.wait()
    own_copy.wait()
    for kind in range(2):
        halo_sent(kind)
    for distance in (1, 2):

        @pl.when(spot < chain - distance)
        def _():
            docs_copy(distance, group + distance).wait_send()

    copies.finish()


def run_attention(tokens, weights, grads, gains, tables, docs, gain2, router, picked, depth, chain, local, number):
    length, width = tokens.shape
    rows = length // 4
    wide = weights[0].shape[1]
    heads = wide // HD
    return pl.pallas_call(
        functools.partial(attention_kernel, depth, rows, heads, chain, local),
        out_shape=(
            jax.ShapeDtypeStruct((width, length), LOW),
            jax.ShapeDtypeStruct((length, wide), FULL),
            jax.ShapeDtypeStruct((length, wide), FULL),
            jax.ShapeDtypeStruct((length, wide), LOW),
            jax.ShapeDtypeStruct((3, length, 2 * wide), LOW),
            jax.ShapeDtypeStruct((3 * length, 1), jnp.int32),
            jax.ShapeDtypeStruct((8, length), FULL),
            jax.ShapeDtypeStruct((length, wide), LOW),
            jax.ShapeDtypeStruct((heads, 8, length), FULL),
            jax.ShapeDtypeStruct((rows, width), FULL),
            jax.ShapeDtypeStruct((rows, width), LOW),
            jax.ShapeDtypeStruct((rows, 128), FULL),
            jax.ShapeDtypeStruct((2 * depth, 8, rows), FULL),
            jax.ShapeDtypeStruct((rows, width), LOW),
            jax.ShapeDtypeStruct((rows, width), LOW),
            jax.ShapeDtypeStruct((depth, 4 * rows, width), LOW),
        ),
        in_specs=[ANY] * 6 + [VMEM] * 9,
        out_specs=(VMEM,) * 15 + (ANY,),
        scratch_shapes=[
            pltpu.VMEM(tokens.shape, LOW), pltpu.VMEM(tokens.shape, LOW), pltpu.VMEM((width, wide), LOW), pltpu.VMEM((width, wide), LOW),
            pltpu.VMEM((width, wide), LOW), pltpu.VMEM((wide, width), LOW), pltpu.VMEM((8, length), jnp.int32),
            pltpu.VMEM((rows, 128), FULL), pltpu.VMEM((2, 8, length), jnp.int32),
            pltpu.VMEM((8, length), FULL), pltpu.VMEM((3, 8, length), FULL),
            pltpu.VMEM((heads, 3 * length, length), FULL), pltpu.VMEM((heads, 8, length), FULL),
            pltpu.VMEM((3 * length, length), FULL),
        ]
        + TensorScatter.scratch(rows, width)[:3]
        + [
            pltpu.VMEM((rows, width), FULL), dma(3), dma(3),
            *Gather.scratch(depth), dma(2, 3), dma(2, 3), dma(3), dma(3), dma(3), dma(3), dma(7),
        ],
        compiler_params=comm_params(number),
    )(tokens, *weights, grads, *gains, *tables, docs, gain2, router, picked)


def attention_back_kernel(
    depth, rows, heads, chain, local,
    sum_ref, gate_cots, probs_ref, picked_ref, state_ref, gain2_ref, router_ref, normed2_ref, grad_ref,
    query_ref, kv_all, attended, logs, key_docs, query_docs, q_raw, k_raw, q_gain_ref, k_gain_ref, cosine_ref, sine_ref, scales,
    w_out, produced_ref, normed_ref, wq_ref, wk_ref, wv_ref,
    state_cot_ref, vectors, out_ref, normed_part, piece0, piece1, piece2, piece3,
    low, lows, by_expert, bias, cots, deltas, turned, query_cot, kv_cot, sending, landed, work, raw_cots, flipped, wq, wk, wv,
    inners, inners_in, staging,
    diagonal, from_x, from_y, from_z, r_send, r_recv, middle, m_send, m_recv,
    t_send, t_recv, h_send, h_recv, i_send, i_recv, load, saves,
):
    z, x, y, core = place()
    group, part = lax.axis_index("expert"), lax.axis_index("tensor")
    spot = group % chain
    length, width = query_ref.shape[0], w_out.shape[1]
    wide = heads * HD
    scale = HD ** (-0.5)
    order = [step for step in range(depth - 1, 0, -2)] + [step for step in range(depth - 2, -1, -2)]
    loads = {}
    for step in order:
        loads[step] = pltpu.make_async_copy(produced_ref.at[step], work.at[step], load.at[step])
        loads[step].start()
    others = []
    for number, (source, target) in enumerate([(wq_ref, wq), (wk_ref, wk), (wv_ref, wv)]):
        others.append(pltpu.make_async_copy(source, target, load.at[depth + number]))
        others[-1].start()
    mates = mates_of()
    greet(
        [device(swapped(z, step), x, y, core) for step in range(1, depth)]
        + [device(z, 1 - x, y, core)]
        + [device(*mate) for mate in mates]
    )
    copies = Copies()
    scatter = Scatter(
        copies, work, diagonal, from_x, from_y, from_z, rows, r_send, r_recv, (middle, m_send, m_recv)
    )

    def corner(step):
        if step % 2 == 0:
            loads[step].wait()
        scatter.corner(step)


    loads[3].wait()
    scatter.share(3)
    loads[1].wait()
    scatter.share(1)
    by_expert[...] = jnp.zeros_like(by_expert)
    for plane in range(depth):
        step = swapped(z, plane)
        for column in range(2):
            first = (2 * plane + column) * local
            by_expert[first : first + local, :] = (gate_cots[step, 2 * column] + gate_cots[step, 2 * column + 1])[:local]
    probs = probs_ref[...]
    prob_cot = by_expert[...].T * picked_ref[...]
    logit_cot = probs * (prob_cot - jnp.sum(probs * prob_cot, axis=-1, keepdims=True))
    normed2_cot = sum_ref[...] + lax.dot_general(
        logit_cot[:, : router_ref.shape[0]], router_ref[...].astype(FULL), (((1,), (0,)), ((), ())),
        precision=HIGHEST_PRECISION, preferred_element_type=FULL,
    )
    state = state_ref[...]
    factor = lax.rsqrt(jnp.mean(state * state, axis=-1, keepdims=True) + NORM_EPSILON)
    groups, _, slice_width = vectors.shape
    vectors[...] = jnp.zeros_like(vectors)
    gain_grad = jnp.sum(normed2_cot * state * factor, axis=0, keepdims=True)
    for index in range(groups):
        vectors[index, 17:18, :] = gain_grad[:, index * slice_width : (index + 1) * slice_width]
    inner = jnp.sum(normed2_cot * gain2_ref[0:1, :] * state, axis=-1, keepdims=True)
    state_cot = (
        grad_ref[...].astype(FULL)
        + factor * gain2_ref[0:1, :] * normed2_cot
        - state * (factor * factor * factor) * inner * (1.0 / width)
    )
    state_cot_ref[...] = state_cot
    low[...] = state_cot.astype(LOW)
    gather = TensorGather(copies, low, lows, t_send, t_recv)
    corner(3)
    corner(1)
    router_grad = jnp.dot(
        logit_cot.T, normed2_ref[...].astype(FULL), precision=HIGHEST_PRECISION, preferred_element_type=FULL
    )[:16]
    for index in range(groups):
        vectors[index, 0:16, :] = router_grad[:, index * slice_width : (index + 1) * slice_width]
    scatter.side(3)
    mask_bias(bias, key_docs, query_docs, length)
    gather.cross()
    gather.finish()
    for index in range(4):
        cots[pl.ds(index * rows, rows), :] = dot_t(lows[index // 2, index % 2], w_out[...]).astype(LOW)
    for head in range(heads):
        columns = pl.ds(head * HD, HD)
        product = cots[:, columns].astype(FULL) * attended[:, columns].astype(FULL)
        deltas[head] = jnp.broadcast_to(jnp.sum(product.T, axis=0, keepdims=True), (8, length))
    scatter.side(1)
    turned[...] = jnp.zeros_like(turned)

    def back(block, store, after):
        @pl.loop(0, heads)
        def _(head):
            columns = pl.ds(pl.multiple_of(head * HD, HD), HD)
            values = pl.ds(pl.multiple_of((heads + head) * HD, HD), HD)
            tile = length // 2

            for index, seen in ((0, pl.ds(0, tile if block == 0 else length)), (1, pl.ds(tile, tile) if block == 2 else pl.ds(0, length))):
                keys = pl.ds(index * tile, tile)
                key, value = kv_all[block, keys, columns], kv_all[block, keys, values]
                query, cot = query_ref[seen, columns], cots[seen, columns]
                log, delta = logs[head, 0:1, seen], deltas[head, 0:1, seen]
                hidden = bias[pl.ds(block * length + index * tile, tile), seen].astype(FULL)
                probs = jnp.exp(dot_t(key, query) * scale + hidden - log)
                score_cot = (probs * (dot_t(value, cot) - delta)).astype(LOW)
                turned[head, :, seen] += t_dot(key, score_cot)
                store(head, keys, dot(score_cot, query) * scale, dot(probs.astype(LOW), cot))

            after(head)

    def store_in(slot):
        def store(head, keys, key_part, value_part):
            sending[slot, head, keys, 0:HD] = key_part.astype(LOW)
            sending[slot, head, keys, HD : 2 * HD] = value_part.astype(LOW)

        return store

    def store_own(head, keys, key_part, value_part):
        kv_cot[keys, pl.ds(pl.multiple_of(head * HD, HD), HD)] = key_part
        kv_cot[keys, pl.ds(pl.multiple_of((heads + head) * HD, HD), HD)] = value_part

    high = lax.rem(z, 2)
    over_x, over_z = device(z, 1 - x, y, core), device(swapped(z, 1), x, y, core)

    def x_copy(head):
        return remote(sending.at[1, head], landed.at[1, head], h_send.at[0, head], h_recv.at[0, head], over_x)

    def z_copy(head):
        return remote(sending.at[0, head], landed.at[0, head], h_send.at[1, head], h_recv.at[1, head], over_z)

    def relay(head):
        @pl.when(spot == 3)
        def _():
            x_copy(head).wait_recv()
            add_rows(sending.at[0, head], [sending.at[0, head], landed.at[1, head]], length, 64)
            z_copy(head).start()

    back(1, store_in(1), lambda head: pl.when(spot >= 1)(lambda: x_copy(head).start()))
    scatter.climb(3)
    back(0, store_in(0), lambda head: pl.when(spot == 2)(lambda: z_copy(head).start()))
    scatter.climb(1)
    corner(2)
    back(2, store_own, relay)
    corner(0)
    scatter.side(2)
    for head in range(heads):
        query_cot[:, pl.ds(head * HD, HD)] = turned[head].T * scale

    scatter.side(0)
    saving = {}

    def weight_piece(number, right, target):
        piece = target.shape[2]
        for index in range(2 * depth):
            slot = index % 2
            if slot in saving:
                saving.pop(slot).wait()
            staging[slot] = dot(flipped[pl.ds(index * piece, piece), :], right).astype(LOW)
            saving[slot] = pltpu.make_async_copy(staging.at[slot], target.at[index // 2, index % 2], saves.at[slot])
            saving[slot].start()

    @pl.loop(0, width // 256)
    def _(index):
        columns = pl.ds(pl.multiple_of(index * 256, 256), 256)
        flipped[columns, :] = jnp.concatenate([lows[block // 2, block % 2, :, columns] for block in range(4)], axis=0).T

    weight_piece(0, attended[...], piece0)
    normed_copy = pltpu.make_async_copy(normed_ref, flipped, load.at[depth + 3])
    normed_copy.start()
    scatter.climb(2)
    factors = as_columns(scales[...])

    def turn_back(cot, raw, gain_ref, factor, first):
        total = jnp.zeros((length, 1), FULL)
        for head in range(heads):
            columns = pl.ds(head * HD, HD)
            mine = cot[:, columns]
            mine = mine * cosine_ref[...] - pltpu.roll(mine, HD // 2, 1) * sine_ref[...]
            cot[:, columns] = mine
            mine = mine * raw[:, columns]
            grad = jnp.sum(mine * factor, axis=0, keepdims=True)
            for index in range(groups):
                vectors[index, first + head : first + head + 1, 0:HD] = grad
            total = total + jnp.sum(mine * gain_ref[0:1, columns], axis=-1, keepdims=True)
        return total

    query_inner = turn_back(query_cot, q_raw, q_gain_ref, factors[:, 0:1], 18)

    def take(slot, head):
        (z_copy, x_copy)[slot](head).wait_recv()
        for part in range(2):
            mine = kv_cot.at[:, pl.ds((part * heads + head) * HD, HD)]
            add_rows(mine, [mine, landed.at[slot, head, :, pl.ds(part * HD, HD)]], length, 64)

    for head in range(heads):
        pl.when(x == 0)(functools.partial(take, 1, head))
    for head in range(heads):
        pl.when(high == 0)(functools.partial(take, 0, head))

    key_inner = turn_back(kv_cot, k_raw, k_gain_ref, factors[:, 1:2], 18 + heads)
    inners[...] = as_rows([query_inner, key_inner])
    sent = exchange(copies, inners, inners_in, i_send, i_recv, mates)
    raw_cots[2] = kv_cot[:, pl.ds(wide, wide)].astype(LOW)
    normed_copy.wait()
    weight_piece(1, raw_cots[2], piece1)
    for copy in sent:
        copies.arrived(copy)
    total = inners[...]
    for number in range(3):
        total = total + inners_in[number]
    totals = as_columns(total * (1.0 / width))

    def raw_cot(number, cot, raw, gain_ref):
        factor = factors[:, number : number + 1]
        shrink = (factor * factor * factor) * totals[:, number : number + 1]
        for head in range(heads):
            columns = pl.ds(head * HD, HD)
            raw_cots[number, :, columns] = (
                factor * gain_ref[0:1, columns] * cot[:, columns] - raw[:, columns] * shrink
            ).astype(LOW)

    raw_cot(0, query_cot, q_raw, q_gain_ref)
    raw_cot(1, kv_cot, k_raw, k_gain_ref)
    for copy in others:
        copy.wait()

    @pl.loop(0, width // 256)
    def _(index):
        columns = pl.ds(pl.multiple_of(index * 256, 256), 256)
        result = (
            dot_t(raw_cots[0], wq[columns, :]) + dot_t(raw_cots[1], wk[columns, :]) + dot_t(raw_cots[2], wv[columns, :])
        ).astype(LOW)
        for block in range(4):
            normed_part[block // 2, block % 2, :, columns] = result[block * rows : (block + 1) * rows]

    weight_piece(2, raw_cots[0], piece2)
    weight_piece(3, raw_cots[1], piece3)
    scatter.climb(0)
    scatter.result(out_ref, [state_ref])
    for head in range(heads):
        pl.when(spot >= 1)(lambda: x_copy(head).wait_send())
        pl.when(spot >= 2)(lambda: z_copy(head).wait_send())

    for copy in saving.values():
        copy.wait()
    copies.finish()


def run_attention_back(rows_of, attention, sources, produced, normed, weights, chain, local, number):
    depth = produced.shape[0]
    rows, width = rows_of[0].shape
    queries, kv_all = attention[0], attention[1]
    length, wide2 = kv_all.shape[1:]
    wide = wide2 // 2
    heads = wide // HD
    piece = jax.ShapeDtypeStruct((depth, 2, width // (2 * depth), wide), LOW)
    return pl.pallas_call(
        functools.partial(attention_back_kernel, depth, rows, heads, chain, local),
        out_shape=(
            jax.ShapeDtypeStruct((rows, width), FULL),
            jax.ShapeDtypeStruct((2 * depth, 32, width // (2 * depth)), FULL),
            jax.ShapeDtypeStruct((rows, width), LOW),
            jax.ShapeDtypeStruct((2, 2, rows, width), LOW),
            piece, piece, piece, piece,
        ),
        in_specs=[VMEM] * 23 + [ANY] * 5,
        out_specs=(VMEM,) * 4 + (ANY,) * 4,
        scratch_shapes=[
            pltpu.VMEM((rows, width), LOW), pltpu.VMEM((2, 2, rows, width), LOW), pltpu.VMEM((128, rows), FULL),
            pltpu.VMEM((3 * length, length), LOW), pltpu.VMEM((length, wide), LOW),
            pltpu.VMEM((heads, 8, length), FULL), pltpu.VMEM((heads, HD, length), FULL),
            pltpu.VMEM((length, wide), FULL), pltpu.VMEM((length, wide2), FULL),
            pltpu.VMEM((2, heads, length, 2 * HD), LOW), pltpu.VMEM((2, heads, length, 2 * HD), LOW),
            pltpu.VMEM(produced.shape, LOW), pltpu.VMEM((3, length, wide), LOW), pltpu.VMEM((width, length), LOW),
            pltpu.VMEM((width, wide), LOW), pltpu.VMEM((width, wide), LOW), pltpu.VMEM((width, wide), LOW),
            pltpu.VMEM((8, length), FULL), pltpu.VMEM((3, 8, length), FULL), pltpu.VMEM((2,) + piece.shape[2:], LOW),
        ]
        + Scatter.scratch(depth, rows, width)
        + [pltpu.VMEM((depth // 2, 4, rows // 4, width), LOW), dma(depth // 2, 4), dma(depth // 2, 4)]
        + [dma(4), dma(3), dma(2, heads), dma(2, heads), dma(3), dma(3), dma(depth + 4), dma(2)],
        compiler_params=comm_params(number),
    )(*rows_of, *attention, *sources, produced, normed, *weights)


def dot(left, right):
    return jnp.dot(left, right, preferred_element_type=FULL)


def dot_t(left, right):
    return lax.dot_general(left, right, (((1,), (1,)), ((), ())), preferred_element_type=FULL)


def t_dot(left, right):
    return lax.dot_general(left, right, (((0,), (0,)), ((), ())), preferred_element_type=FULL)


class ExpertScatter:
    def __init__(self, copies, parts, widths, work, from_x, from_z, load, send, recv):
        self.widths = widths
        self.copies, self.parts, self.work, self.from_x, self.from_z = copies, parts, work, from_x, from_z
        self.load, self.send, self.recv = load, send, recv
        self.z, self.x, y, core = place()
        self.depth, self.rows = work.shape[1], work.shape[2]
        self.over_x = device(self.z, 1 - self.x, y, core)
        self.column = [device(swapped(self.z, step), self.x, y, core) for step in range(self.depth)]
        self.order = sorted(range(self.depth), key=lambda step: (step == 0, step & -step, -step))
        self.steps = self.order[:-1]
        self.loads, self.sides, self.along = {}, {}, {}

    def begin(self, index):
        for step in self.order:
            at = swapped(self.z, step)
            columns = pl.ds(0, self.widths[index])
            self.sides[index, step] = self.copies.start(
                remote(
                    self.parts[index].at[at, 1 - self.x, :, columns], self.from_x.at[index, step, :, columns],
                    self.send.at[0, index, step], self.recv.at[0, index, step], self.over_x,
                )
            )
            load = pltpu.make_async_copy(
                self.parts[index].at[at, self.x, :, columns], self.work.at[index, step, :, columns], self.load.at[index, step]
            )
            load.start()
            self.loads[index, step] = load

    def climb(self, index, step):
        self.loads[index, step].wait()
        self.copies.arrived(self.sides[index, step])
        columns = pl.ds(0, self.widths[index])
        mine = self.work.at[index, step, :, columns]
        low = step & -step
        terms = [mine, self.from_x.at[index, step, :, columns]] + self.below(index, step)
        add_rows(mine, terms, self.rows)
        self.along[index, step] = self.copies.start(
            remote(
                mine, self.from_z.at[index, step, :, columns],
                self.send.at[1, index, step], self.recv.at[1, index, step], self.column[low],
            )
        )

    def below(self, index, step):
        terms, bit = [], 1
        while bit < (step & -step if step else self.depth):
            self.copies.arrived(self.along[index, step | bit])
            terms.append(self.from_z.at[index, step | bit, :, pl.ds(0, self.widths[index])])
            bit *= 2
        return terms

    def result(self, index, target):
        self.loads[index, 0].wait()
        self.copies.arrived(self.sides[index, 0])
        columns = pl.ds(0, self.widths[index])
        terms = [self.work.at[index, 0, :, columns], self.from_x.at[index, 0, :, columns]] + self.below(index, 0)
        add_rows(target.at[:, columns], terms, self.rows)


class ZScatter:
    def __init__(self, copies, part, columns, work, from_z, from_x, load, send, recv):
        self.copies, self.part, self.columns = copies, part, columns
        self.work, self.from_z, self.from_x, self.load, self.send, self.recv = work, from_z, from_x, load, send, recv
        self.z, self.x, y, core = place()
        self.depth, self.rows = work.shape[0], work.shape[2]
        self.over_x = device(self.z, 1 - self.x, y, core)
        self.column = [device(swapped(self.z, step), self.x, y, core) for step in range(self.depth)]
        self.loads, self.along = {}, {}

    def begin(self):
        for step in range(self.depth):
            source = self.part.at[swapped(self.z, step), :, :, self.columns]
            self.loads[step] = pltpu.make_async_copy(source, self.work.at[step], self.load.at[step])
            self.loads[step].start()

    def climb(self, step):
        self.loads[step].wait()
        low = step & -step if step else self.depth
        bit = 1
        while bit < low:
            self.copies.arrived(self.along[step | bit])
            for column in range(2):
                mine = self.work.at[step, column]
                add_rows(mine, [mine, self.from_z.at[step | bit, column]], self.rows, 32)
            bit *= 2
        if step:
            copy = remote(self.work.at[step], self.from_z.at[step], self.send.at[step], self.recv.at[step], self.column[low])
        else:
            copy = remote(self.work.at[0, 1 - self.x], self.from_x, self.send.at[0], self.recv.at[0], self.over_x)
        self.along[step] = self.copies.start(copy)

    def result(self, target):
        self.copies.arrived(self.along[0])
        add_rows(target, [self.work.at[0, self.x], self.from_x], self.rows)


def gradients_kernel(
    depth, rows, local, hidden, matrices, *refs,
):
    parts, refs = refs[:matrices], refs[matrices:]
    (
        normed_part, tokens_ref, state_cot, gain_ref, out_ref, vector_ref,
        normed_ref, grad_ref, gated_ref, gate_grad_ref, up_grad_ref,
    ) = refs[:11]
    sums, refs = refs[11 : 11 + matrices], refs[11 + matrices :]
    (
        input_grads, outputs, vector_sum,
        gate_own, up_own, down_own,
        work, from_x, from_z, partial, from_pair, from_y, normed_grad, low, vectors, vector_in, vector_mid, vector_turn,
        tiles, turned, acts, gated_turned, near, far, near_down, far_down, other, other_down,
        f_work, f_from_z, f_from_x, f_load, f_send, f_recv,
        e_load, e_send, e_recv, t_send, t_recv, g_send, g_recv, o_send, o_recv, v_send, v_recv, u_send, u_recv,
        tile_load, act_load, save, pair_send, pair_recv, local_sem,
    ) = refs
    z, x, y, core = place()
    group = 2 * z + x
    sibling = device(z, x, y, 1 - core)
    groups = [(step, turn) for step in range(depth) for turn in range(2) if step or turn]
    peers = [device(swapped(z, step), swapped(x, turn), y, core) for step, turn in groups]
    mates = [(z, x, swapped(y, turn // 2), swapped(core, turn % 2)) for turn in range(1, 4)]
    greet(peers + [device(*mate) for mate in mates])
    copies = Copies()
    width = normed_ref.shape[1]
    tile = local * hidden
    count = width // tile

    def fetch(source, target, sem):
        copy = pltpu.make_async_copy(source, target, sem)
        copy.start()
        return copy

    wide = work.shape[3]
    widths = [wide] * (matrices - 1) + [wide // 2]
    experts = ExpertScatter(copies, parts, widths, work, from_x, from_z, e_load, e_send, e_recv)
    eighth = pl.ds(wide // 2, wide // 2)
    z_first = ZScatter(copies, parts[-1], eighth, f_work, f_from_z, f_from_x, f_load, f_send, f_recv)
    loaded = fetch(normed_part, partial, local_sem.at[0])
    experts.begin(0)
    z_first.begin()
    loaded.wait()
    scatter = TensorScatter(copies, partial, from_pair, from_y, t_send, t_recv)
    scatter.begin()
    out_gather = TensorGather(copies, out_ref, outputs, o_send, o_recv)
    for index in range(1, matrices):
        experts.begin(index)
    act_copies = [fetch(gate_grad_ref, acts.at[0], act_load.at[0]), fetch(up_grad_ref, acts.at[1], act_load.at[1])]

    def fetch_tile(number):
        source = normed_ref if number < count else grad_ref
        columns = pl.ds((number % count) * tile, tile)
        return fetch(source.at[:, columns], tiles.at[number % 2], tile_load.at[number % 2])

    tile_copies = [fetch_tile(0)]
    saving = {}

    def first_unit(owner):
        return owner * local * hidden

    def gate_and_up(number):
        slot = number % 2
        tile_copies[number].wait()
        tile_copies.append(fetch_tile(number + 1))
        turned[...] = tiles[slot].T
        for copy, remote_one in saving.pop(slot, []):
            copies.sent(copy) if remote_one else copy.wait()
        for which in range(2):
            for owner, target in ((1 - core, far), (core, near)):

                @pl.loop(0, local)
                def _(expert):
                    columns = pl.ds(pl.multiple_of(first_unit(owner) + expert * hidden, hidden), hidden)
                    target[which, slot, expert] = dot(turned[...], acts[which, :, columns]).astype(target.dtype)

        saves = []
        for which in range(2):
            away = remote(
                far.at[which, slot], other.at[which, :, pl.ds(number * tile, tile)],
                pair_send.at[which, number], pair_recv.at[which, number], sibling,
            )
            copies.start(away)
            saves.append((away, True))
        saving[slot] = saves
        if number:
            settle(number - 1)

    def settle(number):
        slot, place_of = number % 2, pl.ds(number * tile, tile)
        for which, own in enumerate((gate_own, up_own)):
            copies.arrived(saving[slot][which][0])
            for expert in range(local):
                mine = near.at[which, slot, expert]
                add_rows(mine, [mine, other.at[which, expert, place_of]], tile, 64)
        for which, own in enumerate((gate_own, up_own)):
            saving[slot].append((fetch(near.at[which, slot], own.at[:, place_of], save.at[which, slot]), False))

    def down(number):
        slot = number % 2
        tile_copies[count + number].wait()
        if number + 1 < count:
            tile_copies.append(fetch_tile(count + number + 1))
        for copy, remote_one in saving.pop(("down", slot), []):
            copies.sent(copy) if remote_one else copy.wait()
        for source, target in ((turned, far_down), (gated_turned, near_down)):

            @pl.loop(0, local)
            def _(expert):
                units = pl.ds(pl.multiple_of(expert * hidden, hidden), hidden)
                target[slot, expert] = dot(source[units, :], tiles[slot]).astype(target.dtype)

        away = remote(
            far_down.at[slot], other_down.at[number], pair_send.at[2, number], pair_recv.at[2, number], sibling
        )
        copies.start(away)
        saving["down", slot] = [(away, True)]
        settle(count - 1) if number == 0 else settle_down(number - 1)

    def settle_down(number):
        slot = number % 2
        copies.arrived(saving["down", slot][0][0])
        for expert in range(local):
            mine = near_down.at[slot, expert]
            add_rows(mine, [mine, other_down.at[number, expert]], hidden, 64)
        target = down_own.at[:, :, pl.ds(number * tile, tile)]
        saving["down", slot].append((fetch(near_down.at[slot], target, save.at[2, slot]), False))

    for copy in act_copies:
        copy.wait()
    z_first.climb(3)
    z_first.climb(1)
    gate_and_up(0)
    scatter.cross()
    experts.climb(0, experts.steps[0])
    gate_and_up(1)
    out_gather.cross()
    experts.climb(0, experts.steps[1])
    z_first.climb(2)
    scatter.result(normed_grad)

    inputs = tokens_ref[...].astype(FULL)
    factor = lax.rsqrt(jnp.mean(inputs * inputs, axis=-1, keepdims=True) + NORM_EPSILON)
    gain = gain_ref[0:1, :]
    normed = normed_grad[...]
    inner = jnp.sum(normed * gain * inputs, axis=-1, keepdims=True)
    low[...] = (
        state_cot[...] + factor * gain * normed - inputs * (factor * factor * factor) * inner * (1.0 / width)
    ).astype(LOW)
    gain_grad = jnp.sum(normed * inputs * factor, axis=0, keepdims=True)
    grad_gather = TensorGather(copies, low, input_grads, g_send, g_recv)
    vectors[...] = vector_ref[...]
    slice_width = vectors.shape[2]
    for index in range(vectors.shape[0]):
        vectors[index, 16:17, :] = gain_grad[:, index * slice_width : (index + 1) * slice_width]
    vector_copies = []
    for number, ((step, turn), peer) in enumerate(zip(groups, peers)):
        to = 2 * swapped(z, step) + swapped(x, turn)
        vector_copies.append(
            copies.start(remote(vectors.at[to], vector_in.at[number], v_send.at[number], v_recv.at[number], peer))
        )

    for step in experts.steps[2:]:
        experts.climb(0, step)
    gate_and_up(2)
    for step in experts.steps[:2]:
        experts.climb(1, step)
    grad_gather.cross()
    z_first.climb(0)
    gate_and_up(3)
    for step in experts.steps[2:]:
        experts.climb(1, step)
    gated_copy = fetch(gated_ref, acts.at[0], act_load.at[0])
    gated_copy.wait()
    for owner, target in ((1 - core, turned), (core, gated_turned)):
        target[...] = acts[0, :, pl.ds(pl.multiple_of(first_unit(owner), hidden), local * hidden)].T
    experts.result(0, sums[0])
    down(0)
    experts.climb(2, experts.steps[0])
    down(1)
    for step in experts.steps[1:]:
        experts.climb(2, step)
    down(2)
    experts.result(1, sums[1])
    down(3)
    settle_down(3)
    for index in range(3, matrices):
        for step in experts.steps:
            experts.climb(index, step)
    for copy in vector_copies:
        copies.arrived(copy)
    total = vectors[group]
    for number in range(len(peers)):
        total = total + vector_in[number]
    vector_mid[...] = total
    turn_copies = [
        copies.start(remote(vector_mid, vector_turn.at[number], u_send.at[number], u_recv.at[number], device(*mate)))
        for number, mate in enumerate(mates)
    ]
    for index in range(2, matrices):
        experts.result(index, sums[index])
    z_first.result(sums[-1].at[:, eighth])
    out_gather.finish()
    grad_gather.finish()
    for copy in turn_copies:
        copies.arrived(copy)
    total = vector_mid[...]
    for number in range(len(mates)):
        total = total + vector_turn[number]
    keep = lax.broadcasted_iota(jnp.int32, total.shape, 0) < 18
    vector_sum[...] = jnp.where(keep, total, vector_mid[...])
    for entries in saving.values():
        for copy, remote_one in entries:
            if not remote_one:
                copy.wait()
    copies.finish()


def run_gradients(parts, normed_part, tokens, state_cot, gain, out, vectors, normed, grads, gated, gate_grad, up_grad, local, number):
    matrices = len(parts)
    depth, _, piece, columns = parts[0].shape
    rows, width = state_cot.shape
    seen, units = gated.shape
    hidden = units // (2 * local)
    tile = units // 2
    sum_of = jax.ShapeDtypeStruct((piece, columns), FULL)
    spread = jax.ShapeDtypeStruct((2, 2, rows, width), LOW)
    wide, tall = (local, width, hidden), (local, hidden, width)
    results = pl.pallas_call(
        functools.partial(gradients_kernel, depth, rows, local, hidden, matrices),
        out_shape=(sum_of,) * matrices
        + (
            spread, spread, jax.ShapeDtypeStruct(vectors.shape[1:], FULL),
            jax.ShapeDtypeStruct(wide, FULL), jax.ShapeDtypeStruct(wide, FULL), jax.ShapeDtypeStruct(tall, FULL),
        ),
        in_specs=[ANY] * (matrices + 1) + [VMEM] * 5 + [ANY] * 5,
        out_specs=(VMEM,) * (matrices + 3) + (ANY,) * 3,
        scratch_shapes=[pltpu.VMEM((matrices, depth, piece, columns), LOW)] * 3
        + TensorScatter.scratch(rows, width)[:3]
        + [
            pltpu.VMEM((rows, width), FULL), pltpu.VMEM((rows, width), LOW),
            pltpu.VMEM(vectors.shape, FULL), pltpu.VMEM((2 * depth - 1,) + vectors.shape[1:], FULL),
            pltpu.VMEM(vectors.shape[1:], FULL), pltpu.VMEM((3,) + vectors.shape[1:], FULL),
            pltpu.VMEM((2, seen, tile), LOW), pltpu.VMEM((tile, seen), LOW),
            pltpu.VMEM((2, seen, units), LOW), pltpu.VMEM((units // 2, seen), LOW),
            pltpu.VMEM((2, 2, local, tile, hidden), FULL), pltpu.VMEM((2, 2, local, tile, hidden), LOW),
            pltpu.VMEM((2, local, hidden, tile), FULL), pltpu.VMEM((2, local, hidden, tile), LOW),
            pltpu.VMEM((2, local, width, hidden), LOW), pltpu.VMEM((width // tile, local, hidden, tile), LOW),
            pltpu.VMEM((depth, 2, piece, columns // 2), LOW), pltpu.VMEM((depth, 2, piece, columns // 2), LOW),
            pltpu.VMEM((piece, columns // 2), LOW), dma(depth), dma(depth), dma(depth),
            dma(matrices, depth), dma(2, matrices, depth), dma(2, matrices, depth),
            dma(3), dma(3), dma(4), dma(3), dma(4), dma(3),
            dma(2 * depth - 1), dma(2 * depth - 1), dma(3), dma(3),
            dma(2), dma(2), dma(3, 2), dma(3, width // tile), dma(3, width // tile), dma(1),
        ],
        compiler_params=comm_params(number),
    )(*parts, normed_part, tokens, state_cot, gain, out, vectors, normed, grads, gated, gate_grad, up_grad)
    return results[:matrices], results[matrices:]


def finish_kernel(
    experts, heads,
    in_grad, in_out, in_query, in_key, in_value, in_gate, in_up, in_down, in_w_out, vector_ref,
    input_grad, output, query, key, value, gate, up, down, w_out, norm1, norm2, router, q_gain, k_gain,
):
    input_grad[...] = in_grad[...].astype(FULL)
    for source, target in (
        (in_out, output), (in_query, query), (in_key, key), (in_value, value), (in_gate, gate), (in_up, up), (in_down, down),
    ):
        target[...] = source[...]

    @pl.when(pl.program_id(0) == 0)
    def _():
        w_out[...] = in_w_out[...].T
        vectors = vector_ref[...]
        norm1[...], norm2[...] = vectors[16:17], vectors[17:18]
        router[...] = vectors[:experts]
        gains = vectors[18 : 18 + 2 * heads, :HD]
        width = q_gain.shape[1]
        group = lax.axis_index("expert")
        total_q, total_k = jnp.zeros(q_gain.shape, FULL), jnp.zeros(k_gain.shape, FULL)
        for index in range(HD // width):
            mine = (group == index).astype(FULL)
            total_q = total_q + gains[:heads, index * width : (index + 1) * width] * mine
            total_k = total_k + gains[heads:, index * width : (index + 1) * width] * mine
        q_gain[...], k_gain[...] = total_q, total_k


def finish(arrays, w_out, vectors, experts, heads, groups):
    steps = 4
    shapes = [jax.ShapeDtypeStruct(a.shape, FULL if i == 0 else a.dtype) for i, a in enumerate(arrays)]
    blocks = [pl.BlockSpec((a.shape[0] // steps, a.shape[1]), lambda i: (i, 0)) for a in arrays]
    whole = pl.BlockSpec(memory_space=pltpu.VMEM)
    piece = vectors.shape[1]
    small = [
        jax.ShapeDtypeStruct(shape, FULL)
        for shape in (w_out.shape[::-1], (1, piece), (1, piece), (experts, piece), (heads, HD // groups), (heads, HD // groups))
    ]
    return pl.pallas_call(
        functools.partial(finish_kernel, experts, heads),
        grid=(steps,),
        out_shape=(*shapes, *small),
        in_specs=blocks + [whole, whole],
        out_specs=(*blocks, *[whole] * len(small)),
        compiler_params=pltpu.CompilerParams(vmem_limit_bytes=VMEM_BYTES),
    )(*arrays, w_out, vectors)


def body(
    groups, parts,
    tokens, documents, routes, norm1_gain, q_gain, k_gain, w_query, w_key, w_value, w_out, norm2_gain, router_w,
    w_gate, w_up, w_down, out_grad,
):
    row_count, width = tokens.shape
    local_experts, _, hidden = w_gate.shape
    experts = local_experts * groups
    chain = LENGTH // row_count
    if not (parts == 4 and groups % 2 == 0 and experts <= min(16, 2 * TOP) and 2 * w_query.shape[1] <= 14 * HD and chain == 4 and groups == 8 and 4 * row_count == LENGTH and WINDOW == 2 * row_count):
        return body_routed(
            tokens, documents, routes, norm1_gain, q_gain, k_gain, w_query, w_key, w_value, w_out, norm2_gain, router_w,
            w_gate, w_up, w_down, out_grad,
        )
    depth = groups // 2
    rows = row_count // parts
    seen = groups * row_count // 2
    heads = w_query.shape[1] // HD
    group, part = lax.axis_index("expert"), lax.axis_index("tensor")
    core = part % 2

    def quarter(array):
        return lax.dynamic_slice_in_dim(array, part * rows, rows, 0)

    def across(vector):
        return vector.reshape(1, -1)

    positions = group * row_count + jnp.arange(row_count, dtype=jnp.int32)
    cosine, sine = (table[:, 0, :] for table in rope_tables(positions % LENGTH))
    sine = jnp.concatenate([-sine[:, : HD // 2], sine[:, HD // 2 :]], axis=1)
    picked = jnp.any(quarter(routes)[:, :, None] == jnp.arange(128, dtype=jnp.int32)[None, None, :], axis=1).astype(FULL)
    query_gain, key_gain = across(q_gain), across(k_gain)
    (
        normed_one, query_raw, key_raw, queries, kv_all, key_docs, scales, attended, logs, state, normed_two, router_probs, gates,
        own_tokens, own_grads, all_grad,
    ) = run_attention(
        tokens, (w_query, w_key, w_value, w_out), out_grad, (across(norm1_gain), query_gain, key_gain), (cosine, sine), across(documents),
        across(norm2_gain), router_w.T, picked, depth, chain, local_experts, 3,
    )

    normed_two_grad, gate_cots, all_normed, gated, gate_pre_grad, up_pre_grad, produced = run_experts(
        normed_two, gates, all_grad, w_gate, w_up, w_down, 5
    )
    units = 2 * local_experts * hidden
    all_normed, all_grad = all_normed.reshape(seen, width), all_grad.reshape(seen, width)
    gated, gate_pre_grad, up_pre_grad = (a.reshape(seen, units) for a in (gated, gate_pre_grad, up_pre_grad))

    state_cot, vectors, output_rows, normed_part, *pieces = run_attention_back(
        (normed_two_grad, gate_cots, router_probs, picked, state, across(norm2_gain), router_w.T, normed_two, own_grads),
        (queries, kv_all, attended, logs, key_docs, across(documents), query_raw, key_raw, query_gain, key_gain, cosine, sine, scales),
        (w_out,), produced, normed_one, (w_query, w_key, w_value), chain, local_experts, 10,
    )
    sums, (input_grad, output, vector_sum, *expert_grads) = run_gradients(
        pieces, normed_part, own_tokens, state_cot, norm1_gain[None], output_rows, vectors, all_normed, all_grad, gated, gate_pre_grad, up_pre_grad,
        local_experts, 14,
    )
    (
        input_grad, output, w_query_grad, w_key_grad, w_value_grad, gate_grad, up_grad, down_grad, w_out_grad,
        norm1_grad, norm2_grad, router_grad, q_gain_grad, k_gain_grad,
    ) = finish(
        (
            input_grad.reshape(row_count, width), output.reshape(row_count, width), sums[2], sums[3], sums[1],
            *(a.reshape(-1, a.shape[2]) for a in expert_grads),
        ),
        sums[0], vector_sum, experts, heads, groups,
    )
    return (
        output, input_grad, norm1_grad.reshape(-1), q_gain_grad, k_gain_grad, w_query_grad, w_key_grad, w_value_grad, w_out_grad,
        norm2_grad.reshape(-1), router_grad.T, gate_grad.reshape(w_gate.shape), up_grad.reshape(w_up.shape),
        down_grad.reshape(w_down.shape),
    )


def solution(mesh):
    placed = (
        P("expert", None),
        P("expert"),
        P("expert", None),
        P(),
        P("tensor", None),
        P("tensor", None),
        P(None, "tensor"),
        P(None, "tensor"),
        P(None, "tensor"),
        P("tensor", None),
        P(),
        P(),
        P("expert", None, "tensor"),
        P("expert", None, "tensor"),
        P("expert", "tensor", None),
        P("expert", None),
    )
    return jax.shard_map(
        functools.partial(body, mesh.shape["expert"], mesh.shape["tensor"]),
        mesh=mesh,
        in_specs=placed,
        out_specs=(
            P("expert", None),
            P("expert", None),
            P("expert"),
            P("tensor", "expert"),
            P("tensor", "expert"),
            P("expert", "tensor"),
            P("expert", "tensor"),
            P("expert", "tensor"),
            P("tensor", "expert"),
            P("expert"),
            P("expert", None),
            P("expert", None, "tensor"),
            P("expert", None, "tensor"),
            P("expert", "tensor", None),
        ),
        check_vma=False,
    )
```

```python
import functools

import jax
import jax.numpy as jnp
from jax import lax
from jax.experimental import pallas as pl
from jax.experimental.pallas import tpu as pltpu
from jax.sharding import PartitionSpec as P

HD = 128
TOP = 8
WINDOW = 1024
LENGTH = 2048


NORM_EPSILON = 1e-05
HIGHEST_PRECISION = lax.Precision.HIGHEST


def for_sending(value):
    return jax.tree.map(lambda a: a.astype(jnp.bfloat16) if a.dtype == jnp.float32 else a, value)


def shifted(value, axis, steps):
    count = lax.axis_size(axis)
    initial, last = (max(0, -steps), min(count, count - steps))
    return lax.ppermute(value, axis, [(source, source + steps) for source in range(initial, last)])


def rope_tables(positions):
    half_width = HD // 2
    frequency = 10000.0 ** (-jnp.arange(half_width, dtype=jnp.float32) * 2.0 / HD)
    angles = positions.astype(jnp.float32)[:, None] * frequency[None, :]
    angles = jnp.concatenate([angles, angles], axis=-1)
    return (jnp.cos(angles)[:, None, :], jnp.sin(angles)[:, None, :])


def rotate(values, cosine, sine):
    half_width = values.shape[-1] // 2
    turned = jnp.concatenate([-values[..., half_width:], values[..., :half_width]], axis=-1)
    return values * cosine + turned * sine


def rotate_back(grads, cosine, sine):
    half_width = grads.shape[-1] // 2
    scaled = grads * sine
    turned = jnp.concatenate([scaled[..., half_width:], -scaled[..., :half_width]], axis=-1)
    return grads * cosine + turned


def previous_block(pieces):
    return jax.tree.map(
        lambda part, own: part.astype(own.dtype), shifted(for_sending(pieces), "expert", 1), pieces
    )


def following_block(pieces):
    return shifted((for_sending(pieces[0]), for_sending(pieces[1])), "expert", -1)


def body_routed(
    tokens,
    documents,
    routes,
    norm1_gain,
    q_gain,
    k_gain,
    w_query,
    w_key,
    w_value,
    w_out,
    norm2_gain,
    router_w,
    w_gate,
    w_up,
    w_down,
    out_grad,
):
    row_count, model_width = tokens.shape
    groups = lax.axis_size("expert")
    local_experts = w_gate.shape[0]
    experts = local_experts * groups
    capacity = 2 * row_count * TOP // experts
    slots_group = local_experts * capacity
    heads = w_query.shape[1] // HD
    score_scale = HD ** (-0.5)
    first_row = lax.axis_index("expert") * row_count
    positions = first_row + jnp.arange(row_count, dtype=jnp.int32)
    cosine, sine = rope_tables(positions % LENGTH)
    inputs = tokens.astype(jnp.float32)
    scale_one = lax.rsqrt(jnp.mean(inputs * inputs, axis=-1, keepdims=True) + NORM_EPSILON)
    normed_one = (inputs * scale_one * norm1_gain).astype(jnp.bfloat16)
    query_raw = jnp.dot(normed_one, w_query, preferred_element_type=jnp.float32)
    key_raw = jnp.dot(normed_one, w_key, preferred_element_type=jnp.float32)
    values = jnp.dot(normed_one, w_value, preferred_element_type=jnp.float32).astype(jnp.bfloat16)
    query_square, key_square = lax.psum(
        (jnp.sum(query_raw * query_raw, axis=-1), jnp.sum(key_raw * key_raw, axis=-1)), "tensor"
    )
    query_scale = lax.rsqrt(query_square / model_width + NORM_EPSILON)[:, None]
    key_scale = lax.rsqrt(key_square / model_width + NORM_EPSILON)[:, None]
    query_gain = q_gain.reshape(-1)
    key_gain = k_gain.reshape(-1)
    queries = rotate(
        (query_raw * query_scale * query_gain).reshape(row_count, heads, HD), cosine, sine
    ).astype(jnp.bfloat16)
    key_heads = rotate(
        (key_raw * key_scale * key_gain).reshape(row_count, heads, HD), cosine, sine
    ).astype(jnp.bfloat16)
    value_heads = values.reshape(row_count, heads, HD)
    labels = jnp.stack([documents // 256, documents % 256]).astype(jnp.bfloat16)
    previous_one = previous_block((key_heads, value_heads, labels))
    previous_two = previous_block(previous_one)
    all_keys = jnp.concatenate([previous_two[0], previous_one[0], key_heads], axis=0)
    all_values = jnp.concatenate([previous_two[1], previous_one[1], value_heads], axis=0)
    all_labels = jnp.concatenate([previous_two[2], previous_one[2], labels], axis=1)
    key_pos = first_row - 2 * row_count + jnp.arange(3 * row_count, dtype=jnp.int32)
    same_doc = (all_labels[0][None, :] == labels[0][:, None]) & (
        all_labels[1][None, :] == labels[1][:, None]
    )
    allowed = (
        same_doc
        & (key_pos[None, :] <= positions[:, None])
        & (positions[:, None] - key_pos[None, :] < WINDOW)
        & (key_pos[None, :] >= 0)
    )

    def masked_scores():
        raw_scores = (
            jnp.einsum("qhd,khd->hqk", queries, all_keys, preferred_element_type=jnp.float32)
            * score_scale
        )
        return jnp.where(allowed[None], raw_scores, -1e30)

    scores = masked_scores()
    highest = jnp.max(scores, axis=-1, keepdims=True)
    weights = jnp.where(allowed[None], jnp.exp(scores - highest), 0.0)
    denominator = jnp.sum(weights, axis=-1, keepdims=True)
    log_total = highest + jnp.log(denominator)
    attn_probs = weights / denominator
    attended = jnp.einsum(
        "hqk,khd->qhd",
        attn_probs.astype(jnp.bfloat16),
        all_values,
        preferred_element_type=jnp.float32,
    )
    attended = attended.reshape(row_count, -1).astype(jnp.bfloat16)
    attention = lax.psum(jnp.dot(attended, w_out, preferred_element_type=jnp.float32), "tensor")
    state = inputs + attention
    scale_two = lax.rsqrt(jnp.mean(state * state, axis=-1, keepdims=True) + NORM_EPSILON)
    normed_two = (state * scale_two * norm2_gain).astype(jnp.bfloat16)
    router_probs = jax.nn.softmax(
        jnp.dot(normed_two, router_w, preferred_element_type=jnp.float32), axis=-1
    )
    chosen = (routes[:, :, None] == jnp.arange(experts, dtype=jnp.int32)[None, None, :]).astype(
        jnp.float32
    )
    gates = jnp.sum(chosen * router_probs[:, None, :], axis=-1)
    flat_routes = routes.reshape(-1)
    onehot = (flat_routes[:, None] == jnp.arange(experts, dtype=jnp.int32)[None, :]).astype(
        jnp.int32
    )
    slot_index = jnp.sum(jnp.cumsum(onehot, axis=0) * onehot, axis=1) - 1
    target = flat_routes * capacity + slot_index
    source = (
        jnp.full((experts * capacity,), -1, jnp.int32)
        .at[target]
        .set(jnp.arange(row_count * TOP, dtype=jnp.int32))
    )
    live_slot = source >= 0
    pick_index = jnp.maximum(source, 0)
    send_rows = jnp.where(
        live_slot[:, None], normed_two[pick_index // TOP], jnp.zeros((), jnp.bfloat16)
    ).reshape(groups, slots_group, model_width)
    grad_float = out_grad.astype(jnp.float32)
    pick_grads = (
        (gates[:, :, None] * grad_float[:, None, :])
        .astype(jnp.bfloat16)
        .reshape(row_count * TOP, model_width)
    )
    send_grads = jnp.where(
        live_slot[:, None], pick_grads[pick_index], jnp.zeros((), jnp.bfloat16)
    ).reshape(groups, slots_group, model_width)
    arrived = lax.all_to_all(send_rows, "expert", split_axis=0, concat_axis=0, tiled=True)
    stacked = arrived.reshape(groups, local_experts, capacity, model_width)
    gate_pre = jnp.einsum("secd,edf->secf", stacked, w_gate, preferred_element_type=jnp.float32)
    up_pre = jnp.einsum("secd,edf->secf", stacked, w_up, preferred_element_type=jnp.float32)
    activated = jax.nn.silu(gate_pre)
    inner_act = (activated * up_pre).astype(jnp.bfloat16)
    produced = jnp.einsum(
        "secf,efd->secd", inner_act, w_down, preferred_element_type=jnp.float32
    ).astype(jnp.bfloat16)
    returned = lax.all_to_all(
        produced.reshape(groups, slots_group, model_width),
        "expert",
        split_axis=0,
        concat_axis=0,
        tiled=True,
    )
    back_rows = (
        returned.reshape(experts * capacity, model_width)[target]
        .reshape(row_count, TOP, model_width)
        .astype(jnp.float32)
    )
    expert_part = jnp.sum(gates[:, :, None] * back_rows, axis=1)
    expert_mix = lax.psum(expert_part.astype(jnp.bfloat16), "tensor").astype(jnp.float32)
    output = (state + expert_mix).astype(jnp.bfloat16)
    gate_part = jnp.sum(grad_float[:, None, :] * back_rows, axis=-1)
    arrived_grad = lax.all_to_all(send_grads, "expert", split_axis=0, concat_axis=0, tiled=True)
    slot_grad = arrived_grad.reshape(groups, local_experts, capacity, model_width)
    w_down_grad = jnp.einsum(
        "secf,secd->efd", inner_act, slot_grad, preferred_element_type=jnp.float32
    )
    inner_grad = jnp.einsum("secd,efd->secf", slot_grad, w_down, preferred_element_type=jnp.float32)
    logistic = jax.nn.sigmoid(gate_pre)
    gate_pre_grad = (inner_grad * up_pre * logistic * (1.0 + gate_pre * (1.0 - logistic))).astype(
        jnp.bfloat16
    )
    up_pre_grad = (inner_grad * activated).astype(jnp.bfloat16)
    w_gate_grad = jnp.einsum(
        "secd,secf->edf", stacked, gate_pre_grad, preferred_element_type=jnp.float32
    )
    w_up_grad = jnp.einsum(
        "secd,secf->edf", stacked, up_pre_grad, preferred_element_type=jnp.float32
    )
    row_grad = jnp.einsum(
        "secf,edf->secd", gate_pre_grad, w_gate, preferred_element_type=jnp.float32
    )
    row_grad = (
        row_grad
        + jnp.einsum("secf,edf->secd", up_pre_grad, w_up, preferred_element_type=jnp.float32)
    ).astype(jnp.bfloat16)
    grad_back = lax.all_to_all(
        row_grad.reshape(groups, slots_group, model_width),
        "expert",
        split_axis=0,
        concat_axis=0,
        tiled=True,
    )
    grad_picks = (
        grad_back.reshape(experts * capacity, model_width)[target]
        .reshape(row_count, TOP, model_width)
        .astype(jnp.float32)
    )
    normed_part = jnp.sum(grad_picks, axis=1)
    normed_two_grad, gate_cot = lax.psum((normed_part, gate_part), "tensor")
    prob_cot = jnp.sum(gate_cot[:, :, None] * chosen, axis=1)
    logit_cot = router_probs * (prob_cot - jnp.sum(router_probs * prob_cot, axis=-1, keepdims=True))
    router_float = router_w.astype(jnp.float32)
    normed_two_grad = normed_two_grad + jnp.einsum(
        "te,de->td", logit_cot, router_float, precision=HIGHEST_PRECISION
    )
    router_grad = jnp.einsum(
        "td,te->de", normed_two.astype(jnp.float32), logit_cot, precision=HIGHEST_PRECISION
    )
    norm2_grad = jnp.sum(normed_two_grad * state * scale_two, axis=0)
    inner_two = jnp.sum(normed_two_grad * norm2_gain * state, axis=-1, keepdims=True)
    state_cot = (
        grad_float
        + scale_two * norm2_gain * normed_two_grad
        - state * scale_two**3 * inner_two / model_width
    )
    state_low = state_cot.astype(jnp.bfloat16)
    w_out_grad = jnp.einsum("tf,td->fd", attended, state_low, preferred_element_type=jnp.float32)
    attended_cot = (
        jnp.einsum("td,fd->tf", state_low, w_out, preferred_element_type=jnp.float32)
        .astype(jnp.bfloat16)
        .reshape(row_count, heads, HD)
    )
    scores = masked_scores()
    attn_probs = jnp.where(allowed[None], jnp.exp(scores - log_total), 0.0)
    value_cot_all = jnp.einsum(
        "hqk,qhd->khd",
        attn_probs.astype(jnp.bfloat16),
        attended_cot,
        preferred_element_type=jnp.float32,
    )
    prob_grad = jnp.einsum(
        "qhd,khd->hqk", attended_cot, all_values, preferred_element_type=jnp.float32
    )
    delta = jnp.sum(attn_probs * prob_grad, axis=-1, keepdims=True)
    score_cot = (attn_probs * (prob_grad - delta)).astype(jnp.bfloat16)
    query_cot = (
        jnp.einsum("hqk,khd->qhd", score_cot, all_keys, preferred_element_type=jnp.float32)
        * score_scale
    )
    key_cot_all = (
        jnp.einsum("hqk,qhd->khd", score_cot, queries, preferred_element_type=jnp.float32)
        * score_scale
    )
    carried = following_block((key_cot_all[:row_count], value_cot_all[:row_count]))
    carried = following_block(
        (
            key_cot_all[row_count : 2 * row_count] + carried[0],
            value_cot_all[row_count : 2 * row_count] + carried[1],
        )
    )
    key_cot = key_cot_all[2 * row_count :] + carried[0]
    value_cot = value_cot_all[2 * row_count :] + carried[1]
    query_norm_cot = rotate_back(query_cot, cosine, sine).reshape(row_count, -1)
    key_norm_cot = rotate_back(key_cot, cosine, sine).reshape(row_count, -1)
    q_gain_local = jnp.sum(query_norm_cot * query_raw * query_scale, axis=0).reshape(heads, HD)
    k_gain_local = jnp.sum(key_norm_cot * key_raw * key_scale, axis=0).reshape(heads, HD)
    query_inner, key_inner = lax.psum(
        (
            jnp.sum(query_norm_cot * query_gain * query_raw, axis=-1),
            jnp.sum(key_norm_cot * key_gain * key_raw, axis=-1),
        ),
        "tensor",
    )
    query_raw_cot = (
        query_scale * query_gain * query_norm_cot
        - query_raw * query_scale**3 * query_inner[:, None] / model_width
    ).astype(jnp.bfloat16)
    key_raw_cot = (
        key_scale * key_gain * key_norm_cot
        - key_raw * key_scale**3 * key_inner[:, None] / model_width
    ).astype(jnp.bfloat16)
    value_low = value_cot.reshape(row_count, -1).astype(jnp.bfloat16)
    w_query_local = jnp.einsum(
        "td,tf->df", normed_one, query_raw_cot, preferred_element_type=jnp.float32
    )
    w_key_local = jnp.einsum(
        "td,tf->df", normed_one, key_raw_cot, preferred_element_type=jnp.float32
    )
    w_value_local = jnp.einsum(
        "td,tf->df", normed_one, value_low, preferred_element_type=jnp.float32
    )
    normed_part_one = jnp.einsum(
        "tf,df->td", query_raw_cot, w_query, preferred_element_type=jnp.float32
    )
    normed_part_one = normed_part_one + jnp.einsum(
        "tf,df->td", key_raw_cot, w_key, preferred_element_type=jnp.float32
    )
    normed_part_one = normed_part_one + jnp.einsum(
        "tf,df->td", value_low, w_value, preferred_element_type=jnp.float32
    )
    normed_one_grad = lax.psum(normed_part_one.astype(jnp.bfloat16), "tensor").astype(jnp.float32)
    norm1_grad = jnp.sum(normed_one_grad * inputs * scale_one, axis=0)
    inner_one = jnp.sum(normed_one_grad * norm1_gain * inputs, axis=-1, keepdims=True)
    input_grad = (
        state_cot
        + scale_one * norm1_gain * normed_one_grad
        - inputs * scale_one**3 * inner_one / model_width
    )
    summed = (
        lax.psum_scatter(
            w_query_local.astype(jnp.bfloat16), "expert", scatter_dimension=0, tiled=True
        ).astype(jnp.float32),
        lax.psum_scatter(
            w_key_local.astype(jnp.bfloat16), "expert", scatter_dimension=0, tiled=True
        ).astype(jnp.float32),
        lax.psum_scatter(
            w_value_local.astype(jnp.bfloat16), "expert", scatter_dimension=0, tiled=True
        ).astype(jnp.float32),
        lax.psum_scatter(
            w_out_grad.astype(jnp.bfloat16), "expert", scatter_dimension=1, tiled=True
        ).astype(jnp.float32),
        lax.psum_scatter(
            router_grad.astype(jnp.bfloat16), "expert", scatter_dimension=0, tiled=True
        ).astype(jnp.float32),
        lax.psum_scatter(
            norm1_grad.astype(jnp.bfloat16), "expert", scatter_dimension=0, tiled=True
        ).astype(jnp.float32),
        lax.psum_scatter(
            norm2_grad.astype(jnp.bfloat16), "expert", scatter_dimension=0, tiled=True
        ).astype(jnp.float32),
        lax.psum_scatter(
            q_gain_local.astype(jnp.bfloat16), "expert", scatter_dimension=1, tiled=True
        ).astype(jnp.float32),
        lax.psum_scatter(
            k_gain_local.astype(jnp.bfloat16), "expert", scatter_dimension=1, tiled=True
        ).astype(jnp.float32),
    )
    return (
        output,
        input_grad,
        summed[5],
        summed[7],
        summed[8],
        summed[0],
        summed[1],
        summed[2],
        summed[3],
        summed[6],
        summed[4],
        w_gate_grad,
        w_up_grad,
        w_down_grad,
    )


MESH = pl.DeviceIdType.MESH
ANY = pl.BlockSpec(memory_space=pl.ANY)
VMEM = pl.BlockSpec(memory_space=pltpu.VMEM)
VMEM_BYTES = 62 * 1024 * 1024
LOW = jnp.bfloat16
FULL = jnp.float32


def place():
    group, part = lax.axis_index("expert"), lax.axis_index("tensor")
    return group // 2, group % 2, part // 2, part % 2


def device(z, x, y, core):
    return (2 * z + x, 2 * y + core)


def swapped(index, step):
    result, bit = index, 1
    while bit <= step:
        if step & bit:
            result = result + bit - 2 * bit * ((index // bit) % 2)
        bit *= 2
    return result


def greet(partners):
    barrier = pltpu.get_barrier_semaphore()
    for partner in partners:
        pl.semaphore_signal(barrier, inc=1, device_id=partner, device_id_type=MESH)
    pl.semaphore_wait(barrier, len(partners))


def remote(source, target, send, arrive, to):
    return pltpu.make_async_remote_copy(
        src_ref=source, dst_ref=target, send_sem=send, recv_sem=arrive, device_id=to, device_id_type=MESH
    )


def dma(*shape):
    return pltpu.SemaphoreType.DMA(shape)


def comm_params(number):
    return pltpu.CompilerParams(collective_id=number, has_side_effects=True, vmem_limit_bytes=VMEM_BYTES)


def add_rows(target, sources, rows, step=16):
    @pl.loop(0, rows // step)
    def _(index):
        part = pl.ds(index * step, step)
        total = sources[0][part].astype(FULL)
        for source in sources[1:]:
            total = total + source[part].astype(FULL)
        target[part] = total.astype(target.dtype)


class Copies:
    def __init__(self):
        self.open = []

    def start(self, copy):
        copy.start()
        self.open.append((copy, set()))
        return copy

    def once(self, copy, what):
        done = next(done for entry, done in self.open if entry is copy)
        new = what not in done
        done.add(what)
        return new

    def arrived(self, copy):
        if self.once(copy, "arrived"):
            copy.wait_recv()

    def sent(self, copy):
        if self.once(copy, "sent"):
            copy.wait_send()

    def finish(self):
        for copy, done in self.open:
            if "sent" not in done:
                copy.wait_send()
            if "arrived" not in done:
                copy.wait_recv()


class Gather:
    def __init__(self, copies, block, target, rows, z_send, z_recv, p_send, p_recv, c_send, c_recv):
        self.copies, self.block, self.target, self.rows = copies, block, target, rows
        self.z_send, self.z_recv, self.p_send, self.p_recv = z_send, z_recv, p_send, p_recv
        self.c_send, self.c_recv = c_send, c_recv
        z, x, y, core = place()
        self.over_x, self.over_y = device(z, 1 - x, y, core), device(z, x, 1 - y, core)
        self.here, self.x_place, self.y_place = 2 * x + y, 2 * (1 - x) + y, 2 * x + 1 - y
        self.far = 2 * (1 - x) + 1 - y
        self.column = [device(swapped(z, step), x, y, core) for step in range(target.shape[0])]
        self.along, self.planes, self.diagonals, self.shared = {}, {}, {}, {}
        edge = rows * 3 // 8
        self.middle = (edge, rows - 2 * edge)
        self.halves = {0: ((0, rows // 2), (rows // 2, rows // 2)), 1: ((0, edge), (rows - edge, edge))}

    def at(self, step, spot, span):
        first, count = span
        return self.target.at[step, pl.ds(pl.multiple_of(spot * self.rows + first, 16), count)]

    def lift(self, step):
        low, whole = step & -step, (0, self.rows)
        source = self.block if step == low else self.at(step - low, self.here, whole)
        self.along[step] = self.copies.start(
            remote(source, self.at(step, self.here, whole), self.z_send.at[step], self.z_recv.at[step], self.column[low])
        )

    def spread(self, step):
        if step:
            self.copies.arrived(self.along[step])
            bit = 1
            while bit < step & -step:
                self.lift(step | bit)
                bit *= 2
        planes = []
        for number, (to, part) in enumerate([(self.over_x, 0), (self.over_y, 1), (self.over_x, 1), (self.over_y, 0)]):
            span = self.halves[step % 2][part]
            here = self.at(step, self.here, span)
            source = here if step else self.block.at[pl.ds(*span)]
            planes.append(self.copies.start(remote(source, here, self.p_send.at[step, number], self.p_recv.at[step, number], to)))
        self.planes[step] = planes

    def turn(self, step):
        passed = []
        for part, spot, to in ((0, self.x_place, self.over_y), (1, self.y_place, self.over_x)):
            self.copies.arrived(self.planes[step][part])
            here = self.at(step, spot, self.halves[step % 2][part])
            passed.append(
                self.copies.start(remote(here, here, self.p_send.at[step, 4 + part], self.p_recv.at[step, 4 + part], to))
            )
        self.diagonals[step] = passed

    def share(self, step):
        self.complete(step)
        copies = []
        for number, spot in enumerate((self.x_place, self.y_place, self.far)):
            copies.append(
                self.copies.start(
                    remote(
                        self.at(step, spot, self.middle), self.at(step + 1, spot, self.middle),
                        self.c_send.at[step // 2, number], self.c_recv.at[step // 2, number], self.column[1],
                    )
                )
            )
        self.shared[step + 1] = copies

    def complete(self, step):
        for copy in self.planes[step] + self.diagonals[step] + self.shared.get(step, []):
            self.copies.arrived(copy)

    @staticmethod
    def scratch(depth):
        return [dma(depth), dma(depth), dma(depth, 6), dma(depth, 6), dma(depth // 2, 3), dma(depth // 2, 3)]


class Scatter:
    def __init__(self, copies, work, diagonal, from_x, from_y, from_z, rows, send, recv, middle=None):
        self.copies, self.work, self.rows, self.send, self.recv = copies, work, rows, send, recv
        self.diagonal, self.from_x, self.from_y, self.from_z = diagonal, from_x, from_y, from_z
        z, x, y, core = place()
        self.over_x, self.over_y = device(z, 1 - x, y, core), device(z, x, 1 - y, core)
        self.here, self.x_place, self.y_place = 2 * x + y, 2 * (1 - x) + y, 2 * x + 1 - y
        self.far = 2 * (1 - x) + 1 - y
        self.column = [device(swapped(z, step), x, y, core) for step in range(work.shape[0])]
        self.corners, self.sides, self.along, self.shared, self.middle = {}, {}, {}, {}, middle
        edge, half = rows * 3 // 8, rows // 2
        self.center = (edge, rows - 2 * edge)
        self.halves = {0: ((0, half), (half, half)), 1: ((0, half), (half, half))}
        self.pieces = {0: ((0, rows),), 1: ((0, rows),)}
        if middle:
            self.halves[1] = self.pieces[1] = ((0, edge), (rows - edge, edge))

    def at(self, step, spot, span):
        first, count = span
        return self.work.at[step, pl.ds(pl.multiple_of(spot * self.rows + first, 16), count)]

    def copy(self, step, number, source, target, to):
        return self.copies.start(remote(source, target, self.send.at[step, number], self.recv.at[step, number], to))

    def share(self, step):
        landed, send, recv = self.middle
        self.shared[step - 1] = [
            self.copies.start(
                remote(
                    self.at(step, spot, self.center), landed.at[step // 2, spot],
                    send.at[step // 2, spot], recv.at[step // 2, spot], self.column[1],
                )
            )
            for spot in range(4)
        ]

    def corner(self, step):
        for spot, copy in enumerate(self.shared.get(step, [])):
            self.copies.arrived(copy)
            mine = self.at(step, spot, self.center)
            add_rows(mine, [mine, self.middle[0].at[step // 2, spot]], self.center[1])
        first, second = self.halves[step % 2]
        self.corners[step] = (
            self.copy(step, 0, self.at(step, self.far, first), self.diagonal.at[step, pl.ds(*first)], self.over_y),
            self.copy(step, 1, self.at(step, self.far, second), self.diagonal.at[step, pl.ds(*second)], self.over_x),
        )

    def side(self, step):
        first, second = self.halves[step % 2]
        via_y, via_x = self.corners[step]

        def to_x(number, span):
            return self.copy(step, number, self.at(step, self.x_place, span), self.from_x.at[step, pl.ds(*span)], self.over_x)

        def to_y(number, span):
            return self.copy(step, number, self.at(step, self.y_place, span), self.from_y.at[step, pl.ds(*span)], self.over_y)

        sides = [to_x(2, second), to_y(3, first)]
        self.copies.arrived(via_y)
        mine = self.at(step, self.x_place, first)
        add_rows(mine, [mine, self.diagonal.at[step, pl.ds(*first)]], first[1])
        sides.append(to_x(4, first))
        self.copies.arrived(via_x)
        mine = self.at(step, self.y_place, second)
        add_rows(mine, [mine, self.diagonal.at[step, pl.ds(*second)]], second[1])
        sides.append(to_y(5, second))
        self.sides[step] = sides

    def below(self, step, odd_rows):
        terms, bit = [], 1
        while bit < (step & -step if step else len(self.column)):
            if odd_rows or (step | bit) % 2 == 0:
                for copy in self.along[step | bit]:
                    self.copies.arrived(copy)
                terms.append(self.from_z.at[step | bit])
            bit *= 2
        return terms

    def spans(self):
        return [(span, True) for span in self.pieces[1]] + ([(self.center, False)] if self.middle else [])

    def climb(self, step):
        for copy in self.sides[step]:
            self.copies.arrived(copy)
        if step:
            for span, odd_rows in self.spans():
                if odd_rows or step % 2 == 0:
                    mine, part = self.at(step, self.here, span), pl.ds(*span)
                    terms = [mine, self.from_x.at[step, part], self.from_y.at[step, part]]
                    terms += [term.at[part] for term in self.below(step, odd_rows)]
                    add_rows(mine, terms, span[1])
            self.along[step] = []
            for number, span in enumerate(self.pieces[step % 2]):
                mine, part = self.at(step, self.here, span), pl.ds(*span)
                self.along[step].append(
                    self.copy(step, 6 + number, mine, self.from_z.at[step, part], self.column[step & -step])
                )

    def result(self, target, more=()):
        for span, odd_rows in self.spans():
            part = pl.ds(*span)
            terms = [self.at(0, self.here, span), self.from_x.at[0, part], self.from_y.at[0, part]]
            terms += [term.at[part] for term in self.below(0, odd_rows)] + [term.at[part] for term in more]
            add_rows(target.at[part], terms, span[1])

    @staticmethod
    def scratch(depth, rows, width):
        return [pltpu.VMEM((depth, rows, width), LOW)] * 4 + [dma(depth, 8), dma(depth, 8)]


def experts_kernel(
    depth, rows, local, hidden,
    x_ref, gates_ref, grad_ref, gate_ref, up_ref, down_ref,
    sum_ref, cots_ref, normed_ref, gated_ref, gate_grad_ref, up_grad_ref, produced_ref,
    wg, wu, wd, x_all, grads, work, y_out, gated, gate_grad, up_grad, gates, gate_wide, cots, cot_rows,
    diagonal, from_x, from_y, from_z, r_send, r_recv,
    z_send, z_recv, p_send, p_recv, c_send, c_recv, s_send, s_recv, w_send, w_recv, w_load, g_load, saves, local_sem,
):
    z, x, y, core = place()
    here, sibling = 2 * x + y, device(z, x, y, 1 - core)
    others = [
        (step, turn, (swapped(z, step), swapped(x, turn // 2), swapped(y, turn % 2)))
        for step in range(depth)
        for turn in range(4)
        if step or turn
    ]
    greet([device(*other, core) for _, _, other in others] + [sibling])
    copies = Copies()
    smalls = []
    for step, turn, other in others:
        oz, ox, oy = other
        smalls.append(
            copies.start(
                remote(
                    gates_ref.at[2 * oz + ox], gates.at[step, here], s_send.at[0, step, turn], s_recv.at[0, step, turn],
                    device(oz, ox, oy, core),
                )
            )
        )
    gather = Gather(copies, x_ref, x_all, rows, z_send, z_recv, p_send, p_recv, c_send, c_recv)
    gather.spread(0)
    gather.lift(1)
    gather.lift(2)
    plain = []

    def fetch(source, target, sem):
        copy = pltpu.make_async_copy(source, target, sem)
        copy.start()
        return copy

    plain.append(fetch(x_ref, gather.at(0, here, (0, rows)), local_sem.at[0]))
    weights = []
    for index in range(local):
        first = pl.multiple_of((core * local + index) * hidden, hidden)
        columns = pl.ds(first, hidden)
        for number, (source, target) in enumerate(
            [(gate_ref, wg.at[:, columns]), (up_ref, wu.at[:, columns]), (down_ref, wd.at[columns])]
        ):
            weights.append(copies.start(remote(source.at[index], target, w_send.at[number, index], w_recv.at[number, index], sibling)))
            plain.append(fetch(source.at[index], target, w_load.at[number, index]))
    plain.append(fetch(gates_ref.at[2 * z + x], gates.at[0, here], local_sem.at[1]))
    sequence = (0, 2, 3, 1)
    grad_copies = [fetch(grad_ref.at[0], grads.at[0], g_load.at[0])]
    scatter = Scatter(copies, work, diagonal, from_x, from_y, from_z, rows, r_send, r_recv)
    saving, producing, keeping = [], [], []
    wave_rows = 4 * rows
    lanes = lax.broadcasted_iota(jnp.int32, (wave_rows, 128), 1)

    def first_half(step):
        for copy in saving:
            copy.wait()
        saving.clear()
        for spot in range(4):
            padded = jnp.concatenate([gates[step, spot], jnp.zeros((120, 128), FULL)], axis=0)
            gate_wide[pl.ds(spot * rows, rows), :] = padded.T
        cots[...] = jnp.zeros_like(cots)
        turn = sequence.index(step)
        grad_copies[turn].wait()
        if turn + 1 < depth:
            slot = (turn + 1) % 2
            grad_copies.append(fetch(grad_ref.at[sequence[turn + 1]], grads.at[slot], g_load.at[slot]))
        grad = grads.at[turn % 2]

        @pl.loop(0, 2 * local)
        def _(unit):
            columns = pl.ds(pl.multiple_of(unit * hidden, hidden), hidden)
            expert = lax.rem(unit, local)
            gate_pre = dot(x_all[step], wg[:, columns])
            up_pre = dot(x_all[step], wu[:, columns])
            back = dot_t(grad[...], wd[columns, :])
            logistic = 1.0 / (1.0 + jnp.exp(-gate_pre))
            activated = gate_pre * logistic
            inner = activated * up_pre
            cot = jnp.sum(inner * back, axis=-1, keepdims=True)
            cots[...] += jnp.where(lanes == expert, cot, 0.0)
            gate = jnp.sum(jnp.where(lanes == expert, gate_wide[...], 0.0), axis=-1, keepdims=True)
            gated[:, columns] = (gate * inner).astype(LOW)
            inner_grad = gate * back
            gate_grad[:, columns] = (inner_grad * up_pre * logistic * (1.0 + gate_pre * (1.0 - logistic))).astype(LOW)
            up_grad[:, columns] = (inner_grad * activated).astype(LOW)

        for spot in range(4):
            cot_rows[step, spot] = cots[pl.ds(spot * rows, rows), :].T[:8]
        for other_step, turn, (oz, ox, oy) in others:
            if other_step == step:
                copies.start(
                    remote(
                        cot_rows.at[step, 2 * ox + oy], cots_ref.at[step, here], s_send.at[1, step, turn], s_recv.at[1, step, turn],
                        device(oz, ox, oy, core),
                    )
                )
        for number, (source, target) in enumerate([(gated, gated_ref), (gate_grad, gate_grad_ref), (up_grad, up_grad_ref)]):
            saving.append(fetch(source, target.at[step], saves.at[number]))
        keeping.append(fetch(x_all.at[step], normed_ref.at[step], saves.at[4 + step]))

    def second_half(step):
        for copy in producing:
            copy.wait()
        producing.clear()
        tile = 512

        @pl.loop(0, x_all.shape[2] // tile)
        def _(index):
            columns = pl.ds(pl.multiple_of(index * tile, tile), tile)
            y_out[:, columns] = dot(gated[...], wd[:, columns]).astype(LOW)
            work[step, :, columns] = (dot_t(gate_grad[...], wg[columns, :]) + dot_t(up_grad[...], wu[columns, :])).astype(LOW)

        producing.append(fetch(y_out, produced_ref.at[step], saves.at[3]))

    gather.turn(0)
    gather.spread(1)
    gather.share(0)
    for copy in plain:
        copy.wait()
    for copy in weights + smalls:
        copies.arrived(copy)
    first_half(0)
    gather.turn(1)
    gather.spread(2)
    second_half(0)
    gather.turn(2)
    gather.spread(3)
    gather.share(2)
    first_half(2)
    gather.turn(3)
    second_half(2)
    scatter.corner(2)
    gather.complete(3)
    first_half(3)
    scatter.side(2)
    second_half(3)
    scatter.corner(3)
    gather.complete(1)
    first_half(1)
    scatter.side(3)
    second_half(1)
    scatter.corner(1)
    scatter.corner(0)
    scatter.climb(3)
    scatter.side(1)
    scatter.climb(2)
    scatter.side(0)
    scatter.climb(1)
    scatter.climb(0)
    scatter.result(sum_ref)
    own_cots = fetch(cot_rows.at[0, here], cots_ref.at[0, here], local_sem.at[2])
    own_cots.wait()
    for copy in saving + producing + keeping:
        copy.wait()
    copies.finish()


def run_experts(block, gates, grads, w_gate, w_up, w_down, number):
    depth, wave, width = grads.shape
    rows = wave // 4
    local, _, hidden = w_gate.shape
    units = 2 * local * hidden
    kept = jax.ShapeDtypeStruct((depth, wave, units), LOW)
    wide = jax.ShapeDtypeStruct((depth, wave, width), LOW)
    return pl.pallas_call(
        functools.partial(experts_kernel, depth, rows, local, hidden),
        out_shape=(
            jax.ShapeDtypeStruct((rows, width), FULL),
            jax.ShapeDtypeStruct((depth, 4, 8, 128), FULL),
            wide, kept, kept, kept, wide,
        ),
        in_specs=[ANY] * 6,
        out_specs=(VMEM, VMEM, ANY, ANY, ANY, ANY, ANY),
        scratch_shapes=[
            pltpu.VMEM((width, units), LOW), pltpu.VMEM((width, units), LOW), pltpu.VMEM((units, width), LOW),
            pltpu.VMEM((depth, wave, width), LOW), pltpu.VMEM((2, wave, width), LOW),
            pltpu.VMEM((depth, wave, width), LOW), pltpu.VMEM((wave, width), LOW),
            pltpu.VMEM((wave, units), LOW), pltpu.VMEM((wave, units), LOW), pltpu.VMEM((wave, units), LOW),
            pltpu.VMEM((depth, 4, 8, 128), FULL), pltpu.VMEM((wave, 128), FULL), pltpu.VMEM((wave, 128), FULL),
            pltpu.VMEM((depth, 4, 8, 128), FULL),
        ]
        + Scatter.scratch(depth, rows, width)
        + [
            *Gather.scratch(depth), dma(2, depth, 4), dma(2, depth, 4),
            dma(3, local), dma(3, local), dma(3, local), dma(2), dma(4 + depth), dma(3),
        ],
        compiler_params=comm_params(number),
    )(block, gates, grads, w_gate, w_up, w_down)


class TensorScatter:
    def __init__(self, copies, work, from_pair, from_y, send, recv):
        self.copies, self.work, self.from_pair, self.from_y, self.send, self.recv = copies, work, from_pair, from_y, send, recv
        z, x, self.y, self.core = place()
        self.sibling, self.over_y = device(z, x, self.y, 1 - self.core), device(z, x, 1 - self.y, self.core)
        self.rows = work.shape[2]

    def begin(self):
        self.pairs = []
        for turn in (1, 0):
            source = self.work.at[swapped(self.y, turn), 1 - self.core]
            self.pairs.append(
                self.copies.start(remote(source, self.from_pair.at[turn], self.send.at[turn], self.recv.at[turn], self.sibling))
            )

    def cross(self):
        self.copies.arrived(self.pairs[0])
        block = self.work.at[1 - self.y, self.core]
        add_rows(block, [block, self.from_pair.at[1]], self.rows)
        self.across = self.copies.start(remote(block, self.from_y, self.send.at[2], self.recv.at[2], self.over_y))

    def result(self, target):
        self.copies.arrived(self.pairs[1])
        self.copies.arrived(self.across)
        add_rows(target, [self.work.at[self.y, self.core], self.from_pair.at[0], self.from_y], self.rows)

    @staticmethod
    def scratch(rows, width):
        return [
            pltpu.VMEM((2, 2, rows, width), LOW),
            pltpu.VMEM((2, rows, width), LOW),
            pltpu.VMEM((rows, width), LOW),
            dma(3),
            dma(3),
        ]


class TensorGather:
    def __init__(self, copies, block, target, send, recv):
        self.copies, self.target, self.send, self.recv = copies, target, send, recv
        z, x, self.y, self.core = place()
        self.sibling, over_y = device(z, x, self.y, 1 - self.core), device(z, x, 1 - self.y, self.core)
        mine = target.at[self.y, self.core]
        self.across = copies.start(remote(block, mine, send.at[0], recv.at[0], over_y))
        self.near = copies.start(remote(block, mine, send.at[1], recv.at[1], self.sibling))
        self.own = pltpu.make_async_copy(block, mine, send.at[3])
        self.own.start()

    def cross(self):
        self.copies.arrived(self.across)
        block = self.target.at[1 - self.y, self.core]
        self.passed = self.copies.start(remote(block, block, self.send.at[2], self.recv.at[2], self.sibling))

    def finish(self):
        self.own.wait()
        self.copies.arrived(self.near)
        self.copies.arrived(self.passed)


def partners_of(depth):
    z, x, y, core = place()
    return [device(swapped(z, step), x, y, core) for step in range(1, depth)] + [
        device(z, 1 - x, y, core),
        device(z, x, 1 - y, core),
        device(z, x, y, 1 - core),
        device(swapped(z, 1), 1 - x, y, core),
    ]


def mask_bias(bias, key_docs, query_docs, length):
    blocks = bias.shape[0] // length

    @pl.loop(0, bias.shape[0] // 128)
    def _(index):
        part = pl.ds(pl.multiple_of(index * 128, 128), 128)
        key = index * 128 + lax.broadcasted_iota(jnp.int32, (128, length), 0) - (blocks - 1) * length
        query = lax.broadcasted_iota(jnp.int32, (128, length), 1)
        seen = (key_docs[part, :] == query_docs[0:1, :]) & (key <= query) & (query - key < WINDOW)
        bias[part, :] = jnp.where(seen, 0.0, -1e30).astype(bias.dtype)


def exchange(copies, mine, landed, send, recv, mates):
    return [
        copies.start(remote(mine, landed.at[number], send.at[number], recv.at[number], device(*mate)))
        for number, mate in enumerate(mates)
    ]


def mates_of():
    z, x, y, core = place()
    return [(z, x, swapped(y, turn // 2), swapped(core, turn % 2)) for turn in range(1, 4)]


def as_rows(columns):
    lanes = lax.broadcasted_iota(jnp.int32, (columns[0].shape[0], 128), 1)
    wide = jnp.zeros(lanes.shape, FULL)
    for index, column in enumerate(columns):
        wide = jnp.where(lanes == index, column, wide)
    return wide.T[:8]


def as_columns(rows_of_eight):
    length = rows_of_eight.shape[1]
    return jnp.concatenate([rows_of_eight, jnp.zeros((120, length), FULL)], axis=0).T


def attention_kernel(
    depth, rows, heads, chain, local,
    tokens_ref, wq_ref, wk_ref, wv_ref, wo_ref, grads_ref,
    gain1_ref, q_gain_ref, k_gain_ref, cosine_ref, sine_ref, docs_row, gain2_ref, router_ref, picked_ref,
    normed_out, q_out, k_out, queries_out, kv_out, key_docs, scales, attended, logs, state_ref, normed2_ref, probs_ref, gates_ref, own_tokens, own_grads,
    all_grad,
    normed_turned, q_raw, k_raw, queries, kv_all, tokens, normed_ref, wq, wk, wv, wo, docs_ref, logits_ref, docs_in, squares, squares_in, scores, totals, bias, partial, from_pair, from_y, sum_ref,
    t_send, t_recv, z_send, z_recv, p_send, p_recv, c_send, c_recv, h_send, h_recv, d_send, d_recv, q_send, q_recv, load, save,
):
    z, x, y, core = place()
    group, part = lax.axis_index("expert"), lax.axis_index("tensor")
    spot = group % chain
    length, width = tokens.shape
    wide = heads * HD
    scale = HD ** (-0.5)
    own_rows = pl.ds(pl.multiple_of(part * rows, rows), rows)
    grad_ref = grads_ref.at[own_rows]
    docs_ref[...] = jnp.broadcast_to(docs_row[...], docs_ref.shape)
    own_copy = pltpu.make_async_copy(grad_ref, own_grads, load.at[6])
    own_copy.start()
    loads = []
    for number, (source, target) in enumerate([(tokens_ref, tokens), (wv_ref, wv), (wk_ref, wk), (wq_ref, wq), (wo_ref, wo)]):
        loads.append(pltpu.make_async_copy(source, target, load.at[number]))
        loads[-1].start()
    mates = mates_of()
    z1, x1 = swapped(z, 1), 1 - x
    greet(
        [device(swapped(z, step), x, y, core) for step in range(1, depth)]
        + [device(z, x1, y, core), device(z1, x1, y, core)]
        + [device(*mate) for mate in mates]
    )
    copies = Copies()
    for distance in (1, 2):

        @pl.when(spot < chain - distance)
        def _():
            remote(
                docs_ref, docs_in.at[2 - distance], d_send.at[distance], d_recv.at[distance], (group + distance, part)
            ).start()

    gather = Gather(copies, grad_ref, all_grad, rows, z_send, z_recv, p_send, p_recv, c_send, c_recv)
    gather.spread(0)
    gather.lift(1)
    own = pltpu.make_async_copy(grad_ref, gather.at(0, gather.here, (0, rows)), load.at[5])
    own.start()
    key_part, value_part = pl.ds(0, wide), pl.ds(wide, wide)

    high = lax.rem(z, 2)
    over_x, over_z = device(z, x1, y, core), device(z1, x, y, core)

    def docs_copy(distance, to):
        return remote(docs_ref, docs_in.at[2 - distance], d_send.at[distance], d_recv.at[distance], (to, part))

    def halo_copy(kind, source, slot, number, to):
        columns = (key_part, value_part)[kind]
        return remote(
            kv_all.at[source, :, columns], kv_all.at[slot, :, columns], h_send.at[kind, number], h_recv.at[kind, number], to
        )

    def x_copy(kind):
        return halo_copy(kind, 2, 1, 0, over_x)

    def z_copy(kind):
        return halo_copy(kind, 2, 0, 1, over_z)

    def relay_copy(kind):
        return halo_copy(kind, 0, 1, 2, over_x)

    def halo_start(kind):
        pl.when(x == 0)(lambda: x_copy(kind).start())
        pl.when(high == 0)(lambda: z_copy(kind).start())

    def halo_relay(kind):
        pl.when(high == 1)(lambda: z_copy(kind).wait_recv())
        pl.when(spot == 3)(lambda: relay_copy(kind).start())

    def halo_arrive(kind):
        columns = (key_part, value_part)[kind]
        pl.when(x == 1)(lambda: x_copy(kind).wait_recv())
        pl.when(spot == 2)(lambda: relay_copy(kind).wait_recv())

        def clear(slot):
            kv_all[slot, :, columns] = jnp.zeros((length, wide), LOW)

        pl.when(spot == 0)(lambda: clear(1))
        pl.when(high == 0)(lambda: clear(0))

    def halo_sent(kind):
        pl.when(x == 0)(lambda: x_copy(kind).wait_send())
        pl.when(high == 0)(lambda: z_copy(kind).wait_send())
        pl.when(spot == 3)(lambda: relay_copy(kind).wait_send())

    loads[0].wait()

    @pl.loop(0, length // 128)
    def _(index):
        part_rows = pl.ds(pl.multiple_of(index * 128, 128), 128)
        values = tokens[part_rows, :].astype(FULL)
        factor = lax.rsqrt(jnp.mean(values * values, axis=-1, keepdims=True) + NORM_EPSILON)
        normed_ref[part_rows, :] = (values * factor * gain1_ref[0:1, :]).astype(LOW)

    def project(weights, store):
        @pl.loop(0, wide // 256)
        def _(index):
            columns = pl.ds(pl.multiple_of(index * 256, 256), 256)
            store(index, columns, dot(normed_ref[...], weights[:, columns]))

    def keep_value(index, columns, result):
        kv_all[2, :, pl.ds(pl.multiple_of(wide + index * 256, 256), 256)] = result.astype(LOW)

    def keep_key(index, columns, result):
        k_raw[:, columns] = result

    def keep_query(index, columns, result):
        q_raw[:, columns] = result

    loads[2].wait()
    project(wk, keep_key)
    loads[3].wait()
    project(wq, keep_query)
    squares[...] = as_rows(
        [jnp.sum(q_raw[...] * q_raw[...], axis=-1, keepdims=True), jnp.sum(k_raw[...] * k_raw[...], axis=-1, keepdims=True)]
    )
    sent = exchange(copies, squares, squares_in, q_send, q_recv, mates)
    saving = []

    def leave(source, target):
        saving.append(pltpu.make_async_copy(source, target, save.at[len(saving)]))
        saving[-1].start()

    leave(q_raw, q_out)
    leave(k_raw, k_out)
    loads[1].wait()
    project(wv, keep_value)
    halo_start(1)
    gather.turn(0)

    @pl.loop(0, width // 256)
    def _(index):
        columns = pl.ds(pl.multiple_of(index * 256, 256), 256)
        normed_turned[columns, :] = normed_ref[:, columns].T

    leave(normed_turned, normed_out)

    for copy in sent:
        copies.arrived(copy)
    total = squares[...]
    for number in range(3):
        total = total + squares_in[number]
    scales[...] = lax.rsqrt(total * (1.0 / width) + NORM_EPSILON)
    factors = as_columns(scales[...])

    def turn_heads(raw, gain_ref, factor, store):
        for head in range(heads):
            columns = pl.ds(head * HD, HD)
            normed = raw[:, columns] * factor * gain_ref[0:1, columns]
            store(head, (normed * cosine_ref[...] + pltpu.roll(normed, HD // 2, 1) * sine_ref[...]).astype(LOW))

    def store_key(head, turned):
        kv_all[2, :, pl.ds(head * HD, HD)] = turned

    def store_query(head, turned):
        queries[:, pl.ds(head * HD, HD)] = turned

    turn_heads(k_raw, k_gain_ref, factors[:, 1:2], store_key)
    halo_start(0)
    gather.spread(1)
    gather.lift(2)
    turn_heads(q_raw, q_gain_ref, factors[:, 0:1], store_query)
    leave(queries, queries_out)
    for distance in (1, 2):

        @pl.when(spot >= distance)
        def _():
            docs_copy(distance, group - distance).wait_recv()

        @pl.when(spot < distance)
        def _():
            docs_in[2 - distance] = jnp.full_like(docs_ref, -1)

    for block in range(3):
        rows_of = docs_in[block] if block < 2 else docs_ref[...]
        key_docs[pl.ds(block * length, length), :] = rows_of.astype(FULL).T[:, 0:1].astype(jnp.int32)
    mask_bias(bias, key_docs, docs_ref, length)

    def score(block):
        @pl.loop(0, heads)
        def _(head):
            columns = pl.ds(pl.multiple_of(head * HD, HD), HD)
            keys = pl.ds(block * length, length)
            scores[head, keys, :] = dot_t(kv_all[block, :, columns], queries[:, columns]) * scale + bias[keys, :]
    score(2)
    halo_relay(1)
    halo_relay(0)
    gather.share(0)
    gather.spread(2)
    halo_arrive(0)
    gather.turn(1)
    score(1)
    score(0)

    @pl.loop(0, heads)
    def _(head):
        mine = scores.at[head]
        highest = jnp.max(mine[...], axis=0, keepdims=True)
        total = jnp.zeros_like(highest)
        for block in range(3):
            weights = jnp.exp(mine[pl.ds(block * length, length), :] - highest)
            total = total + jnp.sum(weights, axis=0, keepdims=True)
            mine[pl.ds(block * length, length), :] = weights
        logs[head] = jnp.broadcast_to(highest + jnp.log(total), (8, length))
        totals[head] = jnp.broadcast_to(1.0 / total, (8, length))

    halo_arrive(1)

    @pl.loop(0, heads)
    def _(head):
        columns = pl.ds(pl.multiple_of(head * HD, HD), HD)
        values = pl.ds(pl.multiple_of((heads + head) * HD, HD), HD)
        mixed = jnp.zeros((HD, length), FULL)
        for block in range(3):
            probs = (scores[head, pl.ds(block * length, length), :] * totals[head, 0:1, :]).astype(LOW)
            mixed = mixed + t_dot(kv_all[block, :, values], probs)
        attended[:, columns] = mixed.T.astype(LOW)

    gather.turn(2)
    gather.spread(3)
    leave(kv_all, kv_out)
    loads[4].wait()
    for index in range(4):
        partial[index // 2, index % 2] = dot(attended[pl.ds(index * rows, rows), :], wo[...]).astype(LOW)
    scatter = TensorScatter(copies, partial, from_pair, from_y, t_send, t_recv)
    scatter.begin()
    scatter.cross()
    gather.share(2)
    gather.turn(3)
    scatter.result(sum_ref)
    own_tokens[...] = tokens[own_rows, :]
    state = own_tokens[...].astype(FULL) + sum_ref[...]
    state_ref[...] = state
    factor = lax.rsqrt(jnp.mean(state * state, axis=-1, keepdims=True) + NORM_EPSILON)
    normed2_ref[...] = (state * factor * gain2_ref[0:1, :]).astype(LOW)
    experts = gates_ref.shape[0] * local
    logits_ref[...] = jnp.full_like(logits_ref, -1e30)
    logits_ref[:, :experts] = dot_t(normed2_ref[...], router_ref[...])
    logits = logits_ref[...]
    weights = jnp.exp(logits - jnp.max(logits, axis=-1, keepdims=True))
    probs = weights / jnp.sum(weights, axis=-1, keepdims=True)
    probs_ref[...] = probs
    gates = (probs * picked_ref[...]).T
    gates_ref[...] = jnp.zeros_like(gates_ref)
    for index in range(gates_ref.shape[0]):
        gates_ref[index, 0:local, :] = gates[index * local : (index + 1) * local]
    own.wait()
    own_copy.wait()
    for copy in saving:
        copy.wait()
    for kind in range(2):
        halo_sent(kind)
    for distance in (1, 2):

        @pl.when(spot < chain - distance)
        def _():
            docs_copy(distance, group + distance).wait_send()

    copies.finish()


def run_attention(tokens, weights, grads, gains, tables, docs, gain2, router, picked, depth, chain, local, number):
    length, width = tokens.shape
    rows = length // 4
    wide = weights[0].shape[1]
    heads = wide // HD
    return pl.pallas_call(
        functools.partial(attention_kernel, depth, rows, heads, chain, local),
        out_shape=(
            jax.ShapeDtypeStruct((width, length), LOW),
            jax.ShapeDtypeStruct((length, wide), FULL),
            jax.ShapeDtypeStruct((length, wide), FULL),
            jax.ShapeDtypeStruct((length, wide), LOW),
            jax.ShapeDtypeStruct((3, length, 2 * wide), LOW),
            jax.ShapeDtypeStruct((3 * length, 1), jnp.int32),
            jax.ShapeDtypeStruct((8, length), FULL),
            jax.ShapeDtypeStruct((length, wide), LOW),
            jax.ShapeDtypeStruct((heads, 8, length), FULL),
            jax.ShapeDtypeStruct((rows, width), FULL),
            jax.ShapeDtypeStruct((rows, width), LOW),
            jax.ShapeDtypeStruct((rows, 128), FULL),
            jax.ShapeDtypeStruct((2 * depth, 8, rows), FULL),
            jax.ShapeDtypeStruct((rows, width), LOW),
            jax.ShapeDtypeStruct((rows, width), LOW),
            jax.ShapeDtypeStruct((depth, 4 * rows, width), LOW),
        ),
        in_specs=[ANY] * 6 + [VMEM] * 9,
        out_specs=(ANY,) * 5 + (VMEM,) * 10 + (ANY,),
        scratch_shapes=[
            pltpu.VMEM((width, length), LOW), pltpu.VMEM((length, wide), FULL), pltpu.VMEM((length, wide), FULL),
            pltpu.VMEM((length, wide), LOW), pltpu.VMEM((3, length, 2 * wide), LOW),
            pltpu.VMEM(tokens.shape, LOW), pltpu.VMEM(tokens.shape, LOW), pltpu.VMEM((width, wide), LOW), pltpu.VMEM((width, wide), LOW),
            pltpu.VMEM((width, wide), LOW), pltpu.VMEM((wide, width), LOW), pltpu.VMEM((8, length), jnp.int32),
            pltpu.VMEM((rows, 128), FULL), pltpu.VMEM((2, 8, length), jnp.int32),
            pltpu.VMEM((8, length), FULL), pltpu.VMEM((3, 8, length), FULL),
            pltpu.VMEM((heads, 3 * length, length), FULL), pltpu.VMEM((heads, 8, length), FULL),
            pltpu.VMEM((3 * length, length), FULL),
        ]
        + TensorScatter.scratch(rows, width)[:3]
        + [
            pltpu.VMEM((rows, width), FULL), dma(3), dma(3),
            *Gather.scratch(depth), dma(2, 3), dma(2, 3), dma(3), dma(3), dma(3), dma(3), dma(7), dma(5),
        ],
        compiler_params=comm_params(number),
    )(tokens, *weights, grads, *gains, *tables, docs, gain2, router, picked)


def attention_back_kernel(
    depth, rows, heads, chain, local,
    sum_ref, gate_cots, probs_ref, picked_ref, state_ref, gain2_ref, router_ref, normed2_ref, grad_ref,
    query_ref, kv_ref, attended, logs, docs_ref, query_docs, q_ref, k_ref, q_gain_ref, k_gain_ref, cosine_ref, sine_ref, scales,
    w_out_ref, produced_ref, normed_ref, wq_ref, wk_ref, wv_ref,
    state_cot_ref, vectors, out_ref, normed_part, piece0, piece1, piece2, piece3,
    kv_all, key_docs, q_raw, k_raw, w_out, low, lows, by_expert, bias, cots, deltas, turned, query_cot, kv_cot, sending, landed, work, raw_cots, flipped, wq, wk, wv,
    inners, inners_in, staging,
    diagonal, from_x, from_y, from_z, r_send, r_recv, middle, m_send, m_recv,
    t_send, t_recv, h_send, h_recv, i_send, i_recv, load, saves, early_load,
):
    z, x, y, core = place()
    group, part = lax.axis_index("expert"), lax.axis_index("tensor")
    spot = group % chain
    length, width = query_ref.shape[0], w_out.shape[1]
    wide = heads * HD
    scale = HD ** (-0.5)
    order = [step for step in range(depth - 1, 0, -2)] + [step for step in range(depth - 2, -1, -2)]
    loads = {}
    for step in order:
        loads[step] = pltpu.make_async_copy(produced_ref.at[step], work.at[step], load.at[step])
        loads[step].start()
    others = []
    for number, (source, target) in enumerate([(wq_ref, wq), (wk_ref, wk), (wv_ref, wv)]):
        others.append(pltpu.make_async_copy(source, target, load.at[depth + number]))
        others[-1].start()
    early = []
    for number, (source, target) in enumerate(
        [(docs_ref, key_docs), (w_out_ref, w_out), (kv_ref, kv_all), (q_ref, q_raw), (k_ref, k_raw)]
    ):
        early.append(pltpu.make_async_copy(source, target, early_load.at[number]))
        early[-1].start()
    mates = mates_of()
    greet(
        [device(swapped(z, step), x, y, core) for step in range(1, depth)]
        + [device(z, 1 - x, y, core)]
        + [device(*mate) for mate in mates]
    )
    copies = Copies()
    scatter = Scatter(
        copies, work, diagonal, from_x, from_y, from_z, rows, r_send, r_recv, (middle, m_send, m_recv)
    )

    def corner(step):
        if step % 2 == 0:
            loads[step].wait()
        scatter.corner(step)


    loads[3].wait()
    scatter.share(3)
    loads[1].wait()
    scatter.share(1)
    corner(3)
    by_expert[...] = jnp.zeros_like(by_expert)
    for plane in range(depth):
        step = swapped(z, plane)
        for column in range(2):
            first = (2 * plane + column) * local
            by_expert[first : first + local, :] = (gate_cots[step, 2 * column] + gate_cots[step, 2 * column + 1])[:local]
    probs = probs_ref[...]
    prob_cot = by_expert[...].T * picked_ref[...]
    logit_cot = probs * (prob_cot - jnp.sum(probs * prob_cot, axis=-1, keepdims=True))
    normed2_cot = sum_ref[...] + lax.dot_general(
        logit_cot[:, : router_ref.shape[0]], router_ref[...].astype(FULL), (((1,), (0,)), ((), ())),
        precision=HIGHEST_PRECISION, preferred_element_type=FULL,
    )
    state = state_ref[...]
    factor = lax.rsqrt(jnp.mean(state * state, axis=-1, keepdims=True) + NORM_EPSILON)
    groups, _, slice_width = vectors.shape
    vectors[...] = jnp.zeros_like(vectors)
    gain_grad = jnp.sum(normed2_cot * state * factor, axis=0, keepdims=True)
    for index in range(groups):
        vectors[index, 17:18, :] = gain_grad[:, index * slice_width : (index + 1) * slice_width]
    inner = jnp.sum(normed2_cot * gain2_ref[0:1, :] * state, axis=-1, keepdims=True)
    state_cot = (
        grad_ref[...].astype(FULL)
        + factor * gain2_ref[0:1, :] * normed2_cot
        - state * (factor * factor * factor) * inner * (1.0 / width)
    )
    state_cot_ref[...] = state_cot
    low[...] = state_cot.astype(LOW)
    gather = TensorGather(copies, low, lows, t_send, t_recv)
    scatter.side(3)
    corner(2)
    router_grad = jnp.dot(
        logit_cot.T, normed2_ref[...].astype(FULL), precision=HIGHEST_PRECISION, preferred_element_type=FULL
    )[:16]
    for index in range(groups):
        vectors[index, 0:16, :] = router_grad[:, index * slice_width : (index + 1) * slice_width]
    early[0].wait()
    mask_bias(bias, key_docs, query_docs, length)
    for copy in early[1:]:
        copy.wait()
    gather.cross()
    scatter.side(2)
    gather.finish()
    for index in range(4):
        cots[pl.ds(index * rows, rows), :] = dot_t(lows[index // 2, index % 2], w_out[...]).astype(LOW)
    for head in range(heads):
        columns = pl.ds(head * HD, HD)
        product = cots[:, columns].astype(FULL) * attended[:, columns].astype(FULL)
        deltas[head] = jnp.broadcast_to(jnp.sum(product.T, axis=0, keepdims=True), (8, length))
    turned[...] = jnp.zeros_like(turned)

    def back(block, store, after):
        @pl.loop(0, heads)
        def _(head):
            columns = pl.ds(pl.multiple_of(head * HD, HD), HD)
            values = pl.ds(pl.multiple_of((heads + head) * HD, HD), HD)
            tile = length // 2

            for index, seen in ((0, pl.ds(0, tile if block == 0 else length)), (1, pl.ds(tile, tile) if block == 2 else pl.ds(0, length))):
                keys = pl.ds(index * tile, tile)
                key, value = kv_all[block, keys, columns], kv_all[block, keys, values]
                query, cot = query_ref[seen, columns], cots[seen, columns]
                log, delta = logs[head, 0:1, seen], deltas[head, 0:1, seen]
                hidden = bias[pl.ds(block * length + index * tile, tile), seen].astype(FULL)
                probs = jnp.exp(dot_t(key, query) * scale + hidden - log)
                score_cot = (probs * (dot_t(value, cot) - delta)).astype(LOW)
                turned[head, :, seen] += t_dot(key, score_cot)
                store(head, keys, dot(score_cot, query) * scale, dot(probs.astype(LOW), cot))

            after(head)

    def store_in(slot):
        def store(head, keys, key_part, value_part):
            sending[slot, head, keys, 0:HD] = key_part.astype(LOW)
            sending[slot, head, keys, HD : 2 * HD] = value_part.astype(LOW)

        return store

    def store_own(head, keys, key_part, value_part):
        kv_cot[keys, pl.ds(pl.multiple_of(head * HD, HD), HD)] = key_part
        kv_cot[keys, pl.ds(pl.multiple_of((heads + head) * HD, HD), HD)] = value_part

    high = lax.rem(z, 2)
    over_x, over_z = device(z, 1 - x, y, core), device(swapped(z, 1), x, y, core)

    def x_copy(head):
        return remote(sending.at[1, head], landed.at[1, head], h_send.at[0, head], h_recv.at[0, head], over_x)

    def z_copy(head):
        return remote(sending.at[0, head], landed.at[0, head], h_send.at[1, head], h_recv.at[1, head], over_z)

    def relay(head):
        @pl.when(spot == 3)
        def _():
            x_copy(head).wait_recv()
            add_rows(sending.at[0, head], [sending.at[0, head], landed.at[1, head]], length, 64)
            z_copy(head).start()

    back(1, store_in(1), lambda head: pl.when(spot >= 1)(lambda: x_copy(head).start()))
    scatter.climb(3)
    back(0, store_in(0), lambda head: pl.when(spot == 2)(lambda: z_copy(head).start()))
    back(2, store_own, relay)
    scatter.climb(2)
    corner(1)
    corner(0)
    for head in range(heads):
        query_cot[:, pl.ds(head * HD, HD)] = turned[head].T * scale

    scatter.side(1)
    saving = {}

    def weight_piece(number, right, target):
        piece = target.shape[2]
        for index in range(2 * depth):
            slot = index % 2
            if slot in saving:
                saving.pop(slot).wait()
            staging[slot] = dot(flipped[pl.ds(index * piece, piece), :], right).astype(LOW)
            saving[slot] = pltpu.make_async_copy(staging.at[slot], target.at[index // 2, index % 2], saves.at[slot])
            saving[slot].start()

    @pl.loop(0, width // 256)
    def _(index):
        columns = pl.ds(pl.multiple_of(index * 256, 256), 256)
        flipped[columns, :] = jnp.concatenate([lows[block // 2, block % 2, :, columns] for block in range(4)], axis=0).T

    weight_piece(0, attended[...], piece0)
    normed_copy = pltpu.make_async_copy(normed_ref, flipped, load.at[depth + 3])
    normed_copy.start()
    scatter.side(0)
    factors = as_columns(scales[...])

    def turn_back(cot, raw, gain_ref, factor, first):
        total = jnp.zeros((length, 1), FULL)
        for head in range(heads):
            columns = pl.ds(head * HD, HD)
            mine = cot[:, columns]
            mine = mine * cosine_ref[...] - pltpu.roll(mine, HD // 2, 1) * sine_ref[...]
            cot[:, columns] = mine
            mine = mine * raw[:, columns]
            grad = jnp.sum(mine * factor, axis=0, keepdims=True)
            for index in range(groups):
                vectors[index, first + head : first + head + 1, 0:HD] = grad
            total = total + jnp.sum(mine * gain_ref[0:1, columns], axis=-1, keepdims=True)
        return total

    query_inner = turn_back(query_cot, q_raw, q_gain_ref, factors[:, 0:1], 18)

    scatter.climb(1)
    def take(slot, head):
        (z_copy, x_copy)[slot](head).wait_recv()
        for part in range(2):
            mine = kv_cot.at[:, pl.ds((part * heads + head) * HD, HD)]
            add_rows(mine, [mine, landed.at[slot, head, :, pl.ds(part * HD, HD)]], length, 64)

    for head in range(heads):
        pl.when(x == 0)(functools.partial(take, 1, head))
    for head in range(heads):
        pl.when(high == 0)(functools.partial(take, 0, head))

    key_inner = turn_back(kv_cot, k_raw, k_gain_ref, factors[:, 1:2], 18 + heads)
    inners[...] = as_rows([query_inner, key_inner])
    sent = exchange(copies, inners, inners_in, i_send, i_recv, mates)
    raw_cots[2] = kv_cot[:, pl.ds(wide, wide)].astype(LOW)
    normed_copy.wait()
    weight_piece(1, raw_cots[2], piece1)
    for copy in sent:
        copies.arrived(copy)
    total = inners[...]
    for number in range(3):
        total = total + inners_in[number]
    totals = as_columns(total * (1.0 / width))

    def raw_cot(number, cot, raw, gain_ref):
        factor = factors[:, number : number + 1]
        shrink = (factor * factor * factor) * totals[:, number : number + 1]
        for head in range(heads):
            columns = pl.ds(head * HD, HD)
            raw_cots[number, :, columns] = (
                factor * gain_ref[0:1, columns] * cot[:, columns] - raw[:, columns] * shrink
            ).astype(LOW)

    raw_cot(0, query_cot, q_raw, q_gain_ref)
    raw_cot(1, kv_cot, k_raw, k_gain_ref)
    for copy in others:
        copy.wait()

    @pl.loop(0, width // 256)
    def _(index):
        columns = pl.ds(pl.multiple_of(index * 256, 256), 256)
        result = (
            dot_t(raw_cots[0], wq[columns, :]) + dot_t(raw_cots[1], wk[columns, :]) + dot_t(raw_cots[2], wv[columns, :])
        ).astype(LOW)
        for block in range(4):
            normed_part[block // 2, block % 2, :, columns] = result[block * rows : (block + 1) * rows]

    weight_piece(2, raw_cots[0], piece2)
    weight_piece(3, raw_cots[1], piece3)
    scatter.climb(0)
    scatter.result(out_ref, [state_ref])
    for head in range(heads):
        pl.when(spot >= 1)(lambda: x_copy(head).wait_send())
        pl.when(spot >= 2)(lambda: z_copy(head).wait_send())

    for copy in saving.values():
        copy.wait()
    copies.finish()


def run_attention_back(rows_of, attention, sources, produced, normed, weights, chain, local, number):
    depth = produced.shape[0]
    rows, width = rows_of[0].shape
    queries, kv_all = attention[0], attention[1]
    length, wide2 = kv_all.shape[1:]
    wide = wide2 // 2
    heads = wide // HD
    piece = jax.ShapeDtypeStruct((depth, 2, width // (2 * depth), wide), LOW)
    return pl.pallas_call(
        functools.partial(attention_back_kernel, depth, rows, heads, chain, local),
        out_shape=(
            jax.ShapeDtypeStruct((rows, width), FULL),
            jax.ShapeDtypeStruct((2 * depth, 32, width // (2 * depth)), FULL),
            jax.ShapeDtypeStruct((rows, width), LOW),
            jax.ShapeDtypeStruct((2, 2, rows, width), LOW),
            piece, piece, piece, piece,
        ),
        in_specs=[VMEM] * 10 + [ANY] + [VMEM] * 2 + [ANY] + [VMEM] + [ANY] * 2 + [VMEM] * 5 + [ANY] * 6,
        out_specs=(VMEM,) * 4 + (ANY,) * 4,
        scratch_shapes=[
            pltpu.VMEM(kv_all.shape, LOW), pltpu.VMEM((3 * length, 1), jnp.int32), pltpu.VMEM((length, wide), FULL),
            pltpu.VMEM((length, wide), FULL), pltpu.VMEM((wide, width), LOW),
            pltpu.VMEM((rows, width), LOW), pltpu.VMEM((2, 2, rows, width), LOW), pltpu.VMEM((128, rows), FULL),
            pltpu.VMEM((3 * length, length), LOW), pltpu.VMEM((length, wide), LOW),
            pltpu.VMEM((heads, 8, length), FULL), pltpu.VMEM((heads, HD, length), FULL),
            pltpu.VMEM((length, wide), FULL), pltpu.VMEM((length, wide2), FULL),
            pltpu.VMEM((2, heads, length, 2 * HD), LOW), pltpu.VMEM((2, heads, length, 2 * HD), LOW),
            pltpu.VMEM(produced.shape, LOW), pltpu.VMEM((3, length, wide), LOW), pltpu.VMEM((width, length), LOW),
            pltpu.VMEM((width, wide), LOW), pltpu.VMEM((width, wide), LOW), pltpu.VMEM((width, wide), LOW),
            pltpu.VMEM((8, length), FULL), pltpu.VMEM((3, 8, length), FULL), pltpu.VMEM((2,) + piece.shape[2:], LOW),
        ]
        + Scatter.scratch(depth, rows, width)
        + [pltpu.VMEM((depth // 2, 4, rows // 4, width), LOW), dma(depth // 2, 4), dma(depth // 2, 4)]
        + [dma(4), dma(3), dma(2, heads), dma(2, heads), dma(3), dma(3), dma(depth + 4), dma(2), dma(5)],
        compiler_params=comm_params(number),
    )(*rows_of, *attention, *sources, produced, normed, *weights)


def dot(left, right):
    return jnp.dot(left, right, preferred_element_type=FULL)


def dot_t(left, right):
    return lax.dot_general(left, right, (((1,), (1,)), ((), ())), preferred_element_type=FULL)


def t_dot(left, right):
    return lax.dot_general(left, right, (((0,), (0,)), ((), ())), preferred_element_type=FULL)


class ExpertScatter:
    def __init__(self, copies, parts, widths, work, from_x, from_z, load, send, recv):
        self.widths = widths
        self.copies, self.parts, self.work, self.from_x, self.from_z = copies, parts, work, from_x, from_z
        self.load, self.send, self.recv = load, send, recv
        self.z, self.x, y, core = place()
        self.depth, self.rows = work.shape[1], work.shape[2]
        self.over_x = device(self.z, 1 - self.x, y, core)
        self.column = [device(swapped(self.z, step), self.x, y, core) for step in range(self.depth)]
        self.order = sorted(range(self.depth), key=lambda step: (step == 0, step & -step, -step))
        self.steps = self.order[:-1]
        self.loads, self.sides, self.along = {}, {}, {}

    def begin(self, index):
        for step in self.order:
            at = swapped(self.z, step)
            columns = pl.ds(0, self.widths[index])
            self.sides[index, step] = self.copies.start(
                remote(
                    self.parts[index].at[at, 1 - self.x, :, columns], self.from_x.at[index, step, :, columns],
                    self.send.at[0, index, step], self.recv.at[0, index, step], self.over_x,
                )
            )
            load = pltpu.make_async_copy(
                self.parts[index].at[at, self.x, :, columns], self.work.at[index, step, :, columns], self.load.at[index, step]
            )
            load.start()
            self.loads[index, step] = load

    def climb(self, index, step):
        self.loads[index, step].wait()
        self.copies.arrived(self.sides[index, step])
        columns = pl.ds(0, self.widths[index])
        mine = self.work.at[index, step, :, columns]
        low = step & -step
        terms = [mine, self.from_x.at[index, step, :, columns]] + self.below(index, step)
        add_rows(mine, terms, self.rows)
        self.along[index, step] = self.copies.start(
            remote(
                mine, self.from_z.at[index, step, :, columns],
                self.send.at[1, index, step], self.recv.at[1, index, step], self.column[low],
            )
        )

    def below(self, index, step):
        terms, bit = [], 1
        while bit < (step & -step if step else self.depth):
            self.copies.arrived(self.along[index, step | bit])
            terms.append(self.from_z.at[index, step | bit, :, pl.ds(0, self.widths[index])])
            bit *= 2
        return terms

    def result(self, index, target):
        self.loads[index, 0].wait()
        self.copies.arrived(self.sides[index, 0])
        columns = pl.ds(0, self.widths[index])
        terms = [self.work.at[index, 0, :, columns], self.from_x.at[index, 0, :, columns]] + self.below(index, 0)
        add_rows(target.at[:, columns], terms, self.rows)


class ZScatter:
    def __init__(self, copies, part, columns, work, from_z, from_x, load, send, recv):
        self.copies, self.part, self.columns = copies, part, columns
        self.work, self.from_z, self.from_x, self.load, self.send, self.recv = work, from_z, from_x, load, send, recv
        self.z, self.x, y, core = place()
        self.depth, self.rows = work.shape[0], work.shape[2]
        self.over_x = device(self.z, 1 - self.x, y, core)
        self.column = [device(swapped(self.z, step), self.x, y, core) for step in range(self.depth)]
        self.loads, self.along = {}, {}

    def begin(self):
        for step in range(self.depth):
            source = self.part.at[swapped(self.z, step), :, :, self.columns]
            self.loads[step] = pltpu.make_async_copy(source, self.work.at[step], self.load.at[step])
            self.loads[step].start()

    def climb(self, step):
        self.loads[step].wait()
        low = step & -step if step else self.depth
        bit = 1
        while bit < low:
            self.copies.arrived(self.along[step | bit])
            for column in range(2):
                mine = self.work.at[step, column]
                add_rows(mine, [mine, self.from_z.at[step | bit, column]], self.rows, 32)
            bit *= 2
        if step:
            copy = remote(self.work.at[step], self.from_z.at[step], self.send.at[step], self.recv.at[step], self.column[low])
        else:
            copy = remote(self.work.at[0, 1 - self.x], self.from_x, self.send.at[0], self.recv.at[0], self.over_x)
        self.along[step] = self.copies.start(copy)

    def result(self, target):
        self.copies.arrived(self.along[0])
        add_rows(target, [self.work.at[0, self.x], self.from_x], self.rows)


def gradients_kernel(
    depth, rows, local, hidden, matrices, *refs,
):
    parts, refs = refs[:matrices], refs[matrices:]
    (
        normed_part, tokens_ref, state_cot, gain_ref, out_ref, vector_ref,
        normed_ref, grad_ref, gated_ref, gate_grad_ref, up_grad_ref,
    ) = refs[:11]
    sums, refs = refs[11 : 11 + matrices], refs[11 + matrices :]
    (
        input_out, output_out, vector_sum,
        gate_own, up_own, down_own,
        input_grads, outputs, work, from_x, from_z, partial, from_pair, from_y, normed_grad, low, vectors, vector_in, vector_mid, vector_turn,
        tiles, turned, acts, gated_turned, near, far, near_down, far_down, other, other_down,
        f_work, f_from_z, f_from_x, f_load, f_send, f_recv,
        e_load, e_send, e_recv, t_send, t_recv, g_send, g_recv, o_send, o_recv, v_send, v_recv, u_send, u_recv,
        tile_load, act_load, save, pair_send, pair_recv, local_sem, leave_sem,
    ) = refs
    z, x, y, core = place()
    group = 2 * z + x
    sibling = device(z, x, y, 1 - core)
    groups = [(step, turn) for step in range(depth) for turn in range(2) if step or turn]
    peers = [device(swapped(z, step), swapped(x, turn), y, core) for step, turn in groups]
    mates = [(z, x, swapped(y, turn // 2), swapped(core, turn % 2)) for turn in range(1, 4)]
    greet(peers + [device(*mate) for mate in mates])
    copies = Copies()
    width = normed_ref.shape[1]
    tile = local * hidden
    count = width // tile

    def fetch(source, target, sem):
        copy = pltpu.make_async_copy(source, target, sem)
        copy.start()
        return copy

    wide = work.shape[3]
    widths = [wide] * (matrices - 1) + [wide // 2]
    experts = ExpertScatter(copies, parts, widths, work, from_x, from_z, e_load, e_send, e_recv)
    eighth = pl.ds(wide // 2, wide // 2)
    z_first = ZScatter(copies, parts[-1], eighth, f_work, f_from_z, f_from_x, f_load, f_send, f_recv)
    loaded = fetch(normed_part, partial, local_sem.at[0])
    experts.begin(0)
    z_first.begin()
    loaded.wait()
    scatter = TensorScatter(copies, partial, from_pair, from_y, t_send, t_recv)
    scatter.begin()
    out_gather = TensorGather(copies, out_ref, outputs, o_send, o_recv)
    experts.begin(1)
    act_copies = [fetch(gate_grad_ref, acts.at[0], act_load.at[0]), fetch(up_grad_ref, acts.at[1], act_load.at[1])]

    def fetch_tile(number):
        source = normed_ref if number < count else grad_ref
        columns = pl.ds((number % count) * tile, tile)
        return fetch(source.at[:, columns], tiles.at[number % 2], tile_load.at[number % 2])

    tile_copies = [fetch_tile(0)]
    saving = {}

    def first_unit(owner):
        return owner * local * hidden

    def gate_and_up(number):
        slot = number % 2
        tile_copies[number].wait()
        tile_copies.append(fetch_tile(number + 1))
        turned[...] = tiles[slot].T
        for copy, remote_one in saving.pop(slot, []):
            copies.sent(copy) if remote_one else copy.wait()
        for which in range(2):
            for owner, target in ((1 - core, far), (core, near)):

                @pl.loop(0, local)
                def _(expert):
                    columns = pl.ds(pl.multiple_of(first_unit(owner) + expert * hidden, hidden), hidden)
                    target[which, slot, expert] = dot(turned[...], acts[which, :, columns]).astype(target.dtype)

        saves = []
        for which in range(2):
            away = remote(
                far.at[which, slot], other.at[which, :, pl.ds(number * tile, tile)],
                pair_send.at[which, number], pair_recv.at[which, number], sibling,
            )
            copies.start(away)
            saves.append((away, True))
        saving[slot] = saves
        if number:
            settle(number - 1)

    def settle(number):
        slot, place_of = number % 2, pl.ds(number * tile, tile)
        for which, own in enumerate((gate_own, up_own)):
            copies.arrived(saving[slot][which][0])
            for expert in range(local):
                mine = near.at[which, slot, expert]
                add_rows(mine, [mine, other.at[which, expert, place_of]], tile, 64)
        for which, own in enumerate((gate_own, up_own)):
            saving[slot].append((fetch(near.at[which, slot], own.at[:, place_of], save.at[which, slot]), False))

    def down(number):
        slot = number % 2
        tile_copies[count + number].wait()
        if number + 1 < count:
            tile_copies.append(fetch_tile(count + number + 1))
        for copy, remote_one in saving.pop(("down", slot), []):
            copies.sent(copy) if remote_one else copy.wait()
        for source, target in ((turned, far_down), (gated_turned, near_down)):

            @pl.loop(0, local)
            def _(expert):
                units = pl.ds(pl.multiple_of(expert * hidden, hidden), hidden)
                target[slot, expert] = dot(source[units, :], tiles[slot]).astype(target.dtype)

        away = remote(
            far_down.at[slot], other_down.at[number], pair_send.at[2, number], pair_recv.at[2, number], sibling
        )
        copies.start(away)
        saving["down", slot] = [(away, True)]
        settle(count - 1) if number == 0 else settle_down(number - 1)

    def settle_down(number):
        slot = number % 2
        copies.arrived(saving["down", slot][0][0])
        for expert in range(local):
            mine = near_down.at[slot, expert]
            add_rows(mine, [mine, other_down.at[number, expert]], hidden, 64)
        target = down_own.at[:, :, pl.ds(number * tile, tile)]
        saving["down", slot].append((fetch(near_down.at[slot], target, save.at[2, slot]), False))

    for copy in act_copies:
        copy.wait()
    z_first.climb(3)
    z_first.climb(1)
    gate_and_up(0)
    scatter.cross()
    experts.climb(0, experts.steps[0])
    gate_and_up(1)
    out_gather.cross()
    experts.climb(0, experts.steps[1])
    z_first.climb(2)
    scatter.result(normed_grad)

    inputs = tokens_ref[...].astype(FULL)
    factor = lax.rsqrt(jnp.mean(inputs * inputs, axis=-1, keepdims=True) + NORM_EPSILON)
    gain = gain_ref[0:1, :]
    normed = normed_grad[...]
    inner = jnp.sum(normed * gain * inputs, axis=-1, keepdims=True)
    low[...] = (
        state_cot[...] + factor * gain * normed - inputs * (factor * factor * factor) * inner * (1.0 / width)
    ).astype(LOW)
    gain_grad = jnp.sum(normed * inputs * factor, axis=0, keepdims=True)
    grad_gather = TensorGather(copies, low, input_grads, g_send, g_recv)
    vectors[...] = vector_ref[...]
    slice_width = vectors.shape[2]
    for index in range(vectors.shape[0]):
        vectors[index, 16:17, :] = gain_grad[:, index * slice_width : (index + 1) * slice_width]
    vector_copies = []
    for number, ((step, turn), peer) in enumerate(zip(groups, peers)):
        to = 2 * swapped(z, step) + swapped(x, turn)
        vector_copies.append(
            copies.start(remote(vectors.at[to], vector_in.at[number], v_send.at[number], v_recv.at[number], peer))
        )
    for index in range(2, matrices):
        experts.begin(index)

    for step in experts.steps[2:]:
        experts.climb(0, step)
    gate_and_up(2)
    for step in experts.steps[:2]:
        experts.climb(1, step)
    grad_gather.cross()
    z_first.climb(0)
    gate_and_up(3)
    for step in experts.steps[2:]:
        experts.climb(1, step)
    gated_copy = fetch(gated_ref, acts.at[0], act_load.at[0])
    gated_copy.wait()
    for owner, target in ((1 - core, turned), (core, gated_turned)):
        target[...] = acts[0, :, pl.ds(pl.multiple_of(first_unit(owner), hidden), local * hidden)].T
    experts.result(0, sums[0])
    out_gather.finish()
    leaving = [fetch(outputs, output_out, leave_sem.at[0])]
    down(0)
    grad_gather.finish()
    leaving.append(fetch(input_grads, input_out, leave_sem.at[1]))
    experts.climb(2, experts.steps[0])
    down(1)
    for step in experts.steps[1:]:
        experts.climb(2, step)
    down(2)
    experts.result(1, sums[1])
    for copy in vector_copies:
        copies.arrived(copy)
    total = vectors[group]
    for number in range(len(peers)):
        total = total + vector_in[number]
    vector_mid[...] = total
    turn_copies = [
        copies.start(remote(vector_mid, vector_turn.at[number], u_send.at[number], u_recv.at[number], device(*mate)))
        for number, mate in enumerate(mates)
    ]
    down(3)
    settle_down(3)
    for copy in turn_copies:
        copies.arrived(copy)
    total = vector_mid[...]
    for number in range(len(mates)):
        total = total + vector_turn[number]
    keep = lax.broadcasted_iota(jnp.int32, total.shape, 0) < 18
    vector_sum[...] = jnp.where(keep, total, vector_mid[...])
    for index in range(3, matrices):
        for step in experts.steps:
            experts.climb(index, step)
    for index in range(2, matrices):
        experts.result(index, sums[index])
    z_first.result(sums[-1].at[:, eighth])
    for copy in leaving:
        copy.wait()
    for entries in saving.values():
        for copy, remote_one in entries:
            if not remote_one:
                copy.wait()
    copies.finish()


def run_gradients(parts, normed_part, tokens, state_cot, gain, out, vectors, normed, grads, gated, gate_grad, up_grad, local, number):
    matrices = len(parts)
    depth, _, piece, columns = parts[0].shape
    rows, width = state_cot.shape
    seen, units = gated.shape
    hidden = units // (2 * local)
    tile = units // 2
    sum_of = jax.ShapeDtypeStruct((piece, columns), FULL)
    spread = jax.ShapeDtypeStruct((2, 2, rows, width), LOW)
    wide, tall = (local, width, hidden), (local, hidden, width)
    results = pl.pallas_call(
        functools.partial(gradients_kernel, depth, rows, local, hidden, matrices),
        out_shape=(sum_of,) * matrices
        + (
            spread, spread, jax.ShapeDtypeStruct(vectors.shape[1:], FULL),
            jax.ShapeDtypeStruct(wide, FULL), jax.ShapeDtypeStruct(wide, FULL), jax.ShapeDtypeStruct(tall, FULL),
        ),
        in_specs=[ANY] * (matrices + 1) + [VMEM] * 5 + [ANY] * 5,
        out_specs=(VMEM,) * matrices + (ANY, ANY, VMEM) + (ANY,) * 3,
        scratch_shapes=[pltpu.VMEM((2, 2, rows, width), LOW)] * 2
        + [pltpu.VMEM((matrices, depth, piece, columns), LOW)] * 3
        + TensorScatter.scratch(rows, width)[:3]
        + [
            pltpu.VMEM((rows, width), FULL), pltpu.VMEM((rows, width), LOW),
            pltpu.VMEM(vectors.shape, FULL), pltpu.VMEM((2 * depth - 1,) + vectors.shape[1:], FULL),
            pltpu.VMEM(vectors.shape[1:], FULL), pltpu.VMEM((3,) + vectors.shape[1:], FULL),
            pltpu.VMEM((2, seen, tile), LOW), pltpu.VMEM((tile, seen), LOW),
            pltpu.VMEM((2, seen, units), LOW), pltpu.VMEM((units // 2, seen), LOW),
            pltpu.VMEM((2, 2, local, tile, hidden), FULL), pltpu.VMEM((2, 2, local, tile, hidden), LOW),
            pltpu.VMEM((2, local, hidden, tile), FULL), pltpu.VMEM((2, local, hidden, tile), LOW),
            pltpu.VMEM((2, local, width, hidden), LOW), pltpu.VMEM((width // tile, local, hidden, tile), LOW),
            pltpu.VMEM((depth, 2, piece, columns // 2), LOW), pltpu.VMEM((depth, 2, piece, columns // 2), LOW),
            pltpu.VMEM((piece, columns // 2), LOW), dma(depth), dma(depth), dma(depth),
            dma(matrices, depth), dma(2, matrices, depth), dma(2, matrices, depth),
            dma(3), dma(3), dma(4), dma(3), dma(4), dma(3),
            dma(2 * depth - 1), dma(2 * depth - 1), dma(3), dma(3),
            dma(2), dma(2), dma(3, 2), dma(3, width // tile), dma(3, width // tile), dma(1), dma(2),
        ],
        compiler_params=comm_params(number),
    )(*parts, normed_part, tokens, state_cot, gain, out, vectors, normed, grads, gated, gate_grad, up_grad)
    return results[:matrices], results[matrices:]


def finish_kernel(
    experts, heads,
    in_grad, in_out, in_query, in_key, in_value, in_gate, in_up, in_down, in_w_out, vector_ref,
    input_grad, output, query, key, value, gate, up, down, w_out, norm1, norm2, router, q_gain, k_gain,
):
    input_grad[...] = in_grad[...].astype(FULL)
    for source, target in (
        (in_out, output), (in_query, query), (in_key, key), (in_value, value), (in_gate, gate), (in_up, up), (in_down, down),
    ):
        target[...] = source[...]

    @pl.when(pl.program_id(0) == 0)
    def _():
        w_out[...] = in_w_out[...].T
        vectors = vector_ref[...]
        norm1[...], norm2[...] = vectors[16:17], vectors[17:18]
        router[...] = vectors[:experts]
        gains = vectors[18 : 18 + 2 * heads, :HD]
        width = q_gain.shape[1]
        group = lax.axis_index("expert")
        total_q, total_k = jnp.zeros(q_gain.shape, FULL), jnp.zeros(k_gain.shape, FULL)
        for index in range(HD // width):
            mine = (group == index).astype(FULL)
            total_q = total_q + gains[:heads, index * width : (index + 1) * width] * mine
            total_k = total_k + gains[heads:, index * width : (index + 1) * width] * mine
        q_gain[...], k_gain[...] = total_q, total_k


def finish(arrays, w_out, vectors, experts, heads, groups):
    steps = 4
    shapes = [jax.ShapeDtypeStruct(a.shape, FULL if i == 0 else a.dtype) for i, a in enumerate(arrays)]
    blocks = [pl.BlockSpec((a.shape[0] // steps, a.shape[1]), lambda i: (i, 0)) for a in arrays]
    whole = pl.BlockSpec(memory_space=pltpu.VMEM)
    piece = vectors.shape[1]
    small = [
        jax.ShapeDtypeStruct(shape, FULL)
        for shape in (w_out.shape[::-1], (1, piece), (1, piece), (experts, piece), (heads, HD // groups), (heads, HD // groups))
    ]
    return pl.pallas_call(
        functools.partial(finish_kernel, experts, heads),
        grid=(steps,),
        out_shape=(*shapes, *small),
        in_specs=blocks + [whole, whole],
        out_specs=(*blocks, *[whole] * len(small)),
        compiler_params=pltpu.CompilerParams(vmem_limit_bytes=VMEM_BYTES),
    )(*arrays, w_out, vectors)


def body(
    groups, parts,
    tokens, documents, routes, norm1_gain, q_gain, k_gain, w_query, w_key, w_value, w_out, norm2_gain, router_w,
    w_gate, w_up, w_down, out_grad,
):
    row_count, width = tokens.shape
    local_experts, _, hidden = w_gate.shape
    experts = local_experts * groups
    chain = LENGTH // row_count
    if not (parts == 4 and groups % 2 == 0 and experts <= min(16, 2 * TOP) and 2 * w_query.shape[1] <= 14 * HD and chain == 4 and groups == 8 and 4 * row_count == LENGTH and WINDOW == 2 * row_count):
        return body_routed(
            tokens, documents, routes, norm1_gain, q_gain, k_gain, w_query, w_key, w_value, w_out, norm2_gain, router_w,
            w_gate, w_up, w_down, out_grad,
        )
    depth = groups // 2
    rows = row_count // parts
    seen = groups * row_count // 2
    heads = w_query.shape[1] // HD
    group, part = lax.axis_index("expert"), lax.axis_index("tensor")
    core = part % 2

    def quarter(array):
        return lax.dynamic_slice_in_dim(array, part * rows, rows, 0)

    def across(vector):
        return vector.reshape(1, -1)

    positions = group * row_count + jnp.arange(row_count, dtype=jnp.int32)
    cosine, sine = (table[:, 0, :] for table in rope_tables(positions % LENGTH))
    sine = jnp.concatenate([-sine[:, : HD // 2], sine[:, HD // 2 :]], axis=1)
    picked = jnp.any(quarter(routes)[:, :, None] == jnp.arange(128, dtype=jnp.int32)[None, None, :], axis=1).astype(FULL)
    query_gain, key_gain = across(q_gain), across(k_gain)
    (
        normed_one, query_raw, key_raw, queries, kv_all, key_docs, scales, attended, logs, state, normed_two, router_probs, gates,
        own_tokens, own_grads, all_grad,
    ) = run_attention(
        tokens, (w_query, w_key, w_value, w_out), out_grad, (across(norm1_gain), query_gain, key_gain), (cosine, sine), across(documents),
        across(norm2_gain), router_w.T, picked, depth, chain, local_experts, 3,
    )

    normed_two_grad, gate_cots, all_normed, gated, gate_pre_grad, up_pre_grad, produced = run_experts(
        normed_two, gates, all_grad, w_gate, w_up, w_down, 5
    )
    units = 2 * local_experts * hidden
    all_normed, all_grad = all_normed.reshape(seen, width), all_grad.reshape(seen, width)
    gated, gate_pre_grad, up_pre_grad = (a.reshape(seen, units) for a in (gated, gate_pre_grad, up_pre_grad))

    state_cot, vectors, output_rows, normed_part, *pieces = run_attention_back(
        (normed_two_grad, gate_cots, router_probs, picked, state, across(norm2_gain), router_w.T, normed_two, own_grads),
        (queries, kv_all, attended, logs, key_docs, across(documents), query_raw, key_raw, query_gain, key_gain, cosine, sine, scales),
        (w_out,), produced, normed_one, (w_query, w_key, w_value), chain, local_experts, 10,
    )
    sums, (input_grad, output, vector_sum, *expert_grads) = run_gradients(
        pieces, normed_part, own_tokens, state_cot, norm1_gain[None], output_rows, vectors, all_normed, all_grad, gated, gate_pre_grad, up_pre_grad,
        local_experts, 14,
    )
    (
        input_grad, output, w_query_grad, w_key_grad, w_value_grad, gate_grad, up_grad, down_grad, w_out_grad,
        norm1_grad, norm2_grad, router_grad, q_gain_grad, k_gain_grad,
    ) = finish(
        (
            input_grad.reshape(row_count, width), output.reshape(row_count, width), sums[2], sums[3], sums[1],
            *(a.reshape(-1, a.shape[2]) for a in expert_grads),
        ),
        sums[0], vector_sum, experts, heads, groups,
    )
    return (
        output, input_grad, norm1_grad.reshape(-1), q_gain_grad, k_gain_grad, w_query_grad, w_key_grad, w_value_grad, w_out_grad,
        norm2_grad.reshape(-1), router_grad.T, gate_grad.reshape(w_gate.shape), up_grad.reshape(w_up.shape),
        down_grad.reshape(w_down.shape),
    )


def solution(mesh):
    placed = (
        P("expert", None),
        P("expert"),
        P("expert", None),
        P(),
        P("tensor", None),
        P("tensor", None),
        P(None, "tensor"),
        P(None, "tensor"),
        P(None, "tensor"),
        P("tensor", None),
        P(),
        P(),
        P("expert", None, "tensor"),
        P("expert", None, "tensor"),
        P("expert", "tensor", None),
        P("expert", None),
    )
    return jax.shard_map(
        functools.partial(body, mesh.shape["expert"], mesh.shape["tensor"]),
        mesh=mesh,
        in_specs=placed,
        out_specs=(
            P("expert", None),
            P("expert", None),
            P("expert"),
            P("tensor", "expert"),
            P("tensor", "expert"),
            P("expert", "tensor"),
            P("expert", "tensor"),
            P("expert", "tensor"),
            P("tensor", "expert"),
            P("expert"),
            P("expert", None),
            P("expert", None, "tensor"),
            P("expert", None, "tensor"),
            P("expert", "tensor", None),
        ),
        check_vma=False,
    )
```

```python
import functools

import numpy as np
import jax
import jax.numpy as jnp
from jax import lax
from jax.experimental import pallas as pl
from jax.experimental.pallas import tpu as pltpu
from jax.sharding import PartitionSpec as P

HD = 128
TOP = 8
WINDOW = 1024
LENGTH = 2048


NORM_EPSILON = 1e-05
HIGHEST_PRECISION = lax.Precision.HIGHEST


def for_sending(value):
    return jax.tree.map(lambda a: a.astype(jnp.bfloat16) if a.dtype == jnp.float32 else a, value)


def shifted(value, axis, steps):
    count = lax.axis_size(axis)
    initial, last = (max(0, -steps), min(count, count - steps))
    return lax.ppermute(value, axis, [(source, source + steps) for source in range(initial, last)])


def rope_tables(positions):
    half_width = HD // 2
    frequency = 10000.0 ** (-jnp.arange(half_width, dtype=jnp.float32) * 2.0 / HD)
    angles = positions.astype(jnp.float32)[:, None] * frequency[None, :]
    angles = jnp.concatenate([angles, angles], axis=-1)
    return (jnp.cos(angles)[:, None, :], jnp.sin(angles)[:, None, :])


def rotate(values, cosine, sine):
    half_width = values.shape[-1] // 2
    turned = jnp.concatenate([-values[..., half_width:], values[..., :half_width]], axis=-1)
    return values * cosine + turned * sine


def rotate_back(grads, cosine, sine):
    half_width = grads.shape[-1] // 2
    scaled = grads * sine
    turned = jnp.concatenate([scaled[..., half_width:], -scaled[..., :half_width]], axis=-1)
    return grads * cosine + turned


def previous_block(pieces):
    return jax.tree.map(
        lambda part, own: part.astype(own.dtype), shifted(for_sending(pieces), "expert", 1), pieces
    )


def following_block(pieces):
    return shifted((for_sending(pieces[0]), for_sending(pieces[1])), "expert", -1)


def body_routed(
    tokens,
    documents,
    routes,
    norm1_gain,
    q_gain,
    k_gain,
    w_query,
    w_key,
    w_value,
    w_out,
    norm2_gain,
    router_w,
    w_gate,
    w_up,
    w_down,
    out_grad,
):
    row_count, model_width = tokens.shape
    groups = lax.axis_size("expert")
    local_experts = w_gate.shape[0]
    experts = local_experts * groups
    capacity = 2 * row_count * TOP // experts
    slots_group = local_experts * capacity
    heads = w_query.shape[1] // HD
    score_scale = HD ** (-0.5)
    first_row = lax.axis_index("expert") * row_count
    positions = first_row + jnp.arange(row_count, dtype=jnp.int32)
    cosine, sine = rope_tables(positions % LENGTH)
    inputs = tokens.astype(jnp.float32)
    scale_one = lax.rsqrt(jnp.mean(inputs * inputs, axis=-1, keepdims=True) + NORM_EPSILON)
    normed_one = (inputs * scale_one * norm1_gain).astype(jnp.bfloat16)
    query_raw = jnp.dot(normed_one, w_query, preferred_element_type=jnp.float32)
    key_raw = jnp.dot(normed_one, w_key, preferred_element_type=jnp.float32)
    values = jnp.dot(normed_one, w_value, preferred_element_type=jnp.float32).astype(jnp.bfloat16)
    query_square, key_square = lax.psum(
        (jnp.sum(query_raw * query_raw, axis=-1), jnp.sum(key_raw * key_raw, axis=-1)), "tensor"
    )
    query_scale = lax.rsqrt(query_square / model_width + NORM_EPSILON)[:, None]
    key_scale = lax.rsqrt(key_square / model_width + NORM_EPSILON)[:, None]
    query_gain = q_gain.reshape(-1)
    key_gain = k_gain.reshape(-1)
    queries = rotate(
        (query_raw * query_scale * query_gain).reshape(row_count, heads, HD), cosine, sine
    ).astype(jnp.bfloat16)
    key_heads = rotate(
        (key_raw * key_scale * key_gain).reshape(row_count, heads, HD), cosine, sine
    ).astype(jnp.bfloat16)
    value_heads = values.reshape(row_count, heads, HD)
    labels = jnp.stack([documents // 256, documents % 256]).astype(jnp.bfloat16)
    previous_one = previous_block((key_heads, value_heads, labels))
    previous_two = previous_block(previous_one)
    all_keys = jnp.concatenate([previous_two[0], previous_one[0], key_heads], axis=0)
    all_values = jnp.concatenate([previous_two[1], previous_one[1], value_heads], axis=0)
    all_labels = jnp.concatenate([previous_two[2], previous_one[2], labels], axis=1)
    key_pos = first_row - 2 * row_count + jnp.arange(3 * row_count, dtype=jnp.int32)
    same_doc = (all_labels[0][None, :] == labels[0][:, None]) & (
        all_labels[1][None, :] == labels[1][:, None]
    )
    allowed = (
        same_doc
        & (key_pos[None, :] <= positions[:, None])
        & (positions[:, None] - key_pos[None, :] < WINDOW)
        & (key_pos[None, :] >= 0)
    )

    def masked_scores():
        raw_scores = (
            jnp.einsum("qhd,khd->hqk", queries, all_keys, preferred_element_type=jnp.float32)
            * score_scale
        )
        return jnp.where(allowed[None], raw_scores, -1e30)

    scores = masked_scores()
    highest = jnp.max(scores, axis=-1, keepdims=True)
    weights = jnp.where(allowed[None], jnp.exp(scores - highest), 0.0)
    denominator = jnp.sum(weights, axis=-1, keepdims=True)
    log_total = highest + jnp.log(denominator)
    attn_probs = weights / denominator
    attended = jnp.einsum(
        "hqk,khd->qhd",
        attn_probs.astype(jnp.bfloat16),
        all_values,
        preferred_element_type=jnp.float32,
    )
    attended = attended.reshape(row_count, -1).astype(jnp.bfloat16)
    attention = lax.psum(jnp.dot(attended, w_out, preferred_element_type=jnp.float32), "tensor")
    state = inputs + attention
    scale_two = lax.rsqrt(jnp.mean(state * state, axis=-1, keepdims=True) + NORM_EPSILON)
    normed_two = (state * scale_two * norm2_gain).astype(jnp.bfloat16)
    router_probs = jax.nn.softmax(
        jnp.dot(normed_two, router_w, preferred_element_type=jnp.float32), axis=-1
    )
    chosen = (routes[:, :, None] == jnp.arange(experts, dtype=jnp.int32)[None, None, :]).astype(
        jnp.float32
    )
    gates = jnp.sum(chosen * router_probs[:, None, :], axis=-1)
    flat_routes = routes.reshape(-1)
    onehot = (flat_routes[:, None] == jnp.arange(experts, dtype=jnp.int32)[None, :]).astype(
        jnp.int32
    )
    slot_index = jnp.sum(jnp.cumsum(onehot, axis=0) * onehot, axis=1) - 1
    target = flat_routes * capacity + slot_index
    source = (
        jnp.full((experts * capacity,), -1, jnp.int32)
        .at[target]
        .set(jnp.arange(row_count * TOP, dtype=jnp.int32))
    )
    live_slot = source >= 0
    pick_index = jnp.maximum(source, 0)
    send_rows = jnp.where(
        live_slot[:, None], normed_two[pick_index // TOP], jnp.zeros((), jnp.bfloat16)
    ).reshape(groups, slots_group, model_width)
    grad_float = out_grad.astype(jnp.float32)
    pick_grads = (
        (gates[:, :, None] * grad_float[:, None, :])
        .astype(jnp.bfloat16)
        .reshape(row_count * TOP, model_width)
    )
    send_grads = jnp.where(
        live_slot[:, None], pick_grads[pick_index], jnp.zeros((), jnp.bfloat16)
    ).reshape(groups, slots_group, model_width)
    arrived = lax.all_to_all(send_rows, "expert", split_axis=0, concat_axis=0, tiled=True)
    stacked = arrived.reshape(groups, local_experts, capacity, model_width)
    gate_pre = jnp.einsum("secd,edf->secf", stacked, w_gate, preferred_element_type=jnp.float32)
    up_pre = jnp.einsum("secd,edf->secf", stacked, w_up, preferred_element_type=jnp.float32)
    activated = jax.nn.silu(gate_pre)
    inner_act = (activated * up_pre).astype(jnp.bfloat16)
    produced = jnp.einsum(
        "secf,efd->secd", inner_act, w_down, preferred_element_type=jnp.float32
    ).astype(jnp.bfloat16)
    returned = lax.all_to_all(
        produced.reshape(groups, slots_group, model_width),
        "expert",
        split_axis=0,
        concat_axis=0,
        tiled=True,
    )
    back_rows = (
        returned.reshape(experts * capacity, model_width)[target]
        .reshape(row_count, TOP, model_width)
        .astype(jnp.float32)
    )
    expert_part = jnp.sum(gates[:, :, None] * back_rows, axis=1)
    expert_mix = lax.psum(expert_part.astype(jnp.bfloat16), "tensor").astype(jnp.float32)
    output = (state + expert_mix).astype(jnp.bfloat16)
    gate_part = jnp.sum(grad_float[:, None, :] * back_rows, axis=-1)
    arrived_grad = lax.all_to_all(send_grads, "expert", split_axis=0, concat_axis=0, tiled=True)
    slot_grad = arrived_grad.reshape(groups, local_experts, capacity, model_width)
    w_down_grad = jnp.einsum(
        "secf,secd->efd", inner_act, slot_grad, preferred_element_type=jnp.float32
    )
    inner_grad = jnp.einsum("secd,efd->secf", slot_grad, w_down, preferred_element_type=jnp.float32)
    logistic = jax.nn.sigmoid(gate_pre)
    gate_pre_grad = (inner_grad * up_pre * logistic * (1.0 + gate_pre * (1.0 - logistic))).astype(
        jnp.bfloat16
    )
    up_pre_grad = (inner_grad * activated).astype(jnp.bfloat16)
    w_gate_grad = jnp.einsum(
        "secd,secf->edf", stacked, gate_pre_grad, preferred_element_type=jnp.float32
    )
    w_up_grad = jnp.einsum(
        "secd,secf->edf", stacked, up_pre_grad, preferred_element_type=jnp.float32
    )
    row_grad = jnp.einsum(
        "secf,edf->secd", gate_pre_grad, w_gate, preferred_element_type=jnp.float32
    )
    row_grad = (
        row_grad
        + jnp.einsum("secf,edf->secd", up_pre_grad, w_up, preferred_element_type=jnp.float32)
    ).astype(jnp.bfloat16)
    grad_back = lax.all_to_all(
        row_grad.reshape(groups, slots_group, model_width),
        "expert",
        split_axis=0,
        concat_axis=0,
        tiled=True,
    )
    grad_picks = (
        grad_back.reshape(experts * capacity, model_width)[target]
        .reshape(row_count, TOP, model_width)
        .astype(jnp.float32)
    )
    normed_part = jnp.sum(grad_picks, axis=1)
    normed_two_grad, gate_cot = lax.psum((normed_part, gate_part), "tensor")
    prob_cot = jnp.sum(gate_cot[:, :, None] * chosen, axis=1)
    logit_cot = router_probs * (prob_cot - jnp.sum(router_probs * prob_cot, axis=-1, keepdims=True))
    router_float = router_w.astype(jnp.float32)
    normed_two_grad = normed_two_grad + jnp.einsum(
        "te,de->td", logit_cot, router_float, precision=HIGHEST_PRECISION
    )
    router_grad = jnp.einsum(
        "td,te->de", normed_two.astype(jnp.float32), logit_cot, precision=HIGHEST_PRECISION
    )
    norm2_grad = jnp.sum(normed_two_grad * state * scale_two, axis=0)
    inner_two = jnp.sum(normed_two_grad * norm2_gain * state, axis=-1, keepdims=True)
    state_cot = (
        grad_float
        + scale_two * norm2_gain * normed_two_grad
        - state * scale_two**3 * inner_two / model_width
    )
    state_low = state_cot.astype(jnp.bfloat16)
    w_out_grad = jnp.einsum("tf,td->fd", attended, state_low, preferred_element_type=jnp.float32)
    attended_cot = (
        jnp.einsum("td,fd->tf", state_low, w_out, preferred_element_type=jnp.float32)
        .astype(jnp.bfloat16)
        .reshape(row_count, heads, HD)
    )
    scores = masked_scores()
    attn_probs = jnp.where(allowed[None], jnp.exp(scores - log_total), 0.0)
    value_cot_all = jnp.einsum(
        "hqk,qhd->khd",
        attn_probs.astype(jnp.bfloat16),
        attended_cot,
        preferred_element_type=jnp.float32,
    )
    prob_grad = jnp.einsum(
        "qhd,khd->hqk", attended_cot, all_values, preferred_element_type=jnp.float32
    )
    delta = jnp.sum(attn_probs * prob_grad, axis=-1, keepdims=True)
    score_cot = (attn_probs * (prob_grad - delta)).astype(jnp.bfloat16)
    query_cot = (
        jnp.einsum("hqk,khd->qhd", score_cot, all_keys, preferred_element_type=jnp.float32)
        * score_scale
    )
    key_cot_all = (
        jnp.einsum("hqk,qhd->khd", score_cot, queries, preferred_element_type=jnp.float32)
        * score_scale
    )
    carried = following_block((key_cot_all[:row_count], value_cot_all[:row_count]))
    carried = following_block(
        (
            key_cot_all[row_count : 2 * row_count] + carried[0],
            value_cot_all[row_count : 2 * row_count] + carried[1],
        )
    )
    key_cot = key_cot_all[2 * row_count :] + carried[0]
    value_cot = value_cot_all[2 * row_count :] + carried[1]
    query_norm_cot = rotate_back(query_cot, cosine, sine).reshape(row_count, -1)
    key_norm_cot = rotate_back(key_cot, cosine, sine).reshape(row_count, -1)
    q_gain_local = jnp.sum(query_norm_cot * query_raw * query_scale, axis=0).reshape(heads, HD)
    k_gain_local = jnp.sum(key_norm_cot * key_raw * key_scale, axis=0).reshape(heads, HD)
    query_inner, key_inner = lax.psum(
        (
            jnp.sum(query_norm_cot * query_gain * query_raw, axis=-1),
            jnp.sum(key_norm_cot * key_gain * key_raw, axis=-1),
        ),
        "tensor",
    )
    query_raw_cot = (
        query_scale * query_gain * query_norm_cot
        - query_raw * query_scale**3 * query_inner[:, None] / model_width
    ).astype(jnp.bfloat16)
    key_raw_cot = (
        key_scale * key_gain * key_norm_cot
        - key_raw * key_scale**3 * key_inner[:, None] / model_width
    ).astype(jnp.bfloat16)
    value_low = value_cot.reshape(row_count, -1).astype(jnp.bfloat16)
    w_query_local = jnp.einsum(
        "td,tf->df", normed_one, query_raw_cot, preferred_element_type=jnp.float32
    )
    w_key_local = jnp.einsum(
        "td,tf->df", normed_one, key_raw_cot, preferred_element_type=jnp.float32
    )
    w_value_local = jnp.einsum(
        "td,tf->df", normed_one, value_low, preferred_element_type=jnp.float32
    )
    normed_part_one = jnp.einsum(
        "tf,df->td", query_raw_cot, w_query, preferred_element_type=jnp.float32
    )
    normed_part_one = normed_part_one + jnp.einsum(
        "tf,df->td", key_raw_cot, w_key, preferred_element_type=jnp.float32
    )
    normed_part_one = normed_part_one + jnp.einsum(
        "tf,df->td", value_low, w_value, preferred_element_type=jnp.float32
    )
    normed_one_grad = lax.psum(normed_part_one.astype(jnp.bfloat16), "tensor").astype(jnp.float32)
    norm1_grad = jnp.sum(normed_one_grad * inputs * scale_one, axis=0)
    inner_one = jnp.sum(normed_one_grad * norm1_gain * inputs, axis=-1, keepdims=True)
    input_grad = (
        state_cot
        + scale_one * norm1_gain * normed_one_grad
        - inputs * scale_one**3 * inner_one / model_width
    )
    summed = (
        lax.psum_scatter(
            w_query_local.astype(jnp.bfloat16), "expert", scatter_dimension=0, tiled=True
        ).astype(jnp.float32),
        lax.psum_scatter(
            w_key_local.astype(jnp.bfloat16), "expert", scatter_dimension=0, tiled=True
        ).astype(jnp.float32),
        lax.psum_scatter(
            w_value_local.astype(jnp.bfloat16), "expert", scatter_dimension=0, tiled=True
        ).astype(jnp.float32),
        lax.psum_scatter(
            w_out_grad.astype(jnp.bfloat16), "expert", scatter_dimension=1, tiled=True
        ).astype(jnp.float32),
        lax.psum_scatter(
            router_grad.astype(jnp.bfloat16), "expert", scatter_dimension=0, tiled=True
        ).astype(jnp.float32),
        lax.psum_scatter(
            norm1_grad.astype(jnp.bfloat16), "expert", scatter_dimension=0, tiled=True
        ).astype(jnp.float32),
        lax.psum_scatter(
            norm2_grad.astype(jnp.bfloat16), "expert", scatter_dimension=0, tiled=True
        ).astype(jnp.float32),
        lax.psum_scatter(
            q_gain_local.astype(jnp.bfloat16), "expert", scatter_dimension=1, tiled=True
        ).astype(jnp.float32),
        lax.psum_scatter(
            k_gain_local.astype(jnp.bfloat16), "expert", scatter_dimension=1, tiled=True
        ).astype(jnp.float32),
    )
    return (
        output,
        input_grad,
        summed[5],
        summed[7],
        summed[8],
        summed[0],
        summed[1],
        summed[2],
        summed[3],
        summed[6],
        summed[4],
        w_gate_grad,
        w_up_grad,
        w_down_grad,
    )


MESH = pl.DeviceIdType.MESH


def whole_tables():
    angles = np.arange(LENGTH)[:, None] * 10000.0 ** (-np.arange(HD // 2) * 2.0 / HD)[None, :]
    cosine, sine = np.cos(angles), np.sin(angles)
    cosine, sine = np.concatenate([cosine, cosine], axis=1), np.concatenate([-sine, sine], axis=1)
    return cosine.astype(np.float32), sine.astype(np.float32)


ANY = pl.BlockSpec(memory_space=pl.ANY)
VMEM = pl.BlockSpec(memory_space=pltpu.VMEM)
VMEM_BYTES = 62 * 1024 * 1024
LOW = jnp.bfloat16
FULL = jnp.float32


def place():
    group, part = lax.axis_index("expert"), lax.axis_index("tensor")
    return group // 2, group % 2, part // 2, part % 2


def device(z, x, y, core):
    return (2 * z + x, 2 * y + core)


def swapped(index, step):
    result, bit = index, 1
    while bit <= step:
        if step & bit:
            result = result + bit - 2 * bit * ((index // bit) % 2)
        bit *= 2
    return result


def greet(partners):
    barrier = pltpu.get_barrier_semaphore()
    for partner in partners:
        pl.semaphore_signal(barrier, inc=1, device_id=partner, device_id_type=MESH)
    pl.semaphore_wait(barrier, len(partners))


def remote(source, target, send, arrive, to):
    return pltpu.make_async_remote_copy(
        src_ref=source, dst_ref=target, send_sem=send, recv_sem=arrive, device_id=to, device_id_type=MESH
    )


def dma(*shape):
    return pltpu.SemaphoreType.DMA(shape)


def comm_params(number):
    return pltpu.CompilerParams(collective_id=number, has_side_effects=True, vmem_limit_bytes=VMEM_BYTES)


def add_rows(target, sources, rows, step=16):
    @pl.loop(0, rows // step)
    def _(index):
        part = pl.ds(index * step, step)
        total = sources[0][part].astype(FULL)
        for source in sources[1:]:
            total = total + source[part].astype(FULL)
        target[part] = total.astype(target.dtype)


class Copies:
    def __init__(self):
        self.open = []

    def start(self, copy):
        copy.start()
        self.open.append((copy, set()))
        return copy

    def once(self, copy, what):
        done = next(done for entry, done in self.open if entry is copy)
        new = what not in done
        done.add(what)
        return new

    def arrived(self, copy):
        if self.once(copy, "arrived"):
            copy.wait_recv()

    def sent(self, copy):
        if self.once(copy, "sent"):
            copy.wait_send()

    def finish(self):
        for copy, done in self.open:
            if "sent" not in done:
                copy.wait_send()
            if "arrived" not in done:
                copy.wait_recv()


class Gather:
    def __init__(self, copies, block, target, rows, cut, z_send, z_recv, p_send, p_recv, c_send, c_recv):
        self.copies, self.block, self.target, self.rows = copies, block, target, rows
        self.z_send, self.z_recv, self.p_send, self.p_recv = z_send, z_recv, p_send, p_recv
        self.c_send, self.c_recv = c_send, c_recv
        z, x, y, core = place()
        self.over_x, self.over_y = device(z, 1 - x, y, core), device(z, x, 1 - y, core)
        self.here, self.x_place, self.y_place = 2 * x + y, 2 * (1 - x) + y, 2 * x + 1 - y
        self.far = 2 * (1 - x) + 1 - y
        self.column = [device(swapped(z, step), x, y, core) for step in range(target.shape[0])]
        self.along, self.planes, self.diagonals, self.shared = {}, {}, {}, {}
        edge = rows * 3 // 8
        self.middle = (edge, rows - 2 * edge)
        self.halves = {0: ((0, cut), (cut, rows - cut)), 1: ((0, edge), (rows - edge, edge))}

    def at(self, step, spot, span):
        first, count = span
        return self.target.at[step, pl.ds(pl.multiple_of(spot * self.rows + first, 16), count)]

    def lift(self, step):
        low, whole = step & -step, (0, self.rows)
        source = self.block if step == low else self.at(step - low, self.here, whole)
        self.along[step] = self.copies.start(
            remote(source, self.at(step, self.here, whole), self.z_send.at[step], self.z_recv.at[step], self.column[low])
        )

    def spread(self, step):
        if step:
            self.copies.arrived(self.along[step])
            bit = 1
            while bit < step & -step:
                self.lift(step | bit)
                bit *= 2
        planes = []
        for number, (to, part) in enumerate([(self.over_x, 0), (self.over_y, 1), (self.over_x, 1), (self.over_y, 0)]):
            span = self.halves[step % 2][part]
            here = self.at(step, self.here, span)
            source = here if step else self.block.at[pl.ds(*span)]
            planes.append(self.copies.start(remote(source, here, self.p_send.at[step, number], self.p_recv.at[step, number], to)))
        self.planes[step] = planes

    def turn(self, step):
        passed = []
        for part, spot, to in ((0, self.x_place, self.over_y), (1, self.y_place, self.over_x)):
            self.copies.arrived(self.planes[step][part])
            here = self.at(step, spot, self.halves[step % 2][part])
            passed.append(
                self.copies.start(remote(here, here, self.p_send.at[step, 4 + part], self.p_recv.at[step, 4 + part], to))
            )
        self.diagonals[step] = passed

    def share(self, step):
        self.complete(step)
        copies = []
        for number, spot in enumerate((self.x_place, self.y_place, self.far)):
            copies.append(
                self.copies.start(
                    remote(
                        self.at(step, spot, self.middle), self.at(step + 1, spot, self.middle),
                        self.c_send.at[step // 2, number], self.c_recv.at[step // 2, number], self.column[1],
                    )
                )
            )
        self.shared[step + 1] = copies

    def complete(self, step):
        for copy in self.planes[step] + self.diagonals[step] + self.shared.get(step, []):
            self.copies.arrived(copy)

    @staticmethod
    def scratch(depth):
        return [dma(depth), dma(depth), dma(depth, 6), dma(depth, 6), dma(depth // 2, 3), dma(depth // 2, 3)]


class Scatter:
    def __init__(self, copies, work, diagonal, from_x, from_y, from_z, rows, send, recv, middle=None):
        self.copies, self.work, self.rows, self.send, self.recv = copies, work, rows, send, recv
        self.diagonal, self.from_x, self.from_y, self.from_z = diagonal, from_x, from_y, from_z
        z, x, y, core = place()
        self.over_x, self.over_y = device(z, 1 - x, y, core), device(z, x, 1 - y, core)
        self.here, self.x_place, self.y_place = 2 * x + y, 2 * (1 - x) + y, 2 * x + 1 - y
        self.far = 2 * (1 - x) + 1 - y
        self.column = [device(swapped(z, step), x, y, core) for step in range(work.shape[0])]
        self.corners, self.sides, self.along, self.shared, self.middle = {}, {}, {}, {}, middle
        edge, half = rows * 3 // 8, rows // 2
        self.center = (edge, rows - 2 * edge)
        self.halves = {0: ((0, half), (half, half)), 1: ((0, half), (half, half))}
        self.pieces = {0: ((0, rows),), 1: ((0, rows),)}
        if middle:
            self.halves[1] = self.pieces[1] = ((0, edge), (rows - edge, edge))

    def at(self, step, spot, span):
        first, count = span
        return self.work.at[step, pl.ds(pl.multiple_of(spot * self.rows + first, 16), count)]

    def copy(self, step, number, source, target, to):
        return self.copies.start(remote(source, target, self.send.at[step, number], self.recv.at[step, number], to))

    def share(self, step):
        landed, send, recv = self.middle
        self.shared[step - 1] = [
            self.copies.start(
                remote(
                    self.at(step, spot, self.center), landed.at[step // 2, spot],
                    send.at[step // 2, spot], recv.at[step // 2, spot], self.column[1],
                )
            )
            for spot in range(4)
        ]

    def corner(self, step):
        for spot, copy in enumerate(self.shared.get(step, [])):
            self.copies.arrived(copy)
            mine = self.at(step, spot, self.center)
            add_rows(mine, [mine, self.middle[0].at[step // 2, spot]], self.center[1])
        first, second = self.halves[step % 2]
        self.corners[step] = (
            self.copy(step, 0, self.at(step, self.far, first), self.diagonal.at[step, pl.ds(*first)], self.over_y),
            self.copy(step, 1, self.at(step, self.far, second), self.diagonal.at[step, pl.ds(*second)], self.over_x),
        )

    def side(self, step):
        first, second = self.halves[step % 2]
        via_y, via_x = self.corners[step]

        def to_x(number, span):
            return self.copy(step, number, self.at(step, self.x_place, span), self.from_x.at[step, pl.ds(*span)], self.over_x)

        def to_y(number, span):
            return self.copy(step, number, self.at(step, self.y_place, span), self.from_y.at[step, pl.ds(*span)], self.over_y)

        sides = [to_x(2, second), to_y(3, first)]
        self.copies.arrived(via_y)
        mine = self.at(step, self.x_place, first)
        add_rows(mine, [mine, self.diagonal.at[step, pl.ds(*first)]], first[1])
        sides.append(to_x(4, first))
        self.copies.arrived(via_x)
        mine = self.at(step, self.y_place, second)
        add_rows(mine, [mine, self.diagonal.at[step, pl.ds(*second)]], second[1])
        sides.append(to_y(5, second))
        self.sides[step] = sides

    def below(self, step, odd_rows):
        terms, bit = [], 1
        while bit < (step & -step if step else len(self.column)):
            if odd_rows or (step | bit) % 2 == 0:
                for copy in self.along[step | bit]:
                    self.copies.arrived(copy)
                terms.append(self.from_z.at[step | bit])
            bit *= 2
        return terms

    def spans(self):
        return [(span, True) for span in self.pieces[1]] + ([(self.center, False)] if self.middle else [])

    def climb(self, step):
        for copy in self.sides[step]:
            self.copies.arrived(copy)
        if step:
            for span, odd_rows in self.spans():
                if odd_rows or step % 2 == 0:
                    mine, part = self.at(step, self.here, span), pl.ds(*span)
                    terms = [mine, self.from_x.at[step, part], self.from_y.at[step, part]]
                    terms += [term.at[part] for term in self.below(step, odd_rows)]
                    add_rows(mine, terms, span[1])
            self.along[step] = []
            for number, span in enumerate(self.pieces[step % 2]):
                mine, part = self.at(step, self.here, span), pl.ds(*span)
                self.along[step].append(
                    self.copy(step, 6 + number, mine, self.from_z.at[step, part], self.column[step & -step])
                )

    def result(self, target, more=()):
        for span, odd_rows in self.spans():
            part = pl.ds(*span)
            terms = [self.at(0, self.here, span), self.from_x.at[0, part], self.from_y.at[0, part]]
            terms += [term.at[part] for term in self.below(0, odd_rows)] + [term.at[part] for term in more]
            add_rows(target.at[part], terms, span[1])

    @staticmethod
    def scratch(depth, rows, width):
        return [pltpu.VMEM((depth, rows, width), LOW)] * 4 + [dma(depth, 8), dma(depth, 8)]


def experts_kernel(
    depth, rows, local, hidden,
    x_ref, gates_ref, grad_ref, gate_ref, up_ref, down_ref,
    sum_ref, cots_ref, normed_ref, gated_ref, gate_grad_ref, up_grad_ref, produced_ref,
    wg, wu, wd, x_all, grads, work, y_out, gated, gate_grad, up_grad, gates, gate_wide, cots, cot_rows,
    diagonal, from_x, from_y, from_z, r_send, r_recv,
    z_send, z_recv, p_send, p_recv, c_send, c_recv, s_send, s_recv, w_send, w_recv, w_load, g_load, saves, local_sem,
):
    z, x, y, core = place()
    here, sibling = 2 * x + y, device(z, x, y, 1 - core)
    others = [
        (step, turn, (swapped(z, step), swapped(x, turn // 2), swapped(y, turn % 2)))
        for step in range(depth)
        for turn in range(4)
        if step or turn
    ]
    greet([device(*other, core) for _, _, other in others] + [sibling])
    copies = Copies()
    smalls = []
    for step, turn, other in others:
        oz, ox, oy = other
        smalls.append(
            copies.start(
                remote(
                    gates_ref.at[2 * oz + ox], gates.at[step, here], s_send.at[0, step, turn], s_recv.at[0, step, turn],
                    device(oz, ox, oy, core),
                )
            )
        )
    gather = Gather(copies, x_ref, x_all, rows, rows // 2, z_send, z_recv, p_send, p_recv, c_send, c_recv)
    gather.spread(0)
    gather.lift(1)
    gather.lift(2)
    plain = []

    def fetch(source, target, sem):
        copy = pltpu.make_async_copy(source, target, sem)
        copy.start()
        return copy

    plain.append(fetch(x_ref, gather.at(0, here, (0, rows)), local_sem.at[0]))
    weights = []
    for index in range(local):
        first = pl.multiple_of((core * local + index) * hidden, hidden)
        columns = pl.ds(first, hidden)
        for number, (source, target) in enumerate(
            [(gate_ref, wg.at[:, columns]), (up_ref, wu.at[:, columns]), (down_ref, wd.at[columns])]
        ):
            weights.append(copies.start(remote(source.at[index], target, w_send.at[number, index], w_recv.at[number, index], sibling)))
            plain.append(fetch(source.at[index], target, w_load.at[number, index]))
    plain.append(fetch(gates_ref.at[2 * z + x], gates.at[0, here], local_sem.at[1]))
    sequence = (0, 2, 3, 1)
    grad_copies = [fetch(grad_ref.at[0], grads.at[0], g_load.at[0])]
    scatter = Scatter(copies, work, diagonal, from_x, from_y, from_z, rows, r_send, r_recv)
    saving, producing, keeping = [], [], []
    wave_rows = 4 * rows
    lanes = lax.broadcasted_iota(jnp.int32, (wave_rows, 128), 1)

    def first_half(step):
        for copy in saving:
            copy.wait()
        saving.clear()
        for spot in range(4):
            padded = jnp.concatenate([gates[step, spot], jnp.zeros((120, 128), FULL)], axis=0)
            gate_wide[pl.ds(spot * rows, rows), :] = padded.T
        cots[...] = jnp.zeros_like(cots)
        turn = sequence.index(step)
        grad_copies[turn].wait()
        if turn + 1 < depth:
            slot = (turn + 1) % 2
            grad_copies.append(fetch(grad_ref.at[sequence[turn + 1]], grads.at[slot], g_load.at[slot]))
        grad = grads.at[turn % 2]

        @pl.loop(0, 2 * local)
        def _(unit):
            columns = pl.ds(pl.multiple_of(unit * hidden, hidden), hidden)
            expert = lax.rem(unit, local)
            gate_pre = dot(x_all[step], wg[:, columns])
            up_pre = dot(x_all[step], wu[:, columns])
            back = dot_t(grad[...], wd[columns, :])
            logistic = 1.0 / (1.0 + jnp.exp(-gate_pre))
            activated = gate_pre * logistic
            inner = activated * up_pre
            cot = jnp.sum(inner * back, axis=-1, keepdims=True)
            cots[...] += jnp.where(lanes == expert, cot, 0.0)
            gate = jnp.sum(jnp.where(lanes == expert, gate_wide[...], 0.0), axis=-1, keepdims=True)
            gated[:, columns] = (gate * inner).astype(LOW)
            inner_grad = gate * back
            gate_grad[:, columns] = (inner_grad * up_pre * logistic * (1.0 + gate_pre * (1.0 - logistic))).astype(LOW)
            up_grad[:, columns] = (inner_grad * activated).astype(LOW)

        for spot in range(4):
            cot_rows[step, spot] = cots[pl.ds(spot * rows, rows), :].T[:8]
        for other_step, turn, (oz, ox, oy) in others:
            if other_step == step:
                copies.start(
                    remote(
                        cot_rows.at[step, 2 * ox + oy], cots_ref.at[step, here], s_send.at[1, step, turn], s_recv.at[1, step, turn],
                        device(oz, ox, oy, core),
                    )
                )
        for number, (source, target) in enumerate([(gated, gated_ref), (gate_grad, gate_grad_ref), (up_grad, up_grad_ref)]):
            saving.append(fetch(source, target.at[step], saves.at[number]))
        keeping.append(fetch(x_all.at[step], normed_ref.at[step], saves.at[4 + step]))

    def second_half(step):
        for copy in producing:
            copy.wait()
        producing.clear()
        tile = 512

        @pl.loop(0, x_all.shape[2] // tile)
        def _(index):
            columns = pl.ds(pl.multiple_of(index * tile, tile), tile)
            y_out[:, columns] = dot(gated[...], wd[:, columns]).astype(LOW)
            work[step, :, columns] = (dot_t(gate_grad[...], wg[columns, :]) + dot_t(up_grad[...], wu[columns, :])).astype(LOW)

        producing.append(fetch(y_out, produced_ref.at[step], saves.at[3]))

    gather.turn(0)
    gather.spread(1)
    gather.share(0)
    for copy in plain:
        copy.wait()
    for copy in weights + smalls:
        copies.arrived(copy)
    first_half(0)
    gather.turn(1)
    gather.spread(2)
    second_half(0)
    gather.turn(2)
    gather.spread(3)
    gather.share(2)
    first_half(2)
    gather.turn(3)
    second_half(2)
    scatter.corner(2)
    gather.complete(3)
    first_half(3)
    scatter.side(2)
    second_half(3)
    scatter.corner(3)
    gather.complete(1)
    first_half(1)
    scatter.side(3)
    second_half(1)
    scatter.corner(1)
    scatter.corner(0)
    scatter.climb(3)
    scatter.side(1)
    scatter.climb(2)
    scatter.side(0)
    scatter.climb(1)
    scatter.climb(0)
    scatter.result(sum_ref)
    own_cots = fetch(cot_rows.at[0, here], cots_ref.at[0, here], local_sem.at[2])
    own_cots.wait()
    for copy in saving + producing + keeping:
        copy.wait()
    copies.finish()


def run_experts(block, gates, grads, w_gate, w_up, w_down, number):
    depth, wave, width = grads.shape
    rows = wave // 4
    local, _, hidden = w_gate.shape
    units = 2 * local * hidden
    kept = jax.ShapeDtypeStruct((depth, wave, units), LOW)
    wide = jax.ShapeDtypeStruct((depth, wave, width), LOW)
    return pl.pallas_call(
        functools.partial(experts_kernel, depth, rows, local, hidden),
        out_shape=(
            jax.ShapeDtypeStruct((rows, width), FULL),
            jax.ShapeDtypeStruct((depth, 4, 8, 128), FULL),
            wide, kept, kept, kept, wide,
        ),
        in_specs=[ANY] * 6,
        out_specs=(VMEM, VMEM, ANY, ANY, ANY, ANY, ANY),
        scratch_shapes=[
            pltpu.VMEM((width, units), LOW), pltpu.VMEM((width, units), LOW), pltpu.VMEM((units, width), LOW),
            pltpu.VMEM((depth, wave, width), LOW), pltpu.VMEM((2, wave, width), LOW),
            pltpu.VMEM((depth, wave, width), LOW), pltpu.VMEM((wave, width), LOW),
            pltpu.VMEM((wave, units), LOW), pltpu.VMEM((wave, units), LOW), pltpu.VMEM((wave, units), LOW),
            pltpu.VMEM((depth, 4, 8, 128), FULL), pltpu.VMEM((wave, 128), FULL), pltpu.VMEM((wave, 128), FULL),
            pltpu.VMEM((depth, 4, 8, 128), FULL),
        ]
        + Scatter.scratch(depth, rows, width)
        + [
            *Gather.scratch(depth), dma(2, depth, 4), dma(2, depth, 4),
            dma(3, local), dma(3, local), dma(3, local), dma(2), dma(4 + depth), dma(3),
        ],
        compiler_params=comm_params(number),
    )(block, gates, grads, w_gate, w_up, w_down)


class TensorScatter:
    def __init__(self, copies, work, from_pair, from_y, send, recv):
        self.copies, self.work, self.from_pair, self.from_y, self.send, self.recv = copies, work, from_pair, from_y, send, recv
        z, x, self.y, self.core = place()
        self.sibling, self.over_y = device(z, x, self.y, 1 - self.core), device(z, x, 1 - self.y, self.core)
        self.rows = work.shape[2]

    def begin(self):
        self.pairs = []
        for turn in (1, 0):
            source = self.work.at[swapped(self.y, turn), 1 - self.core]
            self.pairs.append(
                self.copies.start(remote(source, self.from_pair.at[turn], self.send.at[turn], self.recv.at[turn], self.sibling))
            )

    def cross(self):
        self.copies.arrived(self.pairs[0])
        block = self.work.at[1 - self.y, self.core]
        add_rows(block, [block, self.from_pair.at[1]], self.rows)
        self.across = self.copies.start(remote(block, self.from_y, self.send.at[2], self.recv.at[2], self.over_y))

    def result(self, target):
        self.copies.arrived(self.pairs[1])
        self.copies.arrived(self.across)
        add_rows(target, [self.work.at[self.y, self.core], self.from_pair.at[0], self.from_y], self.rows)

    @staticmethod
    def scratch(rows, width):
        return [
            pltpu.VMEM((2, 2, rows, width), LOW),
            pltpu.VMEM((2, rows, width), LOW),
            pltpu.VMEM((rows, width), LOW),
            dma(3),
            dma(3),
        ]


class TensorGather:
    def __init__(self, copies, block, target, send, recv):
        self.copies, self.target, self.send, self.recv = copies, target, send, recv
        z, x, self.y, self.core = place()
        self.sibling, over_y = device(z, x, self.y, 1 - self.core), device(z, x, 1 - self.y, self.core)
        mine = target.at[self.y, self.core]
        self.across = copies.start(remote(block, mine, send.at[0], recv.at[0], over_y))
        self.near = copies.start(remote(block, mine, send.at[1], recv.at[1], self.sibling))
        self.own = pltpu.make_async_copy(block, mine, send.at[3])
        self.own.start()

    def cross(self):
        self.copies.arrived(self.across)
        block = self.target.at[1 - self.y, self.core]
        self.passed = self.copies.start(remote(block, block, self.send.at[2], self.recv.at[2], self.sibling))

    def finish(self):
        self.own.wait()
        self.copies.arrived(self.near)
        self.copies.arrived(self.passed)


def partners_of(depth):
    z, x, y, core = place()
    return [device(swapped(z, step), x, y, core) for step in range(1, depth)] + [
        device(z, 1 - x, y, core),
        device(z, x, 1 - y, core),
        device(z, x, y, 1 - core),
        device(swapped(z, 1), 1 - x, y, core),
    ]


def mask_bias(bias, key_docs, query_docs, length):
    blocks = bias.shape[0] // length

    @pl.loop(0, bias.shape[0] // 128)
    def _(index):
        part = pl.ds(pl.multiple_of(index * 128, 128), 128)
        key = index * 128 + lax.broadcasted_iota(jnp.int32, (128, length), 0) - (blocks - 1) * length
        query = lax.broadcasted_iota(jnp.int32, (128, length), 1)
        seen = (key_docs[part, :] == query_docs[0:1, :]) & (key <= query) & (query - key < WINDOW)
        bias[part, :] = jnp.where(seen, 0.0, -1e30).astype(bias.dtype)


def exchange(copies, mine, landed, send, recv, mates):
    return [
        copies.start(remote(mine, landed.at[number], send.at[number], recv.at[number], device(*mate)))
        for number, mate in enumerate(mates)
    ]


def mates_of():
    z, x, y, core = place()
    return [(z, x, swapped(y, turn // 2), swapped(core, turn % 2)) for turn in range(1, 4)]


def as_rows(columns):
    lanes = lax.broadcasted_iota(jnp.int32, (columns[0].shape[0], 128), 1)
    wide = jnp.zeros(lanes.shape, FULL)
    for index, column in enumerate(columns):
        wide = jnp.where(lanes == index, column, wide)
    return wide.T[:8]


def as_columns(rows_of_eight):
    length = rows_of_eight.shape[1]
    return jnp.concatenate([rows_of_eight, jnp.zeros((120, length), FULL)], axis=0).T


def attention_kernel(
    depth, rows, heads, chain, local,
    tokens_ref, wq_ref, wk_ref, wv_ref, wo_ref, grads_ref,
    gain1_ref, q_gain_ref, k_gain_ref, cosines_ref, sines_ref, docs_row, gain2_ref, router_ref, picked_ref,
    normed_out, q_out, k_out, queries_out, kv_out, key_docs, scales, attended, logs, state_ref, normed2_ref, probs_ref, gates_ref, own_tokens, own_grads, cosine_ref, sine_ref,
    all_grad,
    normed_turned, q_raw, k_raw, queries, kv_all, tokens, normed_ref, wq, wk, wv, wo, docs_ref, logits_ref, docs_in, squares, squares_in, scores, totals, bias, partial, from_pair, from_y, sum_ref,
    t_send, t_recv, z_send, z_recv, p_send, p_recv, c_send, c_recv, h_send, h_recv, d_send, d_recv, q_send, q_recv, load, save,
):
    z, x, y, core = place()
    group, part = lax.axis_index("expert"), lax.axis_index("tensor")
    spot = group % chain
    length, width = tokens.shape
    wide = heads * HD
    scale = HD ** (-0.5)
    own_rows = pl.ds(pl.multiple_of(part * rows, rows), rows)
    grad_ref = grads_ref.at[own_rows]
    docs_ref[...] = jnp.broadcast_to(docs_row[...], docs_ref.shape)
    own_copy = pltpu.make_async_copy(grad_ref, own_grads, load.at[6])
    own_copy.start()
    positions = pl.ds(pl.multiple_of(lax.rem(lax.axis_index("expert"), chain) * tokens.shape[0], 8), tokens.shape[0])
    tables = []
    for number, (source, target) in enumerate([(cosines_ref, cosine_ref), (sines_ref, sine_ref)]):
        tables.append(pltpu.make_async_copy(source.at[positions], target, load.at[7 + number]))
        tables[-1].start()
    loads = []
    for number, (source, target) in enumerate([(tokens_ref, tokens), (wv_ref, wv), (wk_ref, wk), (wq_ref, wq), (wo_ref, wo)]):
        loads.append(pltpu.make_async_copy(source, target, load.at[number]))
        loads[-1].start()
    mates = mates_of()
    z1, x1 = swapped(z, 1), 1 - x
    greet(
        [device(swapped(z, step), x, y, core) for step in range(1, depth)]
        + [device(z, x1, y, core), device(z1, x1, y, core)]
        + [device(*mate) for mate in mates]
    )
    copies = Copies()
    for distance in (1, 2):

        @pl.when(spot < chain - distance)
        def _():
            remote(
                docs_ref, docs_in.at[2 - distance], d_send.at[distance], d_recv.at[distance], (group + distance, part)
            ).start()

    gather = Gather(copies, grad_ref, all_grad, rows, rows * 3 // 8, z_send, z_recv, p_send, p_recv, c_send, c_recv)
    gather.spread(0)
    gather.lift(1)
    own = pltpu.make_async_copy(grad_ref, gather.at(0, gather.here, (0, rows)), load.at[5])
    own.start()
    key_part, value_part = pl.ds(0, wide), pl.ds(wide, wide)

    high = lax.rem(z, 2)
    over_x, over_z = device(z, x1, y, core), device(z1, x, y, core)

    def docs_copy(distance, to):
        return remote(docs_ref, docs_in.at[2 - distance], d_send.at[distance], d_recv.at[distance], (to, part))

    def halo_copy(kind, source, slot, number, to):
        columns = (key_part, value_part)[kind]
        return remote(
            kv_all.at[source, :, columns], kv_all.at[slot, :, columns], h_send.at[kind, number], h_recv.at[kind, number], to
        )

    def x_copy(kind):
        return halo_copy(kind, 2, 1, 0, over_x)

    def z_copy(kind):
        return halo_copy(kind, 2, 0, 1, over_z)

    def relay_copy(kind):
        return halo_copy(kind, 0, 1, 2, over_x)

    def halo_start(kind):
        pl.when(x == 0)(lambda: x_copy(kind).start())
        pl.when(high == 0)(lambda: z_copy(kind).start())

    def halo_relay(kind):
        pl.when(high == 1)(lambda: z_copy(kind).wait_recv())
        pl.when(spot == 3)(lambda: relay_copy(kind).start())

    def halo_arrive(kind):
        columns = (key_part, value_part)[kind]
        pl.when(x == 1)(lambda: x_copy(kind).wait_recv())
        pl.when(spot == 2)(lambda: relay_copy(kind).wait_recv())

        def clear(slot):
            kv_all[slot, :, columns] = jnp.zeros((length, wide), LOW)

        pl.when(spot == 0)(lambda: clear(1))
        pl.when(high == 0)(lambda: clear(0))

    def halo_sent(kind):
        pl.when(x == 0)(lambda: x_copy(kind).wait_send())
        pl.when(high == 0)(lambda: z_copy(kind).wait_send())
        pl.when(spot == 3)(lambda: relay_copy(kind).wait_send())

    loads[0].wait()

    @pl.loop(0, length // 128)
    def _(index):
        part_rows = pl.ds(pl.multiple_of(index * 128, 128), 128)
        values = tokens[part_rows, :].astype(FULL)
        factor = lax.rsqrt(jnp.mean(values * values, axis=-1, keepdims=True) + NORM_EPSILON)
        normed_ref[part_rows, :] = (values * factor * gain1_ref[0:1, :]).astype(LOW)

    def project(weights, store):
        @pl.loop(0, wide // 256)
        def _(index):
            columns = pl.ds(pl.multiple_of(index * 256, 256), 256)
            store(index, columns, dot(normed_ref[...], weights[:, columns]))

    def keep_value(index, columns, result):
        kv_all[2, :, pl.ds(pl.multiple_of(wide + index * 256, 256), 256)] = result.astype(LOW)

    def keep_key(index, columns, result):
        k_raw[:, columns] = result

    def keep_query(index, columns, result):
        q_raw[:, columns] = result

    loads[2].wait()
    project(wk, keep_key)
    loads[3].wait()
    project(wq, keep_query)
    squares[...] = as_rows(
        [jnp.sum(q_raw[...] * q_raw[...], axis=-1, keepdims=True), jnp.sum(k_raw[...] * k_raw[...], axis=-1, keepdims=True)]
    )
    sent = exchange(copies, squares, squares_in, q_send, q_recv, mates)
    saving = []

    def leave(source, target):
        saving.append(pltpu.make_async_copy(source, target, save.at[len(saving)]))
        saving[-1].start()

    leave(q_raw, q_out)
    leave(k_raw, k_out)
    loads[1].wait()
    project(wv, keep_value)
    halo_start(1)
    gather.turn(0)

    @pl.loop(0, width // 256)
    def _(index):
        columns = pl.ds(pl.multiple_of(index * 256, 256), 256)
        normed_turned[columns, :] = normed_ref[:, columns].T

    leave(normed_turned, normed_out)

    for copy in sent:
        copies.arrived(copy)
    total = squares[...]
    for number in range(3):
        total = total + squares_in[number]
    scales[...] = lax.rsqrt(total * (1.0 / width) + NORM_EPSILON)
    factors = as_columns(scales[...])

    def turn_heads(raw, gain_ref, factor, store):
        for head in range(heads):
            columns = pl.ds(head * HD, HD)
            normed = raw[:, columns] * factor * gain_ref[0:1, columns]
            store(head, (normed * cosine_ref[...] + pltpu.roll(normed, HD // 2, 1) * sine_ref[...]).astype(LOW))

    def store_key(head, turned):
        kv_all[2, :, pl.ds(head * HD, HD)] = turned

    def store_query(head, turned):
        queries[:, pl.ds(head * HD, HD)] = turned

    for copy in tables:
        copy.wait()
    turn_heads(k_raw, k_gain_ref, factors[:, 1:2], store_key)
    halo_start(0)
    gather.spread(1)
    gather.lift(2)
    turn_heads(q_raw, q_gain_ref, factors[:, 0:1], store_query)
    leave(queries, queries_out)
    for distance in (1, 2):

        @pl.when(spot >= distance)
        def _():
            docs_copy(distance, group - distance).wait_recv()

        @pl.when(spot < distance)
        def _():
            docs_in[2 - distance] = jnp.full_like(docs_ref, -1)

    for block in range(3):
        rows_of = docs_in[block] if block < 2 else docs_ref[...]
        key_docs[pl.ds(block * length, length), :] = rows_of.astype(FULL).T[:, 0:1].astype(jnp.int32)
    mask_bias(bias, key_docs, docs_ref, length)

    def score(block):
        @pl.loop(0, heads)
        def _(head):
            columns = pl.ds(pl.multiple_of(head * HD, HD), HD)
            keys = pl.ds(block * length, length)
            scores[head, keys, :] = dot_t(kv_all[block, :, columns], queries[:, columns]) * scale + bias[keys, :]
    score(2)
    halo_relay(1)
    halo_relay(0)
    gather.share(0)
    gather.spread(2)
    halo_arrive(0)
    gather.turn(1)
    score(1)
    score(0)

    @pl.loop(0, heads)
    def _(head):
        mine = scores.at[head]
        highest = jnp.max(mine[...], axis=0, keepdims=True)
        total = jnp.zeros_like(highest)
        for block in range(3):
            weights = jnp.exp(mine[pl.ds(block * length, length), :] - highest)
            total = total + jnp.sum(weights, axis=0, keepdims=True)
            mine[pl.ds(block * length, length), :] = weights
        logs[head] = jnp.broadcast_to(highest + jnp.log(total), (8, length))
        totals[head] = jnp.broadcast_to(1.0 / total, (8, length))

    halo_arrive(1)

    @pl.loop(0, heads)
    def _(head):
        columns = pl.ds(pl.multiple_of(head * HD, HD), HD)
        values = pl.ds(pl.multiple_of((heads + head) * HD, HD), HD)
        mixed = jnp.zeros((HD, length), FULL)
        for block in range(3):
            probs = (scores[head, pl.ds(block * length, length), :] * totals[head, 0:1, :]).astype(LOW)
            mixed = mixed + t_dot(kv_all[block, :, values], probs)
        attended[:, columns] = mixed.T.astype(LOW)

    gather.turn(2)
    gather.spread(3)
    leave(kv_all, kv_out)
    loads[4].wait()
    for index in range(4):
        partial[index // 2, index % 2] = dot(attended[pl.ds(index * rows, rows), :], wo[...]).astype(LOW)
    scatter = TensorScatter(copies, partial, from_pair, from_y, t_send, t_recv)
    scatter.begin()
    scatter.cross()
    gather.share(2)
    gather.turn(3)
    scatter.result(sum_ref)
    own_tokens[...] = tokens[own_rows, :]
    state = own_tokens[...].astype(FULL) + sum_ref[...]
    state_ref[...] = state
    factor = lax.rsqrt(jnp.mean(state * state, axis=-1, keepdims=True) + NORM_EPSILON)
    normed2_ref[...] = (state * factor * gain2_ref[0:1, :]).astype(LOW)
    experts = gates_ref.shape[0] * local
    logits_ref[...] = jnp.full_like(logits_ref, -1e30)
    logits_ref[:, :experts] = dot_t(normed2_ref[...], router_ref[...])
    logits = logits_ref[...]
    weights = jnp.exp(logits - jnp.max(logits, axis=-1, keepdims=True))
    probs = weights / jnp.sum(weights, axis=-1, keepdims=True)
    probs_ref[...] = probs
    gates = (probs * picked_ref[...]).T
    gates_ref[...] = jnp.zeros_like(gates_ref)
    for index in range(gates_ref.shape[0]):
        gates_ref[index, 0:local, :] = gates[index * local : (index + 1) * local]
    own.wait()
    own_copy.wait()
    for copy in saving:
        copy.wait()
    for kind in range(2):
        halo_sent(kind)
    for distance in (1, 2):

        @pl.when(spot < chain - distance)
        def _():
            docs_copy(distance, group + distance).wait_send()

    copies.finish()


def run_attention(tokens, weights, grads, gains, tables, docs, gain2, router, picked, depth, chain, local, number):
    length, width = tokens.shape
    rows = length // 4
    wide = weights[0].shape[1]
    heads = wide // HD
    return pl.pallas_call(
        functools.partial(attention_kernel, depth, rows, heads, chain, local),
        out_shape=(
            jax.ShapeDtypeStruct((width, length), LOW),
            jax.ShapeDtypeStruct((length, wide), FULL),
            jax.ShapeDtypeStruct((length, wide), FULL),
            jax.ShapeDtypeStruct((length, wide), LOW),
            jax.ShapeDtypeStruct((3, length, 2 * wide), LOW),
            jax.ShapeDtypeStruct((3 * length, 1), jnp.int32),
            jax.ShapeDtypeStruct((8, length), FULL),
            jax.ShapeDtypeStruct((length, wide), LOW),
            jax.ShapeDtypeStruct((heads, 8, length), FULL),
            jax.ShapeDtypeStruct((rows, width), FULL),
            jax.ShapeDtypeStruct((rows, width), LOW),
            jax.ShapeDtypeStruct((rows, 128), FULL),
            jax.ShapeDtypeStruct((2 * depth, 8, rows), FULL),
            jax.ShapeDtypeStruct((rows, width), LOW),
            jax.ShapeDtypeStruct((rows, width), LOW),
            jax.ShapeDtypeStruct((length, HD), FULL),
            jax.ShapeDtypeStruct((length, HD), FULL),
            jax.ShapeDtypeStruct((depth, 4 * rows, width), LOW),
        ),
        in_specs=[ANY] * 6 + [VMEM] * 3 + [ANY] * 2 + [VMEM] * 4,
        out_specs=(ANY,) * 5 + (VMEM,) * 12 + (ANY,),
        scratch_shapes=[
            pltpu.VMEM((width, length), LOW), pltpu.VMEM((length, wide), FULL), pltpu.VMEM((length, wide), FULL),
            pltpu.VMEM((length, wide), LOW), pltpu.VMEM((3, length, 2 * wide), LOW),
            pltpu.VMEM(tokens.shape, LOW), pltpu.VMEM(tokens.shape, LOW), pltpu.VMEM((width, wide), LOW), pltpu.VMEM((width, wide), LOW),
            pltpu.VMEM((width, wide), LOW), pltpu.VMEM((wide, width), LOW), pltpu.VMEM((8, length), jnp.int32),
            pltpu.VMEM((rows, 128), FULL), pltpu.VMEM((2, 8, length), jnp.int32),
            pltpu.VMEM((8, length), FULL), pltpu.VMEM((3, 8, length), FULL),
            pltpu.VMEM((heads, 3 * length, length), FULL), pltpu.VMEM((heads, 8, length), FULL),
            pltpu.VMEM((3 * length, length), FULL),
        ]
        + TensorScatter.scratch(rows, width)[:3]
        + [
            pltpu.VMEM((rows, width), FULL), dma(3), dma(3),
            *Gather.scratch(depth), dma(2, 3), dma(2, 3), dma(3), dma(3), dma(3), dma(3), dma(9), dma(5),
        ],
        compiler_params=comm_params(number),
    )(tokens, *weights, grads, *gains, *tables, docs, gain2, router, picked)


def attention_back_kernel(
    depth, rows, heads, chain, local,
    sum_ref, gate_cots, probs_ref, picked_ref, state_ref, gain2_ref, router_ref, normed2_ref, grad_ref,
    query_ref, kv_ref, attended, logs, docs_ref, query_docs, q_ref, k_ref, q_gain_ref, k_gain_ref, cosine_ref, sine_ref, scales,
    w_out_ref, produced_ref, normed_ref, wq_ref, wk_ref, wv_ref,
    state_cot_ref, vectors, out_ref, normed_part, piece0, piece1, piece2, piece3,
    kv_all, key_docs, q_raw, k_raw, w_out, low, lows, by_expert, bias, cots, deltas, turned, query_cot, kv_cot, sending, landed, work, raw_cots, flipped, wq, wk, wv,
    inners, inners_in, staging,
    diagonal, from_x, from_y, from_z, r_send, r_recv, middle, m_send, m_recv,
    t_send, t_recv, h_send, h_recv, i_send, i_recv, load, saves, early_load,
):
    z, x, y, core = place()
    group, part = lax.axis_index("expert"), lax.axis_index("tensor")
    spot = group % chain
    length, width = query_ref.shape[0], w_out.shape[1]
    wide = heads * HD
    scale = HD ** (-0.5)
    order = [step for step in range(depth - 1, 0, -2)] + [step for step in range(depth - 2, -1, -2)]
    loads = {}
    for step in order:
        loads[step] = pltpu.make_async_copy(produced_ref.at[step], work.at[step], load.at[step])
        loads[step].start()
    others = []
    for number, (source, target) in enumerate([(wq_ref, wq), (wk_ref, wk), (wv_ref, wv)]):
        others.append(pltpu.make_async_copy(source, target, load.at[depth + number]))
        others[-1].start()
    early = []
    for number, (source, target) in enumerate(
        [(docs_ref, key_docs), (w_out_ref, w_out), (kv_ref, kv_all), (q_ref, q_raw), (k_ref, k_raw)]
    ):
        early.append(pltpu.make_async_copy(source, target, early_load.at[number]))
        early[-1].start()
    mates = mates_of()
    greet(
        [device(swapped(z, step), x, y, core) for step in range(1, depth)]
        + [device(z, 1 - x, y, core)]
        + [device(*mate) for mate in mates]
    )
    copies = Copies()
    scatter = Scatter(
        copies, work, diagonal, from_x, from_y, from_z, rows, r_send, r_recv, (middle, m_send, m_recv)
    )

    def corner(step):
        if step % 2 == 0:
            loads[step].wait()
        scatter.corner(step)


    loads[3].wait()
    scatter.share(3)
    loads[1].wait()
    scatter.share(1)
    corner(3)
    by_expert[...] = jnp.zeros_like(by_expert)
    for plane in range(depth):
        step = swapped(z, plane)
        for column in range(2):
            first = (2 * plane + column) * local
            by_expert[first : first + local, :] = (gate_cots[step, 2 * column] + gate_cots[step, 2 * column + 1])[:local]
    probs = probs_ref[...]
    prob_cot = by_expert[...].T * picked_ref[...]
    logit_cot = probs * (prob_cot - jnp.sum(probs * prob_cot, axis=-1, keepdims=True))
    normed2_cot = sum_ref[...] + lax.dot_general(
        logit_cot[:, : router_ref.shape[0]], router_ref[...].astype(FULL), (((1,), (0,)), ((), ())),
        precision=HIGHEST_PRECISION, preferred_element_type=FULL,
    )
    state = state_ref[...]
    factor = lax.rsqrt(jnp.mean(state * state, axis=-1, keepdims=True) + NORM_EPSILON)
    groups, _, slice_width = vectors.shape
    vectors[...] = jnp.zeros_like(vectors)
    gain_grad = jnp.sum(normed2_cot * state * factor, axis=0, keepdims=True)
    for index in range(groups):
        vectors[index, 17:18, :] = gain_grad[:, index * slice_width : (index + 1) * slice_width]
    inner = jnp.sum(normed2_cot * gain2_ref[0:1, :] * state, axis=-1, keepdims=True)
    state_cot = (
        grad_ref[...].astype(FULL)
        + factor * gain2_ref[0:1, :] * normed2_cot
        - state * (factor * factor * factor) * inner * (1.0 / width)
    )
    state_cot_ref[...] = state_cot
    low[...] = state_cot.astype(LOW)
    gather = TensorGather(copies, low, lows, t_send, t_recv)
    scatter.side(3)
    corner(2)
    router_grad = jnp.dot(
        logit_cot.T, normed2_ref[...].astype(FULL), precision=HIGHEST_PRECISION, preferred_element_type=FULL
    )[:16]
    for index in range(groups):
        vectors[index, 0:16, :] = router_grad[:, index * slice_width : (index + 1) * slice_width]
    early[0].wait()
    mask_bias(bias, key_docs, query_docs, length)
    for copy in early[1:]:
        copy.wait()
    gather.cross()
    gather.finish()
    for index in range(4):
        cots[pl.ds(index * rows, rows), :] = dot_t(lows[index // 2, index % 2], w_out[...]).astype(LOW)
    for head in range(heads):
        columns = pl.ds(head * HD, HD)
        product = cots[:, columns].astype(FULL) * attended[:, columns].astype(FULL)
        deltas[head] = jnp.broadcast_to(jnp.sum(product.T, axis=0, keepdims=True), (8, length))
    scatter.side(2)
    turned[...] = jnp.zeros_like(turned)

    def back(block, store, after):
        @pl.loop(0, heads)
        def _(head):
            columns = pl.ds(pl.multiple_of(head * HD, HD), HD)
            values = pl.ds(pl.multiple_of((heads + head) * HD, HD), HD)
            tile = length // 2

            for index, seen in ((0, pl.ds(0, tile if block == 0 else length)), (1, pl.ds(tile, tile) if block == 2 else pl.ds(0, length))):
                keys = pl.ds(index * tile, tile)
                key, value = kv_all[block, keys, columns], kv_all[block, keys, values]
                query, cot = query_ref[seen, columns], cots[seen, columns]
                log, delta = logs[head, 0:1, seen], deltas[head, 0:1, seen]
                hidden = bias[pl.ds(block * length + index * tile, tile), seen].astype(FULL)
                probs = jnp.exp(dot_t(key, query) * scale + hidden - log)
                score_cot = (probs * (dot_t(value, cot) - delta)).astype(LOW)
                turned[head, :, seen] += t_dot(key, score_cot)
                store(head, keys, dot(score_cot, query) * scale, dot(probs.astype(LOW), cot))

            after(head)

    def store_in(slot):
        def store(head, keys, key_part, value_part):
            sending[slot, head, keys, 0:HD] = key_part.astype(LOW)
            sending[slot, head, keys, HD : 2 * HD] = value_part.astype(LOW)

        return store

    def store_own(head, keys, key_part, value_part):
        kv_cot[keys, pl.ds(pl.multiple_of(head * HD, HD), HD)] = key_part
        kv_cot[keys, pl.ds(pl.multiple_of((heads + head) * HD, HD), HD)] = value_part

    high = lax.rem(z, 2)
    over_x, over_z = device(z, 1 - x, y, core), device(swapped(z, 1), x, y, core)

    def x_copy(head):
        return remote(sending.at[1, head], landed.at[1, head], h_send.at[0, head], h_recv.at[0, head], over_x)

    def z_copy(head):
        return remote(sending.at[0, head], landed.at[0, head], h_send.at[1, head], h_recv.at[1, head], over_z)

    def relay(head):
        @pl.when(spot == 3)
        def _():
            x_copy(head).wait_recv()
            add_rows(sending.at[0, head], [sending.at[0, head], landed.at[1, head]], length, 64)
            z_copy(head).start()

    back(1, store_in(1), lambda head: pl.when(spot >= 1)(lambda: x_copy(head).start()))
    scatter.climb(3)
    back(0, store_in(0), lambda head: pl.when(spot == 2)(lambda: z_copy(head).start()))
    back(2, store_own, relay)
    scatter.climb(2)
    corner(1)
    corner(0)
    for head in range(heads):
        query_cot[:, pl.ds(head * HD, HD)] = turned[head].T * scale

    scatter.side(1)
    saving = {}

    def weight_piece(number, right, target):
        piece = target.shape[2]
        for index in range(2 * depth):
            slot = index % 2
            if slot in saving:
                saving.pop(slot).wait()
            staging[slot] = dot(flipped[pl.ds(index * piece, piece), :], right).astype(LOW)
            saving[slot] = pltpu.make_async_copy(staging.at[slot], target.at[index // 2, index % 2], saves.at[slot])
            saving[slot].start()

    @pl.loop(0, width // 256)
    def _(index):
        columns = pl.ds(pl.multiple_of(index * 256, 256), 256)
        flipped[columns, :] = jnp.concatenate([lows[block // 2, block % 2, :, columns] for block in range(4)], axis=0).T

    weight_piece(0, attended[...], piece0)
    normed_copy = pltpu.make_async_copy(normed_ref, flipped, load.at[depth + 3])
    normed_copy.start()
    scatter.side(0)
    factors = as_columns(scales[...])

    def turn_back(cot, raw, gain_ref, factor, first):
        total = jnp.zeros((length, 1), FULL)
        for head in range(heads):
            columns = pl.ds(head * HD, HD)
            mine = cot[:, columns]
            mine = mine * cosine_ref[...] - pltpu.roll(mine, HD // 2, 1) * sine_ref[...]
            cot[:, columns] = mine
            mine = mine * raw[:, columns]
            grad = jnp.sum(mine * factor, axis=0, keepdims=True)
            for index in range(groups):
                vectors[index, first + head : first + head + 1, 0:HD] = grad
            total = total + jnp.sum(mine * gain_ref[0:1, columns], axis=-1, keepdims=True)
        return total

    query_inner = turn_back(query_cot, q_raw, q_gain_ref, factors[:, 0:1], 18)

    scatter.climb(1)
    def take(slot, head):
        (z_copy, x_copy)[slot](head).wait_recv()
        for part in range(2):
            mine = kv_cot.at[:, pl.ds((part * heads + head) * HD, HD)]
            add_rows(mine, [mine, landed.at[slot, head, :, pl.ds(part * HD, HD)]], length, 64)

    for head in range(heads):
        pl.when(x == 0)(functools.partial(take, 1, head))
    for head in range(heads):
        pl.when(high == 0)(functools.partial(take, 0, head))

    key_inner = turn_back(kv_cot, k_raw, k_gain_ref, factors[:, 1:2], 18 + heads)
    inners[...] = as_rows([query_inner, key_inner])
    sent = exchange(copies, inners, inners_in, i_send, i_recv, mates)
    raw_cots[2] = kv_cot[:, pl.ds(wide, wide)].astype(LOW)
    normed_copy.wait()
    weight_piece(1, raw_cots[2], piece1)
    for copy in sent:
        copies.arrived(copy)
    total = inners[...]
    for number in range(3):
        total = total + inners_in[number]
    totals = as_columns(total * (1.0 / width))

    def raw_cot(number, cot, raw, gain_ref):
        factor = factors[:, number : number + 1]
        shrink = (factor * factor * factor) * totals[:, number : number + 1]
        for head in range(heads):
            columns = pl.ds(head * HD, HD)
            raw_cots[number, :, columns] = (
                factor * gain_ref[0:1, columns] * cot[:, columns] - raw[:, columns] * shrink
            ).astype(LOW)

    raw_cot(0, query_cot, q_raw, q_gain_ref)
    raw_cot(1, kv_cot, k_raw, k_gain_ref)
    for copy in others:
        copy.wait()

    @pl.loop(0, width // 256)
    def _(index):
        columns = pl.ds(pl.multiple_of(index * 256, 256), 256)
        result = (
            dot_t(raw_cots[0], wq[columns, :]) + dot_t(raw_cots[1], wk[columns, :]) + dot_t(raw_cots[2], wv[columns, :])
        ).astype(LOW)
        for block in range(4):
            normed_part[block // 2, block % 2, :, columns] = result[block * rows : (block + 1) * rows]

    weight_piece(2, raw_cots[0], piece2)
    weight_piece(3, raw_cots[1], piece3)
    scatter.climb(0)
    scatter.result(out_ref, [state_ref])
    for head in range(heads):
        pl.when(spot >= 1)(lambda: x_copy(head).wait_send())
        pl.when(spot >= 2)(lambda: z_copy(head).wait_send())

    for copy in saving.values():
        copy.wait()
    copies.finish()


def run_attention_back(rows_of, attention, sources, produced, normed, weights, chain, local, number):
    depth = produced.shape[0]
    rows, width = rows_of[0].shape
    queries, kv_all = attention[0], attention[1]
    length, wide2 = kv_all.shape[1:]
    wide = wide2 // 2
    heads = wide // HD
    piece = jax.ShapeDtypeStruct((depth, 2, width // (2 * depth), wide), LOW)
    return pl.pallas_call(
        functools.partial(attention_back_kernel, depth, rows, heads, chain, local),
        out_shape=(
            jax.ShapeDtypeStruct((rows, width), FULL),
            jax.ShapeDtypeStruct((2 * depth, 32, width // (2 * depth)), FULL),
            jax.ShapeDtypeStruct((rows, width), LOW),
            jax.ShapeDtypeStruct((2, 2, rows, width), LOW),
            piece, piece, piece, piece,
        ),
        in_specs=[VMEM] * 10 + [ANY] + [VMEM] * 2 + [ANY] + [VMEM] + [ANY] * 2 + [VMEM] * 5 + [ANY] * 6,
        out_specs=(VMEM,) * 4 + (ANY,) * 4,
        scratch_shapes=[
            pltpu.VMEM(kv_all.shape, LOW), pltpu.VMEM((3 * length, 1), jnp.int32), pltpu.VMEM((length, wide), FULL),
            pltpu.VMEM((length, wide), FULL), pltpu.VMEM((wide, width), LOW),
            pltpu.VMEM((rows, width), LOW), pltpu.VMEM((2, 2, rows, width), LOW), pltpu.VMEM((128, rows), FULL),
            pltpu.VMEM((3 * length, length), LOW), pltpu.VMEM((length, wide), LOW),
            pltpu.VMEM((heads, 8, length), FULL), pltpu.VMEM((heads, HD, length), FULL),
            pltpu.VMEM((length, wide), FULL), pltpu.VMEM((length, wide2), FULL),
            pltpu.VMEM((2, heads, length, 2 * HD), LOW), pltpu.VMEM((2, heads, length, 2 * HD), LOW),
            pltpu.VMEM(produced.shape, LOW), pltpu.VMEM((3, length, wide), LOW), pltpu.VMEM((width, length), LOW),
            pltpu.VMEM((width, wide), LOW), pltpu.VMEM((width, wide), LOW), pltpu.VMEM((width, wide), LOW),
            pltpu.VMEM((8, length), FULL), pltpu.VMEM((3, 8, length), FULL), pltpu.VMEM((2,) + piece.shape[2:], LOW),
        ]
        + Scatter.scratch(depth, rows, width)
        + [pltpu.VMEM((depth // 2, 4, rows // 4, width), LOW), dma(depth // 2, 4), dma(depth // 2, 4)]
        + [dma(4), dma(3), dma(2, heads), dma(2, heads), dma(3), dma(3), dma(depth + 4), dma(2), dma(5)],
        compiler_params=comm_params(number),
    )(*rows_of, *attention, *sources, produced, normed, *weights)


def dot(left, right):
    return jnp.dot(left, right, preferred_element_type=FULL)


def dot_t(left, right):
    return lax.dot_general(left, right, (((1,), (1,)), ((), ())), preferred_element_type=FULL)


def t_dot(left, right):
    return lax.dot_general(left, right, (((0,), (0,)), ((), ())), preferred_element_type=FULL)


class ExpertScatter:
    def __init__(self, copies, parts, widths, work, from_x, from_z, load, send, recv):
        self.widths = widths
        self.copies, self.parts, self.work, self.from_x, self.from_z = copies, parts, work, from_x, from_z
        self.load, self.send, self.recv = load, send, recv
        self.z, self.x, y, core = place()
        self.depth, self.rows = work.shape[1], work.shape[2]
        self.over_x = device(self.z, 1 - self.x, y, core)
        self.column = [device(swapped(self.z, step), self.x, y, core) for step in range(self.depth)]
        self.order = sorted(range(self.depth), key=lambda step: (step == 0, step & -step, -step))
        self.steps = self.order[:-1]
        self.loads, self.sides, self.along = {}, {}, {}

    def begin(self, index):
        for step in self.order:
            at = swapped(self.z, step)
            columns = pl.ds(0, self.widths[index])
            self.sides[index, step] = self.copies.start(
                remote(
                    self.parts[index].at[at, 1 - self.x, :, columns], self.from_x.at[index, step, :, columns],
                    self.send.at[0, index, step], self.recv.at[0, index, step], self.over_x,
                )
            )
            load = pltpu.make_async_copy(
                self.parts[index].at[at, self.x, :, columns], self.work.at[index, step, :, columns], self.load.at[index, step]
            )
            load.start()
            self.loads[index, step] = load

    def climb(self, index, step):
        self.loads[index, step].wait()
        self.copies.arrived(self.sides[index, step])
        columns = pl.ds(0, self.widths[index])
        mine = self.work.at[index, step, :, columns]
        low = step & -step
        terms = [mine, self.from_x.at[index, step, :, columns]] + self.below(index, step)
        add_rows(mine, terms, self.rows)
        self.along[index, step] = self.copies.start(
            remote(
                mine, self.from_z.at[index, step, :, columns],
                self.send.at[1, index, step], self.recv.at[1, index, step], self.column[low],
            )
        )

    def below(self, index, step):
        terms, bit = [], 1
        while bit < (step & -step if step else self.depth):
            self.copies.arrived(self.along[index, step | bit])
            terms.append(self.from_z.at[index, step | bit, :, pl.ds(0, self.widths[index])])
            bit *= 2
        return terms

    def result(self, index, target):
        self.loads[index, 0].wait()
        self.copies.arrived(self.sides[index, 0])
        columns = pl.ds(0, self.widths[index])
        terms = [self.work.at[index, 0, :, columns], self.from_x.at[index, 0, :, columns]] + self.below(index, 0)
        add_rows(target.at[:, columns], terms, self.rows)


class ZScatter:
    def __init__(self, copies, part, columns, work, from_z, from_x, load, send, recv):
        self.copies, self.part, self.columns = copies, part, columns
        self.work, self.from_z, self.from_x, self.load, self.send, self.recv = work, from_z, from_x, load, send, recv
        self.z, self.x, y, core = place()
        self.depth, self.rows = work.shape[0], work.shape[2]
        self.over_x = device(self.z, 1 - self.x, y, core)
        self.column = [device(swapped(self.z, step), self.x, y, core) for step in range(self.depth)]
        self.loads, self.along = {}, {}

    def begin(self):
        for step in range(self.depth):
            source = self.part.at[swapped(self.z, step), :, :, self.columns]
            self.loads[step] = pltpu.make_async_copy(source, self.work.at[step], self.load.at[step])
            self.loads[step].start()

    def climb(self, step):
        self.loads[step].wait()
        low = step & -step if step else self.depth
        bit = 1
        while bit < low:
            self.copies.arrived(self.along[step | bit])
            for column in range(2):
                mine = self.work.at[step, column]
                add_rows(mine, [mine, self.from_z.at[step | bit, column]], self.rows, 32)
            bit *= 2
        if step:
            copy = remote(self.work.at[step], self.from_z.at[step], self.send.at[step], self.recv.at[step], self.column[low])
        else:
            copy = remote(self.work.at[0, 1 - self.x], self.from_x, self.send.at[0], self.recv.at[0], self.over_x)
        self.along[step] = self.copies.start(copy)

    def result(self, target):
        self.copies.arrived(self.along[0])
        add_rows(target, [self.work.at[0, self.x], self.from_x], self.rows)


def gradients_kernel(
    depth, rows, local, hidden, matrices, *refs,
):
    parts, refs = refs[:matrices], refs[matrices:]
    (
        normed_part, tokens_ref, state_cot, gain_ref, out_ref, vector_ref,
        normed_ref, grad_ref, gated_ref, gate_grad_ref, up_grad_ref,
    ) = refs[:11]
    sums, refs = refs[11 : 11 + matrices], refs[11 + matrices :]
    (
        input_out, output_out, vector_sum,
        gate_own, up_own, down_own,
        input_grads, outputs, work, from_x, from_z, partial, from_pair, from_y, normed_grad, low, vectors, vector_in, vector_mid, vector_turn,
        tiles, turned, acts, gated_turned, near, far, near_down, far_down, other, other_down,
        f_work, f_from_z, f_from_x, f_load, f_send, f_recv,
        e_load, e_send, e_recv, t_send, t_recv, g_send, g_recv, o_send, o_recv, v_send, v_recv, u_send, u_recv,
        tile_load, act_load, save, pair_send, pair_recv, local_sem, leave_sem,
    ) = refs
    z, x, y, core = place()
    group = 2 * z + x
    sibling = device(z, x, y, 1 - core)
    groups = [(step, turn) for step in range(depth) for turn in range(2) if step or turn]
    peers = [device(swapped(z, step), swapped(x, turn), y, core) for step, turn in groups]
    mates = [(z, x, swapped(y, turn // 2), swapped(core, turn % 2)) for turn in range(1, 4)]
    greet(peers + [device(*mate) for mate in mates])
    copies = Copies()
    width = normed_ref.shape[1]
    tile = local * hidden
    count = width // tile

    def fetch(source, target, sem):
        copy = pltpu.make_async_copy(source, target, sem)
        copy.start()
        return copy

    wide = work.shape[3]
    widths = [wide] * (matrices - 1) + [wide // 2]
    experts = ExpertScatter(copies, parts, widths, work, from_x, from_z, e_load, e_send, e_recv)
    eighth = pl.ds(wide // 2, wide // 2)
    z_first = ZScatter(copies, parts[-1], eighth, f_work, f_from_z, f_from_x, f_load, f_send, f_recv)
    loaded = fetch(normed_part, partial, local_sem.at[0])
    experts.begin(0)
    z_first.begin()
    loaded.wait()
    scatter = TensorScatter(copies, partial, from_pair, from_y, t_send, t_recv)
    scatter.begin()
    out_gather = TensorGather(copies, out_ref, outputs, o_send, o_recv)
    experts.begin(1)
    act_copies = [fetch(gate_grad_ref, acts.at[0], act_load.at[0]), fetch(up_grad_ref, acts.at[1], act_load.at[1])]

    def fetch_tile(number):
        source = normed_ref if number < count else grad_ref
        columns = pl.ds((number % count) * tile, tile)
        return fetch(source.at[:, columns], tiles.at[number % 2], tile_load.at[number % 2])

    tile_copies = [fetch_tile(0)]
    saving = {}

    def first_unit(owner):
        return owner * local * hidden

    def gate_and_up(number):
        slot = number % 2
        tile_copies[number].wait()
        tile_copies.append(fetch_tile(number + 1))
        turned[...] = tiles[slot].T
        for copy, remote_one in saving.pop(slot, []):
            copies.sent(copy) if remote_one else copy.wait()
        for which in range(2):
            for owner, target in ((1 - core, far), (core, near)):

                @pl.loop(0, local)
                def _(expert):
                    columns = pl.ds(pl.multiple_of(first_unit(owner) + expert * hidden, hidden), hidden)
                    target[which, slot, expert] = dot(turned[...], acts[which, :, columns]).astype(target.dtype)

        saves = []
        for which in range(2):
            away = remote(
                far.at[which, slot], other.at[which, :, pl.ds(number * tile, tile)],
                pair_send.at[which, number], pair_recv.at[which, number], sibling,
            )
            copies.start(away)
            saves.append((away, True))
        saving[slot] = saves
        if number:
            settle(number - 1)

    def settle(number):
        slot, place_of = number % 2, pl.ds(number * tile, tile)
        for which, own in enumerate((gate_own, up_own)):
            copies.arrived(saving[slot][which][0])
            for expert in range(local):
                mine = near.at[which, slot, expert]
                add_rows(mine, [mine, other.at[which, expert, place_of]], tile, 64)
        for which, own in enumerate((gate_own, up_own)):
            saving[slot].append((fetch(near.at[which, slot], own.at[:, place_of], save.at[which, slot]), False))

    def down(number):
        slot = number % 2
        tile_copies[count + number].wait()
        if number + 1 < count:
            tile_copies.append(fetch_tile(count + number + 1))
        for copy, remote_one in saving.pop(("down", slot), []):
            copies.sent(copy) if remote_one else copy.wait()
        for source, target in ((turned, far_down), (gated_turned, near_down)):

            @pl.loop(0, local)
            def _(expert):
                units = pl.ds(pl.multiple_of(expert * hidden, hidden), hidden)
                target[slot, expert] = dot(source[units, :], tiles[slot]).astype(target.dtype)

        away = remote(
            far_down.at[slot], other_down.at[number], pair_send.at[2, number], pair_recv.at[2, number], sibling
        )
        copies.start(away)
        saving["down", slot] = [(away, True)]
        settle(count - 1) if number == 0 else settle_down(number - 1)

    def settle_down(number):
        slot = number % 2
        copies.arrived(saving["down", slot][0][0])
        for expert in range(local):
            mine = near_down.at[slot, expert]
            add_rows(mine, [mine, other_down.at[number, expert]], hidden, 64)
        target = down_own.at[:, :, pl.ds(number * tile, tile)]
        saving["down", slot].append((fetch(near_down.at[slot], target, save.at[2, slot]), False))

    for copy in act_copies:
        copy.wait()
    z_first.climb(3)
    z_first.climb(1)
    gate_and_up(0)
    scatter.cross()
    experts.climb(0, experts.steps[0])
    gate_and_up(1)
    out_gather.cross()
    experts.climb(0, experts.steps[1])
    z_first.climb(2)
    scatter.result(normed_grad)

    inputs = tokens_ref[...].astype(FULL)
    factor = lax.rsqrt(jnp.mean(inputs * inputs, axis=-1, keepdims=True) + NORM_EPSILON)
    gain = gain_ref[0:1, :]
    normed = normed_grad[...]
    inner = jnp.sum(normed * gain * inputs, axis=-1, keepdims=True)
    low[...] = (
        state_cot[...] + factor * gain * normed - inputs * (factor * factor * factor) * inner * (1.0 / width)
    ).astype(LOW)
    gain_grad = jnp.sum(normed * inputs * factor, axis=0, keepdims=True)
    grad_gather = TensorGather(copies, low, input_grads, g_send, g_recv)
    vectors[...] = vector_ref[...]
    slice_width = vectors.shape[2]
    for index in range(vectors.shape[0]):
        vectors[index, 16:17, :] = gain_grad[:, index * slice_width : (index + 1) * slice_width]
    vector_copies = []
    for number, ((step, turn), peer) in enumerate(zip(groups, peers)):
        to = 2 * swapped(z, step) + swapped(x, turn)
        vector_copies.append(
            copies.start(remote(vectors.at[to], vector_in.at[number], v_send.at[number], v_recv.at[number], peer))
        )
    for index in range(2, matrices):
        experts.begin(index)

    for step in experts.steps[2:]:
        experts.climb(0, step)
    gate_and_up(2)
    for step in experts.steps[:2]:
        experts.climb(1, step)
    grad_gather.cross()
    z_first.climb(0)
    gate_and_up(3)
    for step in experts.steps[2:]:
        experts.climb(1, step)
    gated_copy = fetch(gated_ref, acts.at[0], act_load.at[0])
    gated_copy.wait()
    for owner, target in ((1 - core, turned), (core, gated_turned)):
        target[...] = acts[0, :, pl.ds(pl.multiple_of(first_unit(owner), hidden), local * hidden)].T
    experts.result(0, sums[0])
    out_gather.finish()
    leaving = [fetch(outputs, output_out, leave_sem.at[0])]
    down(0)
    grad_gather.finish()
    leaving.append(fetch(input_grads, input_out, leave_sem.at[1]))
    experts.climb(2, experts.steps[0])
    down(1)
    for step in experts.steps[1:]:
        experts.climb(2, step)
    down(2)
    experts.result(1, sums[1])
    for copy in vector_copies:
        copies.arrived(copy)
    total = vectors[group]
    for number in range(len(peers)):
        total = total + vector_in[number]
    vector_mid[...] = total
    turn_copies = [
        copies.start(remote(vector_mid, vector_turn.at[number], u_send.at[number], u_recv.at[number], device(*mate)))
        for number, mate in enumerate(mates)
    ]
    down(3)
    settle_down(3)
    for copy in turn_copies:
        copies.arrived(copy)
    total = vector_mid[...]
    for number in range(len(mates)):
        total = total + vector_turn[number]
    keep = lax.broadcasted_iota(jnp.int32, total.shape, 0) < 18
    vector_sum[...] = jnp.where(keep, total, vector_mid[...])
    for index in range(3, matrices):
        for step in experts.steps:
            experts.climb(index, step)
    for index in range(2, matrices):
        experts.result(index, sums[index])
    z_first.result(sums[-1].at[:, eighth])
    for copy in leaving:
        copy.wait()
    for entries in saving.values():
        for copy, remote_one in entries:
            if not remote_one:
                copy.wait()
    copies.finish()


def run_gradients(parts, normed_part, tokens, state_cot, gain, out, vectors, normed, grads, gated, gate_grad, up_grad, local, number):
    matrices = len(parts)
    depth, _, piece, columns = parts[0].shape
    rows, width = state_cot.shape
    seen, units = gated.shape
    hidden = units // (2 * local)
    tile = units // 2
    sum_of = jax.ShapeDtypeStruct((piece, columns), FULL)
    spread = jax.ShapeDtypeStruct((2, 2, rows, width), LOW)
    wide, tall = (local, width, hidden), (local, hidden, width)
    results = pl.pallas_call(
        functools.partial(gradients_kernel, depth, rows, local, hidden, matrices),
        out_shape=(sum_of,) * matrices
        + (
            spread, spread, jax.ShapeDtypeStruct(vectors.shape[1:], FULL),
            jax.ShapeDtypeStruct(wide, FULL), jax.ShapeDtypeStruct(wide, FULL), jax.ShapeDtypeStruct(tall, FULL),
        ),
        in_specs=[ANY] * (matrices + 1) + [VMEM] * 5 + [ANY] * 5,
        out_specs=(VMEM,) * matrices + (ANY, ANY, VMEM) + (ANY,) * 3,
        scratch_shapes=[pltpu.VMEM((2, 2, rows, width), LOW)] * 2
        + [pltpu.VMEM((matrices, depth, piece, columns), LOW)] * 3
        + TensorScatter.scratch(rows, width)[:3]
        + [
            pltpu.VMEM((rows, width), FULL), pltpu.VMEM((rows, width), LOW),
            pltpu.VMEM(vectors.shape, FULL), pltpu.VMEM((2 * depth - 1,) + vectors.shape[1:], FULL),
            pltpu.VMEM(vectors.shape[1:], FULL), pltpu.VMEM((3,) + vectors.shape[1:], FULL),
            pltpu.VMEM((2, seen, tile), LOW), pltpu.VMEM((tile, seen), LOW),
            pltpu.VMEM((2, seen, units), LOW), pltpu.VMEM((units // 2, seen), LOW),
            pltpu.VMEM((2, 2, local, tile, hidden), FULL), pltpu.VMEM((2, 2, local, tile, hidden), LOW),
            pltpu.VMEM((2, local, hidden, tile), FULL), pltpu.VMEM((2, local, hidden, tile), LOW),
            pltpu.VMEM((2, local, width, hidden), LOW), pltpu.VMEM((width // tile, local, hidden, tile), LOW),
            pltpu.VMEM((depth, 2, piece, columns // 2), LOW), pltpu.VMEM((depth, 2, piece, columns // 2), LOW),
            pltpu.VMEM((piece, columns // 2), LOW), dma(depth), dma(depth), dma(depth),
            dma(matrices, depth), dma(2, matrices, depth), dma(2, matrices, depth),
            dma(3), dma(3), dma(4), dma(3), dma(4), dma(3),
            dma(2 * depth - 1), dma(2 * depth - 1), dma(3), dma(3),
            dma(2), dma(2), dma(3, 2), dma(3, width // tile), dma(3, width // tile), dma(1), dma(2),
        ],
        compiler_params=comm_params(number),
    )(*parts, normed_part, tokens, state_cot, gain, out, vectors, normed, grads, gated, gate_grad, up_grad)
    return results[:matrices], results[matrices:]


def finish_kernel(
    experts, heads,
    in_grad, in_out, in_query, in_key, in_value, in_gate, in_up, in_down, in_w_out, vector_ref,
    input_grad, output, query, key, value, gate, up, down, w_out, norm1, norm2, router, q_gain, k_gain,
):
    input_grad[...] = in_grad[...].astype(FULL)
    for source, target in (
        (in_out, output), (in_query, query), (in_key, key), (in_value, value), (in_gate, gate), (in_up, up), (in_down, down),
    ):
        target[...] = source[...]

    @pl.when(pl.program_id(0) == 0)
    def _():
        w_out[...] = in_w_out[...].T
        vectors = vector_ref[...]
        norm1[...], norm2[...] = vectors[16:17], vectors[17:18]
        router[...] = vectors[:experts]
        gains = vectors[18 : 18 + 2 * heads, :HD]
        width = q_gain.shape[1]
        group = lax.axis_index("expert")
        total_q, total_k = jnp.zeros(q_gain.shape, FULL), jnp.zeros(k_gain.shape, FULL)
        for index in range(HD // width):
            mine = (group == index).astype(FULL)
            total_q = total_q + gains[:heads, index * width : (index + 1) * width] * mine
            total_k = total_k + gains[heads:, index * width : (index + 1) * width] * mine
        q_gain[...], k_gain[...] = total_q, total_k


def finish(arrays, w_out, vectors, experts, heads, groups):
    steps = 4
    shapes = [jax.ShapeDtypeStruct(a.shape, FULL if i == 0 else a.dtype) for i, a in enumerate(arrays)]
    blocks = [pl.BlockSpec((a.shape[0] // steps, a.shape[1]), lambda i: (i, 0)) for a in arrays]
    whole = pl.BlockSpec(memory_space=pltpu.VMEM)
    piece = vectors.shape[1]
    small = [
        jax.ShapeDtypeStruct(shape, FULL)
        for shape in (w_out.shape[::-1], (1, piece), (1, piece), (experts, piece), (heads, HD // groups), (heads, HD // groups))
    ]
    return pl.pallas_call(
        functools.partial(finish_kernel, experts, heads),
        grid=(steps,),
        out_shape=(*shapes, *small),
        in_specs=blocks + [whole, whole],
        out_specs=(*blocks, *[whole] * len(small)),
        compiler_params=pltpu.CompilerParams(vmem_limit_bytes=VMEM_BYTES),
    )(*arrays, w_out, vectors)


def body(
    groups, parts,
    tokens, documents, routes, norm1_gain, q_gain, k_gain, w_query, w_key, w_value, w_out, norm2_gain, router_w,
    w_gate, w_up, w_down, out_grad,
):
    row_count, width = tokens.shape
    local_experts, _, hidden = w_gate.shape
    experts = local_experts * groups
    chain = LENGTH // row_count
    if not (parts == 4 and groups % 2 == 0 and experts <= min(16, 2 * TOP) and 2 * w_query.shape[1] <= 14 * HD and chain == 4 and groups == 8 and 4 * row_count == LENGTH and WINDOW == 2 * row_count):
        return body_routed(
            tokens, documents, routes, norm1_gain, q_gain, k_gain, w_query, w_key, w_value, w_out, norm2_gain, router_w,
            w_gate, w_up, w_down, out_grad,
        )
    depth = groups // 2
    rows = row_count // parts
    seen = groups * row_count // 2
    heads = w_query.shape[1] // HD
    group, part = lax.axis_index("expert"), lax.axis_index("tensor")
    core = part % 2

    def quarter(array):
        return lax.dynamic_slice_in_dim(array, part * rows, rows, 0)

    def across(vector):
        return vector.reshape(1, -1)

    picked = jnp.any(quarter(routes)[:, :, None] == jnp.arange(128, dtype=jnp.int32)[None, None, :], axis=1).astype(FULL)
    query_gain, key_gain = across(q_gain), across(k_gain)
    (
        normed_one, query_raw, key_raw, queries, kv_all, key_docs, scales, attended, logs, state, normed_two, router_probs, gates,
        own_tokens, own_grads, cosine, sine, all_grad,
    ) = run_attention(
        tokens, (w_query, w_key, w_value, w_out), out_grad, (across(norm1_gain), query_gain, key_gain), [jnp.asarray(table) for table in whole_tables()], across(documents),
        across(norm2_gain), router_w.T, picked, depth, chain, local_experts, 3,
    )

    normed_two_grad, gate_cots, all_normed, gated, gate_pre_grad, up_pre_grad, produced = run_experts(
        normed_two, gates, all_grad, w_gate, w_up, w_down, 5
    )
    units = 2 * local_experts * hidden
    all_normed, all_grad = all_normed.reshape(seen, width), all_grad.reshape(seen, width)
    gated, gate_pre_grad, up_pre_grad = (a.reshape(seen, units) for a in (gated, gate_pre_grad, up_pre_grad))

    state_cot, vectors, output_rows, normed_part, *pieces = run_attention_back(
        (normed_two_grad, gate_cots, router_probs, picked, state, across(norm2_gain), router_w.T, normed_two, own_grads),
        (queries, kv_all, attended, logs, key_docs, across(documents), query_raw, key_raw, query_gain, key_gain, cosine, sine, scales),
        (w_out,), produced, normed_one, (w_query, w_key, w_value), chain, local_experts, 10,
    )
    sums, (input_grad, output, vector_sum, *expert_grads) = run_gradients(
        pieces, normed_part, own_tokens, state_cot, norm1_gain[None], output_rows, vectors, all_normed, all_grad, gated, gate_pre_grad, up_pre_grad,
        local_experts, 14,
    )
    (
        input_grad, output, w_query_grad, w_key_grad, w_value_grad, gate_grad, up_grad, down_grad, w_out_grad,
        norm1_grad, norm2_grad, router_grad, q_gain_grad, k_gain_grad,
    ) = finish(
        (
            input_grad.reshape(row_count, width), output.reshape(row_count, width), sums[2], sums[3], sums[1],
            *(a.reshape(-1, a.shape[2]) for a in expert_grads),
        ),
        sums[0], vector_sum, experts, heads, groups,
    )
    return (
        output, input_grad, norm1_grad.reshape(-1), q_gain_grad, k_gain_grad, w_query_grad, w_key_grad, w_value_grad, w_out_grad,
        norm2_grad.reshape(-1), router_grad.T, gate_grad.reshape(w_gate.shape), up_grad.reshape(w_up.shape),
        down_grad.reshape(w_down.shape),
    )


def solution(mesh):
    placed = (
        P("expert", None),
        P("expert"),
        P("expert", None),
        P(),
        P("tensor", None),
        P("tensor", None),
        P(None, "tensor"),
        P(None, "tensor"),
        P(None, "tensor"),
        P("tensor", None),
        P(),
        P(),
        P("expert", None, "tensor"),
        P("expert", None, "tensor"),
        P("expert", "tensor", None),
        P("expert", None),
    )
    return jax.shard_map(
        functools.partial(body, mesh.shape["expert"], mesh.shape["tensor"]),
        mesh=mesh,
        in_specs=placed,
        out_specs=(
            P("expert", None),
            P("expert", None),
            P("expert"),
            P("tensor", "expert"),
            P("tensor", "expert"),
            P("expert", "tensor"),
            P("expert", "tensor"),
            P("expert", "tensor"),
            P("tensor", "expert"),
            P("expert"),
            P("expert", None),
            P("expert", None, "tensor"),
            P("expert", None, "tensor"),
            P("expert", "tensor", None),
        ),
        check_vma=False,
    )
```
